32 devices in a mesh: grp: 4 (over y, x), tok: 8 (over z, core).
Axes of the slice: x: 2, y: 2, z: 4, core: 2. Of those that a mesh axis runs over, the one named last changes fastest.
Arguments:
- patches: bfloat16 [32768, 1152], P(('grp', 'tok')), may hold values from -6 to 6
- labels: int32 [32768], P(('grp', 'tok')), may hold values from 0 to 149
- valid_mask: int32 [32768], P(('grp', 'tok')), may hold values from 0 to 1
- crop_counts: int32 [4, 2], P('grp'), may hold values from 31 to 53, as said below
- owners: int32 [13], replicated, may hold values from 0 to 7, as said below
- slot_weight: float32 [16, 409600], P('tok', 'grp')
- slot_moment: float32 [16, 409600], P('tok', 'grp'), may hold values from -0.00048828125 to 0.00048828125
- slot_second: float32 [16, 409600], P('tok', 'grp'), may hold values from 6.1035155e-10 to 2.4414062e-09
- norm_params: float32 [22, 320], replicated
- norm_moment: float32 [22, 320], replicated, may hold values from -0.00048828125 to 0.00048828125
- norm_second: float32 [22, 320], replicated
- head_weight: float32 [320, 150], replicated, may hold values from -0.625 to 0.625
- head_moment: float32 [320, 150], replicated, may hold values from -0.00048828125 to 0.00048828125
- head_second: float32 [320, 150], replicated
Outputs:
- loss_sum: float32 [], replicated
- pixel_total: float32 [], replicated
- new_slot_moment: float32 [16, 409600], P('tok', 'grp')
- new_slot_second: float32 [16, 409600], P('tok', 'grp')
- new_slot_weight: float32 [16, 409600], P('tok', 'grp')
- new_norm_moment: float32 [22, 320], replicated
- new_norm_second: float32 [22, 320], replicated
- new_norm_params: float32 [22, 320], replicated
- new_head_moment: float32 [320, 150], replicated
- new_head_second: float32 [320, 150], replicated
- new_head_weight: float32 [320, 150], replicated
The draws below stay inside these ranges and needn't reach their ends.
Inputs may be any that keep to these rules, and one draw needn't show every extreme that they name: `owners`: each owner holds at most 2 units, and some owner holds exactly 2. `crop_counts`: A group's large crops number 32 to 36; its small crops fill the rest, leaving fewer than 6^2 padding tokens.
All inputs are finite; a program needn't handle non-finite values.
Results may differ from the reference program's by a relative error of at most 0.02.
The reference program's roundings to bfloat16 on the way count: a program that leaves them out, or rounds other values in their place, can miss the bound.
Values may be sent and summed in bfloat16 or wider, within the bound.
A program may use at most 960 MiB of HBM per device.

```python
import math
import jax
import jax.numpy as jnp
from jax import lax

C = 320
HEADS = 5
HD = 64
FF = 1280
PIN = 1152
CLASSES = 150
BLOCKS = 3
BIG_SIDE = 14
SMALL_SIDE = 6
MOST = 2
STEP = 10
TOK_DEV = 1024
GROUP_TOK = 8192
TOKENS = 32768
BIG_LO = 32
BIG_HI = 36
KVH = 49
HALO = 32
UNIT = 409600
NUNIT = 13
SLOTS = 16
NORM_ROWS = 22
N_GRP = 4
N_TOK = 8


def owner_table(key):
    pair_key, perm_key = jax.random.split(key)
    holders = jax.random.permutation(perm_key, N_TOK).astype(jnp.int32)
    top_at = jnp.argmax((holders == N_TOK - 1).astype(jnp.int32))
    holders = holders.at[top_at].set(holders[0]).at[0].set(N_TOK - 1)
    low_at = jnp.argmax((holders == 0).astype(jnp.int32))
    holders = holders.at[low_at].set(holders[1]).at[1].set(0)
    pairing = jax.random.permutation(pair_key, NUNIT) // MOST
    return holders[pairing].astype(jnp.int32)


def draw_owners(key, part):
    holders = owner_table(key)
    return holders


def draw_slot_weight(key, part):
    holders = owner_table(key)
    key = jax.random.fold_in(key, 12)
    unit_order = jnp.arange(NUNIT)
    same_owner = holders[:, None] == holders[None, :]
    rank_of = jnp.sum(same_owner & (unit_order[None, :] < unit_order[:, None]), 1)
    slot_of = holders * MOST + rank_of
    slot_ids = jnp.arange(SLOTS)
    matches = (slot_of[None, :] == slot_ids[:, None]).astype(jnp.int32)
    unit_of = jnp.sum(matches * unit_order[None, :], 1) - (1 - jnp.sum(matches, 1))
    kind_of = jnp.where(unit_of <= 0, unit_of, (unit_of - 1) % 4 + 1)[:, None]
    spot = jnp.arange(C * FF)[None, :]
    width_inv = C ** (-0.5)
    first_scale = jnp.where(spot < PIN * C, PIN ** (-0.5), jnp.where(spot < PIN * C + BLOCKS * 9 * FF, 1.0 / 3.0, 0.05))
    attn_scale = jnp.where(spot < C * C, width_inv, jnp.where(spot < 2 * C * C, 4.0 * width_inv, width_inv))
    scale_all = jnp.where(kind_of == 0, first_scale, jnp.where(kind_of == 1, attn_scale, jnp.where(kind_of == 2, (4 * C) ** (-0.5), jnp.where(kind_of == 4, 2.0 * FF ** (-0.5), width_inv))))
    return jax.random.normal(key, (SLOTS, C * FF), jnp.float32) * scale_all


def draw_valid_mask(key, part):
    key = jax.random.fold_in(key, 13)
    token_at = jnp.arange(TOKENS)
    within = token_at % GROUP_TOK
    group_of = token_at // GROUP_TOK
    offset = within % TOK_DEV
    lower_gap = jnp.where(within >= TOK_DEV, offset, TOK_DEV)
    upper_gap = jnp.where(within < GROUP_TOK - TOK_DEV, TOK_DEV - 1 - offset, TOK_DEV)
    near_cut = jnp.minimum(lower_gap, upper_gap) < HALO
    rise = 1000 + 1000 * within // GROUP_TOK + 1000 * group_of // max(N_GRP - 1, 1)
    threshold = jnp.where(near_cut, 300 * rise // 1000, 15 * rise // 1000)
    return (jax.random.randint(key, (TOKENS,), 0, 1000) < threshold).astype(jnp.int32)


def draw_crop_counts(key, part):
    key = jax.random.fold_in(key, 14)
    big_tok = BIG_SIDE * BIG_SIDE
    small_tok = SMALL_SIDE * SMALL_SIDE
    bigs = jax.random.randint(key, (N_GRP,), BIG_LO, BIG_HI + 1)
    bigs = jnp.where(jnp.arange(N_GRP) == 0, BIG_LO, bigs)
    smalls = (GROUP_TOK - bigs * big_tok) // small_tok
    return jnp.stack([bigs, smalls], 1).astype(jnp.int32)


def draw_norm_params(key, part):
    key = jax.random.fold_in(key, 15)
    row_at = jnp.arange(NORM_ROWS)[:, None]
    gain_part = jax.random.uniform(key, (NORM_ROWS, C), jnp.float32, 0.6, 1.6)
    shift_part = 0.3 * jax.random.normal(jax.random.fold_in(key, 1), (NORM_ROWS, C), jnp.float32)
    return jnp.where(row_at % 2 == 0, gain_part, shift_part)


def spread_states(key, shape, lowest, factor):
    fraction = jax.random.uniform(key, shape, jnp.float32)
    return lowest * jnp.exp(fraction * math.log(factor))


def draw_norm_second(key, part):
    key = jax.random.fold_in(key, 16)
    base_level = (TOKENS // 2) ** (-1.0)
    return spread_states(key, (NORM_ROWS, C), 8.9e-07 * base_level, 16.0)


def draw_head_second(key, part):
    key = jax.random.fold_in(key, 17)
    base_level = (TOKENS // 2) ** (-1.0)
    return spread_states(key, (C, CLASSES), 8.9e-07 * base_level, 16.0)


def set_ends(entries, own_key, low, high):
    dims = entries.shape
    index_at = [jax.random.randint(jax.random.fold_in(own_key, axis), (), 0, dims[axis]) for axis in range(len(dims))]
    entries = entries.at[tuple(index_at)].set(low)
    longest = dims.index(max(dims))
    index_at[longest] = (index_at[longest] + 1) % dims[longest]
    return entries.at[tuple(index_at)].set(high)


def level_of(own_key, extent, shards, least, largest):
    level = 1.0
    for position, shards_of in shards:
        heights = jax.random.uniform(jax.random.fold_in(jax.random.fold_in(own_key, 6), position), (shards_of,), jnp.float32, least / len(shards), largest / len(shards))
        level = level * jnp.repeat(jnp.exp(heights), extent[position] // shards_of).reshape((-1,) + (1,) * (len(extent) - 1 - position))
    return level


def gaussian(own_key, dims, scale, reach, cuts=(), kind=jnp.bfloat16):
    loudness = level_of(own_key, dims, cuts, -0.22, 0.18) if cuts else 1.0
    array = jax.random.normal(own_key, dims, jnp.float32) * scale * loudness
    return jnp.minimum(jnp.maximum(array, -reach), reach).astype(kind)


def setup_inputs(seed: int = 0) -> dict:
    key_list = jax.random.split(jax.random.key(seed), 15)
    patches = gaussian(key_list[0], (TOKENS, PIN), 1.0, 6.0, ((0, 32),))
    labels = set_ends(jax.random.randint(key_list[1], (TOKENS,), 0, CLASSES), jax.random.fold_in(key_list[1], 1), 0, CLASSES - 1).astype(jnp.int32)
    valid_mask = draw_valid_mask(jax.random.fold_in(key_list[14], 71), 0)
    crop_counts = draw_crop_counts(jax.random.fold_in(key_list[14], 71), 0)
    owners = draw_owners(jax.random.fold_in(key_list[14], 71), 0)
    slot_weight = draw_slot_weight(jax.random.fold_in(key_list[14], 71), 0)
    slot_moment = gaussian(key_list[6], (SLOTS, UNIT), (0.011 * (TOKENS // 2) ** -0.5), 0.00048828125, ((0, 8), (1, 4)), jnp.float32)
    slot_second = jnp.clip(jnp.exp(math.log(2.4414061883248905e-09) - 1.3862944 * jax.random.uniform(key_list[7], (SLOTS, UNIT), jnp.float32) ** level_of(key_list[7], (SLOTS, UNIT), ((0, 8), (1, 4)), -0.2, 0.2)), 6.103515470812226e-10, 2.4414061883248905e-09)
    norm_params = draw_norm_params(jax.random.fold_in(key_list[14], 71), 0)
    norm_moment = gaussian(key_list[9], (NORM_ROWS, C), (0.011 * (TOKENS // 2) ** -0.5), 0.00048828125, (), jnp.float32)
    norm_second = draw_norm_second(jax.random.fold_in(key_list[14], 71), 0)
    head_weight = gaussian(key_list[11], (C, CLASSES), (C // 4) ** -0.5, 0.625, (), jnp.float32)
    head_moment = gaussian(key_list[12], (C, CLASSES), (0.011 * (TOKENS // 2) ** -0.5), 0.00048828125, (), jnp.float32)
    head_second = draw_head_second(jax.random.fold_in(key_list[14], 71), 0)
    return dict(patches=patches, labels=labels, valid_mask=valid_mask, crop_counts=crop_counts, owners=owners, slot_weight=slot_weight, slot_moment=slot_moment, slot_second=slot_second, norm_params=norm_params, norm_moment=norm_moment, norm_second=norm_second, head_weight=head_weight, head_moment=head_moment, head_second=head_second)


EPS_NORM = 1e-06
BETA_ONE = 0.9
BETA_TWO = 0.999
ADAM_EPS = 1e-08
RATE_MATRIX = 0.05
RATE_VECTOR = 0.3
DECAY_RATE = 0.05
NEG_FILL = -1e+30
PREC_HIGH = lax.Precision.HIGHEST

@jax.custom_vjp
def low(v):
    return lax.optimization_barrier(v.astype(jnp.bfloat16)).astype(jnp.float32)

@jax.custom_vjp
def low_back(v):
    return v

def low_keep(v):
    return (low(v), None)

def low_pass(kept, grad):
    return (grad,)

def back_keep(v):
    return (v, None)

def back_low(kept, grad):
    return (low(grad),)
low.defvjp(low_keep, low_pass)
low_back.defvjp(back_keep, back_low)

def rounded(values):
    return low_back(low(values))

def layer_norm(values, gain_vec, shift_vec):
    center = values - lax.optimization_barrier(jnp.mean(values, -1, keepdims=True))
    inverse = lax.rsqrt(lax.optimization_barrier(jnp.mean(center * center, -1, keepdims=True)) + EPS_NORM)
    return center * inverse * gain_vec + shift_vec

def gelu_exact(values):
    return jax.nn.gelu(values, approximate=False)

def image_layout(positions, counts):
    big_tok = BIG_SIDE * BIG_SIDE
    small_tok = SMALL_SIDE * SMALL_SIDE
    big_end = counts[0] * big_tok
    small_end = big_end + counts[1] * small_tok
    is_big = positions < big_end
    is_small = jnp.logical_and(positions >= big_end, positions < small_end)
    side_len = jnp.where(is_big, BIG_SIDE, jnp.where(is_small, SMALL_SIDE, 0))
    begin_at = jnp.where(is_big, positions // big_tok * big_tok, jnp.where(is_small, big_end + (positions - big_end) // small_tok * small_tok, small_end))
    image_id = jnp.where(is_big, positions // big_tok, jnp.where(is_small, counts[0] + (positions - big_end) // small_tok, counts[0] + counts[1]))
    half_side = jnp.maximum(side_len // 2, 1)
    within = positions - begin_at
    tile_idx = within // 4
    sub_idx = within % 4
    row_pos = tile_idx // half_side * 2 + sub_idx // 2
    col_pos = tile_idx % half_side * 2 + sub_idx % 2
    neighbours = []
    for shift_y in (-1, 0, 1):
        for shift_x in (-1, 0, 1):
            row_at = row_pos + shift_y
            col_at = col_pos + shift_x
            inside = (row_at >= 0) & (row_at < side_len) & (col_at >= 0) & (col_at < side_len)
            if shift_y == 0 and shift_x == 0:
                inside = jnp.ones_like(inside)
            target = begin_at + (row_at // 2 * half_side + col_at // 2) * 4 + row_at % 2 * 2 + col_at % 2
            neighbours.append(jnp.where(inside, target, -1))
    return (image_id.astype(jnp.int32), jnp.stack(neighbours, 1).astype(jnp.int32), positions < small_end)

def depthwise(values, neighbours, kernel):
    result = jnp.zeros((neighbours.shape[0], values.shape[1]), jnp.float32)
    for offset in range(9):
        column = neighbours[:, offset]
        picked = jnp.take(values, jnp.maximum(column, 0), axis=0).astype(jnp.float32)
        result = result + jnp.where((column >= 0)[:, None], picked, 0.0) * kernel[offset].astype(jnp.float32)
    return result

def unpack(unit_rows):
    embedding = unit_rows[0, :PIN * C].reshape(PIN, C)
    kernels = unit_rows[0, PIN * C:PIN * C + BLOCKS * 9 * FF].reshape(BLOCKS, 9, FF)
    layers = []
    for layer_at in range(BLOCKS):
        anchor = 1 + 4 * layer_at
        layers.append((unit_rows[anchor, :C * C].reshape(C, C), unit_rows[anchor, C * C:2 * C * C].reshape(C, C), unit_rows[anchor, 2 * C * C:].reshape(C, 2 * C), unit_rows[anchor + 1].reshape(4 * C, C), unit_rows[anchor + 2].reshape(C, FF), unit_rows[anchor + 3].reshape(FF, C)))
    return (embedding, kernels, layers)

def adamw_step(weight, moment, second, gradient, rate_now, decay_now):
    moment = BETA_ONE * moment + (1.0 - BETA_ONE) * gradient
    second = BETA_TWO * second + (1.0 - BETA_TWO) * gradient * gradient
    m_hat = moment / (1.0 - BETA_ONE ** STEP)
    v_hat = second / (1.0 - BETA_TWO ** STEP)
    weight = weight - rate_now * (m_hat / (jnp.sqrt(v_hat) + ADAM_EPS) + decay_now * weight)
    return (moment, second, weight)

def attend(queries, keyval, image_id, kv_id):
    rows_all = queries.shape[0]
    block_rows = min(512, rows_all)
    quarter = block_rows // 4
    span_rows = quarter + 2 * KVH
    score_scale = HD ** (-0.5)
    padded = jnp.pad(keyval, ((KVH, KVH), (0, 0)))
    padded_id = jnp.pad(kv_id, (KVH, KVH), constant_values=-7)

    def one_block(block_index):
        q_block = lax.dynamic_slice_in_dim(queries, block_index * block_rows, block_rows, 0).reshape(block_rows, HEADS, HD)
        kv_block = lax.dynamic_slice_in_dim(padded, block_index * quarter, span_rows, 0)
        keys_blk = kv_block[:, :C].reshape(span_rows, HEADS, HD)
        vals_blk = kv_block[:, C:].reshape(span_rows, HEADS, HD)
        allowed = lax.dynamic_slice_in_dim(image_id, block_index * block_rows, block_rows, 0)[:, None] == lax.dynamic_slice_in_dim(padded_id, block_index * quarter, span_rows, 0)[None, :]
        raw_scores = low_back(jnp.einsum('qhd,khd->hqk', q_block, keys_blk, precision=PREC_HIGH))
        scores = raw_scores * score_scale + jnp.where(allowed, 0.0, NEG_FILL)
        probs_low = low(jax.nn.softmax(scores, -1))
        return jnp.einsum('hqk,khd->qhd', probs_low, vals_blk, precision=PREC_HIGH).reshape(block_rows, C)
    return lax.map(jax.checkpoint(one_block), jnp.arange(rows_all // block_rows)).reshape(rows_all, C)

def group_loss(unit_rows, norm_params, head_weight, patches, labels, keep_mask, counts):
    embedding, kernels, layers = unpack(low(unit_rows))
    positions = jnp.arange(patches.shape[0], dtype=jnp.int32)
    image_id, neighbours, is_real = image_layout(positions, counts)
    kv_id = image_id[::4]
    tail = 6 * BLOCKS
    resid = low_back(jnp.dot(patches, embedding, precision=PREC_HIGH))
    resid = layer_norm(resid, norm_params[tail], norm_params[tail + 1])
    for layer_at in range(BLOCKS):
        w_query, w_out, w_keyval, w_reduce, w_up, w_down = layers[layer_at]
        gain_rows = norm_params[6 * layer_at:6 * layer_at + 6]
        normed_in = low(layer_norm(resid, gain_rows[0], gain_rows[1]))
        queries = rounded(jnp.dot(normed_in, w_query, precision=PREC_HIGH))
        reduced = low_back(jnp.dot(normed_in.reshape(-1, 4 * C), w_reduce, precision=PREC_HIGH))
        normed_kv = low(layer_norm(reduced, gain_rows[2], gain_rows[3]))
        keyval = rounded(jnp.dot(normed_kv, w_keyval, precision=PREC_HIGH))
        attended = rounded(attend(queries, keyval, image_id, kv_id))
        resid = resid + low_back(jnp.dot(attended, w_out, precision=PREC_HIGH))
        normed_mlp = low(layer_norm(resid, gain_rows[4], gain_rows[5]))
        hidden = rounded(jnp.dot(normed_mlp, w_up, precision=PREC_HIGH))
        active = rounded(gelu_exact(depthwise(hidden, neighbours, kernels[layer_at])))
        resid = resid + low_back(jnp.dot(active, w_down, precision=PREC_HIGH))
    final = low(layer_norm(resid, norm_params[tail + 2], norm_params[tail + 3]))
    logits = low_back(jnp.dot(final, low(head_weight), precision=PREC_HIGH))
    picked = jnp.take_along_axis(logits, labels[:, None], 1)[:, 0]
    return jnp.sum((jax.nn.logsumexp(logits, -1) - picked) * keep_mask)

def reference(patches, labels, valid_mask, crop_counts, owners, slot_weight, slot_moment, slot_second, norm_params, norm_moment, norm_second, head_weight, head_moment, head_second):
    unit_order = jnp.arange(NUNIT, dtype=jnp.int32)
    same_owner = owners[:, None] == owners[None, :]
    rank_of = lax.optimization_barrier(jnp.sum(same_owner & (unit_order[None, :] < unit_order[:, None]), 1)).astype(jnp.int32)
    slot_of = owners * MOST + rank_of
    unit_rows = jnp.take(slot_weight, slot_of, axis=0)
    positions = jnp.arange(GROUP_TOK, dtype=jnp.int32)
    is_real = jax.vmap(lambda counts: image_layout(positions, counts)[2])(crop_counts)
    keep_mask = (valid_mask.reshape(N_GRP, GROUP_TOK) * is_real.astype(jnp.int32)).astype(jnp.float32)
    pixel_total = jnp.sum(keep_mask)
    patch_groups = patches.astype(jnp.float32).reshape(N_GRP, GROUP_TOK, PIN)
    label_groups = labels.reshape(N_GRP, GROUP_TOK)

    def loss_of(unit_vals, norm_vals, head_vals):
        checked = jax.checkpoint(group_loss)

        def group_step(carry, group_data):
            return (carry + checked(unit_vals, norm_vals, head_vals, *group_data), None)
        loss_total, _ = lax.scan(group_step, jnp.zeros((), jnp.float32), (patch_groups, label_groups, keep_mask, crop_counts))
        return loss_total
    loss_sum, pull_back = jax.vjp(loss_of, unit_rows, norm_params, head_weight)
    grad_units, grad_norms, grad_head = pull_back(1.0 / pixel_total)
    grad_slots = jnp.zeros_like(slot_weight).at[slot_of].set(grad_units)
    slot_m, slot_v, slot_w = adamw_step(slot_weight, slot_moment, slot_second, grad_slots, RATE_MATRIX, DECAY_RATE)
    norm_m, norm_v, norm_w = adamw_step(norm_params, norm_moment, norm_second, grad_norms, RATE_VECTOR, 0.0)
    head_m, head_v, head_w = adamw_step(head_weight, head_moment, head_second, grad_head, RATE_MATRIX, DECAY_RATE)
    return (loss_sum, pixel_total, slot_m, slot_v, slot_w, norm_m, norm_v, norm_w, head_m, head_v, head_w)
```

```python
import jax
import jax.numpy as jnp
from jax import lax
from jax.sharding import PartitionSpec as P

C = 320
HEADS = 5
HD = 64
FF = 1280
PIN = 1152
BLOCKS = 3
BIG_SIDE = 14
SMALL_SIDE = 6
STEP = 10
KVH = 49


EPS_NORM = 1e-06
BETA_ONE = 0.9
BETA_TWO = 0.999
ADAM_EPS = 1e-08
RATE_MATRIX = 0.05
RATE_VECTOR = 0.3
DECAY_RATE = 0.05
NEG_FILL = -1e30
PREC_HIGH = lax.Precision.HIGHEST


def layer_norm(values, gain_vec, shift_vec):
    center = values - jnp.mean(values, -1, keepdims=True)
    inverse = lax.rsqrt(jnp.mean(center * center, -1, keepdims=True) + EPS_NORM)
    return center * inverse * gain_vec + shift_vec


def gelu_exact(values):
    return jax.nn.gelu(values, approximate=False)


def adamw_step(weight, moment, second, gradient, rate_now, decay_now):
    moment = BETA_ONE * moment + (1.0 - BETA_ONE) * gradient
    second = BETA_TWO * second + (1.0 - BETA_TWO) * gradient * gradient
    m_hat = moment / (1.0 - BETA_ONE**STEP)
    v_hat = second / (1.0 - BETA_TWO**STEP)
    weight = weight - rate_now * (m_hat / (jnp.sqrt(v_hat) + ADAM_EPS) + decay_now * weight)
    return (moment, second, weight)


def product(left, right):
    return jnp.dot(left, right, preferred_element_type=jnp.float32)


def outer_sum(left, right):
    return lax.dot_general(
        left, right, (((0,), (0,)), ((), ())), preferred_element_type=jnp.float32
    )


def back_product(gradient, weight):
    return lax.dot_general(
        gradient, weight, (((1,), (1,)), ((), ())), preferred_element_type=jnp.float32
    )


def norm_back(values, gain_vec, shift_vec, gradient):
    _, pull_back = jax.vjp(layer_norm, values, gain_vec, shift_vec)
    return pull_back(gradient)


OVER = 4 * KVH - 4


def image_layout(positions, counts):
    big_tok = BIG_SIDE * BIG_SIDE
    small_tok = SMALL_SIDE * SMALL_SIDE
    big_end = counts[0] * big_tok
    small_end = big_end + counts[1] * small_tok
    is_big = positions < big_end
    is_small = jnp.logical_and(positions >= big_end, positions < small_end)
    half_side = jnp.where(is_big, BIG_SIDE // 2, SMALL_SIDE // 2)
    begin_at = jnp.where(
        is_big,
        positions // big_tok * big_tok,
        jnp.where(is_small, big_end + (positions - big_end) // small_tok * small_tok, small_end),
    )
    tile_idx = (positions - begin_at) // 4
    return (begin_at, half_side, tile_idx // half_side, tile_idx % half_side, positions < small_end)


def shift_matrices(begin_at, half_side, tile_y, tile_x, is_real):
    count = begin_at.shape[0]
    own = jnp.arange(count, dtype=jnp.int32)
    offset = own[None, :] - own[:, None]
    inside = {
        (0, -1): tile_x > 0,
        (0, 1): tile_x < half_side - 1,
        (-1, 0): tile_y > 0,
        (1, 0): tile_y < half_side - 1,
    }
    result = {}
    for step_y in (-1, 0, 1):
        for step_x in (-1, 0, 1):
            if step_y == 0 and step_x == 0:
                continue
            allowed = is_real
            if step_y:
                allowed = allowed & inside[step_y, 0]
            if step_x:
                allowed = allowed & inside[0, step_x]
            hit = (offset == (step_y * half_side + step_x)[:, None]) & allowed[:, None]
            result[step_y, step_x] = hit.astype(jnp.bfloat16)
    return result


def tap_source(sub, tap):
    y_at = sub // 2 + tap // 3 - 1
    x_at = sub % 2 + tap % 3 - 1
    return (y_at % 2 * 2 + x_at % 2, y_at // 2, x_at // 2)


def shifted_planes(planes, shifts):
    moved = {}
    for sub in range(4):
        step_y = 1 - 2 * (sub // 2)
        step_x = 1 - 2 * (sub % 2)
        moved[sub, 0, 0] = planes[sub]
        for key in ((0, step_x), (step_y, 0), (step_y, step_x)):
            moved[(sub,) + key] = product(shifts[key], planes[sub]).astype(jnp.bfloat16)
    return moved


def depthwise(moved, kernel, is_real):
    rows = []
    for sub in range(4):
        center = moved[sub, 0, 0].astype(jnp.float32) * kernel[4]
        total = center
        for tap in range(9):
            if tap != 4:
                total = total + moved[tap_source(sub, tap)].astype(jnp.float32) * kernel[tap]
        rows.append(jnp.where(is_real[:, None], total, center))
    return jnp.stack(rows)


def kernel_grad(moved, hidden):
    taps = []
    for tap in range(9):
        total = 0.0
        for sub in range(4):
            total = total + hidden[sub].astype(jnp.float32) * moved[tap_source(sub, tap)].astype(jnp.float32)
        taps.append(jnp.sum(total, 0))
    return jnp.stack(taps[::-1])


def split_heads(values):
    return values.reshape(values.shape[0], HEADS, HD)


def attend_scores(queries, keyval, allowed):
    scores = jnp.einsum(
        "qhd,khd->hqk", split_heads(queries), split_heads(keyval[:, :C]), preferred_element_type=jnp.float32
    ) * HD ** (-0.5)
    scores = scores + jnp.where(allowed, 0.0, NEG_FILL)
    weights = jnp.exp(scores - jnp.max(scores, -1, keepdims=True))
    return weights / jnp.sum(weights, -1, keepdims=True)


def attend_forward(queries, keyval, allowed):
    probs = attend_scores(queries, keyval, allowed).astype(jnp.bfloat16)
    output = jnp.einsum("hqk,khd->qhd", probs, split_heads(keyval[:, C:]), preferred_element_type=jnp.float32)
    return output.reshape(queries.shape).astype(jnp.bfloat16)


def attend_backward(grad_out, queries, keyval, allowed):
    probs = attend_scores(queries, keyval, allowed)
    g_heads = split_heads(grad_out)
    grad_probs = jnp.einsum(
        "qhd,khd->hqk", g_heads, split_heads(keyval[:, C:]), preferred_element_type=jnp.float32
    )
    inner = jnp.sum(probs * grad_probs, -1, keepdims=True)
    grad_scores = (probs * (grad_probs - inner) * HD ** (-0.5)).astype(jnp.bfloat16)
    grad_q = jnp.einsum(
        "hqk,khd->qhd", grad_scores, split_heads(keyval[:, :C]), preferred_element_type=jnp.float32
    )
    grad_k = jnp.einsum("hqk,qhd->khd", grad_scores, split_heads(queries), preferred_element_type=jnp.float32)
    grad_v = jnp.einsum(
        "hqk,qhd->khd", probs.astype(jnp.bfloat16), g_heads, preferred_element_type=jnp.float32
    )
    rows = keyval.shape[0]
    return (
        grad_q.reshape(queries.shape).astype(jnp.bfloat16),
        jnp.concatenate([grad_k.reshape(rows, C), grad_v.reshape(rows, C)], 1).astype(jnp.bfloat16),
    )


def beside(values):
    tiles = values.shape[0] // 4
    return jnp.concatenate([values[sub * tiles : (sub + 1) * tiles] for sub in range(4)], 1)


def unbeside(values):
    return jnp.concatenate([values[:, sub * C : (sub + 1) * C] for sub in range(4)], 0)


def layer_forward(resid, weights, kernel, gain_rows, context):
    w_query, w_out, w_keyval, w_reduce, w_up, w_down = weights
    allowed, shifts, is_real = context
    normed_in = layer_norm(resid, gain_rows[0], gain_rows[1]).astype(jnp.bfloat16)
    queries = product(normed_in, w_query).astype(jnp.bfloat16)
    grouped = beside(normed_in)
    reduced = product(grouped, w_reduce)
    normed_kv = layer_norm(reduced, gain_rows[2], gain_rows[3]).astype(jnp.bfloat16)
    keyval = product(normed_kv, w_keyval).astype(jnp.bfloat16)
    attended = attend_forward(queries, keyval, allowed)
    middle = resid + product(attended, w_out)
    normed_mlp = layer_norm(middle, gain_rows[4], gain_rows[5]).astype(jnp.bfloat16)
    hidden = product(normed_mlp, w_up).astype(jnp.bfloat16)
    planes = hidden.reshape(4, -1, FF)
    mixed = depthwise(shifted_planes(planes, shifts), kernel, is_real).reshape(hidden.shape)
    active = gelu_exact(mixed).astype(jnp.bfloat16)
    output = middle + product(active, w_down)
    kept = (resid, normed_in, queries, grouped, reduced, normed_kv, keyval, attended, middle, normed_mlp, hidden, mixed, active)
    return (output, kept)


def layer_backward(grad_res, kept, weights, kernel, gain_rows, context):
    w_query, w_out, w_keyval, w_reduce, w_up, w_down = weights
    allowed, shifts, is_real = context
    resid, normed_in, queries, grouped, reduced, normed_kv, keyval, attended, middle, normed_mlp, hidden, mixed, active = kept
    grad_low = grad_res.astype(jnp.bfloat16)
    d_down = outer_sum(active, grad_low)
    d_active = back_product(grad_low, w_down).astype(jnp.bfloat16)
    d_mixed = jax.vjp(gelu_exact, mixed)[1](d_active.astype(jnp.float32))[0]
    moved = shifted_planes(d_mixed.astype(jnp.bfloat16).reshape(4, -1, FF), shifts)
    d_hidden = depthwise(moved, kernel[::-1], is_real).astype(jnp.bfloat16).reshape(hidden.shape)
    d_kernel = kernel_grad(moved, hidden.reshape(4, -1, FF))
    d_up = outer_sum(normed_mlp, d_hidden)
    d_middle, gain_four, gain_five = norm_back(
        middle, gain_rows[4], gain_rows[5], back_product(d_hidden, w_up)
    )
    grad_res = grad_res + d_middle
    grad_low = grad_res.astype(jnp.bfloat16)
    d_out = outer_sum(attended, grad_low)
    d_attended = back_product(grad_low, w_out).astype(jnp.bfloat16)
    d_query, d_keyval = attend_backward(d_attended, queries, keyval, allowed)
    d_wkv = outer_sum(normed_kv, d_keyval)
    d_reduced, gain_two, gain_three = norm_back(
        reduced, gain_rows[2], gain_rows[3], back_product(d_keyval, w_keyval)
    )
    d_reduced = d_reduced.astype(jnp.bfloat16)
    d_reduce = outer_sum(grouped, d_reduced)
    d_grouped = unbeside(back_product(d_reduced, w_reduce))
    d_wq = outer_sum(normed_in, d_query)
    d_first = back_product(d_query, w_query) + d_grouped
    d_resid, gain_zero, gain_one = norm_back(resid, gain_rows[0], gain_rows[1], d_first)
    gain_grads = jnp.stack([gain_zero, gain_one, gain_two, gain_three, gain_four, gain_five])
    low = [part.astype(jnp.bfloat16) for part in (d_wq, d_out, d_wkv, d_reduce, d_up, d_down)]
    units = jnp.stack(
        [
            jnp.concatenate([low[0], low[1], low[2].reshape(-1, C)], 0),
            low[3],
            low[4].reshape(-1, C),
            low[5],
        ]
    )
    return (grad_res + d_resid, units, d_kernel, gain_grads)


BOTH = ("grp", "tok")


def body(
    patches,
    labels,
    valid_mask,
    crop_counts,
    owners,
    slot_weight,
    slot_moment,
    slot_second,
    norm_params,
    norm_moment,
    norm_second,
    head_weight,
    head_moment,
    head_second,
):
    tok_dev = patches.shape[0]
    n_tok = lax.axis_size("tok")
    n_grp = lax.axis_size("grp")
    tok_index = lax.axis_index("tok")
    group_tok = tok_dev * n_tok
    counts = crop_counts[0]
    n_unit = owners.shape[0]
    slot_rows, columns = slot_weight.shape
    unit_order = jnp.arange(n_unit, dtype=jnp.int32)
    same_owner = owners[:, None] == owners[None, :]
    rank_of = jnp.sum(same_owner & (unit_order[None, :] < unit_order[:, None]), 1)
    slot_of = owners * slot_rows + rank_of
    chunk = columns // n_tok // C
    pieces = slot_weight.astype(jnp.bfloat16).reshape(slot_rows, n_tok, chunk, C)
    pieces = lax.all_to_all(pieces, "tok", split_axis=1, concat_axis=0, tiled=True)
    unit_part = jnp.take(pieces.reshape(slot_rows * n_tok, chunk, C), slot_of, axis=0)
    first_unit = lax.all_gather(unit_part[0], BOTH, axis=0, tiled=True)
    embedding = first_unit[:PIN]
    kernels = first_unit[PIN : PIN + BLOCKS * 9 * FF // C].reshape(BLOCKS, 9, FF).astype(jnp.float32)
    layers = []
    for layer_at in range(BLOCKS):
        own = lax.all_gather(unit_part[1 + 4 * layer_at : 5 + 4 * layer_at], BOTH, axis=1, tiled=True)
        layers.append(
            (own[0, :C], own[0, C : 2 * C], own[0, 2 * C :].reshape(C, 2 * C), own[1], own[2].reshape(C, FF), own[3])
        )

    towards = [(i + 1, i) for i in range(n_tok - 1)]
    window = tok_dev + OVER
    tiles = window // 4
    patches = jnp.concatenate([patches, lax.ppermute(patches[:OVER], "tok", towards)], 0)
    marks = jnp.stack([labels, valid_mask])
    marks = jnp.concatenate([marks, lax.ppermute(marks[:, :OVER], "tok", towards)], 1)
    patches = patches.reshape(tiles, 4, PIN).transpose(1, 0, 2).reshape(window, PIN)
    marks = marks.reshape(2, tiles, 4).transpose(0, 2, 1).reshape(2, window)
    labels = marks[0]
    first_tok = tok_index * tok_dev
    positions = first_tok + 4 * jnp.arange(tiles, dtype=jnp.int32)
    begin_at, half_side, tile_y, tile_x, _ = image_layout(positions, counts)
    own_image = (begin_at >= first_tok) & (begin_at < first_tok + tok_dev) & (positions < group_tok)
    is_real = positions < counts[0] * BIG_SIDE**2 + counts[1] * SMALL_SIDE**2
    shifts = shift_matrices(begin_at, half_side, tile_y, tile_x, is_real)
    image_of = jnp.where(positions < group_tok, begin_at, -1)
    allowed = jnp.tile(image_of, 4)[:, None] == image_of[None, :]
    keep_mask = marks[1].astype(jnp.float32) * jnp.tile((own_image & is_real).astype(jnp.float32), 4)
    pixel_total = lax.psum(jnp.sum(keep_mask), BOTH)
    context = (allowed, shifts, is_real)
    tail = 6 * BLOCKS
    embed_pre = product(patches, embedding)
    resid = layer_norm(embed_pre, norm_params[tail], norm_params[tail + 1])
    kept_all = []
    for layer_at in range(BLOCKS):
        resid, kept_state = layer_forward(
            resid,
            layers[layer_at],
            kernels[layer_at],
            norm_params[6 * layer_at : 6 * layer_at + 6],
            context,
        )
        kept_all.append(kept_state)
    final = layer_norm(resid, norm_params[tail + 2], norm_params[tail + 3]).astype(jnp.bfloat16)
    head_low = head_weight.astype(jnp.bfloat16)
    logits = product(final, head_low)
    row_peak = jnp.max(logits, -1, keepdims=True)
    log_norm = row_peak[:, 0] + jnp.log(jnp.sum(jnp.exp(logits - row_peak), -1))
    onehot = (labels[:, None] == jnp.arange(head_weight.shape[1], dtype=jnp.int32)[None, :]).astype(
        jnp.float32
    )
    picked = jnp.sum(logits * onehot, 1)
    loss_local = jnp.sum((log_norm - picked) * keep_mask)
    probs = jnp.exp(logits - log_norm[:, None])
    d_logits = ((probs - onehot) * (keep_mask / pixel_total)[:, None]).astype(jnp.bfloat16)
    d_head = outer_sum(final, d_logits)
    grad_res, gain_final, shift_final = norm_back(
        resid, norm_params[tail + 2], norm_params[tail + 3], back_product(d_logits, head_low)
    )
    unit_grads = [None] * BLOCKS
    kernel_grads = [None] * BLOCKS
    gain_grads = [None] * BLOCKS
    for layer_at in reversed(range(BLOCKS)):
        grad_res, units, kernel_grads[layer_at], gain_grads[layer_at] = (
            layer_backward(
                grad_res,
                kept_all[layer_at],
                layers[layer_at],
                kernels[layer_at],
                norm_params[6 * layer_at : 6 * layer_at + 6],
                context,
            )
        )
        unit_grads[layer_at] = lax.psum_scatter(units, BOTH, scatter_dimension=1, tiled=True)
    d_embed_pre, gain_embed, shift_embed = norm_back(
        embed_pre, norm_params[tail], norm_params[tail + 1], grad_res
    )
    d_embedding = outer_sum(patches, d_embed_pre.astype(jnp.bfloat16))
    first_grad = jnp.concatenate(
        [
            d_embedding.astype(jnp.bfloat16),
            jnp.stack(kernel_grads).reshape(-1, C).astype(jnp.bfloat16),
            jnp.zeros((C * FF // C - PIN - BLOCKS * 9 * FF // C, C), jnp.bfloat16),
        ]
    )
    first_grad = lax.psum_scatter(first_grad, BOTH, scatter_dimension=0, tiled=True)
    stacked = jnp.concatenate([first_grad[None]] + unit_grads, 0)
    norm_grads = jnp.concatenate(
        gain_grads + [jnp.stack([gain_embed, shift_embed, gain_final, shift_final])], 0
    )
    row_ids = jnp.arange(slot_rows * n_tok, dtype=jnp.int32)
    matches = slot_of[None, :] == row_ids[:, None]
    unit_at = jnp.where(jnp.any(matches, 1), jnp.argmax(matches, 1), n_unit)
    padded = jnp.concatenate([stacked, jnp.zeros_like(stacked[:1])], 0)
    placed = jnp.take(padded, unit_at, axis=0)[:, None]
    owned = lax.all_to_all(placed, "tok", split_axis=0, concat_axis=1, tiled=True)
    owned = owned.astype(jnp.float32).reshape(slot_rows, columns)
    norm_total, head_total, loss_sum = lax.psum((norm_grads, d_head, loss_local), BOTH)
    slot_m, slot_v, slot_w = adamw_step(
        slot_weight, slot_moment, slot_second, owned, RATE_MATRIX, DECAY_RATE
    )
    norm_m, norm_v, norm_w = adamw_step(
        norm_params, norm_moment, norm_second, norm_total, RATE_VECTOR, 0.0
    )
    head_m, head_v, head_w = adamw_step(
        head_weight, head_moment, head_second, head_total, RATE_MATRIX, DECAY_RATE
    )
    return (
        loss_sum,
        pixel_total,
        slot_m,
        slot_v,
        slot_w,
        norm_m,
        norm_v,
        norm_w,
        head_m,
        head_v,
        head_w,
    )


def solution(mesh):
    in_specs = (
        P(("grp", "tok"), None),
        P(("grp", "tok")),
        P(("grp", "tok")),
        P("grp", None),
        P(),
        P("tok", "grp"),
        P("tok", "grp"),
        P("tok", "grp"),
        P(),
        P(),
        P(),
        P(),
        P(),
        P(),
    )
    out_specs = (
        P(),
        P(),
        P("tok", "grp"),
        P("tok", "grp"),
        P("tok", "grp"),
        P(),
        P(),
        P(),
        P(),
        P(),
        P(),
    )
    return jax.shard_map(body, mesh=mesh, in_specs=in_specs, out_specs=out_specs, check_vma=False)
```

```python
import jax
import jax.numpy as jnp
from jax import lax
from jax.sharding import PartitionSpec as P

C = 320
HEADS = 5
HD = 64
FF = 1280
PIN = 1152
BLOCKS = 3
BIG_SIDE = 14
SMALL_SIDE = 6
STEP = 10
KVH = 49


EPS_NORM = 1e-06
BETA_ONE = 0.9
BETA_TWO = 0.999
ADAM_EPS = 1e-08
RATE_MATRIX = 0.05
RATE_VECTOR = 0.3
DECAY_RATE = 0.05
NEG_FILL = -1e30
PREC_HIGH = lax.Precision.HIGHEST


def layer_norm(values, gain_vec, shift_vec):
    center = values - jnp.mean(values, -1, keepdims=True)
    inverse = lax.rsqrt(jnp.mean(center * center, -1, keepdims=True) + EPS_NORM)
    return center * inverse * gain_vec + shift_vec


def gelu_exact(values):
    return jax.nn.gelu(values, approximate=False)


def adamw_step(weight, moment, second, gradient, rate_now, decay_now):
    moment = BETA_ONE * moment + (1.0 - BETA_ONE) * gradient
    second = BETA_TWO * second + (1.0 - BETA_TWO) * gradient * gradient
    m_hat = moment / (1.0 - BETA_ONE**STEP)
    v_hat = second / (1.0 - BETA_TWO**STEP)
    weight = weight - rate_now * (m_hat / (jnp.sqrt(v_hat) + ADAM_EPS) + decay_now * weight)
    return (moment, second, weight)


def product(left, right):
    return jnp.dot(left, right, preferred_element_type=jnp.float32)


def outer_sum(left, right):
    return lax.dot_general(
        left, right, (((0,), (0,)), ((), ())), preferred_element_type=jnp.float32
    )


def back_product(gradient, weight):
    return lax.dot_general(
        gradient, weight, (((1,), (1,)), ((), ())), preferred_element_type=jnp.float32
    )


def norm_back(values, gain_vec, shift_vec, gradient):
    _, pull_back = jax.vjp(layer_norm, values, gain_vec, shift_vec)
    return pull_back(gradient)


OVER = 4 * KVH - 4


def image_layout(positions, counts):
    big_tok = BIG_SIDE * BIG_SIDE
    small_tok = SMALL_SIDE * SMALL_SIDE
    big_end = counts[0] * big_tok
    small_end = big_end + counts[1] * small_tok
    is_big = positions < big_end
    is_small = jnp.logical_and(positions >= big_end, positions < small_end)
    half_side = jnp.where(is_big, BIG_SIDE // 2, SMALL_SIDE // 2)
    begin_at = jnp.where(
        is_big,
        positions // big_tok * big_tok,
        jnp.where(is_small, big_end + (positions - big_end) // small_tok * small_tok, small_end),
    )
    tile_idx = (positions - begin_at) // 4
    return (begin_at, half_side, tile_idx // half_side, tile_idx % half_side, positions < small_end)


def shift_matrices(begin_at, half_side, tile_y, tile_x, is_real):
    count = begin_at.shape[0]
    own = jnp.arange(count, dtype=jnp.int32)
    offset = own[None, :] - own[:, None]
    inside = {
        (0, -1): tile_x > 0,
        (0, 1): tile_x < half_side - 1,
        (-1, 0): tile_y > 0,
        (1, 0): tile_y < half_side - 1,
    }
    result = {}
    for step_y in (-1, 0, 1):
        for step_x in (-1, 0, 1):
            if step_y == 0 and step_x == 0:
                continue
            allowed = is_real
            if step_y:
                allowed = allowed & inside[step_y, 0]
            if step_x:
                allowed = allowed & inside[0, step_x]
            hit = (offset == (step_y * half_side + step_x)[:, None]) & allowed[:, None]
            result[step_y, step_x] = hit.astype(jnp.bfloat16)
    return result


def tap_source(sub, tap):
    y_at = sub // 2 + tap // 3 - 1
    x_at = sub % 2 + tap % 3 - 1
    return (y_at % 2 * 2 + x_at % 2, y_at // 2, x_at // 2)


def shifted_planes(planes, shifts):
    moved = {}
    for sub in range(4):
        step_y = 1 - 2 * (sub // 2)
        step_x = 1 - 2 * (sub % 2)
        moved[sub, 0, 0] = planes[sub]
        for key in ((0, step_x), (step_y, 0), (step_y, step_x)):
            moved[(sub,) + key] = product(shifts[key], planes[sub]).astype(jnp.bfloat16)
    return moved


def depthwise(moved, kernel, is_real):
    rows = []
    for sub in range(4):
        center = moved[sub, 0, 0].astype(jnp.float32) * kernel[4]
        total = center
        for tap in range(9):
            if tap != 4:
                total = total + moved[tap_source(sub, tap)].astype(jnp.float32) * kernel[tap]
        rows.append(jnp.where(is_real[:, None], total, center))
    return jnp.stack(rows)


def kernel_grad(moved, hidden):
    taps = []
    for tap in range(9):
        total = 0.0
        for sub in range(4):
            total = total + hidden[sub].astype(jnp.float32) * moved[tap_source(sub, tap)].astype(jnp.float32)
        taps.append(jnp.sum(total, 0))
    return jnp.stack(taps[::-1])


def split_heads(values):
    return values.reshape(values.shape[0], HEADS, HD)


def attend_scores(queries, keyval, allowed):
    scores = jnp.einsum(
        "qhd,khd->hqk", split_heads(queries), split_heads(keyval[:, :C]), preferred_element_type=jnp.float32
    ) * HD ** (-0.5)
    scores = scores + jnp.where(allowed, 0.0, NEG_FILL)
    weights = jnp.exp(scores - jnp.max(scores, -1, keepdims=True))
    return weights / jnp.sum(weights, -1, keepdims=True)


def attend_forward(queries, keyval, allowed):
    probs = attend_scores(queries, keyval, allowed).astype(jnp.bfloat16)
    output = jnp.einsum("hqk,khd->qhd", probs, split_heads(keyval[:, C:]), preferred_element_type=jnp.float32)
    return output.reshape(queries.shape).astype(jnp.bfloat16)


def attend_backward(grad_out, queries, keyval, allowed):
    probs = attend_scores(queries, keyval, allowed)
    g_heads = split_heads(grad_out)
    grad_probs = jnp.einsum(
        "qhd,khd->hqk", g_heads, split_heads(keyval[:, C:]), preferred_element_type=jnp.float32
    )
    inner = jnp.sum(probs * grad_probs, -1, keepdims=True)
    grad_scores = (probs * (grad_probs - inner) * HD ** (-0.5)).astype(jnp.bfloat16)
    grad_q = jnp.einsum(
        "hqk,khd->qhd", grad_scores, split_heads(keyval[:, :C]), preferred_element_type=jnp.float32
    )
    grad_k = jnp.einsum("hqk,qhd->khd", grad_scores, split_heads(queries), preferred_element_type=jnp.float32)
    grad_v = jnp.einsum(
        "hqk,qhd->khd", probs.astype(jnp.bfloat16), g_heads, preferred_element_type=jnp.float32
    )
    rows = keyval.shape[0]
    return (
        grad_q.reshape(queries.shape).astype(jnp.bfloat16),
        jnp.concatenate([grad_k.reshape(rows, C), grad_v.reshape(rows, C)], 1).astype(jnp.bfloat16),
    )


def beside(values):
    tiles = values.shape[0] // 4
    return jnp.concatenate([values[sub * tiles : (sub + 1) * tiles] for sub in range(4)], 1)


def unbeside(values):
    return jnp.concatenate([values[:, sub * C : (sub + 1) * C] for sub in range(4)], 0)


def layer_forward(resid, weights, kernel, gain_rows, context):
    w_query, w_out, w_keyval, w_reduce, w_up, w_down = weights
    allowed, shifts, is_real = context
    normed_in = layer_norm(resid, gain_rows[0], gain_rows[1]).astype(jnp.bfloat16)
    queries = product(normed_in, w_query).astype(jnp.bfloat16)
    grouped = beside(normed_in)
    reduced = product(grouped, w_reduce)
    normed_kv = layer_norm(reduced, gain_rows[2], gain_rows[3]).astype(jnp.bfloat16)
    keyval = product(normed_kv, w_keyval).astype(jnp.bfloat16)
    attended = attend_forward(queries, keyval, allowed)
    middle = resid + product(attended, w_out)
    normed_mlp = layer_norm(middle, gain_rows[4], gain_rows[5]).astype(jnp.bfloat16)
    hidden = product(normed_mlp, w_up).astype(jnp.bfloat16)
    planes = hidden.reshape(4, -1, FF)
    mixed = depthwise(shifted_planes(planes, shifts), kernel, is_real).reshape(hidden.shape)
    active = gelu_exact(mixed).astype(jnp.bfloat16)
    output = middle + product(active, w_down)
    kept = (resid, normed_in, queries, grouped, reduced, normed_kv, keyval, attended, middle, normed_mlp, hidden, mixed, active)
    return (output, kept)


def layer_backward(grad_res, kept, weights, kernel, gain_rows, context):
    w_query, w_out, w_keyval, w_reduce, w_up, w_down = weights
    allowed, shifts, is_real = context
    resid, normed_in, queries, grouped, reduced, normed_kv, keyval, attended, middle, normed_mlp, hidden, mixed, active = kept
    grad_low = grad_res.astype(jnp.bfloat16)
    d_down = outer_sum(active, grad_low)
    d_active = back_product(grad_low, w_down).astype(jnp.bfloat16)
    d_mixed = jax.vjp(gelu_exact, mixed)[1](d_active.astype(jnp.float32))[0]
    moved = shifted_planes(d_mixed.astype(jnp.bfloat16).reshape(4, -1, FF), shifts)
    d_hidden = depthwise(moved, kernel[::-1], is_real).astype(jnp.bfloat16).reshape(hidden.shape)
    d_kernel = kernel_grad(moved, hidden.reshape(4, -1, FF))
    d_up = outer_sum(normed_mlp, d_hidden)
    d_middle, gain_four, gain_five = norm_back(
        middle, gain_rows[4], gain_rows[5], back_product(d_hidden, w_up)
    )
    grad_res = grad_res + d_middle
    grad_low = grad_res.astype(jnp.bfloat16)
    d_out = outer_sum(attended, grad_low)
    d_attended = back_product(grad_low, w_out).astype(jnp.bfloat16)
    d_query, d_keyval = attend_backward(d_attended, queries, keyval, allowed)
    d_wkv = outer_sum(normed_kv, d_keyval)
    d_reduced, gain_two, gain_three = norm_back(
        reduced, gain_rows[2], gain_rows[3], back_product(d_keyval, w_keyval)
    )
    d_reduced = d_reduced.astype(jnp.bfloat16)
    d_reduce = outer_sum(grouped, d_reduced)
    d_grouped = unbeside(back_product(d_reduced, w_reduce))
    d_wq = outer_sum(normed_in, d_query)
    d_first = back_product(d_query, w_query) + d_grouped
    d_resid, gain_zero, gain_one = norm_back(resid, gain_rows[0], gain_rows[1], d_first)
    gain_grads = jnp.stack([gain_zero, gain_one, gain_two, gain_three, gain_four, gain_five])
    low = [part.astype(jnp.bfloat16) for part in (d_wq, d_out, d_wkv, d_reduce, d_up, d_down)]
    units = jnp.stack(
        [
            jnp.concatenate([low[0], low[1], low[2].reshape(-1, C)], 0),
            low[3],
            low[4].reshape(-1, C),
            low[5],
        ]
    )
    return (grad_res + d_resid, units, d_kernel, gain_grads)


BOTH = ("grp", "tok")


def axis_bits(axis):
    count = lax.axis_size(axis)
    return [1 << place for place in reversed(range(count.bit_length() - 1))]


def swap(values, axis, bit):
    count = lax.axis_size(axis)
    return lax.ppermute(values, axis, [(i, i ^ bit) for i in range(count)])


def my_bit(axis, bit):
    return lax.axis_index(axis) // bit % 2


def bit_order():
    tok_bits = axis_bits("tok")
    return [("grp", bit) for bit in axis_bits("grp")] + [("tok", bit) for bit in tok_bits]


def sum_all(values):
    for axis, bit in reversed(bit_order()):
        values = values + swap(values, axis, bit)
    return values


def scatter_order():
    bits = bit_order()
    return [bits[-1]] + bits[:-1][::-1][len(axis_bits("tok")) - 1 :] + bits[:-1][::-1][: len(axis_bits("tok")) - 1]


def scatter_units(units):
    bits = bit_order()
    count = units.shape[0]
    chunk = units.shape[1] >> len(bits)
    left = list(bits)
    values = units.reshape((count,) + (2,) * len(bits) + (chunk, C))
    for axis, bit in scatter_order():
        dim = 1 + left.index((axis, bit))
        left.remove((axis, bit))
        mine = my_bit(axis, bit)
        away = lax.dynamic_index_in_dim(values, 1 - mine, dim, keepdims=False)
        stay = lax.dynamic_index_in_dim(values, mine, dim, keepdims=False)
        back = swap(away, axis, bit)
        values = (stay.astype(jnp.float32) + back.astype(jnp.float32)).astype(jnp.bfloat16)
    return values


def gather_unit(piece):
    bits = bit_order()
    held = []
    values = piece[None]
    for axis, bit in reversed(scatter_order()):
        other = swap(values, axis, bit)
        mine = my_bit(axis, bit) == 0
        pair = jnp.stack([jnp.where(mine, values, other), jnp.where(mine, other, values)])
        held.insert(0, (axis, bit))
        values = pair
    values = values.reshape((2,) * len(bits) + piece.shape)
    order = [held.index(name) for name in bits] + [len(bits), len(bits) + 1]
    return values.transpose(order).reshape(-1, piece.shape[1])


def body(
    patches,
    labels,
    valid_mask,
    crop_counts,
    owners,
    slot_weight,
    slot_moment,
    slot_second,
    norm_params,
    norm_moment,
    norm_second,
    head_weight,
    head_moment,
    head_second,
):
    tok_dev = patches.shape[0]
    n_tok = lax.axis_size("tok")
    n_grp = lax.axis_size("grp")
    tok_index = lax.axis_index("tok")
    group_tok = tok_dev * n_tok
    counts = crop_counts[0]
    n_unit = owners.shape[0]
    slot_rows, columns = slot_weight.shape
    unit_order = jnp.arange(n_unit, dtype=jnp.int32)
    same_owner = owners[:, None] == owners[None, :]
    rank_of = jnp.sum(same_owner & (unit_order[None, :] < unit_order[:, None]), 1)
    slot_of = owners * slot_rows + rank_of
    chunk = columns // n_tok // C
    pieces = slot_weight.astype(jnp.bfloat16).reshape(slot_rows, n_tok, chunk, C)
    pieces = lax.all_to_all(pieces, "tok", split_axis=1, concat_axis=0, tiled=True)
    unit_part = jnp.take(pieces.reshape(slot_rows * n_tok, chunk, C), slot_of, axis=0)
    first_unit = gather_unit(unit_part[0])
    embedding = first_unit[:PIN]
    kernels = first_unit[PIN : PIN + BLOCKS * 9 * FF // C].reshape(BLOCKS, 9, FF).astype(jnp.float32)
    layers = []
    for layer_at in range(BLOCKS):
        own = lax.all_gather(unit_part[1 + 4 * layer_at : 5 + 4 * layer_at], BOTH, axis=1, tiled=True)
        layers.append(
            (own[0, :C], own[0, C : 2 * C], own[0, 2 * C :].reshape(C, 2 * C), own[1], own[2].reshape(C, FF), own[3])
        )

    towards = [(i + 1, i) for i in range(n_tok - 1)]
    window = tok_dev + OVER
    tiles = window // 4
    patches = jnp.concatenate([patches, lax.ppermute(patches[:OVER], "tok", towards)], 0)
    marks = jnp.stack([labels, valid_mask])
    marks = jnp.concatenate([marks, lax.ppermute(marks[:, :OVER], "tok", towards)], 1)
    patches = patches.reshape(tiles, 4, PIN).transpose(1, 0, 2).reshape(window, PIN)
    marks = marks.reshape(2, tiles, 4).transpose(0, 2, 1).reshape(2, window)
    labels = marks[0]
    first_tok = tok_index * tok_dev
    positions = first_tok + 4 * jnp.arange(tiles, dtype=jnp.int32)
    begin_at, half_side, tile_y, tile_x, _ = image_layout(positions, counts)
    own_image = (begin_at >= first_tok) & (begin_at < first_tok + tok_dev) & (positions < group_tok)
    is_real = positions < counts[0] * BIG_SIDE**2 + counts[1] * SMALL_SIDE**2
    shifts = shift_matrices(begin_at, half_side, tile_y, tile_x, is_real)
    image_of = jnp.where(positions < group_tok, begin_at, -1)
    allowed = jnp.tile(image_of, 4)[:, None] == image_of[None, :]
    keep_mask = marks[1].astype(jnp.float32) * jnp.tile((own_image & is_real).astype(jnp.float32), 4)
    pixel_total = sum_all(jnp.sum(keep_mask)[None])[0]
    context = (allowed, shifts, is_real)
    tail = 6 * BLOCKS
    embed_pre = product(patches, embedding)
    resid = layer_norm(embed_pre, norm_params[tail], norm_params[tail + 1])
    kept_all = []
    for layer_at in range(BLOCKS):
        resid, kept_state = layer_forward(
            resid,
            layers[layer_at],
            kernels[layer_at],
            norm_params[6 * layer_at : 6 * layer_at + 6],
            context,
        )
        kept_all.append(kept_state)
    final = layer_norm(resid, norm_params[tail + 2], norm_params[tail + 3]).astype(jnp.bfloat16)
    head_low = head_weight.astype(jnp.bfloat16)
    logits = product(final, head_low)
    row_peak = jnp.max(logits, -1, keepdims=True)
    log_norm = row_peak[:, 0] + jnp.log(jnp.sum(jnp.exp(logits - row_peak), -1))
    onehot = (labels[:, None] == jnp.arange(head_weight.shape[1], dtype=jnp.int32)[None, :]).astype(
        jnp.float32
    )
    picked = jnp.sum(logits * onehot, 1)
    loss_local = jnp.sum((log_norm - picked) * keep_mask)
    probs = jnp.exp(logits - log_norm[:, None])
    d_logits = ((probs - onehot) * (keep_mask / pixel_total)[:, None]).astype(jnp.bfloat16)
    d_head = outer_sum(final, d_logits)
    grad_res, gain_final, shift_final = norm_back(
        resid, norm_params[tail + 2], norm_params[tail + 3], back_product(d_logits, head_low)
    )
    unit_grads = [None] * BLOCKS
    kernel_grads = [None] * BLOCKS
    gain_grads = [None] * BLOCKS
    for layer_at in reversed(range(BLOCKS)):
        grad_res, units, kernel_grads[layer_at], gain_grads[layer_at] = (
            layer_backward(
                grad_res,
                kept_all[layer_at],
                layers[layer_at],
                kernels[layer_at],
                norm_params[6 * layer_at : 6 * layer_at + 6],
                context,
            )
        )
        unit_grads[layer_at] = scatter_units(units)
    d_embed_pre, gain_embed, shift_embed = norm_back(
        embed_pre, norm_params[tail], norm_params[tail + 1], grad_res
    )
    d_embedding = outer_sum(patches, d_embed_pre.astype(jnp.bfloat16))
    first_grad = jnp.concatenate(
        [
            d_embedding.astype(jnp.bfloat16),
            jnp.stack(kernel_grads).reshape(-1, C).astype(jnp.bfloat16),
            jnp.zeros((C * FF // C - PIN - BLOCKS * 9 * FF // C, C), jnp.bfloat16),
        ]
    )
    first_grad = scatter_units(first_grad[None])
    stacked = jnp.concatenate([first_grad] + unit_grads, 0)
    norm_grads = jnp.concatenate(
        gain_grads + [jnp.stack([gain_embed, shift_embed, gain_final, shift_final])], 0
    )
    row_ids = jnp.arange(slot_rows * n_tok, dtype=jnp.int32)
    matches = slot_of[None, :] == row_ids[:, None]
    unit_at = jnp.where(jnp.any(matches, 1), jnp.argmax(matches, 1), n_unit)
    padded = jnp.concatenate([stacked, jnp.zeros_like(stacked[:1])], 0)
    placed = jnp.take(padded, unit_at, axis=0)[:, None]
    owned = lax.all_to_all(placed, "tok", split_axis=0, concat_axis=1, tiled=True)
    owned = owned.astype(jnp.float32).reshape(slot_rows, columns)
    head_total = sum_all(d_head)
    small = jnp.concatenate([norm_grads, jnp.full((1, C), loss_local)], 0)
    small = sum_all(small)
    norm_total, loss_sum = (small[:-1], small[-1, 0])
    slot_m, slot_v, slot_w = adamw_step(
        slot_weight, slot_moment, slot_second, owned, RATE_MATRIX, DECAY_RATE
    )
    norm_m, norm_v, norm_w = adamw_step(
        norm_params, norm_moment, norm_second, norm_total, RATE_VECTOR, 0.0
    )
    head_m, head_v, head_w = adamw_step(
        head_weight, head_moment, head_second, head_total, RATE_MATRIX, DECAY_RATE
    )
    return (
        loss_sum,
        pixel_total,
        slot_m,
        slot_v,
        slot_w,
        norm_m,
        norm_v,
        norm_w,
        head_m,
        head_v,
        head_w,
    )


def solution(mesh):
    in_specs = (
        P(("grp", "tok"), None),
        P(("grp", "tok")),
        P(("grp", "tok")),
        P("grp", None),
        P(),
        P("tok", "grp"),
        P("tok", "grp"),
        P("tok", "grp"),
        P(),
        P(),
        P(),
        P(),
        P(),
        P(),
    )
    out_specs = (
        P(),
        P(),
        P("tok", "grp"),
        P("tok", "grp"),
        P("tok", "grp"),
        P(),
        P(),
        P(),
        P(),
        P(),
        P(),
    )
    return jax.shard_map(body, mesh=mesh, in_specs=in_specs, out_specs=out_specs, check_vma=False)
```

```python
import jax
import jax.numpy as jnp
from jax import lax
from jax.experimental import pallas as pl
from jax.experimental.pallas import tpu as pltpu
from jax.sharding import PartitionSpec as P

C = 320
HEADS = 5
HD = 64
FF = 1280
PIN = 1152
BLOCKS = 3
BIG_SIDE = 14
SMALL_SIDE = 6
STEP = 10
KVH = 49


EPS_NORM = 1e-06
BETA_ONE = 0.9
BETA_TWO = 0.999
ADAM_EPS = 1e-08
RATE_MATRIX = 0.05
RATE_VECTOR = 0.3
DECAY_RATE = 0.05
NEG_FILL = -1e30
PREC_HIGH = lax.Precision.HIGHEST


def layer_norm(values, gain_vec, shift_vec):
    center = values - jnp.mean(values, -1, keepdims=True)
    inverse = lax.rsqrt(jnp.mean(center * center, -1, keepdims=True) + EPS_NORM)
    return center * inverse * gain_vec + shift_vec


def adamw_step(weight, moment, second, gradient, rate_now, decay_now):
    moment = BETA_ONE * moment + (1.0 - BETA_ONE) * gradient
    second = BETA_TWO * second + (1.0 - BETA_TWO) * gradient * gradient
    m_hat = moment / (1.0 - BETA_ONE**STEP)
    v_hat = second / (1.0 - BETA_TWO**STEP)
    weight = weight - rate_now * (m_hat / (jnp.sqrt(v_hat) + ADAM_EPS) + decay_now * weight)
    return (moment, second, weight)


def product(left, right):
    return jnp.dot(left, right, preferred_element_type=jnp.float32)


def outer_sum(left, right):
    return lax.dot_general(
        left, right, (((0,), (0,)), ((), ())), preferred_element_type=jnp.float32
    )


def back_product(gradient, weight):
    return lax.dot_general(
        gradient, weight, (((1,), (1,)), ((), ())), preferred_element_type=jnp.float32
    )


def norm_back(values, gain_vec, shift_vec, gradient):
    _, pull_back = jax.vjp(layer_norm, values, gain_vec, shift_vec)
    return pull_back(gradient)


OVER = 4 * KVH - 4


def image_layout(positions, counts):
    big_tok = BIG_SIDE * BIG_SIDE
    small_tok = SMALL_SIDE * SMALL_SIDE
    big_end = counts[0] * big_tok
    small_end = big_end + counts[1] * small_tok
    is_big = positions < big_end
    is_small = jnp.logical_and(positions >= big_end, positions < small_end)
    half_side = jnp.where(is_big, BIG_SIDE // 2, SMALL_SIDE // 2)
    begin_at = jnp.where(
        is_big,
        positions // big_tok * big_tok,
        jnp.where(is_small, big_end + (positions - big_end) // small_tok * small_tok, small_end),
    )
    tile_idx = (positions - begin_at) // 4
    return (begin_at, half_side, tile_idx // half_side, tile_idx % half_side, positions < small_end)


def shift_matrices(begin_at, half_side, tile_y, tile_x, is_real):
    count = begin_at.shape[0]
    own = jnp.arange(count, dtype=jnp.int32)
    offset = own[None, :] - own[:, None]
    inside = {
        (0, -1): tile_x > 0,
        (0, 1): tile_x < half_side - 1,
        (-1, 0): tile_y > 0,
        (1, 0): tile_y < half_side - 1,
    }
    result = {}
    for step_y in (-1, 0, 1):
        for step_x in (-1, 0, 1):
            if step_y == 0 and step_x == 0:
                continue
            allowed = is_real
            if step_y:
                allowed = allowed & inside[step_y, 0]
            if step_x:
                allowed = allowed & inside[0, step_x]
            hit = (offset == (step_y * half_side + step_x)[:, None]) & allowed[:, None]
            result[step_y, step_x] = hit.astype(jnp.bfloat16)
    return result


def tap_source(sub, tap):
    y_at = sub // 2 + tap // 3 - 1
    x_at = sub % 2 + tap % 3 - 1
    return (y_at % 2 * 2 + x_at % 2, y_at // 2, x_at // 2)


SQRT_HALF = 0.7071067811865476
INV_SQRT_TWO_PI = 0.3989422804014327
TAPS_OF = [[tap_source(sub, tap) for tap in range(9)] for sub in range(4)]
VMEM_LIMIT = 56 * 1024 * 1024
SPAN = 256
ROWS = 16
LANES = 128


def row_cut(tiles):
    return (tiles // 2 + 15) // 16 * 16


def shift_stacks(shifts):
    tiles = shifts[0, 1].shape[0]
    cut = row_cut(tiles)
    upper, lower = [], []
    for sub in range(4):
        step_y = 1 - 2 * (sub // 2)
        step_x = 1 - 2 * (sub % 2)
        for key in ((0, step_x), (step_y, 0), (step_y, step_x)):
            upper.append(shifts[key][:cut, :SPAN])
            lower.append(shifts[key][cut:, tiles - SPAN :])
    return (jnp.stack(upper).reshape(4, 3 * cut, SPAN), jnp.stack(lower).reshape(4, 3 * (tiles - cut), SPAN))


def move_planes(planes_ref, upper_ref, lower_ref, moved_ref):
    tiles = planes_ref.shape[0] // 4
    cut = row_cut(tiles)
    for sub in range(4):
        base = sub * tiles
        part = product(upper_ref[sub], planes_ref[base : base + SPAN, :])
        for key in range(3):
            moved_ref[sub, key, :cut, :] = part[key * cut : (key + 1) * cut]
        part = product(lower_ref[sub], planes_ref[base + tiles - SPAN : base + tiles, :])
        for key in range(3):
            moved_ref[sub, key, cut:, :] = part[key * (tiles - cut) : (key + 1) * (tiles - cut)]


def chunk_sources(planes_ref, moved_ref, row, lanes):
    tiles = planes_ref.shape[0] // 4
    found = {}
    for sub in range(4):
        found[sub, 0, 0] = planes_ref[pl.ds(pl.multiple_of(sub * tiles + row, ROWS), ROWS), lanes].astype(jnp.float32)
        step_y = 1 - 2 * (sub // 2)
        step_x = 1 - 2 * (sub % 2)
        for key, step in enumerate(((0, step_x), (step_y, 0), (step_y, step_x))):
            found[(sub,) + step] = moved_ref[sub, key, pl.ds(row, ROWS), lanes]
    return found


def norm_rows(values, gain, shift):
    center = values - jnp.mean(values, -1, keepdims=True)
    inverse = lax.rsqrt(jnp.mean(center * center, -1, keepdims=True) + EPS_NORM)
    unit = center * inverse
    return (unit, inverse, unit * gain + shift)


def norm_rows_back(unit, inverse, gain, grad):
    scaled = grad * gain
    return inverse * (
        scaled - jnp.mean(scaled, -1, keepdims=True) - unit * jnp.mean(scaled * unit, -1, keepdims=True)
    )


def mlp_forward_kernel(
    middle_ref, gains_ref, up_ref, down_ref, kern_ref, upper_ref, lower_ref, real_ref,
    out_ref, hidden_ref, active_ref, slope_ref,
    normed_ref, moved_ref,
):
    rows = middle_ref.shape[0]
    tiles = rows // 4

    @pl.when(pl.program_id(0) == 0)
    def _():
        @pl.loop(0, rows // 64)
        def _(at):
            span = pl.ds(pl.multiple_of(at * 64, 64), 64)
            normed = norm_rows(middle_ref[span, :], gains_ref[0:1, :], gains_ref[1:2, :])[2]
            normed_ref[span, :] = normed.astype(jnp.bfloat16)
            out_ref[span, :] = middle_ref[span, :]

    for sub in range(4):
        part = product(normed_ref[sub * tiles : (sub + 1) * tiles, :], up_ref[...])
        hidden_ref[sub * tiles : (sub + 1) * tiles, :] = part.astype(jnp.bfloat16)
    move_planes(hidden_ref, upper_ref, lower_ref, moved_ref)

    for lane in range(0, hidden_ref.shape[1], LANES):
        lanes = slice(lane, lane + LANES)
        kern = [kern_ref[tap : tap + 1, lanes] for tap in range(9)]

        @pl.loop(0, tiles // ROWS)
        def _(at):
            row = pl.multiple_of(at * ROWS, ROWS)
            found = chunk_sources(hidden_ref, moved_ref, row, lanes)
            real = real_ref[pl.ds(row, ROWS), :] > 0.0
            for sub in range(4):
                center = found[sub, 0, 0] * kern[4]
                total = center
                for tap in range(9):
                    if tap != 4:
                        total = total + found[TAPS_OF[sub][tap]] * kern[tap]
                mixed = jnp.where(real, total, center)
                half = 0.5 + 0.5 * lax.erf(mixed * SQRT_HALF)
                bell = jnp.exp(-0.5 * mixed * mixed) * INV_SQRT_TWO_PI
                span = pl.ds(pl.multiple_of(sub * tiles + row, ROWS), ROWS)
                active_ref[span, lanes] = (mixed * half).astype(jnp.bfloat16)
                slope_ref[span, lanes] = (half + mixed * bell).astype(jnp.bfloat16)

    for sub in range(4):
        span = slice(sub * tiles, (sub + 1) * tiles)
        out_ref[span, :] += product(active_ref[span, :], down_ref[...])


def untied(kernel, count, ties):
    def run(*refs):
        kernel(*refs[:count], *refs[count + ties :])

    return run


def whole(shape):
    return pl.BlockSpec(shape, lambda j: (0,) * len(shape))


def mlp_forward(middle, gains, w_up, w_down, kernel, stacks, real_rows):
    rows = middle.shape[0]
    block = 256
    by_lane = pl.BlockSpec((rows, block), lambda j: (0, j))
    low = jax.ShapeDtypeStruct((rows, FF), jnp.bfloat16)
    return pl.pallas_call(
        mlp_forward_kernel,
        grid=(FF // block,),
        out_shape=(jax.ShapeDtypeStruct((rows, C), jnp.float32), low, low, low),
        in_specs=[
            whole((rows, C)),
            whole((2, C)),
            pl.BlockSpec((C, block), lambda j: (0, j)),
            pl.BlockSpec((block, C), lambda j: (j, 0)),
            pl.BlockSpec((9, block), lambda j: (0, j)),
            whole(stacks[0].shape),
            whole(stacks[1].shape),
            whole(real_rows.shape),
        ],
        out_specs=(whole((rows, C)), by_lane, by_lane, by_lane),
        scratch_shapes=[
            pltpu.VMEM((rows, C), jnp.bfloat16),
            pltpu.VMEM((4, 3, rows // 4, block), jnp.float32),
        ],
        compiler_params=pltpu.CompilerParams(vmem_limit_bytes=VMEM_LIMIT),
        cost_estimate=pl.CostEstimate(flops=14 * 10**9, bytes_accessed=18 * 10**6, transcendentals=4 * 10**6),
        name="mlp_forward",
    )(middle, gains, w_up, w_down, kernel, stacks[0], stacks[1], real_rows)


def mlp_backward_kernel(
    grad_ref, middle_ref, gains_ref, up_ref, down_ref, kern_ref, upper_ref, lower_ref, real_ref,
    hidden_ref, active_ref, slope_ref,
    out_ref, dup_ref, ddown_ref, dkern_ref, dgain_ref,
    low_ref, low_t_ref, normed_t_ref, mixed_ref, dhid_ref, moved_ref, back_ref,
):
    rows = grad_ref.shape[0]
    tiles = rows // 4
    block = hidden_ref.shape[1]

    @pl.when(pl.program_id(0) == 0)
    def _():
        for sub in range(4):
            span = slice(sub * tiles, (sub + 1) * tiles)
            low_ref[span, :] = grad_ref[span, :].astype(jnp.bfloat16)
        normed = norm_rows(middle_ref[...], gains_ref[0:1, :], gains_ref[1:2, :])[2]
        normed_t_ref[...] = normed.T.astype(jnp.bfloat16)
        low_t_ref[...] = grad_ref[...].T.astype(jnp.bfloat16)
        back_ref[...] = jnp.zeros_like(back_ref)

    for sub in range(4):
        span = slice(sub * tiles, (sub + 1) * tiles)
        part = back_product(low_ref[span, :], down_ref[...]).astype(jnp.bfloat16).astype(jnp.float32)
        mixed_ref[span, :] = (part * slope_ref[span, :].astype(jnp.float32)).astype(jnp.bfloat16)
    ddown_ref[...] = product(low_t_ref[...], active_ref[...]).T.astype(jnp.bfloat16)
    move_planes(mixed_ref, upper_ref, lower_ref, moved_ref)

    for lane in range(0, block, LANES):
        lanes = slice(lane, lane + LANES)
        kern = [kern_ref[tap : tap + 1, lanes] for tap in range(9)]

        def step(at, sums):
            row = pl.multiple_of(at * ROWS, ROWS)
            found = chunk_sources(mixed_ref, moved_ref, row, lanes)
            real = real_ref[pl.ds(row, ROWS), :] > 0.0
            sums = list(sums)
            for sub in range(4):
                span = pl.ds(pl.multiple_of(sub * tiles + row, ROWS), ROWS)
                hidden = hidden_ref[span, lanes].astype(jnp.float32)
                center = found[sub, 0, 0] * kern[4]
                total = center
                for tap in range(9):
                    term = found[TAPS_OF[sub][tap]]
                    if tap != 4:
                        total = total + term * kern[8 - tap]
                    piece = hidden * term
                    sums[tap] = sums[tap] + piece[:8] + piece[8:]
                dhid_ref[span, lanes] = jnp.where(real, total, center).astype(jnp.bfloat16)
            return tuple(sums)

        sums = lax.fori_loop(0, tiles // ROWS, step, (jnp.zeros((8, LANES), jnp.float32),) * 9)
        for tap in range(9):
            dkern_ref[8 - tap : 9 - tap, lanes] = jnp.sum(sums[tap], 0, keepdims=True)

    dup_ref[...] = product(normed_t_ref[...], dhid_ref[...]).astype(jnp.bfloat16)
    for sub in range(4):
        span = slice(sub * tiles, (sub + 1) * tiles)
        back_ref[span, :] += back_product(dhid_ref[span, :], up_ref[...])

    @pl.when(pl.program_id(0) == pl.num_programs(0) - 1)
    def _():
        def step(at, sums):
            span = pl.ds(pl.multiple_of(at * 64, 64), 64)
            grad = back_ref[span, :]
            unit, inverse, _ = norm_rows(middle_ref[span, :], gains_ref[0:1, :], gains_ref[1:2, :])
            out_ref[span, :] = grad_ref[span, :] + norm_rows_back(unit, inverse, gains_ref[0:1, :], grad)
            return (
                sums[0] + jnp.sum(grad * unit, 0, keepdims=True),
                sums[1] + jnp.sum(grad, 0, keepdims=True),
            )

        zero = jnp.zeros((1, C), jnp.float32)
        sums = lax.fori_loop(0, rows // 64, step, (zero, zero))
        dgain_ref[0:1, :] = sums[0]
        dgain_ref[1:2, :] = sums[1]


def mlp_backward(grad, middle, gains, w_up, w_down, kernel, stacks, real_rows, kept, ties):
    rows = middle.shape[0]
    block = 256
    by_lane = pl.BlockSpec((rows, block), lambda j: (0, j))
    up_spec = pl.BlockSpec((C, block), lambda j: (0, j))
    down_spec = pl.BlockSpec((block, C), lambda j: (j, 0))
    tap_spec = pl.BlockSpec((9, block), lambda j: (0, j))
    return pl.pallas_call(
        untied(mlp_backward_kernel, 12, len(ties)),
        grid=(FF // block,),
        out_shape=(
            jax.ShapeDtypeStruct((rows, C), jnp.float32),
            jax.ShapeDtypeStruct((C, FF), jnp.bfloat16),
            jax.ShapeDtypeStruct((FF, C), jnp.bfloat16),
            jax.ShapeDtypeStruct((9, FF), jnp.float32),
            jax.ShapeDtypeStruct((2, C), jnp.float32),
        ),
        in_specs=[
            whole((rows, C)),
            whole((rows, C)),
            whole((2, C)),
            up_spec,
            down_spec,
            tap_spec,
            whole(stacks[0].shape),
            whole(stacks[1].shape),
            whole(real_rows.shape),
            by_lane,
            by_lane,
            by_lane,
        ]
        + [pl.BlockSpec(memory_space=pl.ANY)] * len(ties),
        out_specs=(whole((rows, C)), up_spec, down_spec, tap_spec, whole((2, C))),
        scratch_shapes=[
            pltpu.VMEM((rows, C), jnp.bfloat16),
            pltpu.VMEM((C, rows), jnp.bfloat16),
            pltpu.VMEM((C, rows), jnp.bfloat16),
            pltpu.VMEM((rows, block), jnp.bfloat16),
            pltpu.VMEM((rows, block), jnp.bfloat16),
            pltpu.VMEM((4, 3, rows // 4, block), jnp.float32),
            pltpu.VMEM((rows, C), jnp.float32),
        ],
        compiler_params=pltpu.CompilerParams(vmem_limit_bytes=VMEM_LIMIT),
        cost_estimate=pl.CostEstimate(flops=18 * 10**9, bytes_accessed=18 * 10**6, transcendentals=0),
        name="mlp_backward",
    )(grad, middle, gains, w_up, w_down, kernel, stacks[0], stacks[1], real_rows, *kept, *ties)


WIDE = 384
BLOCK_TILES = 32
KEY_SPAN = 128


def block_places(tiles):
    places = []
    for index in range(-(-tiles // BLOCK_TILES)):
        start = min(index * BLOCK_TILES, tiles - BLOCK_TILES)
        places.append((start, min(max(start - 48, 0), tiles - KEY_SPAN)))
    return places


def block_bias(image_of):
    parts = []
    for start, low in block_places(image_of.shape[0]):
        same = image_of[low : low + KEY_SPAN, None] == jnp.tile(image_of[start : start + BLOCK_TILES], 4)[None, :]
        parts.append(jnp.where(same, 0.0, NEG_FILL))
    return jnp.stack(parts)


def place_of(index, tiles):
    start = jnp.minimum(index * BLOCK_TILES, tiles - BLOCK_TILES)
    low = jnp.clip(start - 48, 0, tiles - KEY_SPAN)
    return (pl.multiple_of(start, ROWS), pl.multiple_of(low, ROWS))


def four_planes(ref, start, lanes):
    tiles = ref.shape[0] // 4
    return jnp.concatenate(
        [ref[pl.ds(pl.multiple_of(sub * tiles + start, ROWS), BLOCK_TILES), lanes] for sub in range(4)], 0
    )


def put_planes(ref, start, lanes, values):
    tiles = ref.shape[0] // 4
    for sub in range(4):
        ref[pl.ds(pl.multiple_of(sub * tiles + start, ROWS), BLOCK_TILES), lanes] = values[
            sub * BLOCK_TILES : (sub + 1) * BLOCK_TILES
        ]


def head_pair(values, group):
    if group == 2:
        return values
    first = lax.broadcasted_iota(jnp.int32, values.shape, 1) < HD
    zero = jnp.zeros_like(values)
    return jnp.concatenate([jnp.where(first, values, zero), jnp.where(first, zero, values)], 0)


def softmax_columns(raw, bias):
    parts = []
    for half in range(raw.shape[0] // KEY_SPAN):
        scores = raw[half * KEY_SPAN : (half + 1) * KEY_SPAN] * HD ** (-0.5) + bias
        weights = jnp.exp(scores - jnp.max(scores, 0, keepdims=True))
        parts.append(weights * (1.0 / jnp.sum(weights, 0, keepdims=True)))
    return parts


def norm_store(source_ref, gains_ref, at, target_ref):
    @pl.loop(0, source_ref.shape[0] // 64)
    def _(step):
        span = pl.ds(pl.multiple_of(step * 64, 64), 64)
        normed = norm_rows(source_ref[span, :], gains_ref[at : at + 1, :], gains_ref[at + 1 : at + 2, :])[2]
        target_ref[span, :] = normed.astype(jnp.bfloat16)


def attention_forward_kernel(
    resid_ref, gains_ref, wq_ref, wo_ref, wk_ref, wv_ref, wr_ref, bias_ref,
    middle_ref, normed_ref, query_ref, reduced_ref, key_ref, value_ref, attended_ref,
):
    rows = resid_ref.shape[0]
    tiles = rows // 4
    norm_store(resid_ref, gains_ref, 0, normed_ref)
    query_ref[:, C:] = jnp.zeros((rows, WIDE - C), jnp.bfloat16)
    reduced = jnp.zeros((tiles, C), jnp.float32)
    for sub in range(4):
        span = slice(sub * tiles, (sub + 1) * tiles)
        query_ref[span, :C] = product(normed_ref[span, :], wq_ref[...]).astype(jnp.bfloat16)
        reduced = reduced + product(normed_ref[span, :], wr_ref[sub * C : (sub + 1) * C, :])
    reduced_ref[...] = reduced
    normed_kv = norm_rows(reduced, gains_ref[2:3, :], gains_ref[3:4, :])[2].astype(jnp.bfloat16)
    for ref, weight in ((key_ref, wk_ref), (value_ref, wv_ref)):
        ref[:, C:] = jnp.zeros((tiles, WIDE - C), jnp.bfloat16)
        ref[:, :C] = product(normed_kv, weight[...]).astype(jnp.bfloat16)

    @pl.loop(0, bias_ref.shape[0])
    def _(index):
        start, low = place_of(index, tiles)
        bias = bias_ref[index]
        for group in range(3):
            lanes = slice(group * LANES, (group + 1) * LANES)
            query = four_planes(query_ref, start, lanes)
            keys = head_pair(key_ref[pl.ds(low, KEY_SPAN), lanes], group)
            values = head_pair(value_ref[pl.ds(low, KEY_SPAN), lanes], group)
            probs = softmax_columns(back_product(keys, query), bias)
            probs = jnp.concatenate(probs, 0).T.astype(jnp.bfloat16)
            put_planes(attended_ref, start, lanes, product(probs, values).astype(jnp.bfloat16))

    for sub in range(4):
        span = slice(sub * tiles, (sub + 1) * tiles)
        middle_ref[span, :] = resid_ref[span, :] + product(attended_ref[span, :C], wo_ref[...])


def in_vmem(count):
    return [pl.BlockSpec(memory_space=pltpu.VMEM)] * count


def attention_forward(resid, gains, wq, wo, wk, wv, wr, bias):
    rows = resid.shape[0]
    tiles = rows // 4
    low = jnp.bfloat16
    shapes = (
        jax.ShapeDtypeStruct((rows, C), jnp.float32),
        jax.ShapeDtypeStruct((rows, C), low),
        jax.ShapeDtypeStruct((rows, WIDE), low),
        jax.ShapeDtypeStruct((tiles, C), jnp.float32),
        jax.ShapeDtypeStruct((tiles, WIDE), low),
        jax.ShapeDtypeStruct((tiles, WIDE), low),
        jax.ShapeDtypeStruct((rows, WIDE), low),
    )
    return pl.pallas_call(
        attention_forward_kernel,
        out_shape=shapes,
        in_specs=in_vmem(8),
        out_specs=tuple(in_vmem(7)),
        compiler_params=pltpu.CompilerParams(vmem_limit_bytes=VMEM_LIMIT),
        cost_estimate=pl.CostEstimate(flops=6 * 10**9, bytes_accessed=14 * 10**6, transcendentals=10**6),
        name="attention_forward",
    )(resid, gains, wq, wo, wk, wv, wr, bias)


def attention_backward_kernel(
    grad_ref, resid_ref, gains_ref, wq_ref, wo_ref, wk_ref, wv_ref, wr_ref, bias_ref,
    normed_ref, query_ref, reduced_ref, key_ref, value_ref, attended_ref,
    out_ref, dqo_ref, dkv_ref, dwr_ref, dgain_ref,
    turned_ref, datt_ref, dquery_ref, dkey_ref, dvalue_ref, first_ref,
):
    rows = resid_ref.shape[0]
    tiles = rows // 4
    low_type = jnp.bfloat16
    datt_ref[:, C:] = jnp.zeros((rows, WIDE - C), low_type)
    turned_ref[...] = grad_ref[...].T.astype(low_type)
    dqo_ref[C:, :] = product(turned_ref[...], attended_ref[:, :C]).T.astype(low_type)
    for sub in range(4):
        span = slice(sub * tiles, (sub + 1) * tiles)
        datt_ref[span, :C] = back_product(grad_ref[span, :].astype(low_type), wo_ref[...]).astype(low_type)
    dkey_ref[...] = jnp.zeros_like(dkey_ref)
    dvalue_ref[...] = jnp.zeros_like(dvalue_ref)
    blocks = bias_ref.shape[0]

    @pl.loop(0, blocks)
    def _(step):
        index = blocks - 1 - step
        start, low = place_of(index, tiles)
        bias = bias_ref[index]
        tile_at = lax.rem(lax.broadcasted_iota(jnp.int32, (4 * BLOCK_TILES, LANES), 0), BLOCK_TILES)
        fresh = tile_at >= index * BLOCK_TILES - start
        span = pl.ds(low, KEY_SPAN)
        for group in range(3):
            lanes = slice(group * LANES, (group + 1) * LANES)
            query = four_planes(query_ref, start, lanes)
            datt = four_planes(datt_ref, start, lanes)
            datt = jnp.where(fresh, datt, jnp.zeros_like(datt))
            keys = head_pair(key_ref[span, lanes], group)
            values = head_pair(value_ref[span, lanes], group)
            probs = softmax_columns(back_product(keys, query), bias)
            dprobs = back_product(values, datt)
            dscores = []
            for half, prob in enumerate(probs):
                dprob = dprobs[half * KEY_SPAN : (half + 1) * KEY_SPAN]
                inner = jnp.sum(prob * dprob, 0, keepdims=True)
                dscores.append(prob * (dprob - inner) * HD ** (-0.5))
            dscores = jnp.concatenate(dscores, 0)
            probs = jnp.concatenate(probs, 0).astype(low_type)
            dquery = product(dscores.T.astype(low_type), keys)
            put_planes(dquery_ref, start, lanes, dquery.astype(low_type))
            dkeys = product(dscores.astype(low_type), query)
            dvalues = product(probs, datt)
            if group < 2:
                first = lax.broadcasted_iota(jnp.int32, (KEY_SPAN, LANES), 1) < HD
                dkeys = jnp.where(first, dkeys[:KEY_SPAN], dkeys[KEY_SPAN:])
                dvalues = jnp.where(first, dvalues[:KEY_SPAN], dvalues[KEY_SPAN:])
            dkey_ref[span, lanes] += dkeys
            dvalue_ref[span, lanes] += dvalues

    unit, inverse, normed = norm_rows(reduced_ref[...], gains_ref[2:3, :], gains_ref[3:4, :])
    normed_t = normed.T.astype(low_type)
    dkeys = dkey_ref[:, :C].astype(low_type)
    dvalues = dvalue_ref[:, :C].astype(low_type)
    dkv_ref[:C, :] = product(normed_t, dkeys).astype(low_type)
    dkv_ref[C:, :] = product(normed_t, dvalues).astype(low_type)
    dnormed = back_product(dkeys, wk_ref[...]) + back_product(dvalues, wv_ref[...])
    dgain_ref[2:3, :] = jnp.sum(dnormed * unit, 0, keepdims=True)
    dgain_ref[3:4, :] = jnp.sum(dnormed, 0, keepdims=True)
    dreduced = norm_rows_back(unit, inverse, gains_ref[2:3, :], dnormed).astype(low_type)
    turned_ref[...] = normed_ref[...].T
    dqo_ref[:C, :] = product(turned_ref[...], dquery_ref[:, :C]).astype(low_type)
    for sub in range(4):
        span = slice(sub * tiles, (sub + 1) * tiles)
        part = slice(sub * C, (sub + 1) * C)
        dwr_ref[part, :] = outer_sum(normed_ref[span, :], dreduced).astype(low_type)
        first_ref[span, :] = back_product(dquery_ref[span, :C], wq_ref[...]) + back_product(dreduced, wr_ref[part, :])

    def step(at, sums):
        span = pl.ds(pl.multiple_of(at * 64, 64), 64)
        grad = first_ref[span, :]
        unit, inverse, _ = norm_rows(resid_ref[span, :], gains_ref[0:1, :], gains_ref[1:2, :])
        out_ref[span, :] = grad_ref[span, :] + norm_rows_back(unit, inverse, gains_ref[0:1, :], grad)
        return (sums[0] + jnp.sum(grad * unit, 0, keepdims=True), sums[1] + jnp.sum(grad, 0, keepdims=True))

    zero = jnp.zeros((1, C), jnp.float32)
    sums = lax.fori_loop(0, rows // 64, step, (zero, zero))
    dgain_ref[0:1, :] = sums[0]
    dgain_ref[1:2, :] = sums[1]


def attention_backward(grad, resid, gains, wq, wo, wk, wv, wr, bias, kept, ties):
    rows = resid.shape[0]
    tiles = rows // 4
    low = jnp.bfloat16
    shapes = (
        jax.ShapeDtypeStruct((rows, C), jnp.float32),
        jax.ShapeDtypeStruct((2 * C, C), low),
        jax.ShapeDtypeStruct((2 * C, C), low),
        jax.ShapeDtypeStruct((4 * C, C), low),
        jax.ShapeDtypeStruct((4, C), jnp.float32),
    )
    return pl.pallas_call(
        untied(attention_backward_kernel, 15, len(ties)),
        out_shape=shapes,
        in_specs=in_vmem(15) + [pl.BlockSpec(memory_space=pl.ANY)] * len(ties),
        out_specs=tuple(in_vmem(5)),
        scratch_shapes=[
            pltpu.VMEM((C, rows), low),
            pltpu.VMEM((rows, WIDE), low),
            pltpu.VMEM((rows, WIDE), low),
            pltpu.VMEM((tiles, WIDE), jnp.float32),
            pltpu.VMEM((tiles, WIDE), jnp.float32),
            pltpu.VMEM((rows, C), jnp.float32),
        ],
        compiler_params=pltpu.CompilerParams(vmem_limit_bytes=VMEM_LIMIT),
        cost_estimate=pl.CostEstimate(flops=12 * 10**9, bytes_accessed=18 * 10**6, transcendentals=10**6),
        name="attention_backward",
    )(grad, resid, gains, wq, wo, wk, wv, wr, bias, *kept, *ties)


BOTH = ("grp", "tok")


def axis_bits(axis):
    count = lax.axis_size(axis)
    return [1 << place for place in reversed(range(count.bit_length() - 1))]


def swap(values, axis, bit):
    count = lax.axis_size(axis)
    return lax.ppermute(values, axis, [(i, i ^ bit) for i in range(count)])


def my_bit(axis, bit):
    return lax.axis_index(axis) // bit % 2


def bit_order():
    tok_bits = axis_bits("tok")
    return [("grp", bit) for bit in axis_bits("grp")] + [("tok", bit) for bit in tok_bits]


def sum_all(values):
    for axis, bit in reversed(bit_order()):
        values = values + swap(values, axis, bit)
    return values


def scatter_order():
    bits = bit_order()
    return [bits[-1]] + bits[:-1][::-1][len(axis_bits("tok")) - 1 :] + bits[:-1][::-1][: len(axis_bits("tok")) - 1]


class Chain:
    def __init__(self, units):
        bits = bit_order()
        self.left = list(bits)
        self.order = scatter_order()
        self.values = units.reshape((units.shape[0],) + (2,) * len(bits) + (units.shape[1] >> len(bits), C))
        self.back = None

    def begin(self):
        axis, bit = self.order.pop(0)
        dim = 1 + self.left.index((axis, bit))
        self.left.remove((axis, bit))
        mine = my_bit(axis, bit)
        self.away = lax.dynamic_index_in_dim(self.values, 1 - mine, dim, keepdims=False)
        self.stay = lax.dynamic_index_in_dim(self.values, mine, dim, keepdims=False)
        self.back = swap(self.away, axis, bit)

    def end(self):
        self.values = (self.stay.astype(jnp.float32) + self.back.astype(jnp.float32)).astype(jnp.bfloat16)
        self.back = None


class SumChain:
    def __init__(self, values):
        self.order = list(reversed(bit_order()))
        self.values = values
        self.back = None

    def begin(self):
        axis, bit = self.order.pop(0)
        self.away = self.values
        self.back = swap(self.away, axis, bit)

    def end(self):
        self.values = self.values + self.back
        self.back = None


class Beside:
    def __init__(self):
        self.chains = []

    def step(self):
        ties = []
        for chain in self.chains:
            if chain.back is not None:
                ties.append(chain.back)
                chain.end()
        for chain in self.chains:
            if chain.order:
                chain.begin()
                ties.append(chain.away)
        return ties

    def finish(self):
        while any(chain.order or chain.back is not None for chain in self.chains):
            self.step()


def gather_unit(piece):
    bits = bit_order()
    held = []
    values = piece[None]
    for axis, bit in reversed(scatter_order()):
        other = swap(values, axis, bit)
        mine = my_bit(axis, bit) == 0
        pair = jnp.stack([jnp.where(mine, values, other), jnp.where(mine, other, values)])
        held.insert(0, (axis, bit))
        values = pair
    values = values.reshape((2,) * len(bits) + piece.shape)
    order = [held.index(name) for name in bits] + [len(bits), len(bits) + 1]
    return values.transpose(order).reshape(-1, piece.shape[1])


def body(
    patches,
    labels,
    valid_mask,
    crop_counts,
    owners,
    slot_weight,
    slot_moment,
    slot_second,
    norm_params,
    norm_moment,
    norm_second,
    head_weight,
    head_moment,
    head_second,
):
    tok_dev = patches.shape[0]
    n_tok = lax.axis_size("tok")
    n_grp = lax.axis_size("grp")
    tok_index = lax.axis_index("tok")
    group_tok = tok_dev * n_tok
    counts = crop_counts[0]
    n_unit = owners.shape[0]
    slot_rows, columns = slot_weight.shape
    unit_order = jnp.arange(n_unit, dtype=jnp.int32)
    same_owner = owners[:, None] == owners[None, :]
    rank_of = jnp.sum(same_owner & (unit_order[None, :] < unit_order[:, None]), 1)
    slot_of = owners * slot_rows + rank_of
    chunk = columns // n_tok // C
    pieces = slot_weight.astype(jnp.bfloat16).reshape(slot_rows, n_tok, chunk, C)
    pieces = lax.all_to_all(pieces, "tok", split_axis=1, concat_axis=0, tiled=True)
    unit_part = jnp.take(pieces.reshape(slot_rows * n_tok, chunk, C), slot_of, axis=0)
    first_unit = gather_unit(unit_part[0])
    embedding = first_unit[:PIN]
    kernels = first_unit[PIN : PIN + BLOCKS * 9 * FF // C].reshape(BLOCKS, 9, FF).astype(jnp.float32)
    layers = []
    for layer_at in range(BLOCKS):
        own = lax.all_gather(unit_part[1 + 4 * layer_at : 5 + 4 * layer_at], BOTH, axis=1, tiled=True)
        keyval = own[0, 2 * C :].reshape(C, 2, C)
        layers.append(
            (
                (own[0, :C], own[0, C : 2 * C], keyval[:, 0], keyval[:, 1], own[1]),
                (own[2].reshape(C, FF), own[3], kernels[layer_at]),
            )
        )

    towards = [(i + 1, i) for i in range(n_tok - 1)]
    window = tok_dev + OVER
    tiles = window // 4
    patches = jnp.concatenate([patches, lax.ppermute(patches[:OVER], "tok", towards)], 0)
    marks = jnp.stack([labels, valid_mask])
    marks = jnp.concatenate([marks, lax.ppermute(marks[:, :OVER], "tok", towards)], 1)
    patches = patches.reshape(tiles, 4, PIN).transpose(1, 0, 2).reshape(window, PIN)
    marks = marks.reshape(2, tiles, 4).transpose(0, 2, 1).reshape(2, window)
    labels = marks[0]
    first_tok = tok_index * tok_dev
    positions = first_tok + 4 * jnp.arange(tiles, dtype=jnp.int32)
    begin_at, half_side, tile_y, tile_x, _ = image_layout(positions, counts)
    own_image = (begin_at >= first_tok) & (begin_at < first_tok + tok_dev) & (positions < group_tok)
    is_real = positions < counts[0] * BIG_SIDE**2 + counts[1] * SMALL_SIDE**2
    shifts = shift_matrices(begin_at, half_side, tile_y, tile_x, is_real)
    image_of = jnp.where(positions < group_tok, begin_at, -1)
    bias = block_bias(image_of)
    stacks = shift_stacks(shifts)
    real_rows = jnp.broadcast_to(is_real.astype(jnp.float32)[:, None], (tiles, LANES))
    keep_mask = marks[1].astype(jnp.float32) * jnp.tile((own_image & is_real).astype(jnp.float32), 4)
    pixel_total = sum_all(jnp.sum(keep_mask)[None])[0]
    tail = 6 * BLOCKS
    embed_pre = product(patches, embedding)
    resid = layer_norm(embed_pre, norm_params[tail], norm_params[tail + 1])
    kept_all = []
    for layer_at in range(BLOCKS):
        attn_part, mlp_part = layers[layer_at]
        at = 6 * layer_at
        middle, *attn_kept = attention_forward(resid, norm_params[at : at + 4], *attn_part, bias)
        output, *mlp_kept = mlp_forward(middle, norm_params[at + 4 : at + 6], *mlp_part, stacks, real_rows)
        kept_all.append((resid, attn_kept, middle, mlp_kept))
        resid = output
    final = layer_norm(resid, norm_params[tail + 2], norm_params[tail + 3]).astype(jnp.bfloat16)
    head_low = head_weight.astype(jnp.bfloat16)
    logits = product(final, head_low)
    row_peak = jnp.max(logits, -1, keepdims=True)
    log_norm = row_peak[:, 0] + jnp.log(jnp.sum(jnp.exp(logits - row_peak), -1))
    onehot = (labels[:, None] == jnp.arange(head_weight.shape[1], dtype=jnp.int32)[None, :]).astype(
        jnp.float32
    )
    picked = jnp.sum(logits * onehot, 1)
    loss_local = jnp.sum((log_norm - picked) * keep_mask)
    probs = jnp.exp(logits - log_norm[:, None])
    d_logits = ((probs - onehot) * (keep_mask / pixel_total)[:, None]).astype(jnp.bfloat16)
    d_head = outer_sum(final, d_logits)
    grad_res, gain_final, shift_final = norm_back(
        resid, norm_params[tail + 2], norm_params[tail + 3], back_product(d_logits, head_low)
    )
    beside = Beside()
    head_chain = SumChain(d_head)
    beside.chains.append(head_chain)
    unit_chains = [None] * BLOCKS
    kernel_grads = [None] * BLOCKS
    gain_grads = [None] * BLOCKS
    for layer_at in reversed(range(BLOCKS)):
        attn_part, mlp_part = layers[layer_at]
        at = 6 * layer_at
        entry, attn_kept, middle, mlp_kept = kept_all[layer_at]
        grad_res, d_up, d_down, kernel_grads[layer_at], mlp_gains = mlp_backward(
            grad_res, middle, norm_params[at + 4 : at + 6], *mlp_part, stacks, real_rows, mlp_kept, beside.step()
        )
        mlp_chain = Chain(jnp.stack([d_up.reshape(-1, C), d_down]))
        beside.chains.append(mlp_chain)
        grad_res, d_qo, d_kv, d_reduce, attn_gains = attention_backward(
            grad_res, entry, norm_params[at : at + 4], *attn_part, bias, attn_kept, beside.step()
        )
        d_kv = jnp.stack([d_kv[:C], d_kv[C:]], 1).reshape(2 * C, C)
        attn_units = jnp.stack([jnp.concatenate([d_qo, d_kv], 0), d_reduce])
        gain_grads[layer_at] = jnp.concatenate([attn_gains, mlp_gains], 0)
        if layer_at:
            attn_chain = Chain(attn_units)
            beside.chains.append(attn_chain)
            unit_chains[layer_at] = (attn_chain, mlp_chain)
    d_embed_pre, gain_embed, shift_embed = norm_back(
        embed_pre, norm_params[tail], norm_params[tail + 1], grad_res
    )
    d_embedding = outer_sum(patches, d_embed_pre.astype(jnp.bfloat16))
    first_grad = jnp.concatenate(
        [
            d_embedding.astype(jnp.bfloat16),
            jnp.stack(kernel_grads).reshape(-1, C).astype(jnp.bfloat16),
            jnp.zeros((C * FF // C - PIN - BLOCKS * 9 * FF // C, C), jnp.bfloat16),
        ]
    )
    last_chain = Chain(jnp.concatenate([first_grad[None], attn_units], 0))
    norm_grads = jnp.concatenate(
        gain_grads + [jnp.stack([gain_embed, shift_embed, gain_final, shift_final])], 0
    )
    small_chain = SumChain(jnp.concatenate([norm_grads, jnp.full((1, C), loss_local)], 0))
    beside.chains += [last_chain, small_chain]
    beside.finish()
    parts = [last_chain.values, mlp_chain.values]
    for attn_chain, mlp_chain in unit_chains[1:]:
        parts += [attn_chain.values, mlp_chain.values]
    stacked = jnp.concatenate(parts, 0)
    row_ids = jnp.arange(slot_rows * n_tok, dtype=jnp.int32)
    matches = slot_of[None, :] == row_ids[:, None]
    unit_at = jnp.where(jnp.any(matches, 1), jnp.argmax(matches, 1), n_unit)
    padded = jnp.concatenate([stacked, jnp.zeros_like(stacked[:1])], 0)
    placed = jnp.take(padded, unit_at, axis=0)[:, None]
    owned = lax.all_to_all(placed, "tok", split_axis=0, concat_axis=1, tiled=True)
    owned = owned.astype(jnp.float32).reshape(slot_rows, columns)
    head_total = head_chain.values
    norm_total, loss_sum = (small_chain.values[:-1], small_chain.values[-1, 0])
    slot_m, slot_v, slot_w = adamw_step(
        slot_weight, slot_moment, slot_second, owned, RATE_MATRIX, DECAY_RATE
    )
    norm_m, norm_v, norm_w = adamw_step(
        norm_params, norm_moment, norm_second, norm_total, RATE_VECTOR, 0.0
    )
    head_m, head_v, head_w = adamw_step(
        head_weight, head_moment, head_second, head_total, RATE_MATRIX, DECAY_RATE
    )
    return (
        loss_sum,
        pixel_total,
        slot_m,
        slot_v,
        slot_w,
        norm_m,
        norm_v,
        norm_w,
        head_m,
        head_v,
        head_w,
    )


def solution(mesh):
    in_specs = (
        P(("grp", "tok"), None),
        P(("grp", "tok")),
        P(("grp", "tok")),
        P("grp", None),
        P(),
        P("tok", "grp"),
        P("tok", "grp"),
        P("tok", "grp"),
        P(),
        P(),
        P(),
        P(),
        P(),
        P(),
    )
    out_specs = (
        P(),
        P(),
        P("tok", "grp"),
        P("tok", "grp"),
        P("tok", "grp"),
        P(),
        P(),
        P(),
        P(),
        P(),
        P(),
    )
    return jax.shard_map(body, mesh=mesh, in_specs=in_specs, out_specs=out_specs, check_vma=False)
```

```python
import functools

import jax
import jax.numpy as jnp
import numpy as np
from jax import lax
from jax.experimental import pallas as pl
from jax.experimental.pallas import tpu as pltpu
from jax.sharding import PartitionSpec as P

C = 320
HEADS = 5
HD = 64
FF = 1280
PIN = 1152
BLOCKS = 3
BIG_SIDE = 14
SMALL_SIDE = 6
STEP = 10
KVH = 49


EPS_NORM = 1e-06
BETA_ONE = 0.9
BETA_TWO = 0.999
ADAM_EPS = 1e-08
RATE_MATRIX = 0.05
RATE_VECTOR = 0.3
DECAY_RATE = 0.05
NEG_FILL = -1e30
PREC_HIGH = lax.Precision.HIGHEST


def layer_norm(values, gain_vec, shift_vec):
    center = values - jnp.mean(values, -1, keepdims=True)
    inverse = lax.rsqrt(jnp.mean(center * center, -1, keepdims=True) + EPS_NORM)
    return center * inverse * gain_vec + shift_vec


def adamw_step(weight, moment, second, gradient, rate_now, decay_now):
    moment = BETA_ONE * moment + (1.0 - BETA_ONE) * gradient
    second = BETA_TWO * second + (1.0 - BETA_TWO) * gradient * gradient
    m_hat = moment / (1.0 - BETA_ONE**STEP)
    v_hat = second / (1.0 - BETA_TWO**STEP)
    weight = weight - rate_now * (m_hat / (jnp.sqrt(v_hat) + ADAM_EPS) + decay_now * weight)
    return (moment, second, weight)


def product(left, right):
    return jnp.dot(left, right, preferred_element_type=jnp.float32)


def outer_sum(left, right):
    return lax.dot_general(
        left, right, (((0,), (0,)), ((), ())), preferred_element_type=jnp.float32
    )


def back_product(gradient, weight):
    return lax.dot_general(
        gradient, weight, (((1,), (1,)), ((), ())), preferred_element_type=jnp.float32
    )


def norm_back(values, gain_vec, shift_vec, gradient):
    _, pull_back = jax.vjp(layer_norm, values, gain_vec, shift_vec)
    return pull_back(gradient)


OVER = 4 * KVH - 4


def image_layout(positions, counts):
    big_tok = BIG_SIDE * BIG_SIDE
    small_tok = SMALL_SIDE * SMALL_SIDE
    big_end = counts[0] * big_tok
    small_end = big_end + counts[1] * small_tok
    is_big = positions < big_end
    is_small = jnp.logical_and(positions >= big_end, positions < small_end)
    half_side = jnp.where(is_big, BIG_SIDE // 2, SMALL_SIDE // 2)
    begin_at = jnp.where(
        is_big,
        positions // big_tok * big_tok,
        jnp.where(is_small, big_end + (positions - big_end) // small_tok * small_tok, small_end),
    )
    tile_idx = (positions - begin_at) // 4
    return (begin_at, half_side, tile_idx // half_side, tile_idx % half_side, positions < small_end)


def shift_stacks(half_side, tile_y, tile_x, is_real):
    tiles = half_side.shape[0]
    step_y = np.array([[0, 1 - 2 * (sub // 2), 1 - 2 * (sub // 2)] for sub in range(4)], np.int32)[:, :, None]
    step_x = np.array([[1 - 2 * (sub % 2), 0, 1 - 2 * (sub % 2)] for sub in range(4)], np.int32)[:, :, None]
    at_y = tile_y + step_y
    at_x = tile_x + step_x
    inside = is_real & (at_y >= 0) & (at_y < half_side) & (at_x >= 0) & (at_x < half_side)
    source = jnp.arange(tiles, dtype=jnp.int32) + step_y * half_side + step_x
    source = jnp.where(inside, source, -1)
    cut = row_cut(tiles)
    columns = jnp.arange(SPAN, dtype=jnp.int32)
    upper = (source[:, :, :cut, None] == columns).astype(jnp.bfloat16)
    lower = (source[:, :, cut:, None] == columns + (tiles - SPAN)).astype(jnp.bfloat16)
    return (upper.reshape(4, 3 * cut, SPAN), lower.reshape(4, 3 * (tiles - cut), SPAN))


def tap_source(sub, tap):
    y_at = sub // 2 + tap // 3 - 1
    x_at = sub % 2 + tap % 3 - 1
    return (y_at % 2 * 2 + x_at % 2, y_at // 2, x_at // 2)


SQRT_HALF = 0.7071067811865476
INV_SQRT_TWO_PI = 0.3989422804014327
TAPS_OF = [[tap_source(sub, tap) for tap in range(9)] for sub in range(4)]
VMEM_LIMIT = 56 * 1024 * 1024
SPAN = 256
ROWS = 16
LANES = 128


def row_cut(tiles):
    return (tiles // 2 + 15) // 16 * 16


def move_planes(planes_ref, upper_ref, lower_ref, moved_ref):
    tiles = planes_ref.shape[0] // 4
    cut = row_cut(tiles)
    for sub in range(4):
        base = sub * tiles
        part = product(upper_ref[sub], planes_ref[base : base + SPAN, :])
        for key in range(3):
            moved_ref[sub, key, :cut, :] = part[key * cut : (key + 1) * cut]
        part = product(lower_ref[sub], planes_ref[base + tiles - SPAN : base + tiles, :])
        for key in range(3):
            moved_ref[sub, key, cut:, :] = part[key * (tiles - cut) : (key + 1) * (tiles - cut)]


def chunk_sources(planes_ref, moved_ref, row, lanes):
    tiles = planes_ref.shape[0] // 4
    found = {}
    for sub in range(4):
        found[sub, 0, 0] = planes_ref[pl.ds(pl.multiple_of(sub * tiles + row, ROWS), ROWS), lanes].astype(jnp.float32)
        step_y = 1 - 2 * (sub // 2)
        step_x = 1 - 2 * (sub % 2)
        for key, step in enumerate(((0, step_x), (step_y, 0), (step_y, step_x))):
            found[(sub,) + step] = moved_ref[sub, key, pl.ds(row, ROWS), lanes]
    return found


def norm_rows(values, gain, shift):
    center = values - jnp.mean(values, -1, keepdims=True)
    inverse = lax.rsqrt(jnp.mean(center * center, -1, keepdims=True) + EPS_NORM)
    unit = center * inverse
    return (unit, inverse, unit * gain + shift)


def norm_rows_back(unit, inverse, gain, grad):
    scaled = grad * gain
    return inverse * (
        scaled - jnp.mean(scaled, -1, keepdims=True) - unit * jnp.mean(scaled * unit, -1, keepdims=True)
    )


def mlp_forward_kernel(
    advance,
    middle_ref, gains_ref, up_ref, down_ref, kern_ref, upper_ref, lower_ref, real_ref,
    out_ref, hidden_ref, active_ref, slope_ref, turned_ref,
    normed_ref, moved_ref, planes_ref,
):
    rows = middle_ref.shape[0]
    block = hidden_ref.shape[1]
    tiles = rows // 4

    @pl.when(pl.program_id(0) == 0)
    def _():
        normed = norm_rows(middle_ref[...], gains_ref[0:1, :], gains_ref[1:2, :])[2]
        normed_ref[...] = normed.astype(jnp.bfloat16)
        out_ref[...] = middle_ref[...]
        spread_rows(up_ref[0], planes_ref)
        for quarter in range(FF // C):
            for at, lane, width in lane_parts(C):
                part = planes_ref[at, pl.ds(quarter, C, stride=FF // C), :][:, :width]
                begin = quarter * C + lane
                turned_ref[:, begin : begin + width] = part.astype(jnp.bfloat16)

    advance()
    for sub in range(4):
        columns = pl.ds(pl.multiple_of(pl.program_id(0) * block, block), block)
        part = product(normed_ref[sub * tiles : (sub + 1) * tiles, :], turned_ref[:, columns])
        hidden_ref[sub * tiles : (sub + 1) * tiles, :] = part.astype(jnp.bfloat16)
    move_planes(hidden_ref, upper_ref, lower_ref, moved_ref)

    for lane in range(0, hidden_ref.shape[1], LANES):
        lanes = slice(lane, lane + LANES)
        kern = [kern_ref[0, tap : tap + 1, lanes] for tap in range(9)]

        @pl.loop(0, tiles // ROWS, unroll=tiles // ROWS)
        def _(at):
            row = pl.multiple_of(at * ROWS, ROWS)
            found = chunk_sources(hidden_ref, moved_ref, row, lanes)
            real = real_ref[pl.ds(row, ROWS), :] > 0.0
            for sub in range(4):
                center = found[sub, 0, 0] * kern[4]
                total = center
                for tap in range(9):
                    if tap != 4:
                        total = total + found[TAPS_OF[sub][tap]] * kern[tap]
                mixed = jnp.where(real, total, center)
                half = 0.5 + 0.5 * lax.erf(mixed * SQRT_HALF)
                bell = jnp.exp(-0.5 * mixed * mixed) * INV_SQRT_TWO_PI
                span = pl.ds(pl.multiple_of(sub * tiles + row, ROWS), ROWS)
                active_ref[span, lanes] = (mixed * half).astype(jnp.bfloat16)
                slope_ref[span, lanes] = (half + mixed * bell).astype(jnp.bfloat16)

    for sub in range(4):
        span = slice(sub * tiles, (sub + 1) * tiles)
        out_ref[span, :] += product(active_ref[span, :], down_ref[0])


def lane_parts(width):
    return [(at, lane, min(LANES, width - lane)) for at, lane in enumerate(range(0, width, LANES))]


def spread_rows(source, planes_ref):
    for at, lane, width in lane_parts(source.shape[1]):
        planes_ref[at, :, :width] = source[:, lane : lane + width].astype(jnp.float32)


class Plan:
    def __init__(self, value, out, scratch, make, space=None):
        self.value, self.out, self.scratch, self.make = value, out, scratch, make
        self.in_spec = whole(value.shape)
        self.out_spec = pl.BlockSpec(memory_space=space) if space is not None else whole(out.shape)


def plan_sum(value):
    return Plan(value, jax.ShapeDtypeStruct(value.shape, value.dtype), sum_scratch(value.shape), SumRide)


def plan_units(value, begin, end):
    if begin == 0:
        value = unit_blocks(value)
    total, (chunk, width) = value.shape[0], value.shape[-2:]
    inside = unit_layout(unit_order(0))[end] if end < len(bit_order()) else ()
    out = jax.ShapeDtypeStruct((total,) + inside + (chunk, width), value.dtype)

    def make(ride_in, ride_out, scratch):
        sources = [(ride_in, at) for at in range(total)]
        return UnitRide(sources, ride_out, scratch, begin, end)

    return Plan(value, out, unit_scratch(total, chunk, width, begin, end), make)


def plan_gather(piece):
    total, chunk, width = piece.shape
    out = jax.ShapeDtypeStruct((total,) + (2,) * len(bit_order()) + (chunk, width), piece.dtype)
    scratch = gather_scratch(total) + [pltpu.VMEM(out.shape, piece.dtype), pltpu.SemaphoreType.DMA((1,))]
    return Plan(piece, out, scratch, PieceRide, pl.ANY)


class Rides:
    def __init__(self, rides):
        self.rides = rides
        self.phases = max(ride.phases for ride in rides)
        names = [name for name in bit_order() if any(name in ride.names for ride in rides)]
        self.peers = [UnitRide.partner(rides[0], name) for name in names]

    def signal(self):
        signal_all(self.peers)

    def advance(self, phase):
        if phase == 0:
            pl.semaphore_wait(pltpu.get_barrier_semaphore(), len(self.peers))
        for ride in self.rides:
            if phase <= ride.phases:
                ride.advance(phase)


def rides_of(plans, ins, outs, scratch):
    rides = []
    for plan, ride_in, ride_out in zip(plans, ins, outs):
        count = len(plan.scratch)
        rides.append(plan.make(ride_in, ride_out, scratch[:count]))
        scratch = scratch[count:]
    return Rides(rides)


def ridden(kernel, inputs, outputs, scratch, steps, plans):
    def run(*refs):
        own_in, refs = refs[:inputs], refs[inputs:]
        ride_in, refs = refs[: len(plans)], refs[len(plans) :]
        own_out, refs = refs[:outputs], refs[outputs:]
        ride_out, rest = refs[: len(plans)], refs[len(plans) :]
        rides = rides_of(plans, ride_in, ride_out, rest[scratch:])
        first = min(steps, rides.phases + 1)

        def advance():
            for phase in range(first):
                pl.when(pl.program_id(0) == phase)(functools.partial(rides.advance, phase))

        pl.when(pl.program_id(0) == 0)(rides.signal)
        kernel(advance, *own_in, *own_out, *rest[:scratch])
        if rides.phases >= first:

            @pl.when(pl.program_id(0) == steps - 1)
            def _():
                for phase in range(first, rides.phases + 1):
                    rides.advance(phase)

    return run


def whole(shape):
    return pl.BlockSpec(shape, lambda j: (0,) * len(shape))


def unit_spec(at):
    return pl.BlockSpec((1, FF, C), lambda j: (at, 0, 0))


def mlp_forward(middle, gains, units, at, kernel, layer_at, stacks, real_rows, plans, meeting):
    rows = middle.shape[0]
    block = 256
    by_lane = pl.BlockSpec((rows, block), lambda j: (0, j))
    low = jax.ShapeDtypeStruct((rows, FF), jnp.bfloat16)
    body_of = functools.partial(mlp_forward_kernel, lambda: None)
    limits = dict(vmem_limit_bytes=VMEM_LIMIT)
    if plans:
        body_of = ridden(mlp_forward_kernel, 8, 5, 3, FF // block, plans)
        limits.update(collective_id=meeting, has_side_effects=True)
    return pl.pallas_call(
        body_of,
        grid=(FF // block,),
        out_shape=(
            jax.ShapeDtypeStruct((rows, C), jnp.float32),
            low,
            low,
            low,
            jax.ShapeDtypeStruct((C, FF), jnp.bfloat16),
            *[plan.out for plan in plans],
        ),
        in_specs=[
            whole((rows, C)),
            whole((2, C)),
            unit_spec(at),
            pl.BlockSpec((1, block, C), lambda j: (at + 1, j, 0)),
            pl.BlockSpec((1, 9, block), lambda j: (layer_at, 0, j)),
            whole(stacks[0].shape),
            whole(stacks[1].shape),
            whole(real_rows.shape),
        ]
        + [plan.in_spec for plan in plans],
        out_specs=(whole((rows, C)), by_lane, by_lane, by_lane, whole((C, FF)))
        + tuple(plan.out_spec for plan in plans),
        scratch_shapes=[
            pltpu.VMEM((rows, C), jnp.bfloat16),
            pltpu.VMEM((4, 3, rows // 4, block), jnp.float32),
            pltpu.VMEM((3, FF, LANES), jnp.float32),
        ]
        + sum([plan.scratch for plan in plans], []),
        compiler_params=pltpu.CompilerParams(**limits),
        cost_estimate=pl.CostEstimate(flops=14 * 10**9, bytes_accessed=18 * 10**6, transcendentals=4 * 10**6),
        name="mlp_forward",
    )(middle, gains, units, units, kernel, stacks[0], stacks[1], real_rows, *[plan.value for plan in plans])


def mlp_backward_kernel(
    advance,
    grad_ref, middle_ref, gains_ref, up_ref, down_ref, kern_ref, upper_ref, lower_ref, real_ref,
    hidden_ref, active_ref, slope_ref,
    out_ref, dunits_ref, dkern_ref, dgain_ref,
    low_ref, low_t_ref, normed_t_ref, mixed_ref, dhid_ref, moved_ref, back_ref, wide_ref, planes_ref,
):
    rows = grad_ref.shape[0]
    tiles = rows // 4
    block = hidden_ref.shape[1]

    @pl.when(pl.program_id(0) == 0)
    def _():
        for sub in range(4):
            span = slice(sub * tiles, (sub + 1) * tiles)
            low_ref[span, :] = grad_ref[span, :].astype(jnp.bfloat16)
        normed = norm_rows(middle_ref[...], gains_ref[0:1, :], gains_ref[1:2, :])[2]
        normed_t_ref[...] = normed.T.astype(jnp.bfloat16)
        low_t_ref[...] = grad_ref[...].T.astype(jnp.bfloat16)
        back_ref[...] = jnp.zeros_like(back_ref)

    advance()
    for sub in range(4):
        span = slice(sub * tiles, (sub + 1) * tiles)
        part = back_product(low_ref[span, :], down_ref[0]).astype(jnp.bfloat16).astype(jnp.float32)
        mixed_ref[span, :] = (part * slope_ref[span, :].astype(jnp.float32)).astype(jnp.bfloat16)
    down_rows = pl.ds(pl.multiple_of(pl.program_id(0) * block, block), block)
    dunits_ref[1, down_rows, :] = product(low_t_ref[...], active_ref[...]).T.astype(jnp.bfloat16)
    move_planes(mixed_ref, upper_ref, lower_ref, moved_ref)

    for lane in range(0, block, LANES):
        lanes = slice(lane, lane + LANES)
        kern = [kern_ref[0, tap : tap + 1, lanes] for tap in range(9)]

        def step(at, sums):
            row = pl.multiple_of(at * ROWS, ROWS)
            found = chunk_sources(mixed_ref, moved_ref, row, lanes)
            real = real_ref[pl.ds(row, ROWS), :] > 0.0
            sums = list(sums)
            for sub in range(4):
                span = pl.ds(pl.multiple_of(sub * tiles + row, ROWS), ROWS)
                hidden = hidden_ref[span, lanes].astype(jnp.float32)
                center = found[sub, 0, 0] * kern[4]
                total = center
                for tap in range(9):
                    term = found[TAPS_OF[sub][tap]]
                    if tap != 4:
                        total = total + term * kern[8 - tap]
                    piece = hidden * term
                    sums[tap] = sums[tap] + piece[:8] + piece[8:]
                dhid_ref[span, lanes] = jnp.where(real, total, center).astype(jnp.bfloat16)
            return tuple(sums)

        sums = lax.fori_loop(0, tiles // ROWS, step, (jnp.zeros((8, LANES), jnp.float32),) * 9, unroll=True)
        for tap in range(9):
            dkern_ref[8 - tap : 9 - tap, lanes] = jnp.sum(sums[tap], 0, keepdims=True)

    columns = pl.ds(pl.multiple_of(pl.program_id(0) * block, block), block)
    wide_ref[:, columns] = product(normed_t_ref[...], dhid_ref[...])
    for sub in range(4):
        span = slice(sub * tiles, (sub + 1) * tiles)
        back_ref[span, :] += back_product(dhid_ref[span, :], up_ref[...])

    @pl.when(pl.program_id(0) == pl.num_programs(0) - 1)
    def _():
        grad = back_ref[...]
        unit, inverse, _ = norm_rows(middle_ref[...], gains_ref[0:1, :], gains_ref[1:2, :])
        out_ref[...] = grad_ref[...] + norm_rows_back(unit, inverse, gains_ref[0:1, :], grad)
        dgain_ref[0:1, :] = jnp.sum(grad * unit, 0, keepdims=True)
        dgain_ref[1:2, :] = jnp.sum(grad, 0, keepdims=True)
        for quarter in range(FF // C):
            for at, lane, width in lane_parts(C):
                begin = quarter * C + lane
                part = wide_ref[:, begin : begin + width]
                if width < LANES:
                    part = jnp.concatenate([part, jnp.zeros((C, LANES - width), jnp.float32)], 1)
                planes_ref[at, pl.ds(quarter, C, stride=FF // C), :] = part
        for at, lane, width in lane_parts(C):
            dunits_ref[0, :, lane : lane + width] = planes_ref[at, :, :width].astype(jnp.bfloat16)


def mlp_backward(grad, middle, gains, w_up, units, at, kernel, layer_at, stacks, real_rows, kept, plans, meeting):
    rows = middle.shape[0]
    block = 256
    by_lane = pl.BlockSpec((rows, block), lambda j: (0, j))
    up_spec = pl.BlockSpec((C, block), lambda j: (0, j))
    tap_spec = pl.BlockSpec((9, block), lambda j: (0, j))
    return pl.pallas_call(
        ridden(mlp_backward_kernel, 12, 4, 9, FF // block, plans),
        grid=(FF // block,),
        out_shape=(
            jax.ShapeDtypeStruct((rows, C), jnp.float32),
            jax.ShapeDtypeStruct((2, FF, C), jnp.bfloat16),
            jax.ShapeDtypeStruct((9, FF), jnp.float32),
            jax.ShapeDtypeStruct((2, C), jnp.float32),
            *[plan.out for plan in plans],
        ),
        in_specs=[
            whole((rows, C)),
            whole((rows, C)),
            whole((2, C)),
            up_spec,
            pl.BlockSpec((1, block, C), lambda j: (at + 1, j, 0)),
            pl.BlockSpec((1, 9, block), lambda j: (layer_at, 0, j)),
            whole(stacks[0].shape),
            whole(stacks[1].shape),
            whole(real_rows.shape),
            by_lane,
            by_lane,
            by_lane,
        ]
        + [plan.in_spec for plan in plans],
        out_specs=(whole((rows, C)), whole((2, FF, C)), tap_spec, whole((2, C)))
        + tuple(plan.out_spec for plan in plans),
        scratch_shapes=[
            pltpu.VMEM((rows, C), jnp.bfloat16),
            pltpu.VMEM((C, rows), jnp.bfloat16),
            pltpu.VMEM((C, rows), jnp.bfloat16),
            pltpu.VMEM((rows, block), jnp.bfloat16),
            pltpu.VMEM((rows, block), jnp.bfloat16),
            pltpu.VMEM((4, 3, rows // 4, block), jnp.float32),
            pltpu.VMEM((rows, C), jnp.float32),
            pltpu.VMEM((C, FF), jnp.float32),
            pltpu.VMEM((3, FF, LANES), jnp.float32),
        ]
        + sum([plan.scratch for plan in plans], []),
        compiler_params=pltpu.CompilerParams(
            collective_id=meeting, has_side_effects=True, vmem_limit_bytes=VMEM_LIMIT
        ),
        cost_estimate=pl.CostEstimate(flops=18 * 10**9, bytes_accessed=18 * 10**6, transcendentals=0),
        name="mlp_backward",
    )(grad, middle, gains, w_up, units, kernel, stacks[0], stacks[1], real_rows, *kept, *[plan.value for plan in plans])


WIDE = 384
BLOCK_TILES = 32
KEY_SPAN = 128


def block_places(tiles):
    places = []
    for index in range(-(-tiles // BLOCK_TILES)):
        start = min(index * BLOCK_TILES, tiles - BLOCK_TILES)
        places.append((start, min(max(start - 48, 0), tiles - KEY_SPAN)))
    return places


def block_bias(tiles, image_at):
    starts, lows = np.array(block_places(tiles), np.int32).T[:, :, None]
    columns = starts + np.tile(np.arange(BLOCK_TILES, dtype=np.int32), 4)
    rows = lows + np.arange(KEY_SPAN, dtype=np.int32)
    same = image_at(jnp.asarray(rows))[:, :, None] == image_at(jnp.asarray(columns))[:, None, :]
    return jnp.where(same, 0.0, NEG_FILL)


def place_of(index, tiles):
    start = jnp.minimum(index * BLOCK_TILES, tiles - BLOCK_TILES)
    low = jnp.clip(start - 48, 0, tiles - KEY_SPAN)
    return (pl.multiple_of(start, ROWS), pl.multiple_of(low, ROWS))


def four_planes(ref, start, lanes):
    tiles = ref.shape[0] // 4
    return jnp.concatenate(
        [ref[pl.ds(pl.multiple_of(sub * tiles + start, ROWS), BLOCK_TILES), lanes] for sub in range(4)], 0
    )


def put_planes(ref, start, lanes, values):
    tiles = ref.shape[0] // 4
    for sub in range(4):
        ref[pl.ds(pl.multiple_of(sub * tiles + start, ROWS), BLOCK_TILES), lanes] = values[
            sub * BLOCK_TILES : (sub + 1) * BLOCK_TILES
        ]


def head_pair(values, group):
    if group == 2:
        return values
    first = lax.broadcasted_iota(jnp.int32, values.shape, 1) < HD
    zero = jnp.zeros_like(values)
    return jnp.concatenate([jnp.where(first, values, zero), jnp.where(first, zero, values)], 0)


def softmax_columns(raw, bias):
    parts = []
    for half in range(raw.shape[0] // KEY_SPAN):
        scores = raw[half * KEY_SPAN : (half + 1) * KEY_SPAN] * HD ** (-0.5) + bias
        weights = jnp.exp(scores - jnp.max(scores, 0, keepdims=True))
        parts.append(weights * (1.0 / jnp.sum(weights, 0, keepdims=True)))
    return parts


def norm_store(source_ref, gains_ref, at, target_ref):
    normed = norm_rows(source_ref[...], gains_ref[at : at + 1, :], gains_ref[at + 1 : at + 2, :])[2]
    target_ref[...] = normed.astype(jnp.bfloat16)


def part_keyval(unit_ref, planes_ref, kv_ref):
    spread_rows(unit_ref[0, 2 * C :, :], planes_ref)
    for which in range(2):
        for at, lane, width in lane_parts(C):
            part = planes_ref[at, pl.ds(which, C, stride=2), :][:, :width]
            kv_ref[which, :, lane : lane + width] = part.astype(jnp.bfloat16)


def attention_forward_kernel(
    resid_ref, gains_ref, unit_ref, reduce_ref, bias_ref,
    middle_ref, normed_ref, query_ref, reduced_ref, key_ref, value_ref, attended_ref, kv_ref,
    planes_ref,
):
    part_keyval(unit_ref, planes_ref, kv_ref)
    rows = resid_ref.shape[0]
    tiles = rows // 4
    norm_store(resid_ref, gains_ref, 0, normed_ref)
    query_ref[:, C:] = jnp.zeros((rows, WIDE - C), jnp.bfloat16)
    reduced = jnp.zeros((tiles, C), jnp.float32)
    for sub in range(4):
        span = slice(sub * tiles, (sub + 1) * tiles)
        query_ref[span, :C] = product(normed_ref[span, :], unit_ref[0, :C, :]).astype(jnp.bfloat16)
        reduced = reduced + product(normed_ref[span, :], reduce_ref[0, sub * C : (sub + 1) * C, :])
    reduced_ref[...] = reduced
    normed_kv = norm_rows(reduced, gains_ref[2:3, :], gains_ref[3:4, :])[2].astype(jnp.bfloat16)
    for which, ref in enumerate((key_ref, value_ref)):
        ref[:, C:] = jnp.zeros((tiles, WIDE - C), jnp.bfloat16)
        ref[:, :C] = product(normed_kv, kv_ref[which]).astype(jnp.bfloat16)

    @pl.loop(0, bias_ref.shape[0], unroll=bias_ref.shape[0])
    def _(index):
        start, low = place_of(index, tiles)
        bias = bias_ref[index]
        for group in range(3):
            lanes = slice(group * LANES, (group + 1) * LANES)
            query = four_planes(query_ref, start, lanes)
            keys = head_pair(key_ref[pl.ds(low, KEY_SPAN), lanes], group)
            values = head_pair(value_ref[pl.ds(low, KEY_SPAN), lanes], group)
            probs = softmax_columns(back_product(keys, query), bias)
            probs = jnp.concatenate(probs, 0).T.astype(jnp.bfloat16)
            put_planes(attended_ref, start, lanes, product(probs, values).astype(jnp.bfloat16))

    for sub in range(4):
        span = slice(sub * tiles, (sub + 1) * tiles)
        middle_ref[span, :] = resid_ref[span, :] + product(attended_ref[span, :C], unit_ref[0, C : 2 * C, :])


def attention_forward(resid, gains, units, at, reduces, reduce_at, bias):
    rows = resid.shape[0]
    tiles = rows // 4
    low = jnp.bfloat16
    shapes = (
        jax.ShapeDtypeStruct((rows, C), jnp.float32),
        jax.ShapeDtypeStruct((rows, C), low),
        jax.ShapeDtypeStruct((rows, WIDE), low),
        jax.ShapeDtypeStruct((tiles, C), jnp.float32),
        jax.ShapeDtypeStruct((tiles, WIDE), low),
        jax.ShapeDtypeStruct((tiles, WIDE), low),
        jax.ShapeDtypeStruct((rows, WIDE), low),
        jax.ShapeDtypeStruct((2, C, C), low),
    )
    return pl.pallas_call(
        attention_forward_kernel,
        grid=(1,),
        out_shape=shapes,
        in_specs=[whole((rows, C)), whole((4, C)), unit_spec(at), unit_spec(reduce_at), whole(bias.shape)],
        out_specs=tuple(whole(shape.shape) for shape in shapes),
        scratch_shapes=[pltpu.VMEM((3, 2 * C, LANES), jnp.float32)],
        compiler_params=pltpu.CompilerParams(vmem_limit_bytes=VMEM_LIMIT),
        cost_estimate=pl.CostEstimate(flops=6 * 10**9, bytes_accessed=14 * 10**6, transcendentals=10**6),
        name="attention_forward",
    )(resid, gains, units, reduces, bias)


def embed_forward_kernel(
    patches_ref, halo_ref, unit_ref, gains_ref, pre_ref, resid_ref, kern_ref, planes_ref, taps_ref
):
    rows = pre_ref.shape[0]
    tiles = rows // 4
    used = FF * 9 * BLOCKS // C
    for ref, base in ((patches_ref, 0), (halo_ref, patches_ref.shape[0])):
        step = 64

        @pl.loop(0, ref.shape[0] // step, unroll=4)
        def _(at):
            span = pl.ds(pl.multiple_of(at * step, step), step)
            into = pl.ds(pl.multiple_of(base + at * step, step), step)
            part = product(ref[span, :], unit_ref[0, :PIN, :])
            for place, lane, width in lane_parts(C):
                planes_ref[place, into, :width] = part[:, lane : lane + width]

    for sub in range(4):
        for place, lane, width in lane_parts(C):
            pre_ref[sub * tiles : (sub + 1) * tiles, lane : lane + width] = planes_ref[
                place, pl.ds(sub, tiles, stride=4), :
            ][:, :width]
    taps = unit_ref[0, PIN : PIN + taps_ref.shape[1], :]
    spread_rows(taps, taps_ref)
    for layer_at in range(BLOCKS):
        for quarter in range(FF // C):
            for place, lane, width in lane_parts(C):
                begin = quarter * C + lane
                kern_ref[layer_at, :, begin : begin + width] = taps_ref[
                    place, pl.ds(layer_at * (used // BLOCKS) + quarter, 9, stride=FF // C), :
                ][:, :width]

    resid_ref[...] = norm_rows(pre_ref[...], gains_ref[0:1, :], gains_ref[1:2, :])[2]


def embed_forward(patches, halo, units, gains):
    rows = patches.shape[0] + halo.shape[0]
    wide = jax.ShapeDtypeStruct((rows, C), jnp.float32)
    taps = jax.ShapeDtypeStruct((BLOCKS, 9, FF), jnp.float32)
    return pl.pallas_call(
        embed_forward_kernel,
        grid=(1,),
        out_shape=(wide, wide, taps),
        in_specs=[whole(patches.shape), whole(halo.shape), unit_spec(0), whole((2, C))],
        out_specs=(whole(wide.shape), whole(wide.shape), whole(taps.shape)),
        scratch_shapes=[
            pltpu.VMEM((3, rows, LANES), jnp.float32),
            pltpu.VMEM((3, FF - PIN, LANES), jnp.float32),
        ],
        compiler_params=pltpu.CompilerParams(vmem_limit_bytes=VMEM_LIMIT),
        cost_estimate=pl.CostEstimate(flops=10**9, bytes_accessed=8 * 10**6, transcendentals=0),
        name="embed_forward",
    )(patches, halo, units, gains)


def embed_backward_kernel(
    grad_ref, pre_ref, gains_ref, patches_ref, halo_ref, *refs
):
    taps_refs = refs[:BLOCKS]
    unit_ref, dgain_ref, planes_ref, turned_ref, taps_ref = refs[BLOCKS:]
    rows = pre_ref.shape[0]
    tiles = rows // 4
    half = tiles // 2
    used = FF * 9 * BLOCKS // C
    sums = [jnp.zeros((1, C), jnp.float32)] * 2
    for sub in range(4):
        for part_at in range(2):
            span = slice(sub * tiles + part_at * half, sub * tiles + (part_at + 1) * half)
            unit, inverse, _ = norm_rows(pre_ref[span, :], gains_ref[0:1, :], gains_ref[1:2, :])
            grad = grad_ref[span, :]
            back = norm_rows_back(unit, inverse, gains_ref[0:1, :], grad)
            sums[0] = sums[0] + jnp.sum(grad * unit, 0, keepdims=True)
            sums[1] = sums[1] + jnp.sum(grad, 0, keepdims=True)
            for place, lane, width in lane_parts(C):
                value = back[:, lane : lane + width]
                if width < LANES:
                    value = jnp.concatenate([value, jnp.zeros((half, LANES - width), jnp.float32)], 1)
                planes_ref[place, pl.ds(4 * part_at * half + sub, half, stride=4), :] = value
    dgain_ref[0:1, :] = sums[0]
    dgain_ref[1:2, :] = sums[1]
    for place, lane, width in lane_parts(C):
        turned_ref[lane : lane + width, :] = planes_ref[place].T[:width, :].astype(jnp.bfloat16)
    split = patches_ref.shape[0]
    grads = product(turned_ref[:, :split], patches_ref[...]) + product(turned_ref[:, split:], halo_ref[...])
    unit_ref[0, :PIN, :] = grads.T.astype(jnp.bfloat16)
    taps_ref[...] = jnp.zeros_like(taps_ref)
    for layer_at, ref in enumerate(taps_refs):
        for quarter in range(FF // C):
            for place, lane, width in lane_parts(C):
                begin = quarter * C + lane
                value = ref[:, begin : begin + width]
                if width < LANES:
                    value = jnp.concatenate([value, jnp.zeros((9, LANES - width), jnp.float32)], 1)
                taps_ref[place, pl.ds(layer_at * (used // BLOCKS) + quarter, 9, stride=FF // C), :] = value
    for place, lane, width in lane_parts(C):
        unit_ref[0, PIN:, lane : lane + width] = taps_ref[place, :, :width].astype(jnp.bfloat16)


def embed_backward(grad, pre, gains, patches, halo, taps):
    rows = pre.shape[0]
    shapes = (jax.ShapeDtypeStruct((1, FF, C), jnp.bfloat16), jax.ShapeDtypeStruct((2, C), jnp.float32))
    operands = (grad, pre, gains, patches, halo, *taps)
    return pl.pallas_call(
        embed_backward_kernel,
        grid=(1,),
        out_shape=shapes,
        in_specs=[whole(part.shape) for part in operands],
        out_specs=tuple(whole(shape.shape) for shape in shapes),
        scratch_shapes=[
            pltpu.VMEM((3, rows, LANES), jnp.float32),
            pltpu.VMEM((C, rows), jnp.bfloat16),
            pltpu.VMEM((3, FF - PIN, LANES), jnp.float32),
        ],
        compiler_params=pltpu.CompilerParams(vmem_limit_bytes=VMEM_LIMIT),
        cost_estimate=pl.CostEstimate(flops=10**9, bytes_accessed=8 * 10**6, transcendentals=0),
        name="embed_backward",
    )(*operands)


def attention_backward_kernel(
    advance,
    grad_ref, resid_ref, gains_ref, unit_ref, reduce_ref, bias_ref,
    normed_ref, query_ref, reduced_ref, key_ref, value_ref, attended_ref, kv_ref,
    out_ref, dunits_ref, dgain_ref,
    turned_ref, datt_ref, dquery_ref, dkey_ref, dvalue_ref, first_ref, planes_ref,
):
    rows = resid_ref.shape[0]
    tiles = rows // 4
    low_type = jnp.bfloat16
    datt_ref[:, C:] = jnp.zeros((rows, WIDE - C), low_type)
    turned_ref[...] = grad_ref[...].T.astype(low_type)
    dunits_ref[0, C : 2 * C, :] = product(turned_ref[...], attended_ref[:, :C]).T.astype(low_type)
    for sub in range(4):
        span = slice(sub * tiles, (sub + 1) * tiles)
        datt_ref[span, :C] = back_product(grad_ref[span, :].astype(low_type), unit_ref[0, C : 2 * C, :]).astype(low_type)
    dkey_ref[...] = jnp.zeros_like(dkey_ref)
    dvalue_ref[...] = jnp.zeros_like(dvalue_ref)
    blocks = bias_ref.shape[0]

    def one_block(step):
        index = blocks - 1 - step
        start, low = place_of(index, tiles)
        bias = bias_ref[index]
        tile_at = lax.rem(lax.broadcasted_iota(jnp.int32, (4 * BLOCK_TILES, LANES), 0), BLOCK_TILES)
        fresh = tile_at >= index * BLOCK_TILES - start
        span = pl.ds(low, KEY_SPAN)
        for group in range(3):
            lanes = slice(group * LANES, (group + 1) * LANES)
            query = four_planes(query_ref, start, lanes)
            datt = four_planes(datt_ref, start, lanes)
            datt = jnp.where(fresh, datt, jnp.zeros_like(datt))
            keys = head_pair(key_ref[span, lanes], group)
            values = head_pair(value_ref[span, lanes], group)
            probs = softmax_columns(back_product(keys, query), bias)
            dprobs = back_product(values, datt)
            dscores = []
            for half, prob in enumerate(probs):
                dprob = dprobs[half * KEY_SPAN : (half + 1) * KEY_SPAN]
                inner = jnp.sum(prob * dprob, 0, keepdims=True)
                dscores.append(prob * (dprob - inner) * HD ** (-0.5))
            dscores = jnp.concatenate(dscores, 0)
            probs = jnp.concatenate(probs, 0).astype(low_type)
            dquery = product(dscores.T.astype(low_type), keys)
            put_planes(dquery_ref, start, lanes, dquery.astype(low_type))
            dkeys = product(dscores.astype(low_type), query)
            dvalues = product(probs, datt)
            if group < 2:
                first = lax.broadcasted_iota(jnp.int32, (KEY_SPAN, LANES), 1) < HD
                dkeys = jnp.where(first, dkeys[:KEY_SPAN], dkeys[KEY_SPAN:])
                dvalues = jnp.where(first, dvalues[:KEY_SPAN], dvalues[KEY_SPAN:])
            dkey_ref[span, lanes] += dkeys
            dvalue_ref[span, lanes] += dvalues

    advance(0)
    pl.loop(0, blocks // 2, unroll=blocks // 2)(one_block)
    advance(1)
    pl.loop(blocks // 2, blocks, unroll=blocks - blocks // 2)(one_block)
    advance(2)
    unit, inverse, normed = norm_rows(reduced_ref[...], gains_ref[2:3, :], gains_ref[3:4, :])
    normed_t = normed.T.astype(low_type)
    dkeys = dkey_ref[:, :C].astype(low_type)
    dvalues = dvalue_ref[:, :C].astype(low_type)
    for which, grads in enumerate((dkeys, dvalues)):
        dweight = product(normed_t, grads)
        for at, lane, width in lane_parts(C):
            part = dweight[:, lane : lane + width]
            if width < LANES:
                part = jnp.concatenate([part, jnp.zeros((C, LANES - width), jnp.float32)], 1)
            planes_ref[at, pl.ds(which, C, stride=2), :] = part
    for at, lane, width in lane_parts(C):
        dunits_ref[0, 2 * C :, lane : lane + width] = planes_ref[at, :, :width].astype(low_type)
    dnormed = back_product(dkeys, kv_ref[0]) + back_product(dvalues, kv_ref[1])
    dgain_ref[2:3, :] = jnp.sum(dnormed * unit, 0, keepdims=True)
    dgain_ref[3:4, :] = jnp.sum(dnormed, 0, keepdims=True)
    dreduced = norm_rows_back(unit, inverse, gains_ref[2:3, :], dnormed).astype(low_type)
    turned_ref[...] = normed_ref[...].T
    dunits_ref[0, :C, :] = product(turned_ref[...], dquery_ref[:, :C]).astype(low_type)
    for sub in range(4):
        span = slice(sub * tiles, (sub + 1) * tiles)
        part = slice(sub * C, (sub + 1) * C)
        dunits_ref[1, part, :] = outer_sum(normed_ref[span, :], dreduced).astype(low_type)
        first_ref[span, :] = back_product(
            dquery_ref[span, :C], unit_ref[0, :C, :]
        ) + back_product(dreduced, reduce_ref[0, part, :])

    grad = first_ref[...]
    unit, inverse, _ = norm_rows(resid_ref[...], gains_ref[0:1, :], gains_ref[1:2, :])
    out_ref[...] = grad_ref[...] + norm_rows_back(unit, inverse, gains_ref[0:1, :], grad)
    dgain_ref[0:1, :] = jnp.sum(grad * unit, 0, keepdims=True)
    dgain_ref[1:2, :] = jnp.sum(grad, 0, keepdims=True)


def attention_backward(grad, resid, gains, units, at, reduces, reduce_at, bias, kept, plans, meeting):
    rows = resid.shape[0]
    tiles = rows // 4
    low = jnp.bfloat16
    shapes = (
        jax.ShapeDtypeStruct((rows, C), jnp.float32),
        jax.ShapeDtypeStruct((2, FF, C), low),
        jax.ShapeDtypeStruct((4, C), jnp.float32),
    )
    count = len(plans)

    def run(*refs):
        own_in, ride_in = refs[:13], refs[13 : 13 + count]
        own_out, ride_out = refs[13 + count : 16 + count], refs[16 + count : 16 + 2 * count]
        rest = refs[16 + 2 * count :]
        rides = rides_of(plans, ride_in, ride_out, rest[7:])
        rides.signal()
        attention_backward_kernel(rides.advance, *own_in, *own_out, *rest[:7])
        for phase in range(3, rides.phases + 1):
            rides.advance(phase)

    return pl.pallas_call(
        run,
        grid=(1,),
        out_shape=shapes + tuple(plan.out for plan in plans),
        in_specs=[
            whole((rows, C)),
            whole((rows, C)),
            whole((4, C)),
            unit_spec(at),
            unit_spec(reduce_at),
            whole(bias.shape),
        ]
        + [whole(part.shape) for part in kept]
        + [plan.in_spec for plan in plans],
        out_specs=tuple(whole(shape.shape) for shape in shapes) + tuple(plan.out_spec for plan in plans),
        scratch_shapes=[
            pltpu.VMEM((C, rows), low),
            pltpu.VMEM((rows, WIDE), low),
            pltpu.VMEM((rows, WIDE), low),
            pltpu.VMEM((tiles, WIDE), jnp.float32),
            pltpu.VMEM((tiles, WIDE), jnp.float32),
            pltpu.VMEM((rows, C), jnp.float32),
            pltpu.VMEM((3, 2 * C, LANES), jnp.float32),
        ]
        + sum([plan.scratch for plan in plans], []),
        compiler_params=pltpu.CompilerParams(collective_id=meeting, has_side_effects=True, vmem_limit_bytes=VMEM_LIMIT),
        cost_estimate=pl.CostEstimate(flops=12 * 10**9, bytes_accessed=18 * 10**6, transcendentals=10**6),
        name="attention_backward",
    )(grad, resid, gains, units, reduces, bias, *kept, *[plan.value for plan in plans])


BOTH = ("grp", "tok")


def axis_bits(axis):
    count = lax.axis_size(axis)
    return [1 << place for place in reversed(range(count.bit_length() - 1))]


def bit_order():
    tok_bits = axis_bits("tok")
    return [("grp", bit) for bit in axis_bits("grp")] + [("tok", bit) for bit in tok_bits]


MESH = pl.DeviceIdType.MESH


def exchange_setup():
    grp, tok = lax.axis_index("grp"), lax.axis_index("tok")
    n_tok = lax.axis_size("tok")
    peers = [(lax.bitwise_xor(grp, bit), tok) for bit in axis_bits("grp")]
    peers += [(grp, lax.bitwise_xor(tok, step)) for step in range(1, n_tok)]
    return (grp, tok, n_tok, peers)


def signal_all(peers):
    barrier = pltpu.get_barrier_semaphore()
    for peer in peers:
        pl.semaphore_signal(barrier, inc=1, device_id=peer, device_id_type=MESH)


def greet(peers):
    signal_all(peers)
    pl.semaphore_wait(pltpu.get_barrier_semaphore(), len(peers))


def send(source, target, sems, at, peer):
    copy = pltpu.make_async_remote_copy(
        src_ref=source,
        dst_ref=target,
        send_sem=sems[0].at[at],
        recv_sem=sems[1].at[at],
        device_id=peer,
        device_id_type=MESH,
    )
    copy.start()
    return copy


def gather_view(ref, unit, place, done):
    index = [slice(None) if name in done else place(name) for name in bit_order()]
    return ref.at[tuple([unit] + index)]


class GatherRide:
    def __init__(self, full_ref, scratch):
        self.grp, self.tok = lax.axis_index("grp"), lax.axis_index("tok")
        self.phases = len(bit_order())
        self.names = bit_order()
        self.full_ref = full_ref
        self.sems = scratch[:2]

    def order(self, unit):
        grp_bits = [("grp", bit) for bit in axis_bits("grp")]
        flip = grp_bits[::-1] if unit % 2 else grp_bits
        return [("tok", bit) for bit in axis_bits("tok")[:-1]] + flip + [("tok", 1)]

    def place(self, name):
        return (self.grp if name[0] == "grp" else self.tok) // name[1] % 2

    def partner(self, name):
        axis, bit = name
        if axis == "grp":
            return (lax.bitwise_xor(self.grp, bit), self.tok)
        return (self.grp, lax.bitwise_xor(self.tok, bit))

    def copy(self, unit, phase):
        order = self.order(unit)
        held = gather_view(self.full_ref, unit, self.place, order[:phase])
        at = phase * self.full_ref.shape[0] + unit
        return pltpu.make_async_remote_copy(
            src_ref=held,
            dst_ref=held,
            send_sem=self.sems[0].at[at],
            recv_sem=self.sems[1].at[at],
            device_id=self.partner(order[phase]),
            device_id_type=MESH,
        )

    def put(self, unit, value):
        self.full_ref[(unit,) + tuple(self.place(name) for name in bit_order())] = value

    def advance(self, phase):
        for unit in range(self.full_ref.shape[0]):
            if phase:
                self.copy(unit, phase - 1).wait()
            if phase < self.phases:
                self.copy(unit, phase).start()


def gather_scratch(total):
    phases = len(bit_order())
    return [pltpu.SemaphoreType.DMA((phases * total,))] * 2


class PieceRide(GatherRide):
    def __init__(self, piece_ref, out_ref, scratch):
        super().__init__(scratch[2], scratch)
        self.piece_ref, self.out_ref = piece_ref, out_ref
        self.out_sem = scratch[3]

    def advance(self, phase):
        if phase == 0:
            for unit in range(self.full_ref.shape[0]):
                self.put(unit, self.piece_ref[unit])
        super().advance(phase)
        if phase == self.phases:
            copy = pltpu.make_async_copy(self.full_ref, self.out_ref, self.out_sem.at[0])
            copy.start()
            copy.wait()


def start_kernel(
    slot_ref, piece_ref, count_ref, patch_ref, mark_ref,
    full_ref, later_ref, total_ref, patch_halo_ref, mark_halo_ref,
    recv_ref, near_s, near_r, halo_s, halo_r, *scratch,
):
    grp, tok, n_tok, peers = exchange_setup()
    slot_rows = piece_ref.shape[1]
    units, first = slot_ref.shape[0], full_ref.shape[0]
    gather = GatherRide(full_ref, scratch[:2])
    count = SumRide(count_ref, total_ref, scratch[2:])
    greet(peers)
    copies = []
    for step in range(1, n_tok):
        peer = lax.bitwise_xor(tok, step)
        landing = recv_ref.at[pl.ds(tok * slot_rows, slot_rows)]
        copies.append(send(piece_ref.at[peer], landing, (near_s, near_r), step, (grp, peer)))
    recv_ref[pl.ds(tok * slot_rows, slot_rows)] = piece_ref[tok]
    count.advance(0)
    for copy in copies:
        copy.wait()
    for unit in range(first):
        gather.put(unit, recv_ref[slot_ref[unit]])
    gather.advance(0)
    before = (grp, lax.rem(tok + n_tok - 1, n_tok))
    mark_copy = send(mark_ref, mark_halo_ref, (halo_s, halo_r), 0, before)
    patch_copy = send(patch_ref.at[pl.ds(0, patch_halo_ref.shape[0])], patch_halo_ref, (halo_s, halo_r), 1, before)
    for unit in range(first, units):
        later_ref[unit - first] = recv_ref[slot_ref[unit]]
    for phase in range(1, gather.phases + 1):
        count.advance(phase)
        gather.advance(phase)
    mark_copy.wait()
    patch_copy.wait()


def start_exchange(slot_of, pieces, count, patches, marks, first):
    n_tok, slot_rows, chunk, width = pieces.shape
    phases = len(bit_order())
    units = slot_of.shape[0]
    vmem = pl.BlockSpec(memory_space=pltpu.VMEM)
    full_shape = (first,) + (2,) * phases + (chunk, width)
    return pl.pallas_call(
        start_kernel,
        out_shape=(
            jax.ShapeDtypeStruct(full_shape, pieces.dtype),
            jax.ShapeDtypeStruct((units - first, chunk, width), pieces.dtype),
            jax.ShapeDtypeStruct(count.shape, count.dtype),
            jax.ShapeDtypeStruct((OVER, patches.shape[1]), patches.dtype),
            jax.ShapeDtypeStruct(marks.shape, marks.dtype),
        ),
        in_specs=[pl.BlockSpec(memory_space=pltpu.SMEM), vmem, vmem, pl.BlockSpec(memory_space=pl.ANY), vmem],
        out_specs=(vmem, vmem, vmem, pl.BlockSpec(memory_space=pl.ANY), vmem),
        scratch_shapes=[
            pltpu.VMEM((n_tok * slot_rows, chunk, width), pieces.dtype),
            pltpu.SemaphoreType.DMA((n_tok,)),
            pltpu.SemaphoreType.DMA((n_tok,)),
            pltpu.SemaphoreType.DMA((2,)),
            pltpu.SemaphoreType.DMA((2,)),
        ]
        + gather_scratch(first)
        + sum_scratch(count.shape),
        compiler_params=pltpu.CompilerParams(collective_id=0, has_side_effects=True, vmem_limit_bytes=VMEM_LIMIT),
        name="start_exchange",
    )(slot_of, pieces, count, patches, marks)


def unit_order(unit):
    grp_bits = [("grp", bit) for bit in axis_bits("grp")]
    if unit % 2:
        grp_bits = grp_bits[::-1]
    return [("tok", 1)] + grp_bits + [("tok", bit) for bit in axis_bits("tok")[:-1][::-1]]


def unit_layout(order):
    left = bit_order()
    shapes = []
    for name in order:
        at = left.index(name)
        shapes.append((1 << at, 2, 1 << (len(left) - 1 - at)))
        left.remove(name)
    return shapes


SPLIT = 3


class UnitRide:
    def __init__(self, sources, out_ref, scratch, begin=0, end=None, base=0):
        self.grp, self.tok = lax.axis_index("grp"), lax.axis_index("tok")
        self.begin = begin
        self.end = len(bit_order()) if end is None else end
        self.phases = self.end - begin
        self.names = unit_order(0)[self.begin : self.end]
        self.sources = sources
        self.out_ref, self.base = out_ref, base
        self.sems = scratch[:2]
        self.buffers = scratch[2:]

    def partner(self, name):
        axis, bit = name
        if axis == "grp":
            return (lax.bitwise_xor(self.grp, bit), self.tok)
        return (self.grp, lax.bitwise_xor(self.tok, bit))

    def half_of(self, name):
        return (self.grp if name[0] == "grp" else self.tok) // name[1] % 2

    def before(self, unit, phase):
        if phase == 0:
            ref, at = self.sources[unit]
            return ref.at[at]
        return self.buffers[unit * 2 * self.phases + 2 * (phase - 1) + 1]

    def landing(self, unit, phase):
        return self.buffers[unit * 2 * self.phases + 2 * phase]

    def copy(self, unit, phase):
        name = unit_order(unit)[self.begin + phase]
        at = phase * len(self.sources) + unit
        return pltpu.make_async_remote_copy(
            src_ref=self.before(unit, phase).at[:, 1 - self.half_of(name)],
            dst_ref=self.landing(unit, phase),
            send_sem=self.sems[0].at[at],
            recv_sem=self.sems[1].at[at],
            device_id=self.partner(name),
            device_id_type=MESH,
        )

    def finish(self, unit, phase):
        order = unit_order(unit)
        shapes = unit_layout(order)
        self.copy(unit, phase).wait()
        outer, _, inner = shapes[self.begin + phase]
        source, landed = self.before(unit, phase), self.landing(unit, phase)
        mine = self.half_of(order[self.begin + phase])
        target = self.out_ref.at[self.base + unit]
        if phase + 1 < self.phases:
            target = self.before(unit, phase + 1)
        whole_done = self.begin + phase + 1 == len(order)
        if not whole_done:
            low = shapes[self.begin + phase + 1][2]

        @pl.loop(0, outer * inner, unroll=min(4, outer * inner))
        def _(at):
            value = source[at // inner, mine, at % inner] + landed[at // inner, at % inner]
            if whole_done:
                target[...] = value
            else:
                target[at // (2 * low), at // low % 2, at % low] = value

    def advance(self, phase):
        for unit in range(len(self.sources)):
            if phase:
                self.finish(unit, phase - 1)
            if phase < self.phases:
                self.copy(unit, phase).start()


def unit_scratch(total, chunk, width, begin=0, end=None):
    end = len(bit_order()) if end is None else end
    dma = pltpu.SemaphoreType.DMA
    buffers = [dma(((end - begin) * total,)), dma(((end - begin) * total,))]
    for unit in range(total):
        shapes = unit_layout(unit_order(unit))
        for phase in range(begin, end):
            outer, _, inner = shapes[phase]
            buffers.append(pltpu.VMEM((outer, inner, chunk, width), jnp.bfloat16))
            following = shapes[phase + 1] if phase + 1 < end else (1, 1, 1)
            buffers.append(pltpu.VMEM(following + (chunk, width), jnp.bfloat16))
    return buffers


def unit_blocks(units):
    chunk = units.shape[1] >> len(bit_order())
    return units.reshape((units.shape[0],) + unit_layout(unit_order(0))[0] + (chunk, units.shape[2]))


class SumRide:
    def __init__(self, source_ref, total_ref, scratch):
        self.grp, self.tok = lax.axis_index("grp"), lax.axis_index("tok")
        self.order = unit_order(0)
        self.names = self.order
        self.phases = len(self.order)
        self.source_ref, self.total_ref = source_ref, total_ref
        self.sums = scratch[2]
        self.sems = scratch[:2]

    partner = UnitRide.partner

    def copy(self, phase):
        return pltpu.make_async_remote_copy(
            src_ref=self.sums.at[2 * phase],
            dst_ref=self.sums.at[2 * phase + 1],
            send_sem=self.sems[0].at[phase],
            recv_sem=self.sems[1].at[phase],
            device_id=self.partner(self.order[phase]),
            device_id_type=MESH,
        )

    def advance(self, phase):
        if phase == 0:
            self.sums[0] = self.source_ref[...]
        else:
            self.copy(phase - 1).wait()
            self.sums[2 * phase] = self.sums[2 * phase - 2] + self.sums[2 * phase - 1]
        if phase < self.phases:
            self.copy(phase).start()
        else:
            self.total_ref[...] = self.sums[2 * phase]


def sum_scratch(shape):
    phases = len(bit_order())
    dma = pltpu.SemaphoreType.DMA
    return [dma((phases,)), dma((phases,)), pltpu.VMEM((2 * phases + 1,) + shape, jnp.float32)]


def tail_kernel(counts, rows, *refs):
    unit_at_ref, early_ref, part_ref = refs[:3]
    blocks, refs = refs[3 : 3 + len(counts)], refs[3 + len(counts) :]
    small_refs, refs = refs[: len(rows)], refs[len(rows) :]
    owned_ref, small_out_ref, chunk_ref, place_ref, near_s, near_r, small_ref = refs[:7]
    scratch = refs[7:]
    sources = [(ref, at) for ref, count in zip(blocks, counts) for at in range(count)]
    total = len(sources)
    parts = part_ref.shape[0]
    grp, tok, n_tok, peers = exchange_setup()
    signal_all(peers)
    begin = 0
    for ref, count in zip(small_refs, rows):
        small_ref[begin : begin + count, :] = ref[...]
        begin += count
    small_ref[begin:, :] = jnp.zeros((small_ref.shape[0] - begin, C), jnp.float32)
    cut = 3 + 2 + 2 * total * len(bit_order())
    rides = Rides(
        [
            UnitRide(sources, chunk_ref, scratch[3:cut]),
            SumRide(small_ref, small_out_ref, scratch[:3]),
            UnitRide([(part_ref, at) for at in range(parts)], chunk_ref, scratch[cut:], SPLIT, None, total),
        ]
    )
    rides.peers = peers
    for phase in range(rides.phases + 1):
        rides.advance(phase)
    total += parts
    for at in range(early_ref.shape[0]):
        chunk_ref[total + at] = early_ref[at]
    last = total + early_ref.shape[0]
    chunk_ref[last] = jnp.zeros(chunk_ref.shape[1:], chunk_ref.dtype)
    slot_rows = owned_ref.shape[1]

    @pl.loop(0, n_tok * slot_rows)
    def _(at):
        place_ref[at // slot_rows, at % slot_rows] = chunk_ref[unit_at_ref[at]]

    copies = []
    for step in range(1, n_tok):
        peer = lax.bitwise_xor(tok, step)
        copies.append(send(place_ref.at[peer], owned_ref.at[tok], (near_s, near_r), step, (grp, peer)))
    owned_ref[tok] = place_ref[tok]
    for copy in copies:
        copy.wait()


def tail_exchange(unit_at, early, part, sources, smalls, n_tok):
    chunk, width = early.shape[1:]
    counts = tuple(source.shape[0] for source in sources)
    rows = tuple(small.shape[0] for small in smalls)
    total = sum(counts)
    low = early.dtype
    vmem = pl.BlockSpec(memory_space=pltpu.VMEM)
    slot_rows = unit_at.shape[0] // n_tok
    dma = pltpu.SemaphoreType.DMA
    small = (-(-sum(rows) // 8) * 8, C)
    return pl.pallas_call(
        lambda *refs: tail_kernel(counts, rows, *refs),
        out_shape=(
            jax.ShapeDtypeStruct((n_tok, slot_rows, chunk, width), low),
            jax.ShapeDtypeStruct(small, jnp.float32),
        ),
        in_specs=[pl.BlockSpec(memory_space=pltpu.SMEM)] + [vmem] * (2 + len(sources) + len(smalls)),
        out_specs=(vmem, vmem),
        scratch_shapes=[
            pltpu.VMEM((total + part.shape[0] + early.shape[0] + 1, chunk, width), low),
            pltpu.VMEM((n_tok, slot_rows, chunk, width), low),
            dma((n_tok,)),
            dma((n_tok,)),
            pltpu.VMEM(small, jnp.float32),
        ]
        + sum_scratch(small)
        + unit_scratch(total, chunk, width)
        + unit_scratch(part.shape[0], chunk, width, SPLIT),
        compiler_params=pltpu.CompilerParams(collective_id=1, has_side_effects=True, vmem_limit_bytes=VMEM_LIMIT),
        name="tail_exchange",
    )(unit_at, early, part, *[unit_blocks(source) for source in sources], *smalls)


def body(
    patches,
    labels,
    valid_mask,
    crop_counts,
    owners,
    slot_weight,
    slot_moment,
    slot_second,
    norm_params,
    norm_moment,
    norm_second,
    head_weight,
    head_moment,
    head_second,
):
    tok_dev = patches.shape[0]
    n_tok = lax.axis_size("tok")
    n_grp = lax.axis_size("grp")
    tok_index = lax.axis_index("tok")
    group_tok = tok_dev * n_tok
    counts = crop_counts[0]
    n_unit = owners.shape[0]
    slot_rows, columns = slot_weight.shape
    unit_order = jnp.arange(n_unit, dtype=jnp.int32)
    same_owner = owners[:, None] == owners[None, :]
    rank_of = jnp.sum(same_owner & (unit_order[None, :] < unit_order[:, None]), 1)
    slot_of = owners * slot_rows + rank_of
    chunk = columns // n_tok // C
    first_tok = tok_index * tok_dev
    small_end = counts[0] * BIG_SIDE**2 + counts[1] * SMALL_SIDE**2
    counted = valid_mask * (first_tok + jnp.arange(tok_dev, dtype=jnp.int32) < small_end)
    counted = jnp.full((8, LANES), jnp.sum(counted.astype(jnp.float32)))
    pieces = slot_weight.astype(jnp.bfloat16).reshape(slot_rows, n_tok, chunk, C).transpose(1, 0, 2, 3)
    first_units = 1 + n_unit // BLOCKS
    marks = jnp.stack([labels, valid_mask])
    own, later, counted, patch_halo, mark_halo = start_exchange(
        slot_of, pieces, counted, patches, marks[:, :OVER], first_units
    )
    pixel_total = counted[0, 0]
    own = own.reshape(first_units, FF, C)
    layers = [((own, 1, own, 2), (own, 3))]
    units = lax.all_gather(later[:4], BOTH, axis=1, tiled=True)
    layers.append(((units, 0, units, 1), (units, 2)))
    last_mlp = lax.all_gather(later[6:], BOTH, axis=1, tiled=True)

    window = tok_dev + OVER
    tiles = window // 4
    marks = jnp.concatenate([marks, mark_halo], 1)
    marks = marks.reshape(2, tiles, 4).transpose(0, 2, 1).reshape(2, window)
    labels = marks[0]
    positions = first_tok + 4 * jnp.arange(tiles, dtype=jnp.int32)
    begin_at, half_side, tile_y, tile_x, is_real = image_layout(positions, counts)
    own_image = (begin_at >= first_tok) & (begin_at < first_tok + tok_dev) & (positions < group_tok)
    stacks = shift_stacks(half_side, tile_y, tile_x, is_real)

    def image_at(tile):
        at = first_tok + 4 * tile
        return jnp.where(at < group_tok, image_layout(at, counts)[0], -1)

    bias = block_bias(tiles, image_at)
    real_rows = jnp.broadcast_to(is_real.astype(jnp.float32)[:, None], (tiles, LANES))
    keep_mask = marks[1].astype(jnp.float32) * jnp.tile((own_image & is_real).astype(jnp.float32), 4)
    tail = 6 * BLOCKS
    embed_pre, resid, kernels = embed_forward(patches, patch_halo, own, norm_params[tail : tail + 2])
    kept_all = []
    single = []
    for layer_at in range(BLOCKS):
        if layer_at == len(layers):
            layers.append(((single[0], 0, single[1], 0), (last_mlp, 0)))
        attn_units, mlp_units = layers[layer_at]
        at = 6 * layer_at
        middle, *attn_kept = attention_forward(resid, norm_params[at : at + 4], *attn_units, bias)
        plans = []
        if layer_at + 1 < BLOCKS:
            plans = [plan_gather(later[4 + layer_at : 5 + layer_at])]
        output, *mlp_kept = mlp_forward(
            middle, norm_params[at + 4 : at + 6], *mlp_units, kernels, layer_at, stacks, real_rows,
            plans, 2 + 2 * BLOCKS + layer_at,
        )
        if plans:
            single.append(mlp_kept.pop().reshape(1, FF, C))
        w_up = mlp_kept.pop()
        kept_all.append((resid, attn_kept, middle, mlp_kept, w_up))
        resid = output
    final = layer_norm(resid, norm_params[tail + 2], norm_params[tail + 3]).astype(jnp.bfloat16)
    head_low = head_weight.astype(jnp.bfloat16)
    logits = product(final, head_low)
    row_peak = jnp.max(logits, -1, keepdims=True)
    log_norm = row_peak[:, 0] + jnp.log(jnp.sum(jnp.exp(logits - row_peak), -1))
    onehot = (labels[:, None] == jnp.arange(head_weight.shape[1], dtype=jnp.int32)[None, :]).astype(
        jnp.float32
    )
    picked = jnp.sum(logits * onehot, 1)
    loss_local = jnp.sum((log_norm - picked) * keep_mask)
    probs = jnp.exp(logits - log_norm[:, None])
    d_logits = ((probs - onehot) * (keep_mask / pixel_total)[:, None]).astype(jnp.bfloat16)
    d_head = outer_sum(final, d_logits)
    grad_res, gain_final, shift_final = norm_back(
        resid, norm_params[tail + 2], norm_params[tail + 3], back_product(d_logits, head_low)
    )
    pad = -d_head.size % (8 * LANES)
    plans = [plan_sum(jnp.pad(d_head.reshape(-1), (0, pad)).reshape(-1, LANES))]
    early = []
    kernel_grads = [None] * BLOCKS
    gain_grads = []
    phases = len(bit_order())
    for layer_at in reversed(range(BLOCKS)):
        attn_units, mlp_units = layers[layer_at]
        at = 6 * layer_at
        entry, attn_kept, middle, mlp_kept, w_up = kept_all[layer_at]
        grad_res, mlp_grads, kernel_grads[layer_at], mlp_gains, *ridden_out = mlp_backward(
            grad_res, middle, norm_params[at + 4 : at + 6], w_up, *mlp_units, kernels, layer_at,
            stacks, real_rows, mlp_kept, plans, 2 + layer_at,
        )
        plans = [plan_units(mlp_grads, 0, SPLIT)]
        if layer_at + 1 == BLOCKS:
            head_total = ridden_out[0].reshape(-1)[: d_head.size].reshape(d_head.shape)
        else:
            early.insert(0, ridden_out[1])
            plans.append(plan_units(ridden_out[0], SPLIT, phases))
        grad_res, attn_grads, attn_gains, *ridden_out = attention_backward(
            grad_res, entry, norm_params[at : at + 4], *attn_units, bias, attn_kept, plans, 2 + BLOCKS + layer_at
        )
        if layer_at + 1 < BLOCKS:
            early.insert(0, ridden_out[1])
        plans = [plan_units(attn_grads, 0, SPLIT), plan_units(ridden_out[0], SPLIT, phases)]
        gain_grads = [attn_gains, mlp_gains] + gain_grads
    part = ridden_out[0]
    first_grad, embed_gains = embed_backward(
        grad_res, embed_pre, norm_params[tail : tail + 2], patches, patch_halo, kernel_grads
    )
    early = jnp.concatenate(early, 0)
    final_gains = jnp.stack([gain_final, shift_final])
    smalls = gain_grads + [embed_gains, final_gains, jnp.full((1, C), loss_local)]
    row_ids = jnp.arange(slot_rows * n_tok, dtype=jnp.int32)
    matches = slot_of[None, :] == row_ids[:, None]
    unit_at = jnp.where(jnp.any(matches, 1), jnp.argmax(matches, 1), n_unit)
    owned, small = tail_exchange(unit_at, early, part, [first_grad, attn_grads], smalls, n_tok)
    owned = owned.transpose(1, 0, 2, 3).astype(jnp.float32).reshape(slot_rows, columns)
    norm_rows_all = norm_params.shape[0]
    norm_total, loss_sum = (small[:norm_rows_all], small[norm_rows_all, 0])
    slot_m, slot_v, slot_w = adamw_step(
        slot_weight, slot_moment, slot_second, owned, RATE_MATRIX, DECAY_RATE
    )
    norm_m, norm_v, norm_w = adamw_step(
        norm_params, norm_moment, norm_second, norm_total, RATE_VECTOR, 0.0
    )
    head_m, head_v, head_w = adamw_step(
        head_weight, head_moment, head_second, head_total, RATE_MATRIX, DECAY_RATE
    )
    return (
        loss_sum,
        pixel_total,
        slot_m,
        slot_v,
        slot_w,
        norm_m,
        norm_v,
        norm_w,
        head_m,
        head_v,
        head_w,
    )


def solution(mesh):
    in_specs = (
        P(("grp", "tok"), None),
        P(("grp", "tok")),
        P(("grp", "tok")),
        P("grp", None),
        P(),
        P("tok", "grp"),
        P("tok", "grp"),
        P("tok", "grp"),
        P(),
        P(),
        P(),
        P(),
        P(),
        P(),
    )
    out_specs = (
        P(),
        P(),
        P("tok", "grp"),
        P("tok", "grp"),
        P("tok", "grp"),
        P(),
        P(),
        P(),
        P(),
        P(),
        P(),
    )
    return jax.shard_map(body, mesh=mesh, in_specs=in_specs, out_specs=out_specs, check_vma=False)
```

```python
import functools

import jax
import jax.numpy as jnp
import numpy as np
from jax import lax
from jax.experimental import pallas as pl
from jax.experimental.pallas import tpu as pltpu
from jax.sharding import PartitionSpec as P

C = 320
HEADS = 5
HD = 64
FF = 1280
PIN = 1152
BLOCKS = 3
BIG_SIDE = 14
SMALL_SIDE = 6
STEP = 10
KVH = 49


EPS_NORM = 1e-06
BETA_ONE = 0.9
BETA_TWO = 0.999
ADAM_EPS = 1e-08
RATE_MATRIX = 0.05
RATE_VECTOR = 0.3
DECAY_RATE = 0.05
NEG_FILL = -1e30
PREC_HIGH = lax.Precision.HIGHEST


def layer_norm(values, gain_vec, shift_vec):
    center = values - jnp.mean(values, -1, keepdims=True)
    inverse = lax.rsqrt(jnp.mean(center * center, -1, keepdims=True) + EPS_NORM)
    return center * inverse * gain_vec + shift_vec


def adamw_step(weight, moment, second, gradient, rate_now, decay_now):
    moment = BETA_ONE * moment + (1.0 - BETA_ONE) * gradient
    second = BETA_TWO * second + (1.0 - BETA_TWO) * gradient * gradient
    m_hat = moment / (1.0 - BETA_ONE**STEP)
    v_hat = second / (1.0 - BETA_TWO**STEP)
    weight = weight - rate_now * (m_hat / (jnp.sqrt(v_hat) + ADAM_EPS) + decay_now * weight)
    return (moment, second, weight)


def product(left, right):
    return jnp.dot(left, right, preferred_element_type=jnp.float32)


def outer_sum(left, right):
    return lax.dot_general(
        left, right, (((0,), (0,)), ((), ())), preferred_element_type=jnp.float32
    )


def back_product(gradient, weight):
    return lax.dot_general(
        gradient, weight, (((1,), (1,)), ((), ())), preferred_element_type=jnp.float32
    )


def norm_back(values, gain_vec, shift_vec, gradient):
    _, pull_back = jax.vjp(layer_norm, values, gain_vec, shift_vec)
    return pull_back(gradient)


OVER = 4 * KVH - 4


def image_layout(positions, counts):
    big_tok = BIG_SIDE * BIG_SIDE
    small_tok = SMALL_SIDE * SMALL_SIDE
    big_end = counts[0] * big_tok
    small_end = big_end + counts[1] * small_tok
    is_big = positions < big_end
    is_small = jnp.logical_and(positions >= big_end, positions < small_end)
    half_side = jnp.where(is_big, BIG_SIDE // 2, SMALL_SIDE // 2)
    begin_at = jnp.where(
        is_big,
        positions // big_tok * big_tok,
        jnp.where(is_small, big_end + (positions - big_end) // small_tok * small_tok, small_end),
    )
    tile_idx = (positions - begin_at) // 4
    return (begin_at, half_side, tile_idx // half_side, tile_idx % half_side, positions < small_end)


def shift_stacks(half_side, tile_y, tile_x, is_real):
    tiles = half_side.shape[0]
    step_y = np.array([[0, 1 - 2 * (sub // 2), 1 - 2 * (sub // 2)] for sub in range(4)], np.int32)[:, :, None]
    step_x = np.array([[1 - 2 * (sub % 2), 0, 1 - 2 * (sub % 2)] for sub in range(4)], np.int32)[:, :, None]
    at_y = tile_y + step_y
    at_x = tile_x + step_x
    inside = is_real & (at_y >= 0) & (at_y < half_side) & (at_x >= 0) & (at_x < half_side)
    source = jnp.arange(tiles, dtype=jnp.int32) + step_y * half_side + step_x
    source = jnp.where(inside, source, -1)
    cut = row_cut(tiles)
    columns = jnp.arange(SPAN, dtype=jnp.int32)
    upper = (source[:, :, :cut, None] == columns).astype(jnp.bfloat16)
    lower = (source[:, :, cut:, None] == columns + (tiles - SPAN)).astype(jnp.bfloat16)
    return (upper.reshape(4, 3 * cut, SPAN), lower.reshape(4, 3 * (tiles - cut), SPAN))


def tap_source(sub, tap):
    y_at = sub // 2 + tap // 3 - 1
    x_at = sub % 2 + tap % 3 - 1
    return (y_at % 2 * 2 + x_at % 2, y_at // 2, x_at // 2)


SQRT_HALF = 0.7071067811865476
INV_SQRT_TWO_PI = 0.3989422804014327
TAPS_OF = [[tap_source(sub, tap) for tap in range(9)] for sub in range(4)]
VMEM_LIMIT = 56 * 1024 * 1024
SPAN = 256
ROWS = 16
LANES = 128


def row_cut(tiles):
    return (tiles // 2 + 15) // 16 * 16


def move_planes(planes_ref, upper_ref, lower_ref, moved_ref):
    tiles = planes_ref.shape[0] // 4
    cut = row_cut(tiles)
    for sub in range(4):
        base = sub * tiles
        part = product(upper_ref[sub], planes_ref[base : base + SPAN, :])
        for key in range(3):
            moved_ref[sub, key, :cut, :] = part[key * cut : (key + 1) * cut]
        part = product(lower_ref[sub], planes_ref[base + tiles - SPAN : base + tiles, :])
        for key in range(3):
            moved_ref[sub, key, cut:, :] = part[key * (tiles - cut) : (key + 1) * (tiles - cut)]


def chunk_sources(planes_ref, moved_ref, row, lanes):
    tiles = planes_ref.shape[0] // 4
    found = {}
    for sub in range(4):
        found[sub, 0, 0] = planes_ref[pl.ds(pl.multiple_of(sub * tiles + row, ROWS), ROWS), lanes].astype(jnp.float32)
        step_y = 1 - 2 * (sub // 2)
        step_x = 1 - 2 * (sub % 2)
        for key, step in enumerate(((0, step_x), (step_y, 0), (step_y, step_x))):
            found[(sub,) + step] = moved_ref[sub, key, pl.ds(row, ROWS), lanes]
    return found


def norm_rows(values, gain, shift):
    center = values - jnp.mean(values, -1, keepdims=True)
    inverse = lax.rsqrt(jnp.mean(center * center, -1, keepdims=True) + EPS_NORM)
    unit = center * inverse
    return (unit, inverse, unit * gain + shift)


def norm_rows_back(unit, inverse, gain, grad):
    scaled = grad * gain
    return inverse * (
        scaled - jnp.mean(scaled, -1, keepdims=True) - unit * jnp.mean(scaled * unit, -1, keepdims=True)
    )


def mlp_forward_kernel(
    middle_ref, gains_ref, up_ref, down_ref, kern_ref, upper_ref, lower_ref, real_ref,
    out_ref, hidden_ref, active_ref, slope_ref, turned_ref,
    normed_ref, moved_ref, planes_ref,
):
    rows = middle_ref.shape[0]
    block = hidden_ref.shape[1]
    tiles = rows // 4

    @pl.when(pl.program_id(0) == 0)
    def _():
        normed = norm_rows(middle_ref[...], gains_ref[0:1, :], gains_ref[1:2, :])[2]
        normed_ref[...] = normed.astype(jnp.bfloat16)
        out_ref[...] = middle_ref[...]
        spread_rows(up_ref[0], planes_ref)
        for quarter in range(FF // C):
            for at, lane, width in lane_parts(C):
                part = planes_ref[at, pl.ds(quarter, C, stride=FF // C), :][:, :width]
                begin = quarter * C + lane
                turned_ref[:, begin : begin + width] = part.astype(jnp.bfloat16)

    for sub in range(4):
        columns = pl.ds(pl.multiple_of(pl.program_id(0) * block, block), block)
        part = product(normed_ref[sub * tiles : (sub + 1) * tiles, :], turned_ref[:, columns])
        hidden_ref[sub * tiles : (sub + 1) * tiles, :] = part.astype(jnp.bfloat16)
    move_planes(hidden_ref, upper_ref, lower_ref, moved_ref)

    for lane in range(0, hidden_ref.shape[1], LANES):
        lanes = slice(lane, lane + LANES)
        kern = [kern_ref[0, tap : tap + 1, lanes] for tap in range(9)]

        @pl.loop(0, tiles // ROWS, unroll=tiles // ROWS)
        def _(at):
            row = pl.multiple_of(at * ROWS, ROWS)
            found = chunk_sources(hidden_ref, moved_ref, row, lanes)
            real = real_ref[pl.ds(row, ROWS), :] > 0.0
            for sub in range(4):
                center = found[sub, 0, 0] * kern[4]
                total = center
                for tap in range(9):
                    if tap != 4:
                        total = total + found[TAPS_OF[sub][tap]] * kern[tap]
                mixed = jnp.where(real, total, center)
                half = 0.5 + 0.5 * lax.erf(mixed * SQRT_HALF)
                bell = jnp.exp(-0.5 * mixed * mixed) * INV_SQRT_TWO_PI
                span = pl.ds(pl.multiple_of(sub * tiles + row, ROWS), ROWS)
                active_ref[span, lanes] = (mixed * half).astype(jnp.bfloat16)
                slope_ref[span, lanes] = (half + mixed * bell).astype(jnp.bfloat16)

    for sub in range(4):
        span = slice(sub * tiles, (sub + 1) * tiles)
        out_ref[span, :] += product(active_ref[span, :], down_ref[0])


def lane_parts(width):
    return [(at, lane, min(LANES, width - lane)) for at, lane in enumerate(range(0, width, LANES))]


def spread_rows(source, planes_ref):
    for at, lane, width in lane_parts(source.shape[1]):
        planes_ref[at, :, :width] = source[:, lane : lane + width].astype(jnp.float32)


class Plan:
    def __init__(self, value, out, scratch, make, space=None):
        self.value, self.out, self.scratch, self.make = value, out, scratch, make
        self.in_spec = whole(value.shape)
        self.out_spec = pl.BlockSpec(memory_space=space) if space is not None else whole(out.shape)


def plan_sum(value, begin, end):
    make = functools.partial(SumRide, begin=begin, end=end)
    return Plan(value, jax.ShapeDtypeStruct(value.shape, value.dtype), sum_scratch(value.shape), make)


def plan_units(value, begin, end):
    if begin == 0:
        value = unit_blocks(value)
    total, (chunk, width) = value.shape[0], value.shape[-2:]
    inside = unit_layout(unit_order(0))[end] if end < len(bit_order()) else ()
    out = jax.ShapeDtypeStruct((total,) + inside + (chunk, width), value.dtype)

    def make(ride_in, ride_out, scratch):
        sources = [(ride_in, at) for at in range(total)]
        return UnitRide(sources, ride_out, scratch, begin, end)

    return Plan(value, out, unit_scratch(total, chunk, width, begin, end), make)


class Rides:
    def __init__(self, rides):
        self.rides = rides
        self.phases = max(ride.phases for ride in rides)
        names = [name for name in bit_order() if any(name in ride.names for ride in rides)]
        self.peers = [UnitRide.partner(rides[0], name) for name in names]

    def signal(self):
        signal_all(self.peers)

    def advance(self, phase):
        if phase == 0:
            pl.semaphore_wait(pltpu.get_barrier_semaphore(), len(self.peers))
        for ride in self.rides:
            if phase <= ride.phases:
                ride.advance(phase)


def rides_of(plans, ins, outs, scratch):
    rides = []
    for plan, ride_in, ride_out in zip(plans, ins, outs):
        count = len(plan.scratch)
        rides.append(plan.make(ride_in, ride_out, scratch[:count]))
        scratch = scratch[count:]
    return Rides(rides)


def ridden(kernel, inputs, outputs, scratch, steps, plans):
    def run(*refs):
        own_in, refs = refs[:inputs], refs[inputs:]
        ride_in, refs = refs[: len(plans)], refs[len(plans) :]
        own_out, refs = refs[:outputs], refs[outputs:]
        ride_out, rest = refs[: len(plans)], refs[len(plans) :]
        rides = rides_of(plans, ride_in, ride_out, rest[scratch:])
        first = min(steps, rides.phases + 1)

        def advance():
            for phase in range(first):
                pl.when(pl.program_id(0) == phase)(functools.partial(rides.advance, phase))

        pl.when(pl.program_id(0) == 0)(rides.signal)
        kernel(advance, *own_in, *own_out, *rest[:scratch])
        if rides.phases >= first:

            @pl.when(pl.program_id(0) == steps - 1)
            def _():
                for phase in range(first, rides.phases + 1):
                    rides.advance(phase)

    return run


def whole(shape):
    return pl.BlockSpec(shape, lambda j: (0,) * len(shape))


def unit_spec(at):
    return pl.BlockSpec((1, FF, C), lambda j: (at, 0, 0))


def mlp_forward(middle, gains, units, at, kernel, layer_at, stacks, real_rows):
    rows = middle.shape[0]
    block = 256
    by_lane = pl.BlockSpec((rows, block), lambda j: (0, j))
    low = jax.ShapeDtypeStruct((rows, FF), jnp.bfloat16)
    return pl.pallas_call(
        mlp_forward_kernel,
        grid=(FF // block,),
        out_shape=(
            jax.ShapeDtypeStruct((rows, C), jnp.float32),
            low,
            low,
            low,
            jax.ShapeDtypeStruct((C, FF), jnp.bfloat16),
        ),
        in_specs=[
            whole((rows, C)),
            whole((2, C)),
            unit_spec(at),
            pl.BlockSpec((1, block, C), lambda j: (at + 1, j, 0)),
            pl.BlockSpec((1, 9, block), lambda j: (layer_at, 0, j)),
            whole(stacks[0].shape),
            whole(stacks[1].shape),
            whole(real_rows.shape),
        ],
        out_specs=(whole((rows, C)), by_lane, by_lane, by_lane, whole((C, FF))),
        scratch_shapes=[
            pltpu.VMEM((rows, C), jnp.bfloat16),
            pltpu.VMEM((4, 3, rows // 4, block), jnp.float32),
            pltpu.VMEM((3, FF, LANES), jnp.float32),
        ],
        compiler_params=pltpu.CompilerParams(vmem_limit_bytes=VMEM_LIMIT),
        cost_estimate=pl.CostEstimate(flops=14 * 10**9, bytes_accessed=18 * 10**6, transcendentals=4 * 10**6),
        name="mlp_forward",
    )(middle, gains, units, units, kernel, stacks[0], stacks[1], real_rows)


def mlp_backward_kernel(
    advance,
    grad_ref, middle_ref, gains_ref, up_ref, down_ref, kern_ref, upper_ref, lower_ref, real_ref,
    hidden_ref, active_ref, slope_ref,
    out_ref, dunits_ref, dkern_ref, dgain_ref,
    low_ref, low_t_ref, normed_t_ref, mixed_ref, dhid_ref, moved_ref, back_ref, wide_ref, planes_ref,
):
    rows = grad_ref.shape[0]
    tiles = rows // 4
    block = hidden_ref.shape[1]

    @pl.when(pl.program_id(0) == 0)
    def _():
        for sub in range(4):
            span = slice(sub * tiles, (sub + 1) * tiles)
            low_ref[span, :] = grad_ref[span, :].astype(jnp.bfloat16)
        normed = norm_rows(middle_ref[...], gains_ref[0:1, :], gains_ref[1:2, :])[2]
        normed_t_ref[...] = normed.T.astype(jnp.bfloat16)
        low_t_ref[...] = grad_ref[...].T.astype(jnp.bfloat16)
        back_ref[...] = jnp.zeros_like(back_ref)

    advance()
    for sub in range(4):
        span = slice(sub * tiles, (sub + 1) * tiles)
        part = back_product(low_ref[span, :], down_ref[0]).astype(jnp.bfloat16).astype(jnp.float32)
        mixed_ref[span, :] = (part * slope_ref[span, :].astype(jnp.float32)).astype(jnp.bfloat16)
    down_rows = pl.ds(pl.multiple_of(pl.program_id(0) * block, block), block)
    dunits_ref[1, down_rows, :] = product(low_t_ref[...], active_ref[...]).T.astype(jnp.bfloat16)
    move_planes(mixed_ref, upper_ref, lower_ref, moved_ref)

    for lane in range(0, block, LANES):
        lanes = slice(lane, lane + LANES)
        kern = [kern_ref[0, tap : tap + 1, lanes] for tap in range(9)]

        def step(at, sums):
            row = pl.multiple_of(at * ROWS, ROWS)
            found = chunk_sources(mixed_ref, moved_ref, row, lanes)
            real = real_ref[pl.ds(row, ROWS), :] > 0.0
            sums = list(sums)
            for sub in range(4):
                span = pl.ds(pl.multiple_of(sub * tiles + row, ROWS), ROWS)
                hidden = hidden_ref[span, lanes].astype(jnp.float32)
                center = found[sub, 0, 0] * kern[4]
                total = center
                for tap in range(9):
                    term = found[TAPS_OF[sub][tap]]
                    if tap != 4:
                        total = total + term * kern[8 - tap]
                    piece = hidden * term
                    sums[tap] = sums[tap] + piece[:8] + piece[8:]
                dhid_ref[span, lanes] = jnp.where(real, total, center).astype(jnp.bfloat16)
            return tuple(sums)

        sums = lax.fori_loop(0, tiles // ROWS, step, (jnp.zeros((8, LANES), jnp.float32),) * 9, unroll=True)
        for tap in range(9):
            dkern_ref[8 - tap : 9 - tap, lanes] = jnp.sum(sums[tap], 0, keepdims=True)

    columns = pl.ds(pl.multiple_of(pl.program_id(0) * block, block), block)
    wide_ref[:, columns] = product(normed_t_ref[...], dhid_ref[...])
    for sub in range(4):
        span = slice(sub * tiles, (sub + 1) * tiles)
        back_ref[span, :] += back_product(dhid_ref[span, :], up_ref[...])

    @pl.when(pl.program_id(0) == pl.num_programs(0) - 1)
    def _():
        grad = back_ref[...]
        unit, inverse, _ = norm_rows(middle_ref[...], gains_ref[0:1, :], gains_ref[1:2, :])
        out_ref[...] = grad_ref[...] + norm_rows_back(unit, inverse, gains_ref[0:1, :], grad)
        dgain_ref[0:1, :] = jnp.sum(grad * unit, 0, keepdims=True)
        dgain_ref[1:2, :] = jnp.sum(grad, 0, keepdims=True)
        for quarter in range(FF // C):
            for at, lane, width in lane_parts(C):
                begin = quarter * C + lane
                part = wide_ref[:, begin : begin + width]
                if width < LANES:
                    part = jnp.concatenate([part, jnp.zeros((C, LANES - width), jnp.float32)], 1)
                planes_ref[at, pl.ds(quarter, C, stride=FF // C), :] = part
        for at, lane, width in lane_parts(C):
            dunits_ref[0, :, lane : lane + width] = planes_ref[at, :, :width].astype(jnp.bfloat16)


def mlp_backward(grad, middle, gains, w_up, units, at, kernel, layer_at, stacks, real_rows, kept, plans, meeting):
    rows = middle.shape[0]
    block = 256
    by_lane = pl.BlockSpec((rows, block), lambda j: (0, j))
    up_spec = pl.BlockSpec((C, block), lambda j: (0, j))
    tap_spec = pl.BlockSpec((9, block), lambda j: (0, j))
    return pl.pallas_call(
        ridden(mlp_backward_kernel, 12, 4, 9, FF // block, plans),
        grid=(FF // block,),
        out_shape=(
            jax.ShapeDtypeStruct((rows, C), jnp.float32),
            jax.ShapeDtypeStruct((2, FF, C), jnp.bfloat16),
            jax.ShapeDtypeStruct((9, FF), jnp.float32),
            jax.ShapeDtypeStruct((2, C), jnp.float32),
            *[plan.out for plan in plans],
        ),
        in_specs=[
            whole((rows, C)),
            whole((rows, C)),
            whole((2, C)),
            up_spec,
            pl.BlockSpec((1, block, C), lambda j: (at + 1, j, 0)),
            pl.BlockSpec((1, 9, block), lambda j: (layer_at, 0, j)),
            whole(stacks[0].shape),
            whole(stacks[1].shape),
            whole(real_rows.shape),
            by_lane,
            by_lane,
            by_lane,
        ]
        + [plan.in_spec for plan in plans],
        out_specs=(whole((rows, C)), whole((2, FF, C)), tap_spec, whole((2, C)))
        + tuple(plan.out_spec for plan in plans),
        scratch_shapes=[
            pltpu.VMEM((rows, C), jnp.bfloat16),
            pltpu.VMEM((C, rows), jnp.bfloat16),
            pltpu.VMEM((C, rows), jnp.bfloat16),
            pltpu.VMEM((rows, block), jnp.bfloat16),
            pltpu.VMEM((rows, block), jnp.bfloat16),
            pltpu.VMEM((4, 3, rows // 4, block), jnp.float32),
            pltpu.VMEM((rows, C), jnp.float32),
            pltpu.VMEM((C, FF), jnp.float32),
            pltpu.VMEM((3, FF, LANES), jnp.float32),
        ]
        + sum([plan.scratch for plan in plans], []),
        compiler_params=pltpu.CompilerParams(
            collective_id=meeting, has_side_effects=True, vmem_limit_bytes=VMEM_LIMIT
        ),
        cost_estimate=pl.CostEstimate(flops=18 * 10**9, bytes_accessed=18 * 10**6, transcendentals=0),
        name="mlp_backward",
    )(grad, middle, gains, w_up, units, kernel, stacks[0], stacks[1], real_rows, *kept, *[plan.value for plan in plans])


WIDE = 384
BLOCK_TILES = 32
KEY_SPAN = 128


def block_places(tiles):
    places = []
    for index in range(-(-tiles // BLOCK_TILES)):
        start = min(index * BLOCK_TILES, tiles - BLOCK_TILES)
        places.append((start, min(max(start - 48, 0), tiles - KEY_SPAN)))
    return places


def block_bias(tiles, image_at):
    starts, lows = np.array(block_places(tiles), np.int32).T[:, :, None]
    columns = starts + np.tile(np.arange(BLOCK_TILES, dtype=np.int32), 4)
    rows = lows + np.arange(KEY_SPAN, dtype=np.int32)
    same = image_at(jnp.asarray(rows))[:, :, None] == image_at(jnp.asarray(columns))[:, None, :]
    return jnp.where(same, 0.0, NEG_FILL)


def place_of(index, tiles):
    start = jnp.minimum(index * BLOCK_TILES, tiles - BLOCK_TILES)
    low = jnp.clip(start - 48, 0, tiles - KEY_SPAN)
    return (pl.multiple_of(start, ROWS), pl.multiple_of(low, ROWS))


def four_planes(ref, start, lanes):
    tiles = ref.shape[0] // 4
    return jnp.concatenate(
        [ref[pl.ds(pl.multiple_of(sub * tiles + start, ROWS), BLOCK_TILES), lanes] for sub in range(4)], 0
    )


def put_planes(ref, start, lanes, values):
    tiles = ref.shape[0] // 4
    for sub in range(4):
        ref[pl.ds(pl.multiple_of(sub * tiles + start, ROWS), BLOCK_TILES), lanes] = values[
            sub * BLOCK_TILES : (sub + 1) * BLOCK_TILES
        ]


def head_pair(values, group):
    if group == 2:
        return values
    first = lax.broadcasted_iota(jnp.int32, values.shape, 1) < HD
    zero = jnp.zeros_like(values)
    return jnp.concatenate([jnp.where(first, values, zero), jnp.where(first, zero, values)], 0)


def softmax_columns(raw, bias):
    parts = []
    for half in range(raw.shape[0] // KEY_SPAN):
        scores = raw[half * KEY_SPAN : (half + 1) * KEY_SPAN] * HD ** (-0.5) + bias
        weights = jnp.exp(scores - jnp.max(scores, 0, keepdims=True))
        parts.append(weights * (1.0 / jnp.sum(weights, 0, keepdims=True)))
    return parts


def norm_store(source_ref, gains_ref, at, target_ref):
    normed = norm_rows(source_ref[...], gains_ref[at : at + 1, :], gains_ref[at + 1 : at + 2, :])[2]
    target_ref[...] = normed.astype(jnp.bfloat16)


def part_keyval(unit_ref, planes_ref, kv_ref):
    spread_rows(unit_ref[0, 2 * C :, :], planes_ref)
    for which in range(2):
        for at, lane, width in lane_parts(C):
            part = planes_ref[at, pl.ds(which, C, stride=2), :][:, :width]
            kv_ref[which, :, lane : lane + width] = part.astype(jnp.bfloat16)


def attention_forward_kernel(
    resid_ref, gains_ref, unit_ref, reduce_ref, bias_ref,
    middle_ref, normed_ref, query_ref, reduced_ref, key_ref, value_ref, attended_ref, kv_ref,
    planes_ref,
):
    part_keyval(unit_ref, planes_ref, kv_ref)
    rows = resid_ref.shape[0]
    tiles = rows // 4
    norm_store(resid_ref, gains_ref, 0, normed_ref)
    query_ref[:, C:] = jnp.zeros((rows, WIDE - C), jnp.bfloat16)
    reduced = jnp.zeros((tiles, C), jnp.float32)
    for sub in range(4):
        span = slice(sub * tiles, (sub + 1) * tiles)
        query_ref[span, :C] = product(normed_ref[span, :], unit_ref[0, :C, :]).astype(jnp.bfloat16)
        reduced = reduced + product(normed_ref[span, :], reduce_ref[0, sub * C : (sub + 1) * C, :])
    reduced_ref[...] = reduced
    normed_kv = norm_rows(reduced, gains_ref[2:3, :], gains_ref[3:4, :])[2].astype(jnp.bfloat16)
    for which, ref in enumerate((key_ref, value_ref)):
        ref[:, C:] = jnp.zeros((tiles, WIDE - C), jnp.bfloat16)
        ref[:, :C] = product(normed_kv, kv_ref[which]).astype(jnp.bfloat16)

    @pl.loop(0, bias_ref.shape[0], unroll=bias_ref.shape[0])
    def _(index):
        start, low = place_of(index, tiles)
        bias = bias_ref[index]
        for group in range(3):
            lanes = slice(group * LANES, (group + 1) * LANES)
            query = four_planes(query_ref, start, lanes)
            keys = head_pair(key_ref[pl.ds(low, KEY_SPAN), lanes], group)
            values = head_pair(value_ref[pl.ds(low, KEY_SPAN), lanes], group)
            probs = softmax_columns(back_product(keys, query), bias)
            probs = jnp.concatenate(probs, 0).T.astype(jnp.bfloat16)
            put_planes(attended_ref, start, lanes, product(probs, values).astype(jnp.bfloat16))

    for sub in range(4):
        span = slice(sub * tiles, (sub + 1) * tiles)
        middle_ref[span, :] = resid_ref[span, :] + product(attended_ref[span, :C], unit_ref[0, C : 2 * C, :])


def attention_forward(resid, gains, units, at, reduces, reduce_at, bias):
    rows = resid.shape[0]
    tiles = rows // 4
    low = jnp.bfloat16
    shapes = (
        jax.ShapeDtypeStruct((rows, C), jnp.float32),
        jax.ShapeDtypeStruct((rows, C), low),
        jax.ShapeDtypeStruct((rows, WIDE), low),
        jax.ShapeDtypeStruct((tiles, C), jnp.float32),
        jax.ShapeDtypeStruct((tiles, WIDE), low),
        jax.ShapeDtypeStruct((tiles, WIDE), low),
        jax.ShapeDtypeStruct((rows, WIDE), low),
        jax.ShapeDtypeStruct((2, C, C), low),
    )
    return pl.pallas_call(
        attention_forward_kernel,
        grid=(1,),
        out_shape=shapes,
        in_specs=[whole((rows, C)), whole((4, C)), unit_spec(at), unit_spec(reduce_at), whole(bias.shape)],
        out_specs=tuple(whole(shape.shape) for shape in shapes),
        scratch_shapes=[pltpu.VMEM((3, 2 * C, LANES), jnp.float32)],
        compiler_params=pltpu.CompilerParams(vmem_limit_bytes=VMEM_LIMIT),
        cost_estimate=pl.CostEstimate(flops=6 * 10**9, bytes_accessed=14 * 10**6, transcendentals=10**6),
        name="attention_forward",
    )(resid, gains, units, reduces, bias)


def embed_forward_kernel(
    patches_ref, halo_ref, unit_ref, gains_ref, pre_ref, resid_ref, kern_ref, planes_ref, taps_ref
):
    rows = pre_ref.shape[0]
    tiles = rows // 4
    used = FF * 9 * BLOCKS // C
    for ref, base in ((patches_ref, 0), (halo_ref, patches_ref.shape[0])):
        step = 64

        @pl.loop(0, ref.shape[0] // step, unroll=4)
        def _(at):
            span = pl.ds(pl.multiple_of(at * step, step), step)
            into = pl.ds(pl.multiple_of(base + at * step, step), step)
            part = product(ref[span, :], unit_ref[0, :PIN, :])
            for place, lane, width in lane_parts(C):
                planes_ref[place, into, :width] = part[:, lane : lane + width]

    for sub in range(4):
        for place, lane, width in lane_parts(C):
            pre_ref[sub * tiles : (sub + 1) * tiles, lane : lane + width] = planes_ref[
                place, pl.ds(sub, tiles, stride=4), :
            ][:, :width]
    taps = unit_ref[0, PIN : PIN + taps_ref.shape[1], :]
    spread_rows(taps, taps_ref)
    for layer_at in range(BLOCKS):
        for quarter in range(FF // C):
            for place, lane, width in lane_parts(C):
                begin = quarter * C + lane
                kern_ref[layer_at, :, begin : begin + width] = taps_ref[
                    place, pl.ds(layer_at * (used // BLOCKS) + quarter, 9, stride=FF // C), :
                ][:, :width]

    resid_ref[...] = norm_rows(pre_ref[...], gains_ref[0:1, :], gains_ref[1:2, :])[2]


def embed_forward(patches, halo, units, gains):
    rows = patches.shape[0] + halo.shape[0]
    wide = jax.ShapeDtypeStruct((rows, C), jnp.float32)
    taps = jax.ShapeDtypeStruct((BLOCKS, 9, FF), jnp.float32)
    return pl.pallas_call(
        embed_forward_kernel,
        grid=(1,),
        out_shape=(wide, wide, taps),
        in_specs=[whole(patches.shape), whole(halo.shape), unit_spec(0), whole((2, C))],
        out_specs=(whole(wide.shape), whole(wide.shape), whole(taps.shape)),
        scratch_shapes=[
            pltpu.VMEM((3, rows, LANES), jnp.float32),
            pltpu.VMEM((3, FF - PIN, LANES), jnp.float32),
        ],
        compiler_params=pltpu.CompilerParams(vmem_limit_bytes=VMEM_LIMIT),
        cost_estimate=pl.CostEstimate(flops=10**9, bytes_accessed=8 * 10**6, transcendentals=0),
        name="embed_forward",
    )(patches, halo, units, gains)


def embed_backward_kernel(
    grad_ref, pre_ref, gains_ref, patches_ref, halo_ref, *refs
):
    taps_refs = refs[:BLOCKS]
    unit_ref, dgain_ref, planes_ref, turned_ref, taps_ref = refs[BLOCKS:]
    rows = pre_ref.shape[0]
    tiles = rows // 4
    half = tiles // 2
    used = FF * 9 * BLOCKS // C
    sums = [jnp.zeros((1, C), jnp.float32)] * 2
    for sub in range(4):
        for part_at in range(2):
            span = slice(sub * tiles + part_at * half, sub * tiles + (part_at + 1) * half)
            unit, inverse, _ = norm_rows(pre_ref[span, :], gains_ref[0:1, :], gains_ref[1:2, :])
            grad = grad_ref[span, :]
            back = norm_rows_back(unit, inverse, gains_ref[0:1, :], grad)
            sums[0] = sums[0] + jnp.sum(grad * unit, 0, keepdims=True)
            sums[1] = sums[1] + jnp.sum(grad, 0, keepdims=True)
            for place, lane, width in lane_parts(C):
                value = back[:, lane : lane + width]
                if width < LANES:
                    value = jnp.concatenate([value, jnp.zeros((half, LANES - width), jnp.float32)], 1)
                planes_ref[place, pl.ds(4 * part_at * half + sub, half, stride=4), :] = value
    dgain_ref[0:1, :] = sums[0]
    dgain_ref[1:2, :] = sums[1]
    for place, lane, width in lane_parts(C):
        turned_ref[lane : lane + width, :] = planes_ref[place].T[:width, :].astype(jnp.bfloat16)
    split = patches_ref.shape[0]
    grads = product(turned_ref[:, :split], patches_ref[...]) + product(turned_ref[:, split:], halo_ref[...])
    unit_ref[0, :PIN, :] = grads.T.astype(jnp.bfloat16)
    taps_ref[...] = jnp.zeros_like(taps_ref)
    for layer_at, ref in enumerate(taps_refs):
        for quarter in range(FF // C):
            for place, lane, width in lane_parts(C):
                begin = quarter * C + lane
                value = ref[:, begin : begin + width]
                if width < LANES:
                    value = jnp.concatenate([value, jnp.zeros((9, LANES - width), jnp.float32)], 1)
                taps_ref[place, pl.ds(layer_at * (used // BLOCKS) + quarter, 9, stride=FF // C), :] = value
    for place, lane, width in lane_parts(C):
        unit_ref[0, PIN:, lane : lane + width] = taps_ref[place, :, :width].astype(jnp.bfloat16)


def embed_backward(grad, pre, gains, patches, halo, taps):
    rows = pre.shape[0]
    shapes = (jax.ShapeDtypeStruct((1, FF, C), jnp.bfloat16), jax.ShapeDtypeStruct((2, C), jnp.float32))
    operands = (grad, pre, gains, patches, halo, *taps)
    return pl.pallas_call(
        embed_backward_kernel,
        grid=(1,),
        out_shape=shapes,
        in_specs=[whole(part.shape) for part in operands],
        out_specs=tuple(whole(shape.shape) for shape in shapes),
        scratch_shapes=[
            pltpu.VMEM((3, rows, LANES), jnp.float32),
            pltpu.VMEM((C, rows), jnp.bfloat16),
            pltpu.VMEM((3, FF - PIN, LANES), jnp.float32),
        ],
        compiler_params=pltpu.CompilerParams(vmem_limit_bytes=VMEM_LIMIT),
        cost_estimate=pl.CostEstimate(flops=10**9, bytes_accessed=8 * 10**6, transcendentals=0),
        name="embed_backward",
    )(*operands)


def head_kernel(
    resid_ref, gains_ref, weight_ref, label_ref, keep_ref, total_ref,
    grad_ref, dhead_ref, dgain_ref, loss_ref,
    final_ref, turned_ref,
):
    rows = resid_ref.shape[0]
    tiles = rows // 4
    classes = weight_ref.shape[1]
    low = weight_ref[...].astype(jnp.bfloat16)
    share = 1.0 / total_ref[0:1, 0:1]
    sums = [jnp.zeros((1, C), jnp.float32)] * 2
    loss = jnp.zeros((1, 1), jnp.float32)
    for sub in range(4):
        span = slice(sub * tiles, (sub + 1) * tiles)
        unit, inverse, final = norm_rows(resid_ref[span, :], gains_ref[0:1, :], gains_ref[1:2, :])
        final = final.astype(jnp.bfloat16)
        final_ref[span, :] = final
        logits = product(final, low)
        peak = jnp.max(logits, -1, keepdims=True)
        log_norm = peak + jnp.log(jnp.sum(jnp.exp(logits - peak), -1, keepdims=True))
        keep = keep_ref[span, :]
        hit = lax.broadcasted_iota(jnp.int32, (tiles, classes), 1) == label_ref[span, :]
        picked = jnp.sum(jnp.where(hit, logits, 0.0), -1, keepdims=True)
        loss = loss + jnp.sum((log_norm - picked) * keep, 0, keepdims=True)
        dlogits = (jnp.exp(logits - log_norm) - jnp.where(hit, 1.0, 0.0)) * (keep * share)
        turned_ref[:, span] = dlogits.T.astype(jnp.bfloat16)
        grad = back_product(dlogits.astype(jnp.bfloat16), low)
        grad_ref[span, :] = norm_rows_back(unit, inverse, gains_ref[0:1, :], grad)
        sums[0] = sums[0] + jnp.sum(grad * unit, 0, keepdims=True)
        sums[1] = sums[1] + jnp.sum(grad, 0, keepdims=True)
    dhead_ref[:classes, :] = product(turned_ref[...], final_ref[...])
    dhead_ref[classes:, :] = jnp.zeros((dhead_ref.shape[0] - classes, C), jnp.float32)
    dgain_ref[0:1, :] = sums[0]
    dgain_ref[1:2, :] = sums[1]
    loss_ref[...] = jnp.broadcast_to(loss, (1, C))


def head_step(resid, gains, weight, labels, keep, total):
    rows = resid.shape[0]
    classes = weight.shape[1]
    wide = jnp.float32
    shapes = (
        jax.ShapeDtypeStruct((rows, C), wide),
        jax.ShapeDtypeStruct((-(-classes // 8) * 8, C), wide),
        jax.ShapeDtypeStruct((2, C), wide),
        jax.ShapeDtypeStruct((1, C), wide),
    )
    operands = (resid, gains, weight, labels, keep, total)
    return pl.pallas_call(
        head_kernel,
        grid=(1,),
        out_shape=shapes,
        in_specs=[whole(part.shape) for part in operands],
        out_specs=tuple(whole(shape.shape) for shape in shapes),
        scratch_shapes=[
            pltpu.VMEM((rows, C), jnp.bfloat16),
            pltpu.VMEM((classes, rows), jnp.bfloat16),
        ],
        compiler_params=pltpu.CompilerParams(vmem_limit_bytes=VMEM_LIMIT),
        cost_estimate=pl.CostEstimate(flops=10**9, bytes_accessed=5 * 10**6, transcendentals=10**6),
        name="head_step",
    )(*operands)


def attention_backward_kernel(
    advance,
    grad_ref, resid_ref, gains_ref, unit_ref, reduce_ref, bias_ref,
    normed_ref, query_ref, reduced_ref, key_ref, value_ref, attended_ref, kv_ref,
    out_ref, dunits_ref, dgain_ref,
    turned_ref, datt_ref, dquery_ref, dkey_ref, dvalue_ref, first_ref, planes_ref,
):
    rows = resid_ref.shape[0]
    tiles = rows // 4
    low_type = jnp.bfloat16
    datt_ref[:, C:] = jnp.zeros((rows, WIDE - C), low_type)
    turned_ref[...] = grad_ref[...].T.astype(low_type)
    dunits_ref[0, C : 2 * C, :] = product(turned_ref[...], attended_ref[:, :C]).T.astype(low_type)
    for sub in range(4):
        span = slice(sub * tiles, (sub + 1) * tiles)
        datt_ref[span, :C] = back_product(grad_ref[span, :].astype(low_type), unit_ref[0, C : 2 * C, :]).astype(low_type)
    dkey_ref[...] = jnp.zeros_like(dkey_ref)
    dvalue_ref[...] = jnp.zeros_like(dvalue_ref)
    blocks = bias_ref.shape[0]

    def one_block(step):
        index = blocks - 1 - step
        start, low = place_of(index, tiles)
        bias = bias_ref[index]
        tile_at = lax.rem(lax.broadcasted_iota(jnp.int32, (4 * BLOCK_TILES, LANES), 0), BLOCK_TILES)
        fresh = tile_at >= index * BLOCK_TILES - start
        span = pl.ds(low, KEY_SPAN)
        for group in range(3):
            lanes = slice(group * LANES, (group + 1) * LANES)
            query = four_planes(query_ref, start, lanes)
            datt = four_planes(datt_ref, start, lanes)
            datt = jnp.where(fresh, datt, jnp.zeros_like(datt))
            keys = head_pair(key_ref[span, lanes], group)
            values = head_pair(value_ref[span, lanes], group)
            probs = softmax_columns(back_product(keys, query), bias)
            dprobs = back_product(values, datt)
            dscores = []
            for half, prob in enumerate(probs):
                dprob = dprobs[half * KEY_SPAN : (half + 1) * KEY_SPAN]
                inner = jnp.sum(prob * dprob, 0, keepdims=True)
                dscores.append(prob * (dprob - inner) * HD ** (-0.5))
            dscores = jnp.concatenate(dscores, 0)
            probs = jnp.concatenate(probs, 0).astype(low_type)
            dquery = product(dscores.T.astype(low_type), keys)
            put_planes(dquery_ref, start, lanes, dquery.astype(low_type))
            dkeys = product(dscores.astype(low_type), query)
            dvalues = product(probs, datt)
            if group < 2:
                first = lax.broadcasted_iota(jnp.int32, (KEY_SPAN, LANES), 1) < HD
                dkeys = jnp.where(first, dkeys[:KEY_SPAN], dkeys[KEY_SPAN:])
                dvalues = jnp.where(first, dvalues[:KEY_SPAN], dvalues[KEY_SPAN:])
            dkey_ref[span, lanes] += dkeys
            dvalue_ref[span, lanes] += dvalues

    advance(0)
    pl.loop(0, blocks // 2, unroll=blocks // 2)(one_block)
    advance(1)
    pl.loop(blocks // 2, blocks, unroll=blocks - blocks // 2)(one_block)
    advance(2)
    unit, inverse, normed = norm_rows(reduced_ref[...], gains_ref[2:3, :], gains_ref[3:4, :])
    normed_t = normed.T.astype(low_type)
    dkeys = dkey_ref[:, :C].astype(low_type)
    dvalues = dvalue_ref[:, :C].astype(low_type)
    for which, grads in enumerate((dkeys, dvalues)):
        dweight = product(normed_t, grads)
        for at, lane, width in lane_parts(C):
            part = dweight[:, lane : lane + width]
            if width < LANES:
                part = jnp.concatenate([part, jnp.zeros((C, LANES - width), jnp.float32)], 1)
            planes_ref[at, pl.ds(which, C, stride=2), :] = part
    for at, lane, width in lane_parts(C):
        dunits_ref[0, 2 * C :, lane : lane + width] = planes_ref[at, :, :width].astype(low_type)
    dnormed = back_product(dkeys, kv_ref[0]) + back_product(dvalues, kv_ref[1])
    dgain_ref[2:3, :] = jnp.sum(dnormed * unit, 0, keepdims=True)
    dgain_ref[3:4, :] = jnp.sum(dnormed, 0, keepdims=True)
    dreduced = norm_rows_back(unit, inverse, gains_ref[2:3, :], dnormed).astype(low_type)
    turned_ref[...] = normed_ref[...].T
    dunits_ref[0, :C, :] = product(turned_ref[...], dquery_ref[:, :C]).astype(low_type)
    for sub in range(4):
        span = slice(sub * tiles, (sub + 1) * tiles)
        part = slice(sub * C, (sub + 1) * C)
        dunits_ref[1, part, :] = outer_sum(normed_ref[span, :], dreduced).astype(low_type)
        first_ref[span, :] = back_product(
            dquery_ref[span, :C], unit_ref[0, :C, :]
        ) + back_product(dreduced, reduce_ref[0, part, :])

    grad = first_ref[...]
    unit, inverse, _ = norm_rows(resid_ref[...], gains_ref[0:1, :], gains_ref[1:2, :])
    out_ref[...] = grad_ref[...] + norm_rows_back(unit, inverse, gains_ref[0:1, :], grad)
    dgain_ref[0:1, :] = jnp.sum(grad * unit, 0, keepdims=True)
    dgain_ref[1:2, :] = jnp.sum(grad, 0, keepdims=True)


def attention_backward(grad, resid, gains, units, at, reduces, reduce_at, bias, kept, plans, meeting):
    rows = resid.shape[0]
    tiles = rows // 4
    low = jnp.bfloat16
    shapes = (
        jax.ShapeDtypeStruct((rows, C), jnp.float32),
        jax.ShapeDtypeStruct((2, FF, C), low),
        jax.ShapeDtypeStruct((4, C), jnp.float32),
    )
    count = len(plans)

    def run(*refs):
        own_in, ride_in = refs[:13], refs[13 : 13 + count]
        own_out, ride_out = refs[13 + count : 16 + count], refs[16 + count : 16 + 2 * count]
        rest = refs[16 + 2 * count :]
        rides = rides_of(plans, ride_in, ride_out, rest[7:])
        rides.signal()
        attention_backward_kernel(rides.advance, *own_in, *own_out, *rest[:7])
        for phase in range(3, rides.phases + 1):
            rides.advance(phase)

    return pl.pallas_call(
        run,
        grid=(1,),
        out_shape=shapes + tuple(plan.out for plan in plans),
        in_specs=[
            whole((rows, C)),
            whole((rows, C)),
            whole((4, C)),
            unit_spec(at),
            unit_spec(reduce_at),
            whole(bias.shape),
        ]
        + [whole(part.shape) for part in kept]
        + [plan.in_spec for plan in plans],
        out_specs=tuple(whole(shape.shape) for shape in shapes) + tuple(plan.out_spec for plan in plans),
        scratch_shapes=[
            pltpu.VMEM((C, rows), low),
            pltpu.VMEM((rows, WIDE), low),
            pltpu.VMEM((rows, WIDE), low),
            pltpu.VMEM((tiles, WIDE), jnp.float32),
            pltpu.VMEM((tiles, WIDE), jnp.float32),
            pltpu.VMEM((rows, C), jnp.float32),
            pltpu.VMEM((3, 2 * C, LANES), jnp.float32),
        ]
        + sum([plan.scratch for plan in plans], []),
        compiler_params=pltpu.CompilerParams(collective_id=meeting, has_side_effects=True, vmem_limit_bytes=VMEM_LIMIT),
        cost_estimate=pl.CostEstimate(flops=12 * 10**9, bytes_accessed=18 * 10**6, transcendentals=10**6),
        name="attention_backward",
    )(grad, resid, gains, units, reduces, bias, *kept, *[plan.value for plan in plans])


BOTH = ("grp", "tok")


def axis_bits(axis):
    count = lax.axis_size(axis)
    return [1 << place for place in reversed(range(count.bit_length() - 1))]


def bit_order():
    tok_bits = axis_bits("tok")
    return [("grp", bit) for bit in axis_bits("grp")] + [("tok", bit) for bit in tok_bits]


MESH = pl.DeviceIdType.MESH


def exchange_setup():
    grp, tok = lax.axis_index("grp"), lax.axis_index("tok")
    n_tok = lax.axis_size("tok")
    peers = [(lax.bitwise_xor(grp, bit), tok) for bit in axis_bits("grp")]
    peers += [(grp, lax.bitwise_xor(tok, step)) for step in range(1, n_tok)]
    return (grp, tok, n_tok, peers)


def signal_all(peers):
    barrier = pltpu.get_barrier_semaphore()
    for peer in peers:
        pl.semaphore_signal(barrier, inc=1, device_id=peer, device_id_type=MESH)


def greet(peers):
    signal_all(peers)
    pl.semaphore_wait(pltpu.get_barrier_semaphore(), len(peers))


def send(source, target, sems, at, peer):
    copy = pltpu.make_async_remote_copy(
        src_ref=source,
        dst_ref=target,
        send_sem=sems[0].at[at],
        recv_sem=sems[1].at[at],
        device_id=peer,
        device_id_type=MESH,
    )
    copy.start()
    return copy


def gather_view(ref, unit, place, done):
    index = [slice(None) if name in done else place(name) for name in bit_order()]
    return ref.at[tuple([unit] + index)]


class GatherRide:
    def __init__(self, full_ref, scratch):
        self.grp, self.tok = lax.axis_index("grp"), lax.axis_index("tok")
        self.phases = len(bit_order())
        self.names = bit_order()
        self.full_ref = full_ref
        self.sems = scratch[:2]

    def order(self, unit):
        grp_bits = [("grp", bit) for bit in axis_bits("grp")]
        flip = grp_bits[::-1] if unit % 2 else grp_bits
        return [("tok", bit) for bit in axis_bits("tok")[:-1]] + flip + [("tok", 1)]

    def place(self, name):
        return (self.grp if name[0] == "grp" else self.tok) // name[1] % 2

    def partner(self, name):
        axis, bit = name
        if axis == "grp":
            return (lax.bitwise_xor(self.grp, bit), self.tok)
        return (self.grp, lax.bitwise_xor(self.tok, bit))

    def copy(self, unit, phase):
        order = self.order(unit)
        held = gather_view(self.full_ref, unit, self.place, order[:phase])
        at = phase * self.full_ref.shape[0] + unit
        return pltpu.make_async_remote_copy(
            src_ref=held,
            dst_ref=held,
            send_sem=self.sems[0].at[at],
            recv_sem=self.sems[1].at[at],
            device_id=self.partner(order[phase]),
            device_id_type=MESH,
        )

    def put(self, unit, value):
        self.full_ref[(unit,) + tuple(self.place(name) for name in bit_order())] = value

    def advance(self, phase):
        for unit in range(self.full_ref.shape[0]):
            if phase:
                self.copy(unit, phase - 1).wait()
            if phase < self.phases:
                self.copy(unit, phase).start()


def gather_scratch(total):
    phases = len(bit_order())
    return [pltpu.SemaphoreType.DMA((phases * total,))] * 2


def start_kernel(
    slot_ref, piece_ref, count_ref, patch_ref, mark_ref,
    full_ref, later_ref, total_ref, patch_halo_ref, mark_halo_ref,
    recv_ref, near_s, near_r, halo_s, halo_r, *scratch,
):
    grp, tok, n_tok, peers = exchange_setup()
    slot_rows = piece_ref.shape[1]
    units, first = slot_ref.shape[0], full_ref.shape[0]
    gather = GatherRide(full_ref, scratch[:2])
    count = SumRide(count_ref, total_ref, scratch[2:])
    greet(peers)
    copies = []
    for step in range(1, n_tok):
        peer = lax.bitwise_xor(tok, step)
        landing = recv_ref.at[pl.ds(tok * slot_rows, slot_rows)]
        copies.append(send(piece_ref.at[peer], landing, (near_s, near_r), step, (grp, peer)))
    recv_ref[pl.ds(tok * slot_rows, slot_rows)] = piece_ref[tok]
    count.advance(0)
    for copy in copies:
        copy.wait()
    for unit in range(first):
        gather.put(unit, recv_ref[slot_ref[unit]])
    gather.advance(0)
    before = (grp, lax.rem(tok + n_tok - 1, n_tok))
    mark_copy = send(mark_ref, mark_halo_ref, (halo_s, halo_r), 0, before)
    patch_copy = send(patch_ref.at[pl.ds(0, patch_halo_ref.shape[0])], patch_halo_ref, (halo_s, halo_r), 1, before)
    for unit in range(first, units):
        later_ref[unit - first] = recv_ref[slot_ref[unit]]
    for phase in range(1, gather.phases + 1):
        count.advance(phase)
        gather.advance(phase)
    mark_copy.wait()
    patch_copy.wait()


def start_exchange(slot_of, pieces, count, patches, marks, first):
    n_tok, slot_rows, chunk, width = pieces.shape
    phases = len(bit_order())
    units = slot_of.shape[0]
    vmem = pl.BlockSpec(memory_space=pltpu.VMEM)
    full_shape = (first,) + (2,) * phases + (chunk, width)
    return pl.pallas_call(
        start_kernel,
        out_shape=(
            jax.ShapeDtypeStruct(full_shape, pieces.dtype),
            jax.ShapeDtypeStruct((units - first, chunk, width), pieces.dtype),
            jax.ShapeDtypeStruct(count.shape, count.dtype),
            jax.ShapeDtypeStruct((OVER, patches.shape[1]), patches.dtype),
            jax.ShapeDtypeStruct(marks.shape, marks.dtype),
        ),
        in_specs=[pl.BlockSpec(memory_space=pltpu.SMEM), vmem, vmem, pl.BlockSpec(memory_space=pl.ANY), vmem],
        out_specs=(vmem, vmem, vmem, pl.BlockSpec(memory_space=pl.ANY), vmem),
        scratch_shapes=[
            pltpu.VMEM((n_tok * slot_rows, chunk, width), pieces.dtype),
            pltpu.SemaphoreType.DMA((n_tok,)),
            pltpu.SemaphoreType.DMA((n_tok,)),
            pltpu.SemaphoreType.DMA((2,)),
            pltpu.SemaphoreType.DMA((2,)),
        ]
        + gather_scratch(first)
        + sum_scratch(count.shape),
        compiler_params=pltpu.CompilerParams(collective_id=0, has_side_effects=True, vmem_limit_bytes=VMEM_LIMIT),
        name="start_exchange",
    )(slot_of, pieces, count, patches, marks)


def unit_order(unit):
    grp_bits = [("grp", bit) for bit in axis_bits("grp")]
    if unit % 2:
        grp_bits = grp_bits[::-1]
    return [("tok", 1)] + grp_bits + [("tok", bit) for bit in axis_bits("tok")[:-1][::-1]]


def unit_layout(order):
    left = bit_order()
    shapes = []
    for name in order:
        at = left.index(name)
        shapes.append((1 << at, 2, 1 << (len(left) - 1 - at)))
        left.remove(name)
    return shapes


SPLIT = 3


class UnitRide:
    def __init__(self, sources, out_ref, scratch, begin=0, end=None, base=0):
        self.grp, self.tok = lax.axis_index("grp"), lax.axis_index("tok")
        self.begin = begin
        self.end = len(bit_order()) if end is None else end
        self.phases = self.end - begin
        self.names = unit_order(0)[self.begin : self.end]
        self.sources = sources
        self.out_ref, self.base = out_ref, base
        self.sems = scratch[:2]
        self.buffers = scratch[2:]

    def partner(self, name):
        axis, bit = name
        if axis == "grp":
            return (lax.bitwise_xor(self.grp, bit), self.tok)
        return (self.grp, lax.bitwise_xor(self.tok, bit))

    def half_of(self, name):
        return (self.grp if name[0] == "grp" else self.tok) // name[1] % 2

    def before(self, unit, phase):
        if phase == 0:
            ref, at = self.sources[unit]
            return ref.at[at]
        return self.buffers[unit * 2 * self.phases + 2 * (phase - 1) + 1]

    def landing(self, unit, phase):
        return self.buffers[unit * 2 * self.phases + 2 * phase]

    def copy(self, unit, phase):
        name = unit_order(unit)[self.begin + phase]
        at = phase * len(self.sources) + unit
        return pltpu.make_async_remote_copy(
            src_ref=self.before(unit, phase).at[:, 1 - self.half_of(name)],
            dst_ref=self.landing(unit, phase),
            send_sem=self.sems[0].at[at],
            recv_sem=self.sems[1].at[at],
            device_id=self.partner(name),
            device_id_type=MESH,
        )

    def finish(self, unit, phase):
        order = unit_order(unit)
        shapes = unit_layout(order)
        self.copy(unit, phase).wait()
        outer, _, inner = shapes[self.begin + phase]
        source, landed = self.before(unit, phase), self.landing(unit, phase)
        mine = self.half_of(order[self.begin + phase])
        target = self.out_ref.at[self.base + unit]
        if phase + 1 < self.phases:
            target = self.before(unit, phase + 1)
        whole_done = self.begin + phase + 1 == len(order)
        if not whole_done:
            low = shapes[self.begin + phase + 1][2]

        @pl.loop(0, outer * inner, unroll=min(4, outer * inner))
        def _(at):
            value = source[at // inner, mine, at % inner] + landed[at // inner, at % inner]
            if whole_done:
                target[...] = value
            else:
                target[at // (2 * low), at // low % 2, at % low] = value

    def advance(self, phase):
        for unit in range(len(self.sources)):
            if phase:
                self.finish(unit, phase - 1)
            if phase < self.phases:
                self.copy(unit, phase).start()


def unit_scratch(total, chunk, width, begin=0, end=None):
    end = len(bit_order()) if end is None else end
    dma = pltpu.SemaphoreType.DMA
    buffers = [dma(((end - begin) * total,)), dma(((end - begin) * total,))]
    for unit in range(total):
        shapes = unit_layout(unit_order(unit))
        for phase in range(begin, end):
            outer, _, inner = shapes[phase]
            buffers.append(pltpu.VMEM((outer, inner, chunk, width), jnp.bfloat16))
            following = shapes[phase + 1] if phase + 1 < end else (1, 1, 1)
            buffers.append(pltpu.VMEM(following + (chunk, width), jnp.bfloat16))
    return buffers


def unit_blocks(units):
    chunk = units.shape[1] >> len(bit_order())
    return units.reshape((units.shape[0],) + unit_layout(unit_order(0))[0] + (chunk, units.shape[2]))


class SumRide:
    def __init__(self, source_ref, total_ref, scratch, begin=0, end=None):
        self.grp, self.tok = lax.axis_index("grp"), lax.axis_index("tok")
        self.order = unit_order(0)[begin:end]
        self.names = self.order
        self.phases = len(self.order)
        self.source_ref, self.total_ref = source_ref, total_ref
        self.sums = scratch[2]
        self.sems = scratch[:2]

    partner = UnitRide.partner

    def copy(self, phase):
        return pltpu.make_async_remote_copy(
            src_ref=self.sums.at[2 * phase],
            dst_ref=self.sums.at[2 * phase + 1],
            send_sem=self.sems[0].at[phase],
            recv_sem=self.sems[1].at[phase],
            device_id=self.partner(self.order[phase]),
            device_id_type=MESH,
        )

    def advance(self, phase):
        if phase == 0:
            self.sums[0] = self.source_ref[...]
        else:
            self.copy(phase - 1).wait()
            self.sums[2 * phase] = self.sums[2 * phase - 2] + self.sums[2 * phase - 1]
        if phase < self.phases:
            self.copy(phase).start()
        else:
            self.total_ref[...] = self.sums[2 * phase]


def sum_scratch(shape):
    phases = len(bit_order())
    dma = pltpu.SemaphoreType.DMA
    return [dma((phases,)), dma((phases,)), pltpu.VMEM((2 * phases + 1,) + shape, jnp.float32)]


def tail_kernel(counts, rows, *refs):
    unit_at_ref, early_ref, part_ref = refs[:3]
    blocks, refs = refs[3 : 3 + len(counts)], refs[3 + len(counts) :]
    small_refs, refs = refs[: len(rows)], refs[len(rows) :]
    owned_ref, small_out_ref, chunk_ref, place_ref, near_s, near_r, small_ref = refs[:7]
    scratch = refs[7:]
    sources = [(ref, at) for ref, count in zip(blocks, counts) for at in range(count)]
    total = len(sources)
    parts = part_ref.shape[0]
    grp, tok, n_tok, peers = exchange_setup()
    signal_all(peers)
    begin = 0
    for ref, count in zip(small_refs, rows):
        small_ref[begin : begin + count, :] = ref[...]
        begin += count
    small_ref[begin:, :] = jnp.zeros((small_ref.shape[0] - begin, C), jnp.float32)
    cut = 3 + 2 + 2 * total * len(bit_order())
    rides = Rides(
        [
            UnitRide(sources, chunk_ref, scratch[3:cut]),
            SumRide(small_ref, small_out_ref, scratch[:3]),
            UnitRide([(part_ref, at) for at in range(parts)], chunk_ref, scratch[cut:], SPLIT, None, total),
        ]
    )
    rides.peers = peers
    for phase in range(rides.phases + 1):
        rides.advance(phase)
    total += parts
    for at in range(early_ref.shape[0]):
        chunk_ref[total + at] = early_ref[at]
    last = total + early_ref.shape[0]
    chunk_ref[last] = jnp.zeros(chunk_ref.shape[1:], chunk_ref.dtype)
    slot_rows = owned_ref.shape[1]

    @pl.loop(0, n_tok * slot_rows)
    def _(at):
        place_ref[at // slot_rows, at % slot_rows] = chunk_ref[unit_at_ref[at]]

    copies = []
    for step in range(1, n_tok):
        peer = lax.bitwise_xor(tok, step)
        copies.append(send(place_ref.at[peer], owned_ref.at[tok], (near_s, near_r), step, (grp, peer)))
    owned_ref[tok] = place_ref[tok]
    for copy in copies:
        copy.wait()


def tail_exchange(unit_at, early, part, sources, smalls, n_tok):
    chunk, width = early.shape[1:]
    counts = tuple(source.shape[0] for source in sources)
    rows = tuple(small.shape[0] for small in smalls)
    total = sum(counts)
    low = early.dtype
    vmem = pl.BlockSpec(memory_space=pltpu.VMEM)
    slot_rows = unit_at.shape[0] // n_tok
    dma = pltpu.SemaphoreType.DMA
    small = (-(-sum(rows) // 8) * 8, C)
    return pl.pallas_call(
        lambda *refs: tail_kernel(counts, rows, *refs),
        out_shape=(
            jax.ShapeDtypeStruct((n_tok, slot_rows, chunk, width), low),
            jax.ShapeDtypeStruct(small, jnp.float32),
        ),
        in_specs=[pl.BlockSpec(memory_space=pltpu.SMEM)] + [vmem] * (2 + len(sources) + len(smalls)),
        out_specs=(vmem, vmem),
        scratch_shapes=[
            pltpu.VMEM((total + part.shape[0] + early.shape[0] + 1, chunk, width), low),
            pltpu.VMEM((n_tok, slot_rows, chunk, width), low),
            dma((n_tok,)),
            dma((n_tok,)),
            pltpu.VMEM(small, jnp.float32),
        ]
        + sum_scratch(small)
        + unit_scratch(total, chunk, width)
        + unit_scratch(part.shape[0], chunk, width, SPLIT),
        compiler_params=pltpu.CompilerParams(collective_id=1, has_side_effects=True, vmem_limit_bytes=VMEM_LIMIT),
        name="tail_exchange",
    )(unit_at, early, part, *[unit_blocks(source) for source in sources], *smalls)


def body(
    patches,
    labels,
    valid_mask,
    crop_counts,
    owners,
    slot_weight,
    slot_moment,
    slot_second,
    norm_params,
    norm_moment,
    norm_second,
    head_weight,
    head_moment,
    head_second,
):
    tok_dev = patches.shape[0]
    n_tok = lax.axis_size("tok")
    n_grp = lax.axis_size("grp")
    tok_index = lax.axis_index("tok")
    group_tok = tok_dev * n_tok
    counts = crop_counts[0]
    n_unit = owners.shape[0]
    slot_rows, columns = slot_weight.shape
    unit_order = jnp.arange(n_unit, dtype=jnp.int32)
    same_owner = owners[:, None] == owners[None, :]
    rank_of = jnp.sum(same_owner & (unit_order[None, :] < unit_order[:, None]), 1)
    slot_of = owners * slot_rows + rank_of
    chunk = columns // n_tok // C
    first_tok = tok_index * tok_dev
    small_end = counts[0] * BIG_SIDE**2 + counts[1] * SMALL_SIDE**2
    counted = valid_mask * (first_tok + jnp.arange(tok_dev, dtype=jnp.int32) < small_end)
    counted = jnp.full((8, LANES), jnp.sum(counted.astype(jnp.float32)))
    pieces = slot_weight.astype(jnp.bfloat16).reshape(slot_rows, n_tok, chunk, C).transpose(1, 0, 2, 3)
    first_units = 1 + 2 * (n_unit // BLOCKS)
    marks = jnp.stack([labels, valid_mask])
    own, later, counted, patch_halo, mark_halo = start_exchange(
        slot_of, pieces, counted, patches, marks[:, :OVER], first_units
    )
    pixel_total = counted[0, 0]
    own = own.reshape(first_units, FF, C)
    units = lax.all_gather(later, BOTH, axis=1, tiled=True)
    layers = [
        ((own, 1, own, 2), (own, 3)),
        ((own, 5, own, 6), (own, 7)),
        ((units, 0, units, 1), (units, 2)),
    ]

    window = tok_dev + OVER
    tiles = window // 4
    marks = jnp.concatenate([marks, mark_halo], 1)
    marks = marks.reshape(2, tiles, 4).transpose(0, 2, 1).reshape(2, window)
    labels = marks[0]
    positions = first_tok + 4 * jnp.arange(tiles, dtype=jnp.int32)
    begin_at, half_side, tile_y, tile_x, is_real = image_layout(positions, counts)
    own_image = (begin_at >= first_tok) & (begin_at < first_tok + tok_dev) & (positions < group_tok)
    stacks = shift_stacks(half_side, tile_y, tile_x, is_real)

    def image_at(tile):
        at = first_tok + 4 * tile
        return jnp.where(at < group_tok, image_layout(at, counts)[0], -1)

    bias = block_bias(tiles, image_at)
    real_rows = jnp.broadcast_to(is_real.astype(jnp.float32)[:, None], (tiles, LANES))
    keep_mask = marks[1].astype(jnp.float32) * jnp.tile((own_image & is_real).astype(jnp.float32), 4)
    tail = 6 * BLOCKS
    embed_pre, resid, kernels = embed_forward(patches, patch_halo, own, norm_params[tail : tail + 2])
    kept_all = []
    for layer_at in range(BLOCKS):
        attn_units, mlp_units = layers[layer_at]
        at = 6 * layer_at
        middle, *attn_kept = attention_forward(resid, norm_params[at : at + 4], *attn_units, bias)
        output, *mlp_kept = mlp_forward(
            middle, norm_params[at + 4 : at + 6], *mlp_units, kernels, layer_at, stacks, real_rows,
        )
        w_up = mlp_kept.pop()
        kept_all.append((resid, attn_kept, middle, mlp_kept, w_up))
        resid = output
    grad_res, d_head, final_gains, loss_row = head_step(
        resid, norm_params[tail + 2 : tail + 4], head_weight, labels[:, None], keep_mask[:, None], counted
    )
    plans = [plan_sum(d_head, 0, SPLIT)]
    early = []
    kernel_grads = [None] * BLOCKS
    gain_grads = []
    phases = len(bit_order())
    for layer_at in reversed(range(BLOCKS)):
        attn_units, mlp_units = layers[layer_at]
        at = 6 * layer_at
        entry, attn_kept, middle, mlp_kept, w_up = kept_all[layer_at]
        grad_res, mlp_grads, kernel_grads[layer_at], mlp_gains, *ridden_out = mlp_backward(
            grad_res, middle, norm_params[at + 4 : at + 6], w_up, *mlp_units, kernels, layer_at,
            stacks, real_rows, mlp_kept, plans, 2 + layer_at,
        )
        plans = [plan_units(mlp_grads, 0, SPLIT)]
        if layer_at + 1 == BLOCKS:
            plans.append(plan_sum(ridden_out[0], SPLIT, phases))
        else:
            early.insert(0, ridden_out[1])
            plans.append(plan_units(ridden_out[0], SPLIT, phases))
        grad_res, attn_grads, attn_gains, *ridden_out = attention_backward(
            grad_res, entry, norm_params[at : at + 4], *attn_units, bias, attn_kept, plans, 2 + BLOCKS + layer_at
        )
        if layer_at + 1 < BLOCKS:
            early.insert(0, ridden_out[1])
        else:
            head_total = ridden_out[1][: head_weight.shape[1]].T
        plans = [plan_units(attn_grads, 0, SPLIT), plan_units(ridden_out[0], SPLIT, phases)]
        gain_grads = [attn_gains, mlp_gains] + gain_grads
    part = ridden_out[0]
    first_grad, embed_gains = embed_backward(
        grad_res, embed_pre, norm_params[tail : tail + 2], patches, patch_halo, kernel_grads
    )
    early = jnp.concatenate(early, 0)
    smalls = gain_grads + [embed_gains, final_gains, loss_row]
    row_ids = jnp.arange(slot_rows * n_tok, dtype=jnp.int32)
    matches = slot_of[None, :] == row_ids[:, None]
    unit_at = jnp.where(jnp.any(matches, 1), jnp.argmax(matches, 1), n_unit)
    owned, small = tail_exchange(unit_at, early, part, [first_grad, attn_grads], smalls, n_tok)
    owned = owned.transpose(1, 0, 2, 3).astype(jnp.float32).reshape(slot_rows, columns)
    norm_rows_all = norm_params.shape[0]
    norm_total, loss_sum = (small[:norm_rows_all], small[norm_rows_all, 0])
    slot_m, slot_v, slot_w = adamw_step(
        slot_weight, slot_moment, slot_second, owned, RATE_MATRIX, DECAY_RATE
    )
    norm_m, norm_v, norm_w = adamw_step(
        norm_params, norm_moment, norm_second, norm_total, RATE_VECTOR, 0.0
    )
    head_m, head_v, head_w = adamw_step(
        head_weight, head_moment, head_second, head_total, RATE_MATRIX, DECAY_RATE
    )
    return (
        loss_sum,
        pixel_total,
        slot_m,
        slot_v,
        slot_w,
        norm_m,
        norm_v,
        norm_w,
        head_m,
        head_v,
        head_w,
    )


def solution(mesh):
    in_specs = (
        P(("grp", "tok"), None),
        P(("grp", "tok")),
        P(("grp", "tok")),
        P("grp", None),
        P(),
        P("tok", "grp"),
        P("tok", "grp"),
        P("tok", "grp"),
        P(),
        P(),
        P(),
        P(),
        P(),
        P(),
    )
    out_specs = (
        P(),
        P(),
        P("tok", "grp"),
        P("tok", "grp"),
        P("tok", "grp"),
        P(),
        P(),
        P(),
        P(),
        P(),
        P(),
    )
    return jax.shard_map(body, mesh=mesh, in_specs=in_specs, out_specs=out_specs, check_vma=False)
```

```python
import functools

import jax
import jax.numpy as jnp
import numpy as np
from jax import lax
from jax.experimental import pallas as pl
from jax.experimental.pallas import tpu as pltpu
from jax.sharding import PartitionSpec as P

C = 320
HEADS = 5
HD = 64
FF = 1280
PIN = 1152
BLOCKS = 3
BIG_SIDE = 14
SMALL_SIDE = 6
STEP = 10
KVH = 49


EPS_NORM = 1e-06
BETA_ONE = 0.9
BETA_TWO = 0.999
ADAM_EPS = 1e-08
RATE_MATRIX = 0.05
RATE_VECTOR = 0.3
DECAY_RATE = 0.05
NEG_FILL = -1e30
PREC_HIGH = lax.Precision.HIGHEST


def layer_norm(values, gain_vec, shift_vec):
    center = values - jnp.mean(values, -1, keepdims=True)
    inverse = lax.rsqrt(jnp.mean(center * center, -1, keepdims=True) + EPS_NORM)
    return center * inverse * gain_vec + shift_vec


def adamw_step(weight, moment, second, gradient, rate_now, decay_now):
    moment = BETA_ONE * moment + (1.0 - BETA_ONE) * gradient
    second = BETA_TWO * second + (1.0 - BETA_TWO) * gradient * gradient
    m_hat = moment / (1.0 - BETA_ONE**STEP)
    v_hat = second / (1.0 - BETA_TWO**STEP)
    weight = weight - rate_now * (m_hat / (jnp.sqrt(v_hat) + ADAM_EPS) + decay_now * weight)
    return (moment, second, weight)


def product(left, right):
    return jnp.dot(left, right, preferred_element_type=jnp.float32)


def outer_sum(left, right):
    return lax.dot_general(
        left, right, (((0,), (0,)), ((), ())), preferred_element_type=jnp.float32
    )


def back_product(gradient, weight):
    return lax.dot_general(
        gradient, weight, (((1,), (1,)), ((), ())), preferred_element_type=jnp.float32
    )


def norm_back(values, gain_vec, shift_vec, gradient):
    _, pull_back = jax.vjp(layer_norm, values, gain_vec, shift_vec)
    return pull_back(gradient)


OVER = 4 * KVH - 4


def image_layout(positions, counts):
    big_tok = BIG_SIDE * BIG_SIDE
    small_tok = SMALL_SIDE * SMALL_SIDE
    big_end = counts[0] * big_tok
    small_end = big_end + counts[1] * small_tok
    is_big = positions < big_end
    is_small = jnp.logical_and(positions >= big_end, positions < small_end)
    half_side = jnp.where(is_big, BIG_SIDE // 2, SMALL_SIDE // 2)
    begin_at = jnp.where(
        is_big,
        positions // big_tok * big_tok,
        jnp.where(is_small, big_end + (positions - big_end) // small_tok * small_tok, small_end),
    )
    tile_idx = (positions - begin_at) // 4
    return (begin_at, half_side, tile_idx // half_side, tile_idx % half_side, positions < small_end)


def shift_stacks(half_side, tile_y, tile_x, is_real):
    tiles = half_side.shape[0]
    step_y = np.array([[0, 1 - 2 * (sub // 2), 1 - 2 * (sub // 2)] for sub in range(4)], np.int32)[:, :, None]
    step_x = np.array([[1 - 2 * (sub % 2), 0, 1 - 2 * (sub % 2)] for sub in range(4)], np.int32)[:, :, None]
    at_y = tile_y + step_y
    at_x = tile_x + step_x
    inside = is_real & (at_y >= 0) & (at_y < half_side) & (at_x >= 0) & (at_x < half_side)
    source = jnp.arange(tiles, dtype=jnp.int32) + step_y * half_side + step_x
    source = jnp.where(inside, source, -1)
    cut = row_cut(tiles)
    columns = jnp.arange(SPAN, dtype=jnp.int32)
    upper = (source[:, :, :cut, None] == columns).astype(jnp.bfloat16)
    lower = (source[:, :, cut:, None] == columns + (tiles - SPAN)).astype(jnp.bfloat16)
    return (upper.reshape(4, 3 * cut, SPAN), lower.reshape(4, 3 * (tiles - cut), SPAN))


def tap_source(sub, tap):
    y_at = sub // 2 + tap // 3 - 1
    x_at = sub % 2 + tap % 3 - 1
    return (y_at % 2 * 2 + x_at % 2, y_at // 2, x_at // 2)


SQRT_HALF = 0.7071067811865476
INV_SQRT_TWO_PI = 0.3989422804014327
TAPS_OF = [[tap_source(sub, tap) for tap in range(9)] for sub in range(4)]
VMEM_LIMIT = 56 * 1024 * 1024
SPAN = 256
ROWS = 16
LANES = 128


def row_cut(tiles):
    return (tiles // 2 + 15) // 16 * 16


def move_planes(planes_ref, upper_ref, lower_ref, moved_ref):
    tiles = planes_ref.shape[0] // 4
    cut = row_cut(tiles)
    for sub in range(4):
        base = sub * tiles
        part = product(upper_ref[sub], planes_ref[base : base + SPAN, :])
        for key in range(3):
            moved_ref[sub, key, :cut, :] = part[key * cut : (key + 1) * cut]
        part = product(lower_ref[sub], planes_ref[base + tiles - SPAN : base + tiles, :])
        for key in range(3):
            moved_ref[sub, key, cut:, :] = part[key * (tiles - cut) : (key + 1) * (tiles - cut)]


def chunk_sources(planes_ref, moved_ref, row, lanes):
    tiles = planes_ref.shape[0] // 4
    found = {}
    for sub in range(4):
        found[sub, 0, 0] = planes_ref[pl.ds(pl.multiple_of(sub * tiles + row, ROWS), ROWS), lanes].astype(jnp.float32)
        step_y = 1 - 2 * (sub // 2)
        step_x = 1 - 2 * (sub % 2)
        for key, step in enumerate(((0, step_x), (step_y, 0), (step_y, step_x))):
            found[(sub,) + step] = moved_ref[sub, key, pl.ds(row, ROWS), lanes]
    return found


def norm_rows(values, gain, shift):
    center = values - jnp.mean(values, -1, keepdims=True)
    inverse = lax.rsqrt(jnp.mean(center * center, -1, keepdims=True) + EPS_NORM)
    unit = center * inverse
    return (unit, inverse, unit * gain + shift)


def norm_rows_back(unit, inverse, gain, grad):
    scaled = grad * gain
    return inverse * (
        scaled - jnp.mean(scaled, -1, keepdims=True) - unit * jnp.mean(scaled * unit, -1, keepdims=True)
    )


def mlp_forward_kernel(
    middle_ref, gains_ref, up_ref, down_ref, kern_ref, upper_ref, lower_ref, real_ref,
    out_ref, hidden_ref, active_ref, slope_ref, turned_ref,
    normed_ref, moved_ref, planes_ref,
):
    rows = middle_ref.shape[0]
    block = hidden_ref.shape[1]
    tiles = rows // 4

    @pl.when(pl.program_id(0) == 0)
    def _():
        normed = norm_rows(middle_ref[...], gains_ref[0:1, :], gains_ref[1:2, :])[2]
        normed_ref[...] = normed.astype(jnp.bfloat16)
        out_ref[...] = middle_ref[...]
        spread_rows(up_ref[0], planes_ref)
        for quarter in range(FF // C):
            for at, lane, width in lane_parts(C):
                part = planes_ref[at, pl.ds(quarter, C, stride=FF // C), :][:, :width]
                begin = quarter * C + lane
                turned_ref[:, begin : begin + width] = part.astype(jnp.bfloat16)

    for sub in range(4):
        columns = pl.ds(pl.multiple_of(pl.program_id(0) * block, block), block)
        part = product(normed_ref[sub * tiles : (sub + 1) * tiles, :], turned_ref[:, columns])
        hidden_ref[sub * tiles : (sub + 1) * tiles, :] = part.astype(jnp.bfloat16)
    move_planes(hidden_ref, upper_ref, lower_ref, moved_ref)

    for lane in range(0, hidden_ref.shape[1], LANES):
        lanes = slice(lane, lane + LANES)
        kern = [kern_ref[0, tap : tap + 1, lanes] for tap in range(9)]

        @pl.loop(0, tiles // ROWS, unroll=tiles // ROWS)
        def _(at):
            row = pl.multiple_of(at * ROWS, ROWS)
            found = chunk_sources(hidden_ref, moved_ref, row, lanes)
            real = real_ref[pl.ds(row, ROWS), :] > 0.0
            for sub in range(4):
                center = found[sub, 0, 0] * kern[4]
                total = center
                for tap in range(9):
                    if tap != 4:
                        total = total + found[TAPS_OF[sub][tap]] * kern[tap]
                mixed = jnp.where(real, total, center)
                half = 0.5 + 0.5 * lax.erf(mixed * SQRT_HALF)
                bell = jnp.exp(-0.5 * mixed * mixed) * INV_SQRT_TWO_PI
                span = pl.ds(pl.multiple_of(sub * tiles + row, ROWS), ROWS)
                active_ref[span, lanes] = (mixed * half).astype(jnp.bfloat16)
                slope_ref[span, lanes] = (half + mixed * bell).astype(jnp.bfloat16)

    for sub in range(4):
        span = slice(sub * tiles, (sub + 1) * tiles)
        out_ref[span, :] += product(active_ref[span, :], down_ref[0])


def lane_parts(width):
    return [(at, lane, min(LANES, width - lane)) for at, lane in enumerate(range(0, width, LANES))]


def spread_rows(source, planes_ref):
    for at, lane, width in lane_parts(source.shape[1]):
        planes_ref[at, :, :width] = source[:, lane : lane + width].astype(jnp.float32)


class Plan:
    def __init__(self, value, out, scratch, make, space=None):
        self.value, self.out, self.scratch, self.make = value, out, scratch, make
        self.in_spec = whole(value.shape)
        self.out_spec = pl.BlockSpec(memory_space=space) if space is not None else whole(out.shape)


def plan_sum(value, begin, end):
    make = functools.partial(SumRide, begin=begin, end=end)
    return Plan(value, jax.ShapeDtypeStruct(value.shape, value.dtype), sum_scratch(value.shape), make)


def plan_units(value, begin, end):
    if begin == 0:
        value = unit_blocks(value)
    total, (chunk, width) = value.shape[0], value.shape[-2:]
    inside = unit_layout(unit_order(0))[end] if end < len(bit_order()) else ()
    out = jax.ShapeDtypeStruct((total,) + inside + (chunk, width), value.dtype)

    def make(ride_in, ride_out, scratch):
        sources = [(ride_in, at) for at in range(total)]
        return UnitRide(sources, ride_out, scratch, begin, end)

    return Plan(value, out, unit_scratch(total, chunk, width, begin, end), make)


class Rides:
    def __init__(self, rides):
        self.rides = rides
        self.phases = max(ride.phases for ride in rides)
        names = [name for name in bit_order() if any(name in ride.names for ride in rides)]
        self.peers = [UnitRide.partner(rides[0], name) for name in names]

    def signal(self):
        signal_all(self.peers)

    def advance(self, phase):
        if phase == 0:
            pl.semaphore_wait(pltpu.get_barrier_semaphore(), len(self.peers))
        for ride in self.rides:
            if phase <= ride.phases:
                ride.advance(phase)


def rides_of(plans, ins, outs, scratch):
    rides = []
    for plan, ride_in, ride_out in zip(plans, ins, outs):
        count = len(plan.scratch)
        rides.append(plan.make(ride_in, ride_out, scratch[:count]))
        scratch = scratch[count:]
    return Rides(rides)


def ridden(kernel, inputs, outputs, scratch, steps, plans):
    def run(*refs):
        own_in, refs = refs[:inputs], refs[inputs:]
        ride_in, refs = refs[: len(plans)], refs[len(plans) :]
        own_out, refs = refs[:outputs], refs[outputs:]
        ride_out, rest = refs[: len(plans)], refs[len(plans) :]
        rides = rides_of(plans, ride_in, ride_out, rest[scratch:])
        places = [0] + list(range(1, steps - 1, 2))
        for phase, step in enumerate(places):
            if phase == 0:

                @pl.when(pl.program_id(0) == step)
                def _():
                    rides.signal()
                    rides.advance(0)
            elif phase <= rides.phases:
                pl.when(pl.program_id(0) == step)(functools.partial(rides.advance, phase))
        kernel(*own_in, *own_out, *rest[:scratch])

        @pl.when(pl.program_id(0) == steps - 1)
        def _():
            for phase in range(len(places), rides.phases + 1):
                rides.advance(phase)

    return run


def whole(shape):
    return pl.BlockSpec(shape, lambda j: (0,) * len(shape))


def unit_spec(at):
    return pl.BlockSpec((1, FF, C), lambda j: (at, 0, 0))


def mlp_forward(middle, gains, units, at, kernel, layer_at, stacks, real_rows):
    rows = middle.shape[0]
    block = 256
    by_lane = pl.BlockSpec((rows, block), lambda j: (0, j))
    low = jax.ShapeDtypeStruct((rows, FF), jnp.bfloat16)
    return pl.pallas_call(
        mlp_forward_kernel,
        grid=(FF // block,),
        out_shape=(
            jax.ShapeDtypeStruct((rows, C), jnp.float32),
            low,
            low,
            low,
            jax.ShapeDtypeStruct((C, FF), jnp.bfloat16),
        ),
        in_specs=[
            whole((rows, C)),
            whole((2, C)),
            unit_spec(at),
            pl.BlockSpec((1, block, C), lambda j: (at + 1, j, 0)),
            pl.BlockSpec((1, 9, block), lambda j: (layer_at, 0, j)),
            whole(stacks[0].shape),
            whole(stacks[1].shape),
            whole(real_rows.shape),
        ],
        out_specs=(whole((rows, C)), by_lane, by_lane, by_lane, whole((C, FF))),
        scratch_shapes=[
            pltpu.VMEM((rows, C), jnp.bfloat16),
            pltpu.VMEM((4, 3, rows // 4, block), jnp.float32),
            pltpu.VMEM((3, FF, LANES), jnp.float32),
        ],
        compiler_params=pltpu.CompilerParams(vmem_limit_bytes=VMEM_LIMIT),
        cost_estimate=pl.CostEstimate(flops=14 * 10**9, bytes_accessed=18 * 10**6, transcendentals=4 * 10**6),
        name="mlp_forward",
    )(middle, gains, units, units, kernel, stacks[0], stacks[1], real_rows)


def mlp_backward_kernel(
    grad_ref, middle_ref, gains_ref, up_ref, down_ref, kern_ref, upper_ref, lower_ref, real_ref,
    hidden_ref, active_ref, slope_ref,
    out_ref, dunits_ref, dkern_ref, dgain_ref,
    low_ref, low_t_ref, normed_t_ref, mixed_ref, dhid_ref, moved_ref, back_ref, wide_ref, planes_ref,
):
    rows = grad_ref.shape[0]
    tiles = rows // 4
    block = hidden_ref.shape[1]

    @pl.when(pl.program_id(0) == 0)
    def _():
        for sub in range(4):
            span = slice(sub * tiles, (sub + 1) * tiles)
            low_ref[span, :] = grad_ref[span, :].astype(jnp.bfloat16)
        normed = norm_rows(middle_ref[...], gains_ref[0:1, :], gains_ref[1:2, :])[2]
        normed_t_ref[...] = normed.T.astype(jnp.bfloat16)
        low_t_ref[...] = grad_ref[...].T.astype(jnp.bfloat16)
        back_ref[...] = jnp.zeros_like(back_ref)

    for sub in range(4):
        span = slice(sub * tiles, (sub + 1) * tiles)
        part = back_product(low_ref[span, :], down_ref[0]).astype(jnp.bfloat16).astype(jnp.float32)
        mixed_ref[span, :] = (part * slope_ref[span, :].astype(jnp.float32)).astype(jnp.bfloat16)
    down_rows = pl.ds(pl.multiple_of(pl.program_id(0) * block, block), block)
    dunits_ref[1, down_rows, :] = product(low_t_ref[...], active_ref[...]).T.astype(jnp.bfloat16)
    move_planes(mixed_ref, upper_ref, lower_ref, moved_ref)

    for lane in range(0, block, LANES):
        lanes = slice(lane, lane + LANES)
        kern = [kern_ref[0, tap : tap + 1, lanes] for tap in range(9)]

        def step(at, sums):
            row = pl.multiple_of(at * ROWS, ROWS)
            found = chunk_sources(mixed_ref, moved_ref, row, lanes)
            real = real_ref[pl.ds(row, ROWS), :] > 0.0
            sums = list(sums)
            for sub in range(4):
                span = pl.ds(pl.multiple_of(sub * tiles + row, ROWS), ROWS)
                hidden = hidden_ref[span, lanes].astype(jnp.float32)
                center = found[sub, 0, 0] * kern[4]
                total = center
                for tap in range(9):
                    term = found[TAPS_OF[sub][tap]]
                    if tap != 4:
                        total = total + term * kern[8 - tap]
                    piece = hidden * term
                    sums[tap] = sums[tap] + piece[:8] + piece[8:]
                dhid_ref[span, lanes] = jnp.where(real, total, center).astype(jnp.bfloat16)
            return tuple(sums)

        sums = lax.fori_loop(0, tiles // ROWS, step, (jnp.zeros((8, LANES), jnp.float32),) * 9, unroll=True)
        for tap in range(9):
            dkern_ref[8 - tap : 9 - tap, lanes] = jnp.sum(sums[tap], 0, keepdims=True)

    columns = pl.ds(pl.multiple_of(pl.program_id(0) * block, block), block)
    wide_ref[:, columns] = product(normed_t_ref[...], dhid_ref[...])
    for sub in range(4):
        span = slice(sub * tiles, (sub + 1) * tiles)
        back_ref[span, :] += back_product(dhid_ref[span, :], up_ref[...])

    @pl.when(pl.program_id(0) == pl.num_programs(0) - 1)
    def _():
        grad = back_ref[...]
        unit, inverse, _ = norm_rows(middle_ref[...], gains_ref[0:1, :], gains_ref[1:2, :])
        out_ref[...] = grad_ref[...] + norm_rows_back(unit, inverse, gains_ref[0:1, :], grad)
        dgain_ref[0:1, :] = jnp.sum(grad * unit, 0, keepdims=True)
        dgain_ref[1:2, :] = jnp.sum(grad, 0, keepdims=True)
        for quarter in range(FF // C):
            for at, lane, width in lane_parts(C):
                begin = quarter * C + lane
                part = wide_ref[:, begin : begin + width]
                if width < LANES:
                    part = jnp.concatenate([part, jnp.zeros((C, LANES - width), jnp.float32)], 1)
                planes_ref[at, pl.ds(quarter, C, stride=FF // C), :] = part
        for at, lane, width in lane_parts(C):
            dunits_ref[0, :, lane : lane + width] = planes_ref[at, :, :width].astype(jnp.bfloat16)


def mlp_backward(grad, middle, gains, w_up, units, at, kernel, layer_at, stacks, real_rows, kept, plans, meeting):
    rows = middle.shape[0]
    block = 256
    by_lane = pl.BlockSpec((rows, block), lambda j: (0, j))
    up_spec = pl.BlockSpec((C, block), lambda j: (0, j))
    tap_spec = pl.BlockSpec((9, block), lambda j: (0, j))
    return pl.pallas_call(
        ridden(mlp_backward_kernel, 12, 4, 9, FF // block, plans),
        grid=(FF // block,),
        out_shape=(
            jax.ShapeDtypeStruct((rows, C), jnp.float32),
            jax.ShapeDtypeStruct((2, FF, C), jnp.bfloat16),
            jax.ShapeDtypeStruct((9, FF), jnp.float32),
            jax.ShapeDtypeStruct((2, C), jnp.float32),
            *[plan.out for plan in plans],
        ),
        in_specs=[
            whole((rows, C)),
            whole((rows, C)),
            whole((2, C)),
            up_spec,
            pl.BlockSpec((1, block, C), lambda j: (at + 1, j, 0)),
            pl.BlockSpec((1, 9, block), lambda j: (layer_at, 0, j)),
            whole(stacks[0].shape),
            whole(stacks[1].shape),
            whole(real_rows.shape),
            by_lane,
            by_lane,
            by_lane,
        ]
        + [plan.in_spec for plan in plans],
        out_specs=(whole((rows, C)), whole((2, FF, C)), tap_spec, whole((2, C)))
        + tuple(plan.out_spec for plan in plans),
        scratch_shapes=[
            pltpu.VMEM((rows, C), jnp.bfloat16),
            pltpu.VMEM((C, rows), jnp.bfloat16),
            pltpu.VMEM((C, rows), jnp.bfloat16),
            pltpu.VMEM((rows, block), jnp.bfloat16),
            pltpu.VMEM((rows, block), jnp.bfloat16),
            pltpu.VMEM((4, 3, rows // 4, block), jnp.float32),
            pltpu.VMEM((rows, C), jnp.float32),
            pltpu.VMEM((C, FF), jnp.float32),
            pltpu.VMEM((3, FF, LANES), jnp.float32),
        ]
        + sum([plan.scratch for plan in plans], []),
        compiler_params=pltpu.CompilerParams(
            collective_id=meeting, has_side_effects=True, vmem_limit_bytes=VMEM_LIMIT
        ),
        cost_estimate=pl.CostEstimate(flops=18 * 10**9, bytes_accessed=18 * 10**6, transcendentals=0),
        name="mlp_backward",
    )(grad, middle, gains, w_up, units, kernel, stacks[0], stacks[1], real_rows, *kept, *[plan.value for plan in plans])


WIDE = 384
BLOCK_TILES = 32
KEY_SPAN = 128


def block_places(tiles):
    places = []
    for index in range(-(-tiles // BLOCK_TILES)):
        start = min(index * BLOCK_TILES, tiles - BLOCK_TILES)
        places.append((start, min(max(start - 48, 0), tiles - KEY_SPAN)))
    return places


def block_bias(tiles, image_at):
    starts, lows = np.array(block_places(tiles), np.int32).T[:, :, None]
    columns = starts + np.tile(np.arange(BLOCK_TILES, dtype=np.int32), 4)
    rows = lows + np.arange(KEY_SPAN, dtype=np.int32)
    same = image_at(jnp.asarray(rows))[:, :, None] == image_at(jnp.asarray(columns))[:, None, :]
    return jnp.where(same, 0.0, NEG_FILL)


def place_of(index, tiles):
    start = jnp.minimum(index * BLOCK_TILES, tiles - BLOCK_TILES)
    low = jnp.clip(start - 48, 0, tiles - KEY_SPAN)
    return (pl.multiple_of(start, ROWS), pl.multiple_of(low, ROWS))


def four_planes(ref, start, lanes):
    tiles = ref.shape[0] // 4
    return jnp.concatenate(
        [ref[pl.ds(pl.multiple_of(sub * tiles + start, ROWS), BLOCK_TILES), lanes] for sub in range(4)], 0
    )


def put_planes(ref, start, lanes, values):
    tiles = ref.shape[0] // 4
    for sub in range(4):
        ref[pl.ds(pl.multiple_of(sub * tiles + start, ROWS), BLOCK_TILES), lanes] = values[
            sub * BLOCK_TILES : (sub + 1) * BLOCK_TILES
        ]


def head_pair(values, group):
    if group == 2:
        return values
    first = lax.broadcasted_iota(jnp.int32, values.shape, 1) < HD
    zero = jnp.zeros_like(values)
    return jnp.concatenate([jnp.where(first, values, zero), jnp.where(first, zero, values)], 0)


def softmax_columns(raw, bias):
    parts = []
    for half in range(raw.shape[0] // KEY_SPAN):
        scores = raw[half * KEY_SPAN : (half + 1) * KEY_SPAN] * HD ** (-0.5) + bias
        weights = jnp.exp(scores - jnp.max(scores, 0, keepdims=True))
        parts.append(weights * (1.0 / jnp.sum(weights, 0, keepdims=True)))
    return parts


def norm_store(source_ref, gains_ref, at, target_ref):
    normed = norm_rows(source_ref[...], gains_ref[at : at + 1, :], gains_ref[at + 1 : at + 2, :])[2]
    target_ref[...] = normed.astype(jnp.bfloat16)


def part_keyval(unit_ref, planes_ref, kv_ref):
    spread_rows(unit_ref[0, 2 * C :, :], planes_ref)
    for which in range(2):
        for at, lane, width in lane_parts(C):
            part = planes_ref[at, pl.ds(which, C, stride=2), :][:, :width]
            kv_ref[which, :, lane : lane + width] = part.astype(jnp.bfloat16)


def attention_forward_kernel(
    resid_ref, gains_ref, unit_ref, reduce_ref, bias_ref,
    middle_ref, normed_ref, query_ref, reduced_ref, key_ref, value_ref, attended_ref, kv_ref,
    planes_ref,
):
    part_keyval(unit_ref, planes_ref, kv_ref)
    rows = resid_ref.shape[0]
    tiles = rows // 4
    norm_store(resid_ref, gains_ref, 0, normed_ref)
    query_ref[:, C:] = jnp.zeros((rows, WIDE - C), jnp.bfloat16)
    reduced = jnp.zeros((tiles, C), jnp.float32)
    for sub in range(4):
        span = slice(sub * tiles, (sub + 1) * tiles)
        query_ref[span, :C] = product(normed_ref[span, :], unit_ref[0, :C, :]).astype(jnp.bfloat16)
        reduced = reduced + product(normed_ref[span, :], reduce_ref[0, sub * C : (sub + 1) * C, :])
    reduced_ref[...] = reduced
    normed_kv = norm_rows(reduced, gains_ref[2:3, :], gains_ref[3:4, :])[2].astype(jnp.bfloat16)
    for which, ref in enumerate((key_ref, value_ref)):
        ref[:, C:] = jnp.zeros((tiles, WIDE - C), jnp.bfloat16)
        ref[:, :C] = product(normed_kv, kv_ref[which]).astype(jnp.bfloat16)

    @pl.loop(0, bias_ref.shape[0], unroll=bias_ref.shape[0])
    def _(index):
        start, low = place_of(index, tiles)
        bias = bias_ref[index]
        for group in range(3):
            lanes = slice(group * LANES, (group + 1) * LANES)
            query = four_planes(query_ref, start, lanes)
            keys = head_pair(key_ref[pl.ds(low, KEY_SPAN), lanes], group)
            values = head_pair(value_ref[pl.ds(low, KEY_SPAN), lanes], group)
            probs = softmax_columns(back_product(keys, query), bias)
            probs = jnp.concatenate(probs, 0).T.astype(jnp.bfloat16)
            put_planes(attended_ref, start, lanes, product(probs, values).astype(jnp.bfloat16))

    for sub in range(4):
        span = slice(sub * tiles, (sub + 1) * tiles)
        middle_ref[span, :] = resid_ref[span, :] + product(attended_ref[span, :C], unit_ref[0, C : 2 * C, :])


def attention_forward(resid, gains, units, at, reduces, reduce_at, bias):
    rows = resid.shape[0]
    tiles = rows // 4
    low = jnp.bfloat16
    shapes = (
        jax.ShapeDtypeStruct((rows, C), jnp.float32),
        jax.ShapeDtypeStruct((rows, C), low),
        jax.ShapeDtypeStruct((rows, WIDE), low),
        jax.ShapeDtypeStruct((tiles, C), jnp.float32),
        jax.ShapeDtypeStruct((tiles, WIDE), low),
        jax.ShapeDtypeStruct((tiles, WIDE), low),
        jax.ShapeDtypeStruct((rows, WIDE), low),
        jax.ShapeDtypeStruct((2, C, C), low),
    )
    return pl.pallas_call(
        attention_forward_kernel,
        grid=(1,),
        out_shape=shapes,
        in_specs=[whole((rows, C)), whole((4, C)), unit_spec(at), unit_spec(reduce_at), whole(bias.shape)],
        out_specs=tuple(whole(shape.shape) for shape in shapes),
        scratch_shapes=[pltpu.VMEM((3, 2 * C, LANES), jnp.float32)],
        compiler_params=pltpu.CompilerParams(vmem_limit_bytes=VMEM_LIMIT),
        cost_estimate=pl.CostEstimate(flops=6 * 10**9, bytes_accessed=14 * 10**6, transcendentals=10**6),
        name="attention_forward",
    )(resid, gains, units, reduces, bias)


def embed_forward_kernel(
    patches_ref, halo_ref, unit_ref, gains_ref, pre_ref, resid_ref, kern_ref, planes_ref, taps_ref
):
    rows = pre_ref.shape[0]
    tiles = rows // 4
    used = FF * 9 * BLOCKS // C
    for ref, base in ((patches_ref, 0), (halo_ref, patches_ref.shape[0])):
        step = 64

        @pl.loop(0, ref.shape[0] // step, unroll=4)
        def _(at):
            span = pl.ds(pl.multiple_of(at * step, step), step)
            into = pl.ds(pl.multiple_of(base + at * step, step), step)
            part = product(ref[span, :], unit_ref[0, :PIN, :])
            for place, lane, width in lane_parts(C):
                planes_ref[place, into, :width] = part[:, lane : lane + width]

    for sub in range(4):
        for place, lane, width in lane_parts(C):
            pre_ref[sub * tiles : (sub + 1) * tiles, lane : lane + width] = planes_ref[
                place, pl.ds(sub, tiles, stride=4), :
            ][:, :width]
    taps = unit_ref[0, PIN : PIN + taps_ref.shape[1], :]
    spread_rows(taps, taps_ref)
    for layer_at in range(BLOCKS):
        for quarter in range(FF // C):
            for place, lane, width in lane_parts(C):
                begin = quarter * C + lane
                kern_ref[layer_at, :, begin : begin + width] = taps_ref[
                    place, pl.ds(layer_at * (used // BLOCKS) + quarter, 9, stride=FF // C), :
                ][:, :width]

    resid_ref[...] = norm_rows(pre_ref[...], gains_ref[0:1, :], gains_ref[1:2, :])[2]


def embed_forward(patches, halo, units, gains):
    rows = patches.shape[0] + halo.shape[0]
    wide = jax.ShapeDtypeStruct((rows, C), jnp.float32)
    taps = jax.ShapeDtypeStruct((BLOCKS, 9, FF), jnp.float32)
    return pl.pallas_call(
        embed_forward_kernel,
        grid=(1,),
        out_shape=(wide, wide, taps),
        in_specs=[whole(patches.shape), whole(halo.shape), unit_spec(0), whole((2, C))],
        out_specs=(whole(wide.shape), whole(wide.shape), whole(taps.shape)),
        scratch_shapes=[
            pltpu.VMEM((3, rows, LANES), jnp.float32),
            pltpu.VMEM((3, FF - PIN, LANES), jnp.float32),
        ],
        compiler_params=pltpu.CompilerParams(vmem_limit_bytes=VMEM_LIMIT),
        cost_estimate=pl.CostEstimate(flops=10**9, bytes_accessed=8 * 10**6, transcendentals=0),
        name="embed_forward",
    )(patches, halo, units, gains)


def embed_backward_kernel(
    grad_ref, pre_ref, gains_ref, patches_ref, halo_ref, *refs
):
    taps_refs = refs[:BLOCKS]
    unit_ref, dgain_ref, planes_ref, turned_ref, taps_ref = refs[BLOCKS:]
    rows = pre_ref.shape[0]
    tiles = rows // 4
    half = tiles // 2
    used = FF * 9 * BLOCKS // C
    sums = [jnp.zeros((1, C), jnp.float32)] * 2
    for sub in range(4):
        for part_at in range(2):
            span = slice(sub * tiles + part_at * half, sub * tiles + (part_at + 1) * half)
            unit, inverse, _ = norm_rows(pre_ref[span, :], gains_ref[0:1, :], gains_ref[1:2, :])
            grad = grad_ref[span, :]
            back = norm_rows_back(unit, inverse, gains_ref[0:1, :], grad)
            sums[0] = sums[0] + jnp.sum(grad * unit, 0, keepdims=True)
            sums[1] = sums[1] + jnp.sum(grad, 0, keepdims=True)
            for place, lane, width in lane_parts(C):
                value = back[:, lane : lane + width]
                if width < LANES:
                    value = jnp.concatenate([value, jnp.zeros((half, LANES - width), jnp.float32)], 1)
                planes_ref[place, pl.ds(4 * part_at * half + sub, half, stride=4), :] = value
    dgain_ref[0:1, :] = sums[0]
    dgain_ref[1:2, :] = sums[1]
    for place, lane, width in lane_parts(C):
        turned_ref[lane : lane + width, :] = planes_ref[place].T[:width, :].astype(jnp.bfloat16)
    split = patches_ref.shape[0]
    grads = product(turned_ref[:, :split], patches_ref[...]) + product(turned_ref[:, split:], halo_ref[...])
    unit_ref[0, :PIN, :] = grads.T.astype(jnp.bfloat16)
    taps_ref[...] = jnp.zeros_like(taps_ref)
    for layer_at, ref in enumerate(taps_refs):
        for quarter in range(FF // C):
            for place, lane, width in lane_parts(C):
                begin = quarter * C + lane
                value = ref[:, begin : begin + width]
                if width < LANES:
                    value = jnp.concatenate([value, jnp.zeros((9, LANES - width), jnp.float32)], 1)
                taps_ref[place, pl.ds(layer_at * (used // BLOCKS) + quarter, 9, stride=FF // C), :] = value
    for place, lane, width in lane_parts(C):
        unit_ref[0, PIN:, lane : lane + width] = taps_ref[place, :, :width].astype(jnp.bfloat16)


def embed_backward(grad, pre, gains, patches, halo, taps):
    rows = pre.shape[0]
    shapes = (jax.ShapeDtypeStruct((1, FF, C), jnp.bfloat16), jax.ShapeDtypeStruct((2, C), jnp.float32))
    operands = (grad, pre, gains, patches, halo, *taps)
    return pl.pallas_call(
        embed_backward_kernel,
        grid=(1,),
        out_shape=shapes,
        in_specs=[whole(part.shape) for part in operands],
        out_specs=tuple(whole(shape.shape) for shape in shapes),
        scratch_shapes=[
            pltpu.VMEM((3, rows, LANES), jnp.float32),
            pltpu.VMEM((C, rows), jnp.bfloat16),
            pltpu.VMEM((3, FF - PIN, LANES), jnp.float32),
        ],
        compiler_params=pltpu.CompilerParams(vmem_limit_bytes=VMEM_LIMIT),
        cost_estimate=pl.CostEstimate(flops=10**9, bytes_accessed=8 * 10**6, transcendentals=0),
        name="embed_backward",
    )(*operands)


def head_kernel(
    resid_ref, gains_ref, weight_ref, label_ref, keep_ref, total_ref,
    grad_ref, dhead_ref, dgain_ref, loss_ref,
    final_ref, turned_ref,
):
    rows = resid_ref.shape[0]
    tiles = rows // 4
    classes = weight_ref.shape[1]
    low = weight_ref[...].astype(jnp.bfloat16)
    share = 1.0 / total_ref[0:1, 0:1]
    sums = [jnp.zeros((1, C), jnp.float32)] * 2
    loss = jnp.zeros((1, 1), jnp.float32)
    for sub in range(4):
        span = slice(sub * tiles, (sub + 1) * tiles)
        unit, inverse, final = norm_rows(resid_ref[span, :], gains_ref[0:1, :], gains_ref[1:2, :])
        final = final.astype(jnp.bfloat16)
        final_ref[span, :] = final
        logits = product(final, low)
        peak = jnp.max(logits, -1, keepdims=True)
        log_norm = peak + jnp.log(jnp.sum(jnp.exp(logits - peak), -1, keepdims=True))
        keep = keep_ref[span, :]
        hit = lax.broadcasted_iota(jnp.int32, (tiles, classes), 1) == label_ref[span, :]
        picked = jnp.sum(jnp.where(hit, logits, 0.0), -1, keepdims=True)
        loss = loss + jnp.sum((log_norm - picked) * keep, 0, keepdims=True)
        dlogits = (jnp.exp(logits - log_norm) - jnp.where(hit, 1.0, 0.0)) * (keep * share)
        turned_ref[:, span] = dlogits.T.astype(jnp.bfloat16)
        grad = back_product(dlogits.astype(jnp.bfloat16), low)
        grad_ref[span, :] = norm_rows_back(unit, inverse, gains_ref[0:1, :], grad)
        sums[0] = sums[0] + jnp.sum(grad * unit, 0, keepdims=True)
        sums[1] = sums[1] + jnp.sum(grad, 0, keepdims=True)
    dhead_ref[:classes, :] = product(turned_ref[...], final_ref[...])
    dhead_ref[classes:, :] = jnp.zeros((dhead_ref.shape[0] - classes, C), jnp.float32)
    dgain_ref[0:1, :] = sums[0]
    dgain_ref[1:2, :] = sums[1]
    loss_ref[...] = jnp.broadcast_to(loss, (1, C))


def head_step(resid, gains, weight, labels, keep, total):
    rows = resid.shape[0]
    classes = weight.shape[1]
    wide = jnp.float32
    shapes = (
        jax.ShapeDtypeStruct((rows, C), wide),
        jax.ShapeDtypeStruct((-(-classes // 8) * 8, C), wide),
        jax.ShapeDtypeStruct((2, C), wide),
        jax.ShapeDtypeStruct((1, C), wide),
    )
    operands = (resid, gains, weight, labels, keep, total)
    return pl.pallas_call(
        head_kernel,
        grid=(1,),
        out_shape=shapes,
        in_specs=[whole(part.shape) for part in operands],
        out_specs=tuple(whole(shape.shape) for shape in shapes),
        scratch_shapes=[
            pltpu.VMEM((rows, C), jnp.bfloat16),
            pltpu.VMEM((classes, rows), jnp.bfloat16),
        ],
        compiler_params=pltpu.CompilerParams(vmem_limit_bytes=VMEM_LIMIT),
        cost_estimate=pl.CostEstimate(flops=10**9, bytes_accessed=5 * 10**6, transcendentals=10**6),
        name="head_step",
    )(*operands)


def attention_backward_kernel(
    advance,
    grad_ref, resid_ref, gains_ref, unit_ref, reduce_ref, bias_ref,
    normed_ref, query_ref, reduced_ref, key_ref, value_ref, attended_ref, kv_ref,
    out_ref, dunits_ref, dgain_ref,
    turned_ref, datt_ref, dquery_ref, dkey_ref, dvalue_ref, first_ref, planes_ref,
):
    rows = resid_ref.shape[0]
    tiles = rows // 4
    low_type = jnp.bfloat16
    advance(0)
    datt_ref[:, C:] = jnp.zeros((rows, WIDE - C), low_type)
    turned_ref[...] = grad_ref[...].T.astype(low_type)
    dunits_ref[0, C : 2 * C, :] = product(turned_ref[...], attended_ref[:, :C]).T.astype(low_type)
    for sub in range(4):
        span = slice(sub * tiles, (sub + 1) * tiles)
        datt_ref[span, :C] = back_product(grad_ref[span, :].astype(low_type), unit_ref[0, C : 2 * C, :]).astype(low_type)
    dkey_ref[...] = jnp.zeros_like(dkey_ref)
    dvalue_ref[...] = jnp.zeros_like(dvalue_ref)
    blocks = bias_ref.shape[0]

    def one_block(step):
        index = blocks - 1 - step
        start, low = place_of(index, tiles)
        bias = bias_ref[index]
        tile_at = lax.rem(lax.broadcasted_iota(jnp.int32, (4 * BLOCK_TILES, LANES), 0), BLOCK_TILES)
        fresh = tile_at >= index * BLOCK_TILES - start
        span = pl.ds(low, KEY_SPAN)
        for group in range(3):
            lanes = slice(group * LANES, (group + 1) * LANES)
            query = four_planes(query_ref, start, lanes)
            datt = four_planes(datt_ref, start, lanes)
            datt = jnp.where(fresh, datt, jnp.zeros_like(datt))
            keys = head_pair(key_ref[span, lanes], group)
            values = head_pair(value_ref[span, lanes], group)
            probs = softmax_columns(back_product(keys, query), bias)
            dprobs = back_product(values, datt)
            dscores = []
            for half, prob in enumerate(probs):
                dprob = dprobs[half * KEY_SPAN : (half + 1) * KEY_SPAN]
                inner = jnp.sum(prob * dprob, 0, keepdims=True)
                dscores.append(prob * (dprob - inner) * HD ** (-0.5))
            dscores = jnp.concatenate(dscores, 0)
            probs = jnp.concatenate(probs, 0).astype(low_type)
            dquery = product(dscores.T.astype(low_type), keys)
            put_planes(dquery_ref, start, lanes, dquery.astype(low_type))
            dkeys = product(dscores.astype(low_type), query)
            dvalues = product(probs, datt)
            if group < 2:
                first = lax.broadcasted_iota(jnp.int32, (KEY_SPAN, LANES), 1) < HD
                dkeys = jnp.where(first, dkeys[:KEY_SPAN], dkeys[KEY_SPAN:])
                dvalues = jnp.where(first, dvalues[:KEY_SPAN], dvalues[KEY_SPAN:])
            dkey_ref[span, lanes] += dkeys
            dvalue_ref[span, lanes] += dvalues

    pl.loop(0, blocks // 2, unroll=blocks // 2)(one_block)
    advance(1)
    pl.loop(blocks // 2, blocks, unroll=blocks - blocks // 2)(one_block)
    unit, inverse, normed = norm_rows(reduced_ref[...], gains_ref[2:3, :], gains_ref[3:4, :])
    normed_t = normed.T.astype(low_type)
    dkeys = dkey_ref[:, :C].astype(low_type)
    dvalues = dvalue_ref[:, :C].astype(low_type)
    for which, grads in enumerate((dkeys, dvalues)):
        dweight = product(normed_t, grads)
        for at, lane, width in lane_parts(C):
            part = dweight[:, lane : lane + width]
            if width < LANES:
                part = jnp.concatenate([part, jnp.zeros((C, LANES - width), jnp.float32)], 1)
            planes_ref[at, pl.ds(which, C, stride=2), :] = part
    for at, lane, width in lane_parts(C):
        dunits_ref[0, 2 * C :, lane : lane + width] = planes_ref[at, :, :width].astype(low_type)
    dnormed = back_product(dkeys, kv_ref[0]) + back_product(dvalues, kv_ref[1])
    dgain_ref[2:3, :] = jnp.sum(dnormed * unit, 0, keepdims=True)
    dgain_ref[3:4, :] = jnp.sum(dnormed, 0, keepdims=True)
    dreduced = norm_rows_back(unit, inverse, gains_ref[2:3, :], dnormed).astype(low_type)
    advance(2)
    turned_ref[...] = normed_ref[...].T
    dunits_ref[0, :C, :] = product(turned_ref[...], dquery_ref[:, :C]).astype(low_type)
    for sub in range(4):
        span = slice(sub * tiles, (sub + 1) * tiles)
        part = slice(sub * C, (sub + 1) * C)
        dunits_ref[1, part, :] = outer_sum(normed_ref[span, :], dreduced).astype(low_type)
        first_ref[span, :] = back_product(
            dquery_ref[span, :C], unit_ref[0, :C, :]
        ) + back_product(dreduced, reduce_ref[0, part, :])

    grad = first_ref[...]
    unit, inverse, _ = norm_rows(resid_ref[...], gains_ref[0:1, :], gains_ref[1:2, :])
    out_ref[...] = grad_ref[...] + norm_rows_back(unit, inverse, gains_ref[0:1, :], grad)
    dgain_ref[0:1, :] = jnp.sum(grad * unit, 0, keepdims=True)
    dgain_ref[1:2, :] = jnp.sum(grad, 0, keepdims=True)


def attention_backward(grad, resid, gains, units, at, reduces, reduce_at, bias, kept, plans, meeting):
    rows = resid.shape[0]
    tiles = rows // 4
    low = jnp.bfloat16
    shapes = (
        jax.ShapeDtypeStruct((rows, C), jnp.float32),
        jax.ShapeDtypeStruct((2, FF, C), low),
        jax.ShapeDtypeStruct((4, C), jnp.float32),
    )
    count = len(plans)

    def run(*refs):
        own_in, ride_in = refs[:13], refs[13 : 13 + count]
        own_out, ride_out = refs[13 + count : 16 + count], refs[16 + count : 16 + 2 * count]
        rest = refs[16 + 2 * count :]
        rides = rides_of(plans, ride_in, ride_out, rest[7:])
        rides.signal()
        attention_backward_kernel(rides.advance, *own_in, *own_out, *rest[:7])
        for phase in range(3, rides.phases + 1):
            rides.advance(phase)

    return pl.pallas_call(
        run,
        grid=(1,),
        out_shape=shapes + tuple(plan.out for plan in plans),
        in_specs=[
            whole((rows, C)),
            whole((rows, C)),
            whole((4, C)),
            unit_spec(at),
            unit_spec(reduce_at),
            whole(bias.shape),
        ]
        + [whole(part.shape) for part in kept]
        + [plan.in_spec for plan in plans],
        out_specs=tuple(whole(shape.shape) for shape in shapes) + tuple(plan.out_spec for plan in plans),
        scratch_shapes=[
            pltpu.VMEM((C, rows), low),
            pltpu.VMEM((rows, WIDE), low),
            pltpu.VMEM((rows, WIDE), low),
            pltpu.VMEM((tiles, WIDE), jnp.float32),
            pltpu.VMEM((tiles, WIDE), jnp.float32),
            pltpu.VMEM((rows, C), jnp.float32),
            pltpu.VMEM((3, 2 * C, LANES), jnp.float32),
        ]
        + sum([plan.scratch for plan in plans], []),
        compiler_params=pltpu.CompilerParams(collective_id=meeting, has_side_effects=True, vmem_limit_bytes=VMEM_LIMIT),
        cost_estimate=pl.CostEstimate(flops=12 * 10**9, bytes_accessed=18 * 10**6, transcendentals=10**6),
        name="attention_backward",
    )(grad, resid, gains, units, reduces, bias, *kept, *[plan.value for plan in plans])


BOTH = ("grp", "tok")


def axis_bits(axis):
    count = lax.axis_size(axis)
    return [1 << place for place in reversed(range(count.bit_length() - 1))]


def bit_order():
    tok_bits = axis_bits("tok")
    return [("grp", bit) for bit in axis_bits("grp")] + [("tok", bit) for bit in tok_bits]


MESH = pl.DeviceIdType.MESH


def exchange_setup():
    grp, tok = lax.axis_index("grp"), lax.axis_index("tok")
    n_tok = lax.axis_size("tok")
    peers = [(lax.bitwise_xor(grp, bit), tok) for bit in axis_bits("grp")]
    peers += [(grp, lax.bitwise_xor(tok, step)) for step in range(1, n_tok)]
    return (grp, tok, n_tok, peers)


def signal_all(peers):
    barrier = pltpu.get_barrier_semaphore()
    for peer in peers:
        pl.semaphore_signal(barrier, inc=1, device_id=peer, device_id_type=MESH)


def greet(peers):
    signal_all(peers)
    pl.semaphore_wait(pltpu.get_barrier_semaphore(), len(peers))


def send(source, target, sems, at, peer):
    copy = pltpu.make_async_remote_copy(
        src_ref=source,
        dst_ref=target,
        send_sem=sems[0].at[at],
        recv_sem=sems[1].at[at],
        device_id=peer,
        device_id_type=MESH,
    )
    copy.start()
    return copy


def gather_view(ref, unit, place, done):
    index = [slice(None) if name in done else place(name) for name in bit_order()]
    return ref.at[tuple([unit] + index)]


class GatherRide:
    def __init__(self, full_ref, scratch):
        self.grp, self.tok = lax.axis_index("grp"), lax.axis_index("tok")
        self.phases = len(bit_order())
        self.names = bit_order()
        self.full_ref = full_ref
        self.sems = scratch[:2]

    def order(self, unit):
        grp_bits = [("grp", bit) for bit in axis_bits("grp")]
        flip = grp_bits[::-1] if unit % 2 else grp_bits
        return [("tok", bit) for bit in axis_bits("tok")[:-1]] + flip + [("tok", 1)]

    def place(self, name):
        return (self.grp if name[0] == "grp" else self.tok) // name[1] % 2

    def partner(self, name):
        axis, bit = name
        if axis == "grp":
            return (lax.bitwise_xor(self.grp, bit), self.tok)
        return (self.grp, lax.bitwise_xor(self.tok, bit))

    def copy(self, unit, phase):
        order = self.order(unit)
        held = gather_view(self.full_ref, unit, self.place, order[:phase])
        at = phase * self.full_ref.shape[0] + unit
        return pltpu.make_async_remote_copy(
            src_ref=held,
            dst_ref=held,
            send_sem=self.sems[0].at[at],
            recv_sem=self.sems[1].at[at],
            device_id=self.partner(order[phase]),
            device_id_type=MESH,
        )

    def put(self, unit, value):
        self.full_ref[(unit,) + tuple(self.place(name) for name in bit_order())] = value

    def advance(self, phase):
        for unit in range(self.full_ref.shape[0]):
            if phase:
                self.copy(unit, phase - 1).wait()
            if phase < self.phases:
                self.copy(unit, phase).start()


def gather_scratch(total):
    phases = len(bit_order())
    return [pltpu.SemaphoreType.DMA((phases * total,))] * 2


def slot_numbers(owner_ref, slot_rows):
    owners = [owner_ref[unit] for unit in range(owner_ref.shape[0])]
    slots = []
    for unit, owner in enumerate(owners):
        rank = jnp.int32(0)
        for earlier in owners[:unit]:
            rank = rank + (earlier == owner).astype(jnp.int32)
        slots.append(owner * slot_rows + rank)
    return slots


def start_kernel(
    owner_ref, piece_ref, count_ref, patch_ref, mark_ref,
    full_ref, later_ref, total_ref, patch_halo_ref, mark_halo_ref,
    recv_ref, near_s, near_r, halo_s, halo_r, *scratch,
):
    grp, tok, n_tok, peers = exchange_setup()
    slot_rows = piece_ref.shape[1]
    units, first = owner_ref.shape[0], full_ref.shape[0]
    slots = slot_numbers(owner_ref, slot_rows)
    gather = GatherRide(full_ref, scratch[:2])
    count = SumRide(count_ref, total_ref, scratch[2:])
    greet(peers)
    copies = []
    for step in range(1, n_tok):
        peer = lax.bitwise_xor(tok, step)
        landing = recv_ref.at[pl.ds(tok * slot_rows, slot_rows)]
        copies.append(send(piece_ref.at[peer], landing, (near_s, near_r), step, (grp, peer)))
    recv_ref[pl.ds(tok * slot_rows, slot_rows)] = piece_ref[tok]
    count.advance(0)
    for copy in copies:
        copy.wait()
    for unit in range(first):
        gather.put(unit, recv_ref[slots[unit]])
    gather.advance(0)
    before = (grp, lax.rem(tok + n_tok - 1, n_tok))
    mark_copy = send(mark_ref, mark_halo_ref, (halo_s, halo_r), 0, before)
    patch_copy = send(patch_ref.at[pl.ds(0, patch_halo_ref.shape[0])], patch_halo_ref, (halo_s, halo_r), 1, before)
    for unit in range(first, units):
        later_ref[unit - first] = recv_ref[slots[unit]]
    for phase in range(1, gather.phases + 1):
        count.advance(phase)
        gather.advance(phase)
    total_ref[...] = jnp.broadcast_to(
        jnp.sum(jnp.sum(total_ref[...], 0, keepdims=True), 1, keepdims=True), total_ref.shape
    )
    mark_copy.wait()
    patch_copy.wait()


def start_exchange(owners, pieces, count, patches, marks, first):
    n_tok, slot_rows, chunk, width = pieces.shape
    phases = len(bit_order())
    units = owners.shape[0]
    vmem = pl.BlockSpec(memory_space=pltpu.VMEM)
    full_shape = (first,) + (2,) * phases + (chunk, width)
    return pl.pallas_call(
        start_kernel,
        out_shape=(
            jax.ShapeDtypeStruct(full_shape, pieces.dtype),
            jax.ShapeDtypeStruct((units - first, chunk, width), pieces.dtype),
            jax.ShapeDtypeStruct(count.shape, count.dtype),
            jax.ShapeDtypeStruct((OVER, patches.shape[1]), patches.dtype),
            jax.ShapeDtypeStruct(marks.shape, marks.dtype),
        ),
        in_specs=[pl.BlockSpec(memory_space=pltpu.SMEM), vmem, vmem, pl.BlockSpec(memory_space=pl.ANY), vmem],
        out_specs=(vmem, vmem, vmem, pl.BlockSpec(memory_space=pl.ANY), vmem),
        scratch_shapes=[
            pltpu.VMEM((n_tok * slot_rows, chunk, width), pieces.dtype),
            pltpu.SemaphoreType.DMA((n_tok,)),
            pltpu.SemaphoreType.DMA((n_tok,)),
            pltpu.SemaphoreType.DMA((2,)),
            pltpu.SemaphoreType.DMA((2,)),
        ]
        + gather_scratch(first)
        + sum_scratch(count.shape),
        compiler_params=pltpu.CompilerParams(collective_id=0, has_side_effects=True, vmem_limit_bytes=VMEM_LIMIT),
        name="start_exchange",
    )(owners, pieces, count, patches, marks)


def unit_order(unit):
    grp_bits = [("grp", bit) for bit in axis_bits("grp")]
    if unit % 2:
        grp_bits = grp_bits[::-1]
    return [("tok", 1)] + grp_bits + [("tok", bit) for bit in axis_bits("tok")[:-1][::-1]]


def unit_layout(order):
    left = bit_order()
    shapes = []
    for name in order:
        at = left.index(name)
        shapes.append((1 << at, 2, 1 << (len(left) - 1 - at)))
        left.remove(name)
    return shapes


SPLIT = 3


class UnitRide:
    def __init__(self, sources, out_ref, scratch, begin=0, end=None, base=0):
        self.grp, self.tok = lax.axis_index("grp"), lax.axis_index("tok")
        self.begin = begin
        self.end = len(bit_order()) if end is None else end
        self.phases = self.end - begin
        self.names = unit_order(0)[self.begin : self.end]
        self.sources = sources
        self.out_ref, self.base = out_ref, base
        self.sems = scratch[:2]
        self.buffers = scratch[2:]

    def partner(self, name):
        axis, bit = name
        if axis == "grp":
            return (lax.bitwise_xor(self.grp, bit), self.tok)
        return (self.grp, lax.bitwise_xor(self.tok, bit))

    def half_of(self, name):
        return (self.grp if name[0] == "grp" else self.tok) // name[1] % 2

    def before(self, unit, phase):
        if phase == 0:
            ref, at = self.sources[unit]
            return ref.at[at]
        return self.buffers[unit * 2 * self.phases + 2 * (phase - 1) + 1]

    def landing(self, unit, phase):
        return self.buffers[unit * 2 * self.phases + 2 * phase]

    def copy(self, unit, phase):
        name = unit_order(unit)[self.begin + phase]
        at = phase * len(self.sources) + unit
        return pltpu.make_async_remote_copy(
            src_ref=self.before(unit, phase).at[:, 1 - self.half_of(name)],
            dst_ref=self.landing(unit, phase),
            send_sem=self.sems[0].at[at],
            recv_sem=self.sems[1].at[at],
            device_id=self.partner(name),
            device_id_type=MESH,
        )

    def finish(self, unit, phase):
        order = unit_order(unit)
        shapes = unit_layout(order)
        self.copy(unit, phase).wait()
        outer, _, inner = shapes[self.begin + phase]
        source, landed = self.before(unit, phase), self.landing(unit, phase)
        mine = self.half_of(order[self.begin + phase])
        target = self.out_ref.at[self.base + unit]
        if phase + 1 < self.phases:
            target = self.before(unit, phase + 1)
        whole_done = self.begin + phase + 1 == len(order)
        if not whole_done:
            low = shapes[self.begin + phase + 1][2]

        @pl.loop(0, outer * inner, unroll=min(4, outer * inner))
        def _(at):
            value = source[at // inner, mine, at % inner] + landed[at // inner, at % inner]
            if whole_done:
                target[...] = value
            else:
                target[at // (2 * low), at // low % 2, at % low] = value

    def advance(self, phase):
        for unit in range(len(self.sources)):
            if phase:
                self.finish(unit, phase - 1)
            if phase < self.phases:
                self.copy(unit, phase).start()


def unit_scratch(total, chunk, width, begin=0, end=None):
    end = len(bit_order()) if end is None else end
    dma = pltpu.SemaphoreType.DMA
    buffers = [dma(((end - begin) * total,)), dma(((end - begin) * total,))]
    for unit in range(total):
        shapes = unit_layout(unit_order(unit))
        for phase in range(begin, end):
            outer, _, inner = shapes[phase]
            buffers.append(pltpu.VMEM((outer, inner, chunk, width), jnp.bfloat16))
            following = shapes[phase + 1] if phase + 1 < end else (1, 1, 1)
            buffers.append(pltpu.VMEM(following + (chunk, width), jnp.bfloat16))
    return buffers


def unit_blocks(units):
    chunk = units.shape[1] >> len(bit_order())
    return units.reshape((units.shape[0],) + unit_layout(unit_order(0))[0] + (chunk, units.shape[2]))


class SumRide:
    def __init__(self, source_ref, total_ref, scratch, begin=0, end=None):
        self.grp, self.tok = lax.axis_index("grp"), lax.axis_index("tok")
        self.order = unit_order(0)[begin:end]
        self.names = self.order
        self.phases = len(self.order)
        self.source_ref, self.total_ref = source_ref, total_ref
        self.sums = scratch[2]
        self.sems = scratch[:2]

    partner = UnitRide.partner

    def copy(self, phase):
        return pltpu.make_async_remote_copy(
            src_ref=self.sums.at[2 * phase],
            dst_ref=self.sums.at[2 * phase + 1],
            send_sem=self.sems[0].at[phase],
            recv_sem=self.sems[1].at[phase],
            device_id=self.partner(self.order[phase]),
            device_id_type=MESH,
        )

    def advance(self, phase):
        if phase == 0:
            self.sums[0] = self.source_ref[...]
        else:
            self.copy(phase - 1).wait()
            self.sums[2 * phase] = self.sums[2 * phase - 2] + self.sums[2 * phase - 1]
        if phase < self.phases:
            self.copy(phase).start()
        else:
            self.total_ref[...] = self.sums[2 * phase]


def sum_scratch(shape):
    phases = len(bit_order())
    dma = pltpu.SemaphoreType.DMA
    return [dma((phases,)), dma((phases,)), pltpu.VMEM((2 * phases + 1,) + shape, jnp.float32)]


def tail_kernel(counts, rows, *refs):
    owner_ref, early_ref, part_ref = refs[:3]
    blocks, refs = refs[3 : 3 + len(counts)], refs[3 + len(counts) :]
    small_refs, refs = refs[: len(rows)], refs[len(rows) :]
    owned_ref, small_out_ref, chunk_ref, place_ref, near_s, near_r, small_ref = refs[:7]
    scratch = refs[7:]
    sources = [(ref, at) for ref, count in zip(blocks, counts) for at in range(count)]
    total = len(sources)
    parts = part_ref.shape[0]
    grp, tok, n_tok, peers = exchange_setup()
    signal_all(peers)
    begin = 0
    for ref, count in zip(small_refs, rows):
        small_ref[begin : begin + count, :] = ref[...]
        begin += count
    small_ref[begin:, :] = jnp.zeros((small_ref.shape[0] - begin, C), jnp.float32)
    cut = 3 + 2 + 2 * total * len(bit_order())
    rides = Rides(
        [
            UnitRide(sources, chunk_ref, scratch[3:cut]),
            SumRide(small_ref, small_out_ref, scratch[:3]),
            UnitRide([(part_ref, at) for at in range(parts)], chunk_ref, scratch[cut:], SPLIT, None, total),
        ]
    )
    rides.peers = peers
    for phase in range(rides.phases + 1):
        rides.advance(phase)
    total += parts
    for at in range(early_ref.shape[0]):
        chunk_ref[total + at] = early_ref[at]
    last = total + early_ref.shape[0]
    chunk_ref[last] = jnp.zeros(chunk_ref.shape[1:], chunk_ref.dtype)
    slot_rows = owned_ref.shape[1]
    slots = slot_numbers(owner_ref, slot_rows)

    @pl.loop(0, n_tok * slot_rows)
    def _(at):
        unit_at = jnp.int32(last)
        for unit, slot in enumerate(slots):
            unit_at = jnp.where(slot == at, unit, unit_at)
        place_ref[at // slot_rows, at % slot_rows] = chunk_ref[unit_at]

    copies = []
    for step in range(1, n_tok):
        peer = lax.bitwise_xor(tok, step)
        copies.append(send(place_ref.at[peer], owned_ref.at[tok], (near_s, near_r), step, (grp, peer)))
    owned_ref[tok] = place_ref[tok]
    for copy in copies:
        copy.wait()


def tail_exchange(owners, slot_rows, early, part, sources, smalls, n_tok):
    chunk, width = early.shape[1:]
    counts = tuple(source.shape[0] for source in sources)
    rows = tuple(small.shape[0] for small in smalls)
    total = sum(counts)
    low = early.dtype
    vmem = pl.BlockSpec(memory_space=pltpu.VMEM)
    dma = pltpu.SemaphoreType.DMA
    small = (-(-sum(rows) // 8) * 8, C)
    return pl.pallas_call(
        lambda *refs: tail_kernel(counts, rows, *refs),
        out_shape=(
            jax.ShapeDtypeStruct((n_tok, slot_rows, chunk, width), low),
            jax.ShapeDtypeStruct(small, jnp.float32),
        ),
        in_specs=[pl.BlockSpec(memory_space=pltpu.SMEM)] + [vmem] * (2 + len(sources) + len(smalls)),
        out_specs=(vmem, vmem),
        scratch_shapes=[
            pltpu.VMEM((total + part.shape[0] + early.shape[0] + 1, chunk, width), low),
            pltpu.VMEM((n_tok, slot_rows, chunk, width), low),
            dma((n_tok,)),
            dma((n_tok,)),
            pltpu.VMEM(small, jnp.float32),
        ]
        + sum_scratch(small)
        + unit_scratch(total, chunk, width)
        + unit_scratch(part.shape[0], chunk, width, SPLIT),
        compiler_params=pltpu.CompilerParams(collective_id=1, has_side_effects=True, vmem_limit_bytes=VMEM_LIMIT),
        name="tail_exchange",
    )(owners, early, part, *[unit_blocks(source) for source in sources], *smalls)


def body(
    patches,
    labels,
    valid_mask,
    crop_counts,
    owners,
    slot_weight,
    slot_moment,
    slot_second,
    norm_params,
    norm_moment,
    norm_second,
    head_weight,
    head_moment,
    head_second,
):
    tok_dev = patches.shape[0]
    n_tok = lax.axis_size("tok")
    n_grp = lax.axis_size("grp")
    tok_index = lax.axis_index("tok")
    group_tok = tok_dev * n_tok
    counts = crop_counts[0]
    n_unit = owners.shape[0]
    slot_rows, columns = slot_weight.shape
    chunk = columns // n_tok // C
    first_tok = tok_index * tok_dev
    small_end = counts[0] * BIG_SIDE**2 + counts[1] * SMALL_SIDE**2
    counted = valid_mask * (first_tok + jnp.arange(tok_dev, dtype=jnp.int32) < small_end)
    counted = counted.astype(jnp.float32).reshape(-1, LANES)
    pieces = slot_weight.astype(jnp.bfloat16).reshape(slot_rows, n_tok, chunk, C).transpose(1, 0, 2, 3)
    first_units = 1 + 2 * (n_unit // BLOCKS)
    marks = jnp.stack([labels, valid_mask])
    own, later, counted, patch_halo, mark_halo = start_exchange(
        owners, pieces, counted, patches, marks[:, :OVER], first_units
    )
    pixel_total = counted[0, 0]
    own = own.reshape(first_units, FF, C)
    units = lax.all_gather(later, BOTH, axis=1, tiled=True)
    layers = [
        ((own, 1, own, 2), (own, 3)),
        ((own, 5, own, 6), (own, 7)),
        ((units, 0, units, 1), (units, 2)),
    ]

    window = tok_dev + OVER
    tiles = window // 4
    marks = jnp.concatenate([marks, mark_halo], 1)
    marks = marks.reshape(2, tiles, 4).transpose(0, 2, 1).reshape(2, window)
    labels = marks[0]
    positions = first_tok + 4 * jnp.arange(tiles, dtype=jnp.int32)
    begin_at, half_side, tile_y, tile_x, is_real = image_layout(positions, counts)
    own_image = (begin_at >= first_tok) & (begin_at < first_tok + tok_dev) & (positions < group_tok)
    stacks = shift_stacks(half_side, tile_y, tile_x, is_real)

    def image_at(tile):
        at = first_tok + 4 * tile
        return jnp.where(at < group_tok, image_layout(at, counts)[0], -1)

    bias = block_bias(tiles, image_at)
    real_rows = jnp.broadcast_to(is_real.astype(jnp.float32)[:, None], (tiles, LANES))
    keep_mask = marks[1].astype(jnp.float32) * jnp.tile((own_image & is_real).astype(jnp.float32), 4)
    tail = 6 * BLOCKS
    embed_pre, resid, kernels = embed_forward(patches, patch_halo, own, norm_params[tail : tail + 2])
    kept_all = []
    for layer_at in range(BLOCKS):
        attn_units, mlp_units = layers[layer_at]
        at = 6 * layer_at
        middle, *attn_kept = attention_forward(resid, norm_params[at : at + 4], *attn_units, bias)
        output, *mlp_kept = mlp_forward(
            middle, norm_params[at + 4 : at + 6], *mlp_units, kernels, layer_at, stacks, real_rows,
        )
        w_up = mlp_kept.pop()
        kept_all.append((resid, attn_kept, middle, mlp_kept, w_up))
        resid = output
    grad_res, d_head, final_gains, loss_row = head_step(
        resid, norm_params[tail + 2 : tail + 4], head_weight, labels[:, None], keep_mask[:, None], counted
    )
    unit_plans = []
    head_cuts = [0, 1, 2, 3, 4, len(bit_order())]
    early = []
    kernel_grads = [None] * BLOCKS
    gain_grads = []
    phases = len(bit_order())

    def head_plans(value):
        if len(head_cuts) < 2:
            return []
        begin = head_cuts.pop(0)
        return [plan_sum(value, begin, head_cuts[0])]

    for layer_at in reversed(range(BLOCKS)):
        attn_units, mlp_units = layers[layer_at]
        at = 6 * layer_at
        entry, attn_kept, middle, mlp_kept, w_up = kept_all[layer_at]
        grad_res, mlp_grads, kernel_grads[layer_at], mlp_gains, *ridden_out = mlp_backward(
            grad_res, middle, norm_params[at + 4 : at + 6], w_up, *mlp_units, kernels, layer_at,
            stacks, real_rows, mlp_kept, unit_plans + head_plans(d_head), 2 + layer_at,
        )
        d_head = ridden_out.pop()
        unit_plans = [plan_units(mlp_grads, 0, SPLIT)]
        if ridden_out:
            early.insert(0, ridden_out[1])
            unit_plans.append(plan_units(ridden_out[0], SPLIT, phases))
        plans = unit_plans + head_plans(d_head)
        grad_res, attn_grads, attn_gains, *ridden_out = attention_backward(
            grad_res, entry, norm_params[at : at + 4], *attn_units, bias, attn_kept, plans, 2 + BLOCKS + layer_at
        )
        if len(plans) > len(unit_plans):
            d_head = ridden_out.pop()
        if layer_at + 1 < BLOCKS:
            early.insert(0, ridden_out[1])
        unit_plans = [plan_units(attn_grads, 0, SPLIT), plan_units(ridden_out[0], SPLIT, phases)]
        gain_grads = [attn_gains, mlp_gains] + gain_grads
    head_total = d_head[: head_weight.shape[1]].T
    part = ridden_out[0]
    first_grad, embed_gains = embed_backward(
        grad_res, embed_pre, norm_params[tail : tail + 2], patches, patch_halo, kernel_grads
    )
    early = jnp.concatenate(early, 0)
    smalls = gain_grads + [embed_gains, final_gains, loss_row]
    owned, small = tail_exchange(owners, slot_rows, early, part, [first_grad, attn_grads], smalls, n_tok)
    owned = owned.transpose(1, 0, 2, 3).astype(jnp.float32).reshape(slot_rows, columns)
    norm_rows_all = norm_params.shape[0]
    norm_total, loss_sum = (small[:norm_rows_all], small[norm_rows_all, 0])
    slot_m, slot_v, slot_w = adamw_step(
        slot_weight, slot_moment, slot_second, owned, RATE_MATRIX, DECAY_RATE
    )
    norm_m, norm_v, norm_w = adamw_step(
        norm_params, norm_moment, norm_second, norm_total, RATE_VECTOR, 0.0
    )
    head_m, head_v, head_w = adamw_step(
        head_weight, head_moment, head_second, head_total, RATE_MATRIX, DECAY_RATE
    )
    return (
        loss_sum,
        pixel_total,
        slot_m,
        slot_v,
        slot_w,
        norm_m,
        norm_v,
        norm_w,
        head_m,
        head_v,
        head_w,
    )


def solution(mesh):
    in_specs = (
        P(("grp", "tok"), None),
        P(("grp", "tok")),
        P(("grp", "tok")),
        P("grp", None),
        P(),
        P("tok", "grp"),
        P("tok", "grp"),
        P("tok", "grp"),
        P(),
        P(),
        P(),
        P(),
        P(),
        P(),
    )
    out_specs = (
        P(),
        P(),
        P("tok", "grp"),
        P("tok", "grp"),
        P("tok", "grp"),
        P(),
        P(),
        P(),
        P(),
        P(),
        P(),
    )
    return jax.shard_map(body, mesh=mesh, in_specs=in_specs, out_specs=out_specs, check_vma=False)
```

```python
import functools

import jax
import jax.numpy as jnp
import numpy as np
from jax import lax
from jax.experimental import pallas as pl
from jax.experimental.pallas import tpu as pltpu
from jax.sharding import PartitionSpec as P

C = 320
HEADS = 5
HD = 64
FF = 1280
PIN = 1152
BLOCKS = 3
BIG_SIDE = 14
SMALL_SIDE = 6
STEP = 10
KVH = 49


EPS_NORM = 1e-06
BETA_ONE = 0.9
BETA_TWO = 0.999
ADAM_EPS = 1e-08
RATE_MATRIX = 0.05
RATE_VECTOR = 0.3
DECAY_RATE = 0.05
NEG_FILL = -1e30
PREC_HIGH = lax.Precision.HIGHEST


def layer_norm(values, gain_vec, shift_vec):
    center = values - jnp.mean(values, -1, keepdims=True)
    inverse = lax.rsqrt(jnp.mean(center * center, -1, keepdims=True) + EPS_NORM)
    return center * inverse * gain_vec + shift_vec


def adamw_step(weight, moment, second, gradient, rate_now, decay_now):
    moment = BETA_ONE * moment + (1.0 - BETA_ONE) * gradient
    second = BETA_TWO * second + (1.0 - BETA_TWO) * gradient * gradient
    m_hat = moment / (1.0 - BETA_ONE**STEP)
    v_hat = second / (1.0 - BETA_TWO**STEP)
    weight = weight - rate_now * (m_hat / (jnp.sqrt(v_hat) + ADAM_EPS) + decay_now * weight)
    return (moment, second, weight)


def product(left, right):
    return jnp.dot(left, right, preferred_element_type=jnp.float32)


def outer_sum(left, right):
    return lax.dot_general(
        left, right, (((0,), (0,)), ((), ())), preferred_element_type=jnp.float32
    )


def back_product(gradient, weight):
    return lax.dot_general(
        gradient, weight, (((1,), (1,)), ((), ())), preferred_element_type=jnp.float32
    )


def norm_back(values, gain_vec, shift_vec, gradient):
    _, pull_back = jax.vjp(layer_norm, values, gain_vec, shift_vec)
    return pull_back(gradient)


OVER = 4 * KVH - 4


def image_layout(positions, counts):
    big_tok = BIG_SIDE * BIG_SIDE
    small_tok = SMALL_SIDE * SMALL_SIDE
    big_end = counts[0] * big_tok
    small_end = big_end + counts[1] * small_tok
    is_big = positions < big_end
    is_small = jnp.logical_and(positions >= big_end, positions < small_end)
    half_side = jnp.where(is_big, BIG_SIDE // 2, SMALL_SIDE // 2)
    begin_at = jnp.where(
        is_big,
        positions // big_tok * big_tok,
        jnp.where(is_small, big_end + (positions - big_end) // small_tok * small_tok, small_end),
    )
    tile_idx = (positions - begin_at) // 4
    return (begin_at, half_side, tile_idx // half_side, tile_idx % half_side, positions < small_end)


def shift_stacks(half_side, tile_y, tile_x, is_real):
    tiles = half_side.shape[0]
    step_y = np.array([[0, 1 - 2 * (sub // 2), 1 - 2 * (sub // 2)] for sub in range(4)], np.int32)[:, :, None]
    step_x = np.array([[1 - 2 * (sub % 2), 0, 1 - 2 * (sub % 2)] for sub in range(4)], np.int32)[:, :, None]
    at_y = tile_y + step_y
    at_x = tile_x + step_x
    inside = is_real & (at_y >= 0) & (at_y < half_side) & (at_x >= 0) & (at_x < half_side)
    source = jnp.arange(tiles, dtype=jnp.int32) + step_y * half_side + step_x
    source = jnp.where(inside, source, -1)
    cut = row_cut(tiles)
    columns = jnp.arange(SPAN, dtype=jnp.int32)
    upper = (source[:, :, :cut, None] == columns).astype(jnp.bfloat16)
    lower = (source[:, :, cut:, None] == columns + (tiles - SPAN)).astype(jnp.bfloat16)
    return (upper.reshape(4, 3 * cut, SPAN), lower.reshape(4, 3 * (tiles - cut), SPAN))


def tap_source(sub, tap):
    y_at = sub // 2 + tap // 3 - 1
    x_at = sub % 2 + tap % 3 - 1
    return (y_at % 2 * 2 + x_at % 2, y_at // 2, x_at // 2)


SQRT_HALF = 0.7071067811865476
INV_SQRT_TWO_PI = 0.3989422804014327
TAPS_OF = [[tap_source(sub, tap) for tap in range(9)] for sub in range(4)]
VMEM_LIMIT = 56 * 1024 * 1024
SPAN = 256
ROWS = 16
LANES = 128


def row_cut(tiles):
    return (tiles // 2 + 15) // 16 * 16


def move_planes(planes_ref, upper_ref, lower_ref, moved_ref):
    tiles = planes_ref.shape[0] // 4
    cut = row_cut(tiles)
    for sub in range(4):
        base = sub * tiles
        part = product(upper_ref[sub], planes_ref[base : base + SPAN, :])
        for key in range(3):
            moved_ref[sub, key, :cut, :] = part[key * cut : (key + 1) * cut]
        part = product(lower_ref[sub], planes_ref[base + tiles - SPAN : base + tiles, :])
        for key in range(3):
            moved_ref[sub, key, cut:, :] = part[key * (tiles - cut) : (key + 1) * (tiles - cut)]


def chunk_sources(planes_ref, moved_ref, row, lanes):
    tiles = planes_ref.shape[0] // 4
    found = {}
    for sub in range(4):
        found[sub, 0, 0] = planes_ref[pl.ds(pl.multiple_of(sub * tiles + row, ROWS), ROWS), lanes].astype(jnp.float32)
        step_y = 1 - 2 * (sub // 2)
        step_x = 1 - 2 * (sub % 2)
        for key, step in enumerate(((0, step_x), (step_y, 0), (step_y, step_x))):
            found[(sub,) + step] = moved_ref[sub, key, pl.ds(row, ROWS), lanes]
    return found


def norm_rows(values, gain, shift):
    center = values - jnp.mean(values, -1, keepdims=True)
    inverse = lax.rsqrt(jnp.mean(center * center, -1, keepdims=True) + EPS_NORM)
    unit = center * inverse
    return (unit, inverse, unit * gain + shift)


def norm_rows_back(unit, inverse, gain, grad):
    scaled = grad * gain
    return inverse * (
        scaled - jnp.mean(scaled, -1, keepdims=True) - unit * jnp.mean(scaled * unit, -1, keepdims=True)
    )


def mlp_forward_kernel(
    middle_ref, gains_ref, up_ref, down_ref, kern_ref, upper_ref, lower_ref, real_ref,
    out_ref, hidden_ref, active_ref, slope_ref, turned_ref,
    normed_ref, moved_ref, planes_ref,
):
    rows = middle_ref.shape[0]
    block = hidden_ref.shape[1]
    tiles = rows // 4

    @pl.when(pl.program_id(0) == 0)
    def _():
        normed = norm_rows(middle_ref[...], gains_ref[0:1, :], gains_ref[1:2, :])[2]
        normed_ref[...] = normed.astype(jnp.bfloat16)
        out_ref[...] = middle_ref[...]
        spread_rows(up_ref[0], planes_ref)
        for quarter in range(FF // C):
            for at, lane, width in lane_parts(C):
                part = planes_ref[at, pl.ds(quarter, C, stride=FF // C), :][:, :width]
                begin = quarter * C + lane
                turned_ref[:, begin : begin + width] = part.astype(jnp.bfloat16)

    for sub in range(4):
        columns = pl.ds(pl.multiple_of(pl.program_id(0) * block, block), block)
        part = product(normed_ref[sub * tiles : (sub + 1) * tiles, :], turned_ref[:, columns])
        hidden_ref[sub * tiles : (sub + 1) * tiles, :] = part.astype(jnp.bfloat16)
    move_planes(hidden_ref, upper_ref, lower_ref, moved_ref)

    for lane in range(0, hidden_ref.shape[1], LANES):
        lanes = slice(lane, lane + LANES)
        kern = [kern_ref[0, tap : tap + 1, lanes] for tap in range(9)]

        @pl.loop(0, tiles // ROWS, unroll=tiles // ROWS)
        def _(at):
            row = pl.multiple_of(at * ROWS, ROWS)
            found = chunk_sources(hidden_ref, moved_ref, row, lanes)
            real = real_ref[pl.ds(row, ROWS), :] > 0.0
            for sub in range(4):
                center = found[sub, 0, 0] * kern[4]
                total = center
                for tap in range(9):
                    if tap != 4:
                        total = total + found[TAPS_OF[sub][tap]] * kern[tap]
                mixed = jnp.where(real, total, center)
                half = 0.5 + 0.5 * lax.erf(mixed * SQRT_HALF)
                bell = jnp.exp(-0.5 * mixed * mixed) * INV_SQRT_TWO_PI
                span = pl.ds(pl.multiple_of(sub * tiles + row, ROWS), ROWS)
                active_ref[span, lanes] = (mixed * half).astype(jnp.bfloat16)
                slope_ref[span, lanes] = (half + mixed * bell).astype(jnp.bfloat16)

    for sub in range(4):
        span = slice(sub * tiles, (sub + 1) * tiles)
        out_ref[span, :] += product(active_ref[span, :], down_ref[0])


def lane_parts(width):
    return [(at, lane, min(LANES, width - lane)) for at, lane in enumerate(range(0, width, LANES))]


def spread_rows(source, planes_ref):
    for at, lane, width in lane_parts(source.shape[1]):
        planes_ref[at, :, :width] = source[:, lane : lane + width].astype(jnp.float32)


class Plan:
    def __init__(self, value, out, scratch, make, space=None):
        self.value, self.out, self.scratch, self.make = value, out, scratch, make
        self.in_spec = whole(value.shape)
        self.out_spec = pl.BlockSpec(memory_space=space) if space is not None else whole(out.shape)


def plan_sum(value, begin, end):
    make = functools.partial(SumRide, begin=begin, end=end)
    return Plan(value, jax.ShapeDtypeStruct(value.shape, value.dtype), sum_scratch(value.shape, jnp.bfloat16), make)


def plan_units(value, begin, end):
    if begin == 0:
        value = unit_blocks(value)
    total, (chunk, width) = value.shape[0], value.shape[-2:]
    inside = unit_layout(unit_order(0))[end] if end < len(bit_order()) else ()
    out = jax.ShapeDtypeStruct((total,) + inside + (chunk, width), value.dtype)

    def make(ride_in, ride_out, scratch):
        sources = [(ride_in, at) for at in range(total)]
        return UnitRide(sources, ride_out, scratch, begin, end)

    return Plan(value, out, unit_scratch(total, chunk, width, begin, end), make)


class Rides:
    def __init__(self, rides):
        self.rides = rides
        self.phases = max(ride.phases for ride in rides)
        names = [name for name in bit_order() if any(name in ride.names for ride in rides)]
        self.peers = [UnitRide.partner(rides[0], name) for name in names]

    def signal(self):
        signal_all(self.peers)

    def advance(self, phase):
        if phase == 0:
            pl.semaphore_wait(pltpu.get_barrier_semaphore(), len(self.peers))
        for ride in self.rides:
            if phase <= ride.phases:
                ride.advance(phase)


def rides_of(plans, ins, outs, scratch):
    rides = []
    for plan, ride_in, ride_out in zip(plans, ins, outs):
        count = len(plan.scratch)
        rides.append(plan.make(ride_in, ride_out, scratch[:count]))
        scratch = scratch[count:]
    return Rides(rides)


def ridden(kernel, inputs, outputs, scratch, steps, plans):
    def run(*refs):
        own_in, refs = refs[:inputs], refs[inputs:]
        ride_in, refs = refs[: len(plans)], refs[len(plans) :]
        own_out, refs = refs[:outputs], refs[outputs:]
        ride_out, rest = refs[: len(plans)], refs[len(plans) :]
        rides = rides_of(plans, ride_in, ride_out, rest[scratch:])
        places = [0] + list(range(1, steps - 1, 2))
        for phase, step in enumerate(places):
            if phase == 0:

                @pl.when(pl.program_id(0) == step)
                def _():
                    rides.signal()
                    rides.advance(0)
            elif phase <= rides.phases:
                pl.when(pl.program_id(0) == step)(functools.partial(rides.advance, phase))
        kernel(*own_in, *own_out, *rest[:scratch])

        @pl.when(pl.program_id(0) == steps - 1)
        def _():
            for phase in range(len(places), rides.phases + 1):
                rides.advance(phase)

    return run


def whole(shape):
    return pl.BlockSpec(shape, lambda j: (0,) * len(shape))


def unit_spec(at):
    return pl.BlockSpec((1, FF, C), lambda j: (at, 0, 0))


def mlp_forward(middle, gains, units, at, kernel, layer_at, stacks, real_rows):
    rows = middle.shape[0]
    block = 256
    by_lane = pl.BlockSpec((rows, block), lambda j: (0, j))
    low = jax.ShapeDtypeStruct((rows, FF), jnp.bfloat16)
    return pl.pallas_call(
        mlp_forward_kernel,
        grid=(FF // block,),
        out_shape=(
            jax.ShapeDtypeStruct((rows, C), jnp.float32),
            low,
            low,
            low,
            jax.ShapeDtypeStruct((C, FF), jnp.bfloat16),
        ),
        in_specs=[
            whole((rows, C)),
            whole((2, C)),
            unit_spec(at),
            pl.BlockSpec((1, block, C), lambda j: (at + 1, j, 0)),
            pl.BlockSpec((1, 9, block), lambda j: (layer_at, 0, j)),
            whole(stacks[0].shape),
            whole(stacks[1].shape),
            whole(real_rows.shape),
        ],
        out_specs=(whole((rows, C)), by_lane, by_lane, by_lane, whole((C, FF))),
        scratch_shapes=[
            pltpu.VMEM((rows, C), jnp.bfloat16),
            pltpu.VMEM((4, 3, rows // 4, block), jnp.float32),
            pltpu.VMEM((3, FF, LANES), jnp.float32),
        ],
        compiler_params=pltpu.CompilerParams(vmem_limit_bytes=VMEM_LIMIT),
        cost_estimate=pl.CostEstimate(flops=14 * 10**9, bytes_accessed=18 * 10**6, transcendentals=4 * 10**6),
        name="mlp_forward",
    )(middle, gains, units, units, kernel, stacks[0], stacks[1], real_rows)


def mlp_backward_kernel(
    grad_ref, middle_ref, gains_ref, up_ref, down_ref, kern_ref, upper_ref, lower_ref, real_ref,
    hidden_ref, active_ref, slope_ref,
    out_ref, dunits_ref, dkern_ref, dgain_ref,
    low_ref, low_t_ref, normed_t_ref, mixed_ref, dhid_ref, moved_ref, back_ref, wide_ref, planes_ref,
):
    rows = grad_ref.shape[0]
    tiles = rows // 4
    block = hidden_ref.shape[1]

    @pl.when(pl.program_id(0) == 0)
    def _():
        for sub in range(4):
            span = slice(sub * tiles, (sub + 1) * tiles)
            low_ref[span, :] = grad_ref[span, :].astype(jnp.bfloat16)
        normed = norm_rows(middle_ref[...], gains_ref[0:1, :], gains_ref[1:2, :])[2]
        normed_t_ref[...] = normed.astype(jnp.bfloat16).T
        low_t_ref[...] = low_ref[...].T
        back_ref[...] = jnp.zeros_like(back_ref)

    for sub in range(4):
        span = slice(sub * tiles, (sub + 1) * tiles)
        part = back_product(low_ref[span, :], down_ref[0]).astype(jnp.bfloat16).astype(jnp.float32)
        mixed_ref[span, :] = (part * slope_ref[span, :].astype(jnp.float32)).astype(jnp.bfloat16)
    down_rows = pl.ds(pl.multiple_of(pl.program_id(0) * block, block), block)
    dunits_ref[1, down_rows, :] = product(low_t_ref[...], active_ref[...]).T.astype(jnp.bfloat16)
    move_planes(mixed_ref, upper_ref, lower_ref, moved_ref)

    for lane in range(0, block, LANES):
        lanes = slice(lane, lane + LANES)
        kern = [kern_ref[0, tap : tap + 1, lanes] for tap in range(9)]

        def step(at, sums):
            row = pl.multiple_of(at * ROWS, ROWS)
            found = chunk_sources(mixed_ref, moved_ref, row, lanes)
            real = real_ref[pl.ds(row, ROWS), :] > 0.0
            sums = list(sums)
            for sub in range(4):
                span = pl.ds(pl.multiple_of(sub * tiles + row, ROWS), ROWS)
                hidden = hidden_ref[span, lanes].astype(jnp.float32)
                center = found[sub, 0, 0] * kern[4]
                total = center
                for tap in range(9):
                    term = found[TAPS_OF[sub][tap]]
                    if tap != 4:
                        total = total + term * kern[8 - tap]
                    piece = hidden * term
                    sums[tap] = sums[tap] + piece[:8] + piece[8:]
                dhid_ref[span, lanes] = jnp.where(real, total, center).astype(jnp.bfloat16)
            return tuple(sums)

        sums = lax.fori_loop(0, tiles // ROWS, step, (jnp.zeros((8, LANES), jnp.float32),) * 9, unroll=True)
        for tap in range(9):
            dkern_ref[8 - tap : 9 - tap, lanes] = jnp.sum(sums[tap], 0, keepdims=True)

    columns = pl.ds(pl.multiple_of(pl.program_id(0) * block, block), block)
    wide_ref[:, columns] = product(normed_t_ref[...], dhid_ref[...])
    for sub in range(4):
        span = slice(sub * tiles, (sub + 1) * tiles)
        back_ref[span, :] += back_product(dhid_ref[span, :], up_ref[...])

    @pl.when(pl.program_id(0) == pl.num_programs(0) - 1)
    def _():
        grad = back_ref[...]
        unit, inverse, _ = norm_rows(middle_ref[...], gains_ref[0:1, :], gains_ref[1:2, :])
        out_ref[...] = grad_ref[...] + norm_rows_back(unit, inverse, gains_ref[0:1, :], grad)
        dgain_ref[0:1, :] = jnp.sum(grad * unit, 0, keepdims=True)
        dgain_ref[1:2, :] = jnp.sum(grad, 0, keepdims=True)
        for quarter in range(FF // C):
            for at, lane, width in lane_parts(C):
                begin = quarter * C + lane
                part = wide_ref[:, begin : begin + width]
                if width < LANES:
                    part = jnp.concatenate([part, jnp.zeros((C, LANES - width), jnp.float32)], 1)
                planes_ref[at, pl.ds(quarter, C, stride=FF // C), :] = part
        for at, lane, width in lane_parts(C):
            dunits_ref[0, :, lane : lane + width] = planes_ref[at, :, :width].astype(jnp.bfloat16)


def mlp_backward(grad, middle, gains, w_up, units, at, kernel, layer_at, stacks, real_rows, kept, plans, meeting):
    rows = middle.shape[0]
    block = 256
    by_lane = pl.BlockSpec((rows, block), lambda j: (0, j))
    up_spec = pl.BlockSpec((C, block), lambda j: (0, j))
    tap_spec = pl.BlockSpec((9, block), lambda j: (0, j))
    return pl.pallas_call(
        ridden(mlp_backward_kernel, 12, 4, 9, FF // block, plans),
        grid=(FF // block,),
        out_shape=(
            jax.ShapeDtypeStruct((rows, C), jnp.float32),
            jax.ShapeDtypeStruct((2, FF, C), jnp.bfloat16),
            jax.ShapeDtypeStruct((9, FF), jnp.float32),
            jax.ShapeDtypeStruct((2, C), jnp.float32),
            *[plan.out for plan in plans],
        ),
        in_specs=[
            whole((rows, C)),
            whole((rows, C)),
            whole((2, C)),
            up_spec,
            pl.BlockSpec((1, block, C), lambda j: (at + 1, j, 0)),
            pl.BlockSpec((1, 9, block), lambda j: (layer_at, 0, j)),
            whole(stacks[0].shape),
            whole(stacks[1].shape),
            whole(real_rows.shape),
            by_lane,
            by_lane,
            by_lane,
        ]
        + [plan.in_spec for plan in plans],
        out_specs=(whole((rows, C)), whole((2, FF, C)), tap_spec, whole((2, C)))
        + tuple(plan.out_spec for plan in plans),
        scratch_shapes=[
            pltpu.VMEM((rows, C), jnp.bfloat16),
            pltpu.VMEM((C, rows), jnp.bfloat16),
            pltpu.VMEM((C, rows), jnp.bfloat16),
            pltpu.VMEM((rows, block), jnp.bfloat16),
            pltpu.VMEM((rows, block), jnp.bfloat16),
            pltpu.VMEM((4, 3, rows // 4, block), jnp.float32),
            pltpu.VMEM((rows, C), jnp.float32),
            pltpu.VMEM((C, FF), jnp.float32),
            pltpu.VMEM((3, FF, LANES), jnp.float32),
        ]
        + sum([plan.scratch for plan in plans], []),
        compiler_params=pltpu.CompilerParams(
            collective_id=meeting, has_side_effects=True, vmem_limit_bytes=VMEM_LIMIT
        ),
        cost_estimate=pl.CostEstimate(flops=18 * 10**9, bytes_accessed=18 * 10**6, transcendentals=0),
        name="mlp_backward",
    )(grad, middle, gains, w_up, units, kernel, stacks[0], stacks[1], real_rows, *kept, *[plan.value for plan in plans])


WIDE = 384
BLOCK_TILES = 32
KEY_SPAN = 128


def block_places(tiles):
    places = []
    for index in range(-(-tiles // BLOCK_TILES)):
        start = min(index * BLOCK_TILES, tiles - BLOCK_TILES)
        places.append((start, min(max(start - 48, 0), tiles - KEY_SPAN)))
    return places


def block_bias(tiles, image_at):
    starts, lows = np.array(block_places(tiles), np.int32).T[:, :, None]
    columns = starts + np.tile(np.arange(BLOCK_TILES, dtype=np.int32), 4)
    rows = lows + np.arange(KEY_SPAN, dtype=np.int32)
    same = image_at(jnp.asarray(rows))[:, :, None] == image_at(jnp.asarray(columns))[:, None, :]
    return jnp.where(same, 0.0, NEG_FILL)


def place_of(index, tiles):
    start = jnp.minimum(index * BLOCK_TILES, tiles - BLOCK_TILES)
    low = jnp.clip(start - 48, 0, tiles - KEY_SPAN)
    return (pl.multiple_of(start, ROWS), pl.multiple_of(low, ROWS))


def four_planes(ref, start, lanes):
    tiles = ref.shape[0] // 4
    return jnp.concatenate(
        [ref[pl.ds(pl.multiple_of(sub * tiles + start, ROWS), BLOCK_TILES), lanes] for sub in range(4)], 0
    )


def put_planes(ref, start, lanes, values):
    tiles = ref.shape[0] // 4
    for sub in range(4):
        ref[pl.ds(pl.multiple_of(sub * tiles + start, ROWS), BLOCK_TILES), lanes] = values[
            sub * BLOCK_TILES : (sub + 1) * BLOCK_TILES
        ]


def head_pair(values, group):
    if group == 2:
        return values
    first = lax.broadcasted_iota(jnp.int32, values.shape, 1) < HD
    zero = jnp.zeros_like(values)
    return jnp.concatenate([jnp.where(first, values, zero), jnp.where(first, zero, values)], 0)


def softmax_columns(raw, bias):
    parts = []
    for half in range(raw.shape[0] // KEY_SPAN):
        scores = raw[half * KEY_SPAN : (half + 1) * KEY_SPAN] * HD ** (-0.5) + bias
        weights = jnp.exp(scores - jnp.max(scores, 0, keepdims=True))
        parts.append(weights * (1.0 / jnp.sum(weights, 0, keepdims=True)))
    return parts


def norm_store(source_ref, gains_ref, at, target_ref):
    normed = norm_rows(source_ref[...], gains_ref[at : at + 1, :], gains_ref[at + 1 : at + 2, :])[2]
    target_ref[...] = normed.astype(jnp.bfloat16)


def part_keyval(unit_ref, planes_ref, kv_ref):
    spread_rows(unit_ref[0, 2 * C :, :], planes_ref)
    for which in range(2):
        for at, lane, width in lane_parts(C):
            part = planes_ref[at, pl.ds(which, C, stride=2), :][:, :width]
            kv_ref[which, :, lane : lane + width] = part.astype(jnp.bfloat16)


def attention_forward_kernel(
    resid_ref, gains_ref, unit_ref, reduce_ref, bias_ref,
    middle_ref, normed_ref, query_ref, reduced_ref, key_ref, value_ref, attended_ref, kv_ref,
    planes_ref,
):
    part_keyval(unit_ref, planes_ref, kv_ref)
    rows = resid_ref.shape[0]
    tiles = rows // 4
    norm_store(resid_ref, gains_ref, 0, normed_ref)
    query_ref[:, C:] = jnp.zeros((rows, WIDE - C), jnp.bfloat16)
    reduced = jnp.zeros((tiles, C), jnp.float32)
    for sub in range(4):
        span = slice(sub * tiles, (sub + 1) * tiles)
        query_ref[span, :C] = product(normed_ref[span, :], unit_ref[0, :C, :]).astype(jnp.bfloat16)
        reduced = reduced + product(normed_ref[span, :], reduce_ref[0, sub * C : (sub + 1) * C, :])
    reduced_ref[...] = reduced
    normed_kv = norm_rows(reduced, gains_ref[2:3, :], gains_ref[3:4, :])[2].astype(jnp.bfloat16)
    for which, ref in enumerate((key_ref, value_ref)):
        ref[:, C:] = jnp.zeros((tiles, WIDE - C), jnp.bfloat16)
        ref[:, :C] = product(normed_kv, kv_ref[which]).astype(jnp.bfloat16)

    @pl.loop(0, bias_ref.shape[0], unroll=bias_ref.shape[0])
    def _(index):
        start, low = place_of(index, tiles)
        bias = bias_ref[index]
        for group in range(3):
            lanes = slice(group * LANES, (group + 1) * LANES)
            query = four_planes(query_ref, start, lanes)
            keys = head_pair(key_ref[pl.ds(low, KEY_SPAN), lanes], group)
            values = head_pair(value_ref[pl.ds(low, KEY_SPAN), lanes], group)
            probs = softmax_columns(back_product(keys, query), bias)
            probs = jnp.concatenate(probs, 0).astype(jnp.bfloat16).T
            put_planes(attended_ref, start, lanes, product(probs, values).astype(jnp.bfloat16))

    for sub in range(4):
        span = slice(sub * tiles, (sub + 1) * tiles)
        middle_ref[span, :] = resid_ref[span, :] + product(attended_ref[span, :C], unit_ref[0, C : 2 * C, :])


def attention_forward(resid, gains, units, at, reduces, reduce_at, bias):
    rows = resid.shape[0]
    tiles = rows // 4
    low = jnp.bfloat16
    shapes = (
        jax.ShapeDtypeStruct((rows, C), jnp.float32),
        jax.ShapeDtypeStruct((rows, C), low),
        jax.ShapeDtypeStruct((rows, WIDE), low),
        jax.ShapeDtypeStruct((tiles, C), jnp.float32),
        jax.ShapeDtypeStruct((tiles, WIDE), low),
        jax.ShapeDtypeStruct((tiles, WIDE), low),
        jax.ShapeDtypeStruct((rows, WIDE), low),
        jax.ShapeDtypeStruct((2, C, C), low),
    )
    return pl.pallas_call(
        attention_forward_kernel,
        grid=(1,),
        out_shape=shapes,
        in_specs=[whole((rows, C)), whole((4, C)), unit_spec(at), unit_spec(reduce_at), whole(bias.shape)],
        out_specs=tuple(whole(shape.shape) for shape in shapes),
        scratch_shapes=[pltpu.VMEM((3, 2 * C, LANES), jnp.float32)],
        compiler_params=pltpu.CompilerParams(vmem_limit_bytes=VMEM_LIMIT),
        cost_estimate=pl.CostEstimate(flops=6 * 10**9, bytes_accessed=14 * 10**6, transcendentals=10**6),
        name="attention_forward",
    )(resid, gains, units, reduces, bias)


def embed_forward_kernel(
    patches_ref, halo_ref, unit_ref, gains_ref, pre_ref, resid_ref, kern_ref, planes_ref, taps_ref
):
    rows = pre_ref.shape[0]
    tiles = rows // 4
    used = FF * 9 * BLOCKS // C
    for ref, base in ((patches_ref, 0), (halo_ref, patches_ref.shape[0])):
        step = 64

        @pl.loop(0, ref.shape[0] // step, unroll=4)
        def _(at):
            span = pl.ds(pl.multiple_of(at * step, step), step)
            into = pl.ds(pl.multiple_of(base + at * step, step), step)
            part = product(ref[span, :], unit_ref[0, :PIN, :])
            for place, lane, width in lane_parts(C):
                planes_ref[place, into, :width] = part[:, lane : lane + width]

    for sub in range(4):
        for place, lane, width in lane_parts(C):
            pre_ref[sub * tiles : (sub + 1) * tiles, lane : lane + width] = planes_ref[
                place, pl.ds(sub, tiles, stride=4), :
            ][:, :width]
    taps = unit_ref[0, PIN : PIN + taps_ref.shape[1], :]
    spread_rows(taps, taps_ref)
    for layer_at in range(BLOCKS):
        for quarter in range(FF // C):
            for place, lane, width in lane_parts(C):
                begin = quarter * C + lane
                kern_ref[layer_at, :, begin : begin + width] = taps_ref[
                    place, pl.ds(layer_at * (used // BLOCKS) + quarter, 9, stride=FF // C), :
                ][:, :width]

    resid_ref[...] = norm_rows(pre_ref[...], gains_ref[0:1, :], gains_ref[1:2, :])[2]


def embed_forward(patches, halo, units, gains):
    rows = patches.shape[0] + halo.shape[0]
    wide = jax.ShapeDtypeStruct((rows, C), jnp.float32)
    taps = jax.ShapeDtypeStruct((BLOCKS, 9, FF), jnp.float32)
    return pl.pallas_call(
        embed_forward_kernel,
        grid=(1,),
        out_shape=(wide, wide, taps),
        in_specs=[whole(patches.shape), whole(halo.shape), unit_spec(0), whole((2, C))],
        out_specs=(whole(wide.shape), whole(wide.shape), whole(taps.shape)),
        scratch_shapes=[
            pltpu.VMEM((3, rows, LANES), jnp.float32),
            pltpu.VMEM((3, FF - PIN, LANES), jnp.float32),
        ],
        compiler_params=pltpu.CompilerParams(vmem_limit_bytes=VMEM_LIMIT),
        cost_estimate=pl.CostEstimate(flops=10**9, bytes_accessed=8 * 10**6, transcendentals=0),
        name="embed_forward",
    )(patches, halo, units, gains)


def embed_backward_kernel(
    grad_ref, pre_ref, gains_ref, patches_ref, halo_ref, *refs
):
    taps_refs = refs[:BLOCKS]
    unit_ref, dgain_ref, planes_ref, turned_ref, taps_ref = refs[BLOCKS:]
    rows = pre_ref.shape[0]
    tiles = rows // 4
    half = tiles // 2
    used = FF * 9 * BLOCKS // C
    sums = [jnp.zeros((1, C), jnp.float32)] * 2
    for sub in range(4):
        for part_at in range(2):
            span = slice(sub * tiles + part_at * half, sub * tiles + (part_at + 1) * half)
            unit, inverse, _ = norm_rows(pre_ref[span, :], gains_ref[0:1, :], gains_ref[1:2, :])
            grad = grad_ref[span, :]
            back = norm_rows_back(unit, inverse, gains_ref[0:1, :], grad)
            sums[0] = sums[0] + jnp.sum(grad * unit, 0, keepdims=True)
            sums[1] = sums[1] + jnp.sum(grad, 0, keepdims=True)
            for place, lane, width in lane_parts(C):
                value = back[:, lane : lane + width]
                if width < LANES:
                    value = jnp.concatenate([value, jnp.zeros((half, LANES - width), jnp.float32)], 1)
                planes_ref[place, pl.ds(4 * part_at * half + sub, half, stride=4), :] = value
    dgain_ref[0:1, :] = sums[0]
    dgain_ref[1:2, :] = sums[1]
    for place, lane, width in lane_parts(C):
        turned_ref[lane : lane + width, :] = planes_ref[place].T[:width, :].astype(jnp.bfloat16)
    split = patches_ref.shape[0]
    grads = product(turned_ref[:, :split], patches_ref[...]) + product(turned_ref[:, split:], halo_ref[...])
    unit_ref[0, :PIN, :] = grads.T.astype(jnp.bfloat16)
    taps_ref[...] = jnp.zeros_like(taps_ref)
    for layer_at, ref in enumerate(taps_refs):
        for quarter in range(FF // C):
            for place, lane, width in lane_parts(C):
                begin = quarter * C + lane
                value = ref[:, begin : begin + width]
                if width < LANES:
                    value = jnp.concatenate([value, jnp.zeros((9, LANES - width), jnp.float32)], 1)
                taps_ref[place, pl.ds(layer_at * (used // BLOCKS) + quarter, 9, stride=FF // C), :] = value
    for place, lane, width in lane_parts(C):
        unit_ref[0, PIN:, lane : lane + width] = taps_ref[place, :, :width].astype(jnp.bfloat16)


def embed_backward(grad, pre, gains, patches, halo, taps):
    rows = pre.shape[0]
    shapes = (jax.ShapeDtypeStruct((1, FF, C), jnp.bfloat16), jax.ShapeDtypeStruct((2, C), jnp.float32))
    operands = (grad, pre, gains, patches, halo, *taps)
    return pl.pallas_call(
        embed_backward_kernel,
        grid=(1,),
        out_shape=shapes,
        in_specs=[whole(part.shape) for part in operands],
        out_specs=tuple(whole(shape.shape) for shape in shapes),
        scratch_shapes=[
            pltpu.VMEM((3, rows, LANES), jnp.float32),
            pltpu.VMEM((C, rows), jnp.bfloat16),
            pltpu.VMEM((3, FF - PIN, LANES), jnp.float32),
        ],
        compiler_params=pltpu.CompilerParams(vmem_limit_bytes=VMEM_LIMIT),
        cost_estimate=pl.CostEstimate(flops=10**9, bytes_accessed=8 * 10**6, transcendentals=0),
        name="embed_backward",
    )(*operands)


def head_kernel(
    resid_ref, gains_ref, weight_ref, label_ref, keep_ref, total_ref,
    grad_ref, dhead_ref, dgain_ref, loss_ref,
    final_ref, turned_ref,
):
    rows = resid_ref.shape[0]
    tiles = rows // 4
    classes = weight_ref.shape[1]
    low = weight_ref[...].astype(jnp.bfloat16)
    share = 1.0 / total_ref[0:1, 0:1]
    sums = [jnp.zeros((1, C), jnp.float32)] * 2
    loss = jnp.zeros((1, 1), jnp.float32)
    for sub in range(4):
        span = slice(sub * tiles, (sub + 1) * tiles)
        unit, inverse, final = norm_rows(resid_ref[span, :], gains_ref[0:1, :], gains_ref[1:2, :])
        final = final.astype(jnp.bfloat16)
        final_ref[span, :] = final
        logits = product(final, low)
        peak = jnp.max(logits, -1, keepdims=True)
        log_norm = peak + jnp.log(jnp.sum(jnp.exp(logits - peak), -1, keepdims=True))
        keep = keep_ref[span, :]
        hit = lax.broadcasted_iota(jnp.int32, (tiles, classes), 1) == label_ref[span, :]
        picked = jnp.sum(jnp.where(hit, logits, 0.0), -1, keepdims=True)
        loss = loss + jnp.sum((log_norm - picked) * keep, 0, keepdims=True)
        dlogits = (jnp.exp(logits - log_norm) - jnp.where(hit, 1.0, 0.0)) * (keep * share)
        turned_ref[:, span] = dlogits.T.astype(jnp.bfloat16)
        grad = back_product(dlogits.astype(jnp.bfloat16), low)
        grad_ref[span, :] = norm_rows_back(unit, inverse, gains_ref[0:1, :], grad)
        sums[0] = sums[0] + jnp.sum(grad * unit, 0, keepdims=True)
        sums[1] = sums[1] + jnp.sum(grad, 0, keepdims=True)
    dhead_ref[:classes, :] = product(turned_ref[...], final_ref[...])
    dhead_ref[classes:, :] = jnp.zeros((dhead_ref.shape[0] - classes, C), jnp.float32)
    dgain_ref[0:1, :] = sums[0]
    dgain_ref[1:2, :] = sums[1]
    loss_ref[...] = jnp.broadcast_to(loss, (1, C))


def head_step(resid, gains, weight, labels, keep, total):
    rows = resid.shape[0]
    classes = weight.shape[1]
    wide = jnp.float32
    shapes = (
        jax.ShapeDtypeStruct((rows, C), wide),
        jax.ShapeDtypeStruct((-(-classes // 8) * 8, C), wide),
        jax.ShapeDtypeStruct((2, C), wide),
        jax.ShapeDtypeStruct((1, C), wide),
    )
    operands = (resid, gains, weight, labels, keep, total)
    return pl.pallas_call(
        head_kernel,
        grid=(1,),
        out_shape=shapes,
        in_specs=[whole(part.shape) for part in operands],
        out_specs=tuple(whole(shape.shape) for shape in shapes),
        scratch_shapes=[
            pltpu.VMEM((rows, C), jnp.bfloat16),
            pltpu.VMEM((classes, rows), jnp.bfloat16),
        ],
        compiler_params=pltpu.CompilerParams(vmem_limit_bytes=VMEM_LIMIT),
        cost_estimate=pl.CostEstimate(flops=10**9, bytes_accessed=5 * 10**6, transcendentals=10**6),
        name="head_step",
    )(*operands)


def attention_backward_kernel(
    advance,
    grad_ref, resid_ref, gains_ref, unit_ref, reduce_ref, bias_ref,
    normed_ref, query_ref, reduced_ref, key_ref, value_ref, attended_ref, kv_ref,
    out_ref, dunits_ref, dgain_ref,
    turned_ref, datt_ref, dquery_ref, dkey_ref, dvalue_ref, first_ref, planes_ref,
):
    rows = resid_ref.shape[0]
    tiles = rows // 4
    low_type = jnp.bfloat16
    advance(0)
    datt_ref[:, C:] = jnp.zeros((rows, WIDE - C), low_type)
    turned_ref[...] = grad_ref[...].astype(low_type).T
    dunits_ref[0, C : 2 * C, :] = product(turned_ref[...], attended_ref[:, :C]).T.astype(low_type)
    for sub in range(4):
        span = slice(sub * tiles, (sub + 1) * tiles)
        datt_ref[span, :C] = back_product(grad_ref[span, :].astype(low_type), unit_ref[0, C : 2 * C, :]).astype(low_type)
    dkey_ref[...] = jnp.zeros_like(dkey_ref)
    dvalue_ref[...] = jnp.zeros_like(dvalue_ref)
    blocks = bias_ref.shape[0]

    def one_block(step):
        index = blocks - 1 - step
        start, low = place_of(index, tiles)
        bias = bias_ref[index]
        tile_at = lax.rem(lax.broadcasted_iota(jnp.int32, (4 * BLOCK_TILES, LANES), 0), BLOCK_TILES)
        fresh = tile_at >= index * BLOCK_TILES - start
        span = pl.ds(low, KEY_SPAN)
        for group in range(3):
            lanes = slice(group * LANES, (group + 1) * LANES)
            query = four_planes(query_ref, start, lanes)
            datt = four_planes(datt_ref, start, lanes)
            datt = jnp.where(fresh, datt, jnp.zeros_like(datt))
            keys = head_pair(key_ref[span, lanes], group)
            values = head_pair(value_ref[span, lanes], group)
            probs = softmax_columns(back_product(keys, query), bias)
            dprobs = back_product(values, datt)
            dscores = []
            for half, prob in enumerate(probs):
                dprob = dprobs[half * KEY_SPAN : (half + 1) * KEY_SPAN]
                inner = jnp.sum(prob * dprob, 0, keepdims=True)
                dscores.append(prob * (dprob - inner) * HD ** (-0.5))
            dscores = jnp.concatenate(dscores, 0)
            probs = jnp.concatenate(probs, 0).astype(low_type)
            dscores = dscores.astype(low_type)
            dquery = product(dscores.T, keys)
            put_planes(dquery_ref, start, lanes, dquery.astype(low_type))
            dkeys = product(dscores, query)
            dvalues = product(probs, datt)
            if group < 2:
                first = lax.broadcasted_iota(jnp.int32, (KEY_SPAN, LANES), 1) < HD
                dkeys = jnp.where(first, dkeys[:KEY_SPAN], dkeys[KEY_SPAN:])
                dvalues = jnp.where(first, dvalues[:KEY_SPAN], dvalues[KEY_SPAN:])
            dkey_ref[span, lanes] += dkeys
            dvalue_ref[span, lanes] += dvalues

    pl.loop(0, blocks // 2, unroll=blocks // 2)(one_block)
    advance(1)
    pl.loop(blocks // 2, blocks, unroll=blocks - blocks // 2)(one_block)
    unit, inverse, normed = norm_rows(reduced_ref[...], gains_ref[2:3, :], gains_ref[3:4, :])
    normed_t = normed.T.astype(low_type)
    dkeys = dkey_ref[:, :C].astype(low_type)
    dvalues = dvalue_ref[:, :C].astype(low_type)
    for which, grads in enumerate((dkeys, dvalues)):
        dweight = product(normed_t, grads)
        for at, lane, width in lane_parts(C):
            part = dweight[:, lane : lane + width]
            if width < LANES:
                part = jnp.concatenate([part, jnp.zeros((C, LANES - width), jnp.float32)], 1)
            planes_ref[at, pl.ds(which, C, stride=2), :] = part
    for at, lane, width in lane_parts(C):
        dunits_ref[0, 2 * C :, lane : lane + width] = planes_ref[at, :, :width].astype(low_type)
    dnormed = back_product(dkeys, kv_ref[0]) + back_product(dvalues, kv_ref[1])
    dgain_ref[2:3, :] = jnp.sum(dnormed * unit, 0, keepdims=True)
    dgain_ref[3:4, :] = jnp.sum(dnormed, 0, keepdims=True)
    dreduced = norm_rows_back(unit, inverse, gains_ref[2:3, :], dnormed).astype(low_type)
    advance(2)
    turned_ref[...] = normed_ref[...].T
    dunits_ref[0, :C, :] = product(turned_ref[...], dquery_ref[:, :C]).astype(low_type)
    for sub in range(4):
        span = slice(sub * tiles, (sub + 1) * tiles)
        part = slice(sub * C, (sub + 1) * C)
        dunits_ref[1, part, :] = outer_sum(normed_ref[span, :], dreduced).astype(low_type)
        first_ref[span, :] = back_product(
            dquery_ref[span, :C], unit_ref[0, :C, :]
        ) + back_product(dreduced, reduce_ref[0, part, :])

    grad = first_ref[...]
    unit, inverse, _ = norm_rows(resid_ref[...], gains_ref[0:1, :], gains_ref[1:2, :])
    out_ref[...] = grad_ref[...] + norm_rows_back(unit, inverse, gains_ref[0:1, :], grad)
    dgain_ref[0:1, :] = jnp.sum(grad * unit, 0, keepdims=True)
    dgain_ref[1:2, :] = jnp.sum(grad, 0, keepdims=True)


def attention_backward(grad, resid, gains, units, at, reduces, reduce_at, bias, kept, plans, meeting):
    rows = resid.shape[0]
    tiles = rows // 4
    low = jnp.bfloat16
    shapes = (
        jax.ShapeDtypeStruct((rows, C), jnp.float32),
        jax.ShapeDtypeStruct((2, FF, C), low),
        jax.ShapeDtypeStruct((4, C), jnp.float32),
    )
    count = len(plans)

    def run(*refs):
        own_in, ride_in = refs[:13], refs[13 : 13 + count]
        own_out, ride_out = refs[13 + count : 16 + count], refs[16 + count : 16 + 2 * count]
        rest = refs[16 + 2 * count :]
        rides = rides_of(plans, ride_in, ride_out, rest[7:])
        rides.signal()
        attention_backward_kernel(rides.advance, *own_in, *own_out, *rest[:7])
        for phase in range(3, rides.phases + 1):
            rides.advance(phase)

    return pl.pallas_call(
        run,
        grid=(1,),
        out_shape=shapes + tuple(plan.out for plan in plans),
        in_specs=[
            whole((rows, C)),
            whole((rows, C)),
            whole((4, C)),
            unit_spec(at),
            unit_spec(reduce_at),
            whole(bias.shape),
        ]
        + [whole(part.shape) for part in kept]
        + [plan.in_spec for plan in plans],
        out_specs=tuple(whole(shape.shape) for shape in shapes) + tuple(plan.out_spec for plan in plans),
        scratch_shapes=[
            pltpu.VMEM((C, rows), low),
            pltpu.VMEM((rows, WIDE), low),
            pltpu.VMEM((rows, WIDE), low),
            pltpu.VMEM((tiles, WIDE), jnp.float32),
            pltpu.VMEM((tiles, WIDE), jnp.float32),
            pltpu.VMEM((rows, C), jnp.float32),
            pltpu.VMEM((3, 2 * C, LANES), jnp.float32),
        ]
        + sum([plan.scratch for plan in plans], []),
        compiler_params=pltpu.CompilerParams(collective_id=meeting, has_side_effects=True, vmem_limit_bytes=VMEM_LIMIT),
        cost_estimate=pl.CostEstimate(flops=12 * 10**9, bytes_accessed=18 * 10**6, transcendentals=10**6),
        name="attention_backward",
    )(grad, resid, gains, units, reduces, bias, *kept, *[plan.value for plan in plans])


BOTH = ("grp", "tok")


def axis_bits(axis):
    count = lax.axis_size(axis)
    return [1 << place for place in reversed(range(count.bit_length() - 1))]


def bit_order():
    tok_bits = axis_bits("tok")
    return [("grp", bit) for bit in axis_bits("grp")] + [("tok", bit) for bit in tok_bits]


MESH = pl.DeviceIdType.MESH


def exchange_setup():
    grp, tok = lax.axis_index("grp"), lax.axis_index("tok")
    n_tok = lax.axis_size("tok")
    peers = [(lax.bitwise_xor(grp, bit), tok) for bit in axis_bits("grp")]
    peers += [(grp, lax.bitwise_xor(tok, step)) for step in range(1, n_tok)]
    return (grp, tok, n_tok, peers)


def signal_all(peers):
    barrier = pltpu.get_barrier_semaphore()
    for peer in peers:
        pl.semaphore_signal(barrier, inc=1, device_id=peer, device_id_type=MESH)


def greet(peers):
    signal_all(peers)
    pl.semaphore_wait(pltpu.get_barrier_semaphore(), len(peers))


def send(source, target, sems, at, peer):
    copy = pltpu.make_async_remote_copy(
        src_ref=source,
        dst_ref=target,
        send_sem=sems[0].at[at],
        recv_sem=sems[1].at[at],
        device_id=peer,
        device_id_type=MESH,
    )
    copy.start()
    return copy


def gather_view(ref, unit, place, done):
    index = [slice(None) if name in done else place(name) for name in bit_order()]
    return ref.at[tuple([unit] + index)]


class GatherRide:
    def __init__(self, full_ref, scratch):
        self.grp, self.tok = lax.axis_index("grp"), lax.axis_index("tok")
        self.phases = len(bit_order())
        self.names = bit_order()
        self.full_ref = full_ref
        self.sems = scratch[:2]

    def order(self, unit):
        grp_bits = [("grp", bit) for bit in axis_bits("grp")]
        flip = grp_bits[::-1] if unit % 2 else grp_bits
        return [("tok", bit) for bit in axis_bits("tok")[:-1]] + flip + [("tok", 1)]

    def place(self, name):
        return (self.grp if name[0] == "grp" else self.tok) // name[1] % 2

    def partner(self, name):
        axis, bit = name
        if axis == "grp":
            return (lax.bitwise_xor(self.grp, bit), self.tok)
        return (self.grp, lax.bitwise_xor(self.tok, bit))

    def copy(self, unit, phase):
        order = self.order(unit)
        held = gather_view(self.full_ref, unit, self.place, order[:phase])
        at = phase * self.full_ref.shape[0] + unit
        return pltpu.make_async_remote_copy(
            src_ref=held,
            dst_ref=held,
            send_sem=self.sems[0].at[at],
            recv_sem=self.sems[1].at[at],
            device_id=self.partner(order[phase]),
            device_id_type=MESH,
        )

    def put(self, unit, value):
        self.full_ref[(unit,) + tuple(self.place(name) for name in bit_order())] = value

    def advance(self, phase):
        for unit in range(self.full_ref.shape[0]):
            if phase:
                self.copy(unit, phase - 1).wait()
            if phase < self.phases:
                self.copy(unit, phase).start()


def gather_scratch(total):
    phases = len(bit_order())
    return [pltpu.SemaphoreType.DMA((phases * total,))] * 2


def slot_numbers(owner_ref, slot_rows):
    owners = [owner_ref[unit] for unit in range(owner_ref.shape[0])]
    slots = []
    for unit, owner in enumerate(owners):
        rank = jnp.int32(0)
        for earlier in owners[:unit]:
            rank = rank + (earlier == owner).astype(jnp.int32)
        slots.append(owner * slot_rows + rank)
    return slots


def start_kernel(
    owner_ref, piece_ref, count_ref, patch_ref, mark_ref,
    full_ref, later_ref, total_ref, patch_halo_ref, mark_halo_ref,
    recv_ref, near_s, near_r, halo_s, halo_r, *scratch,
):
    grp, tok, n_tok, peers = exchange_setup()
    slot_rows = piece_ref.shape[1]
    units, first = owner_ref.shape[0], full_ref.shape[0]
    slots = slot_numbers(owner_ref, slot_rows)
    gather = GatherRide(full_ref, scratch[:2])
    count = SumRide(count_ref, total_ref, scratch[2:])
    greet(peers)
    copies = []
    for step in range(1, n_tok):
        peer = lax.bitwise_xor(tok, step)
        landing = recv_ref.at[pl.ds(tok * slot_rows, slot_rows)]
        copies.append(send(piece_ref.at[peer], landing, (near_s, near_r), step, (grp, peer)))
    recv_ref[pl.ds(tok * slot_rows, slot_rows)] = piece_ref[tok]
    count.advance(0)
    for copy in copies:
        copy.wait()
    for unit in range(first):
        gather.put(unit, recv_ref[slots[unit]])
    gather.advance(0)
    before = (grp, lax.rem(tok + n_tok - 1, n_tok))
    mark_copy = send(mark_ref, mark_halo_ref, (halo_s, halo_r), 0, before)
    patch_copy = send(patch_ref.at[pl.ds(0, patch_halo_ref.shape[0])], patch_halo_ref, (halo_s, halo_r), 1, before)
    for unit in range(first, units):
        later_ref[unit - first] = recv_ref[slots[unit]]
    for phase in range(1, gather.phases + 1):
        count.advance(phase)
        gather.advance(phase)
    total_ref[...] = jnp.broadcast_to(
        jnp.sum(jnp.sum(total_ref[...], 0, keepdims=True), 1, keepdims=True), total_ref.shape
    )
    mark_copy.wait()
    patch_copy.wait()


def start_exchange(owners, pieces, count, patches, marks, first):
    n_tok, slot_rows, chunk, width = pieces.shape
    phases = len(bit_order())
    units = owners.shape[0]
    vmem = pl.BlockSpec(memory_space=pltpu.VMEM)
    full_shape = (first,) + (2,) * phases + (chunk, width)
    return pl.pallas_call(
        start_kernel,
        out_shape=(
            jax.ShapeDtypeStruct(full_shape, pieces.dtype),
            jax.ShapeDtypeStruct((units - first, chunk, width), pieces.dtype),
            jax.ShapeDtypeStruct(count.shape, count.dtype),
            jax.ShapeDtypeStruct((OVER, patches.shape[1]), patches.dtype),
            jax.ShapeDtypeStruct(marks.shape, marks.dtype),
        ),
        in_specs=[pl.BlockSpec(memory_space=pltpu.SMEM), vmem, vmem, pl.BlockSpec(memory_space=pl.ANY), vmem],
        out_specs=(vmem, vmem, vmem, pl.BlockSpec(memory_space=pl.ANY), vmem),
        scratch_shapes=[
            pltpu.VMEM((n_tok * slot_rows, chunk, width), pieces.dtype),
            pltpu.SemaphoreType.DMA((n_tok,)),
            pltpu.SemaphoreType.DMA((n_tok,)),
            pltpu.SemaphoreType.DMA((2,)),
            pltpu.SemaphoreType.DMA((2,)),
        ]
        + gather_scratch(first)
        + sum_scratch(count.shape),
        compiler_params=pltpu.CompilerParams(collective_id=0, has_side_effects=True, vmem_limit_bytes=VMEM_LIMIT),
        name="start_exchange",
    )(owners, pieces, count, patches, marks)


def unit_order(unit):
    grp_bits = [("grp", bit) for bit in axis_bits("grp")]
    if unit % 2:
        grp_bits = grp_bits[::-1]
    return [("tok", 1)] + grp_bits + [("tok", bit) for bit in axis_bits("tok")[:-1][::-1]]


def unit_layout(order):
    left = bit_order()
    shapes = []
    for name in order:
        at = left.index(name)
        shapes.append((1 << at, 2, 1 << (len(left) - 1 - at)))
        left.remove(name)
    return shapes


SPLIT = 3


class UnitRide:
    def __init__(self, sources, out_ref, scratch, begin=0, end=None, base=0):
        self.grp, self.tok = lax.axis_index("grp"), lax.axis_index("tok")
        self.begin = begin
        self.end = len(bit_order()) if end is None else end
        self.phases = self.end - begin
        self.names = unit_order(0)[self.begin : self.end]
        self.sources = sources
        self.out_ref, self.base = out_ref, base
        self.sems = scratch[:2]
        self.buffers = scratch[2:]

    def partner(self, name):
        axis, bit = name
        if axis == "grp":
            return (lax.bitwise_xor(self.grp, bit), self.tok)
        return (self.grp, lax.bitwise_xor(self.tok, bit))

    def half_of(self, name):
        return (self.grp if name[0] == "grp" else self.tok) // name[1] % 2

    def before(self, unit, phase):
        if phase == 0:
            ref, at = self.sources[unit]
            return ref.at[at]
        return self.buffers[unit * 2 * self.phases + 2 * (phase - 1) + 1]

    def landing(self, unit, phase):
        return self.buffers[unit * 2 * self.phases + 2 * phase]

    def copy(self, unit, phase):
        name = unit_order(unit)[self.begin + phase]
        at = phase * len(self.sources) + unit
        return pltpu.make_async_remote_copy(
            src_ref=self.before(unit, phase).at[:, 1 - self.half_of(name)],
            dst_ref=self.landing(unit, phase),
            send_sem=self.sems[0].at[at],
            recv_sem=self.sems[1].at[at],
            device_id=self.partner(name),
            device_id_type=MESH,
        )

    def finish(self, unit, phase):
        order = unit_order(unit)
        shapes = unit_layout(order)
        self.copy(unit, phase).wait()
        outer, _, inner = shapes[self.begin + phase]
        source, landed = self.before(unit, phase), self.landing(unit, phase)
        mine = self.half_of(order[self.begin + phase])
        target = self.out_ref.at[self.base + unit]
        if phase + 1 < self.phases:
            target = self.before(unit, phase + 1)
        whole_done = self.begin + phase + 1 == len(order)
        if not whole_done:
            low = shapes[self.begin + phase + 1][2]

        @pl.loop(0, outer * inner, unroll=min(4, outer * inner))
        def _(at):
            value = source[at // inner, mine, at % inner] + landed[at // inner, at % inner]
            if whole_done:
                target[...] = value
            else:
                target[at // (2 * low), at // low % 2, at % low] = value

    def advance(self, phase):
        for unit in range(len(self.sources)):
            if phase:
                self.finish(unit, phase - 1)
            if phase < self.phases:
                self.copy(unit, phase).start()


def unit_scratch(total, chunk, width, begin=0, end=None):
    end = len(bit_order()) if end is None else end
    dma = pltpu.SemaphoreType.DMA
    buffers = [dma(((end - begin) * total,)), dma(((end - begin) * total,))]
    for unit in range(total):
        shapes = unit_layout(unit_order(unit))
        for phase in range(begin, end):
            outer, _, inner = shapes[phase]
            buffers.append(pltpu.VMEM((outer, inner, chunk, width), jnp.bfloat16))
            following = shapes[phase + 1] if phase + 1 < end else (1, 1, 1)
            buffers.append(pltpu.VMEM(following + (chunk, width), jnp.bfloat16))
    return buffers


def unit_blocks(units):
    chunk = units.shape[1] >> len(bit_order())
    return units.reshape((units.shape[0],) + unit_layout(unit_order(0))[0] + (chunk, units.shape[2]))


class SumRide:
    def __init__(self, source_ref, total_ref, scratch, begin=0, end=None):
        self.grp, self.tok = lax.axis_index("grp"), lax.axis_index("tok")
        self.order = unit_order(0)[begin:end]
        self.names = self.order
        self.phases = len(self.order)
        self.source_ref, self.total_ref = source_ref, total_ref
        self.sums = scratch[2]
        self.sems = scratch[:2]

    partner = UnitRide.partner

    def copy(self, phase):
        return pltpu.make_async_remote_copy(
            src_ref=self.sums.at[2 * phase],
            dst_ref=self.sums.at[2 * phase + 1],
            send_sem=self.sems[0].at[phase],
            recv_sem=self.sems[1].at[phase],
            device_id=self.partner(self.order[phase]),
            device_id_type=MESH,
        )

    def advance(self, phase):
        if phase == 0:
            self.sums[0] = self.source_ref[...].astype(self.sums.dtype)
        else:
            self.copy(phase - 1).wait()
            self.sums[2 * phase] = self.sums[2 * phase - 2] + self.sums[2 * phase - 1]
        if phase < self.phases:
            self.copy(phase).start()
        else:
            self.total_ref[...] = self.sums[2 * phase].astype(self.total_ref.dtype)


def sum_scratch(shape, dtype=jnp.float32):
    phases = len(bit_order())
    dma = pltpu.SemaphoreType.DMA
    return [dma((phases,)), dma((phases,)), pltpu.VMEM((2 * phases + 1,) + shape, dtype)]


def tail_kernel(counts, rows, *refs):
    owner_ref, early_ref, part_ref = refs[:3]
    blocks, refs = refs[3 : 3 + len(counts)], refs[3 + len(counts) :]
    small_refs, refs = refs[: len(rows)], refs[len(rows) :]
    owned_ref, small_out_ref, chunk_ref, place_ref, near_s, near_r, small_ref = refs[:7]
    scratch = refs[7:]
    sources = [(ref, at) for ref, count in zip(blocks, counts) for at in range(count)]
    total = len(sources)
    parts = part_ref.shape[0]
    grp, tok, n_tok, peers = exchange_setup()
    signal_all(peers)
    begin = 0
    for ref, count in zip(small_refs, rows):
        small_ref[begin : begin + count, :] = ref[...]
        begin += count
    small_ref[begin:, :] = jnp.zeros((small_ref.shape[0] - begin, C), jnp.float32)
    cut = 3 + 2 + 2 * total * len(bit_order())
    rides = Rides(
        [
            UnitRide(sources, chunk_ref, scratch[3:cut]),
            SumRide(small_ref, small_out_ref, scratch[:3]),
            UnitRide([(part_ref, at) for at in range(parts)], chunk_ref, scratch[cut:], SPLIT, None, total),
        ]
    )
    rides.peers = peers
    for phase in range(rides.phases + 1):
        rides.advance(phase)
    total += parts
    for at in range(early_ref.shape[0]):
        chunk_ref[total + at] = early_ref[at]
    last = total + early_ref.shape[0]
    chunk_ref[last] = jnp.zeros(chunk_ref.shape[1:], chunk_ref.dtype)
    slot_rows = owned_ref.shape[1]
    slots = slot_numbers(owner_ref, slot_rows)

    @pl.loop(0, n_tok * slot_rows)
    def _(at):
        unit_at = jnp.int32(last)
        for unit, slot in enumerate(slots):
            unit_at = jnp.where(slot == at, unit, unit_at)
        place_ref[at // slot_rows, at % slot_rows] = chunk_ref[unit_at]

    copies = []
    for step in range(1, n_tok):
        peer = lax.bitwise_xor(tok, step)
        copies.append(send(place_ref.at[peer], owned_ref.at[tok], (near_s, near_r), step, (grp, peer)))
    owned_ref[tok] = place_ref[tok]
    for copy in copies:
        copy.wait()


def tail_exchange(owners, slot_rows, early, part, sources, smalls, n_tok):
    chunk, width = early.shape[1:]
    counts = tuple(source.shape[0] for source in sources)
    rows = tuple(small.shape[0] for small in smalls)
    total = sum(counts)
    low = early.dtype
    vmem = pl.BlockSpec(memory_space=pltpu.VMEM)
    dma = pltpu.SemaphoreType.DMA
    small = (-(-sum(rows) // 8) * 8, C)
    return pl.pallas_call(
        lambda *refs: tail_kernel(counts, rows, *refs),
        out_shape=(
            jax.ShapeDtypeStruct((n_tok, slot_rows, chunk, width), low),
            jax.ShapeDtypeStruct(small, jnp.float32),
        ),
        in_specs=[pl.BlockSpec(memory_space=pltpu.SMEM)] + [vmem] * (2 + len(sources) + len(smalls)),
        out_specs=(vmem, vmem),
        scratch_shapes=[
            pltpu.VMEM((total + part.shape[0] + early.shape[0] + 1, chunk, width), low),
            pltpu.VMEM((n_tok, slot_rows, chunk, width), low),
            dma((n_tok,)),
            dma((n_tok,)),
            pltpu.VMEM(small, jnp.float32),
        ]
        + sum_scratch(small)
        + unit_scratch(total, chunk, width)
        + unit_scratch(part.shape[0], chunk, width, SPLIT),
        compiler_params=pltpu.CompilerParams(collective_id=1, has_side_effects=True, vmem_limit_bytes=VMEM_LIMIT),
        name="tail_exchange",
    )(owners, early, part, *[unit_blocks(source) for source in sources], *smalls)


def body(
    patches,
    labels,
    valid_mask,
    crop_counts,
    owners,
    slot_weight,
    slot_moment,
    slot_second,
    norm_params,
    norm_moment,
    norm_second,
    head_weight,
    head_moment,
    head_second,
):
    tok_dev = patches.shape[0]
    n_tok = lax.axis_size("tok")
    n_grp = lax.axis_size("grp")
    tok_index = lax.axis_index("tok")
    group_tok = tok_dev * n_tok
    counts = crop_counts[0]
    n_unit = owners.shape[0]
    slot_rows, columns = slot_weight.shape
    chunk = columns // n_tok // C
    first_tok = tok_index * tok_dev
    small_end = counts[0] * BIG_SIDE**2 + counts[1] * SMALL_SIDE**2
    counted = valid_mask * (first_tok + jnp.arange(tok_dev, dtype=jnp.int32) < small_end)
    counted = counted.astype(jnp.float32).reshape(-1, LANES)
    pieces = slot_weight.astype(jnp.bfloat16).reshape(slot_rows, n_tok, chunk, C).transpose(1, 0, 2, 3)
    first_units = 1 + 2 * (n_unit // BLOCKS)
    marks = jnp.stack([labels, valid_mask])
    own, later, counted, patch_halo, mark_halo = start_exchange(
        owners, pieces, counted, patches, marks[:, :OVER], first_units
    )
    pixel_total = counted[0, 0]
    own = own.reshape(first_units, FF, C)
    units = lax.all_gather(later, BOTH, axis=1, tiled=True)
    layers = [
        ((own, 1, own, 2), (own, 3)),
        ((own, 5, own, 6), (own, 7)),
        ((units, 0, units, 1), (units, 2)),
    ]

    window = tok_dev + OVER
    tiles = window // 4
    marks = jnp.concatenate([marks, mark_halo], 1)
    marks = marks.reshape(2, tiles, 4).transpose(0, 2, 1).reshape(2, window)
    labels = marks[0]
    positions = first_tok + 4 * jnp.arange(tiles, dtype=jnp.int32)
    begin_at, half_side, tile_y, tile_x, is_real = image_layout(positions, counts)
    own_image = (begin_at >= first_tok) & (begin_at < first_tok + tok_dev) & (positions < group_tok)
    stacks = shift_stacks(half_side, tile_y, tile_x, is_real)

    def image_at(tile):
        at = first_tok + 4 * tile
        return jnp.where(at < group_tok, image_layout(at, counts)[0], -1)

    bias = block_bias(tiles, image_at)
    real_rows = jnp.broadcast_to(is_real.astype(jnp.float32)[:, None], (tiles, LANES))
    keep_mask = marks[1].astype(jnp.float32) * jnp.tile((own_image & is_real).astype(jnp.float32), 4)
    tail = 6 * BLOCKS
    embed_pre, resid, kernels = embed_forward(patches, patch_halo, own, norm_params[tail : tail + 2])
    kept_all = []
    for layer_at in range(BLOCKS):
        attn_units, mlp_units = layers[layer_at]
        at = 6 * layer_at
        middle, *attn_kept = attention_forward(resid, norm_params[at : at + 4], *attn_units, bias)
        output, *mlp_kept = mlp_forward(
            middle, norm_params[at + 4 : at + 6], *mlp_units, kernels, layer_at, stacks, real_rows,
        )
        w_up = mlp_kept.pop()
        kept_all.append((resid, attn_kept, middle, mlp_kept, w_up))
        resid = output
    grad_res, d_head, final_gains, loss_row = head_step(
        resid, norm_params[tail + 2 : tail + 4], head_weight, labels[:, None], keep_mask[:, None], counted
    )
    unit_plans = []
    head_cuts = [0, SPLIT, len(bit_order())]
    early = []
    kernel_grads = [None] * BLOCKS
    gain_grads = []
    phases = len(bit_order())

    def head_plans(value):
        if len(head_cuts) < 2:
            return []
        begin = head_cuts.pop(0)
        return [plan_sum(value, begin, head_cuts[0])]

    for layer_at in reversed(range(BLOCKS)):
        attn_units, mlp_units = layers[layer_at]
        at = 6 * layer_at
        entry, attn_kept, middle, mlp_kept, w_up = kept_all[layer_at]
        grad_res, mlp_grads, kernel_grads[layer_at], mlp_gains, *ridden_out = mlp_backward(
            grad_res, middle, norm_params[at + 4 : at + 6], w_up, *mlp_units, kernels, layer_at,
            stacks, real_rows, mlp_kept, unit_plans + head_plans(d_head), 2 + layer_at,
        )
        if layer_at + 1 == BLOCKS:
            d_head = ridden_out.pop()
        unit_plans = [plan_units(mlp_grads, 0, SPLIT)]
        if ridden_out:
            early.insert(0, ridden_out[1])
            unit_plans.append(plan_units(ridden_out[0], SPLIT, phases))
        plans = unit_plans + head_plans(d_head)
        grad_res, attn_grads, attn_gains, *ridden_out = attention_backward(
            grad_res, entry, norm_params[at : at + 4], *attn_units, bias, attn_kept, plans, 2 + BLOCKS + layer_at
        )
        if len(plans) > len(unit_plans):
            d_head = ridden_out.pop()
        if layer_at + 1 < BLOCKS:
            early.insert(0, ridden_out[1])
        unit_plans = [plan_units(attn_grads, 0, SPLIT), plan_units(ridden_out[0], SPLIT, phases)]
        gain_grads = [attn_gains, mlp_gains] + gain_grads
    head_total = d_head[: head_weight.shape[1]].T
    part = ridden_out[0]
    first_grad, embed_gains = embed_backward(
        grad_res, embed_pre, norm_params[tail : tail + 2], patches, patch_halo, kernel_grads
    )
    early = jnp.concatenate(early, 0)
    smalls = gain_grads + [embed_gains, final_gains, loss_row]
    owned, small = tail_exchange(owners, slot_rows, early, part, [first_grad, attn_grads], smalls, n_tok)
    owned = owned.transpose(1, 0, 2, 3).astype(jnp.float32).reshape(slot_rows, columns)
    norm_rows_all = norm_params.shape[0]
    norm_total, loss_sum = (small[:norm_rows_all], small[norm_rows_all, 0])
    slot_m, slot_v, slot_w = adamw_step(
        slot_weight, slot_moment, slot_second, owned, RATE_MATRIX, DECAY_RATE
    )
    norm_m, norm_v, norm_w = adamw_step(
        norm_params, norm_moment, norm_second, norm_total, RATE_VECTOR, 0.0
    )
    head_m, head_v, head_w = adamw_step(
        head_weight, head_moment, head_second, head_total, RATE_MATRIX, DECAY_RATE
    )
    return (
        loss_sum,
        pixel_total,
        slot_m,
        slot_v,
        slot_w,
        norm_m,
        norm_v,
        norm_w,
        head_m,
        head_v,
        head_w,
    )


def solution(mesh):
    in_specs = (
        P(("grp", "tok"), None),
        P(("grp", "tok")),
        P(("grp", "tok")),
        P("grp", None),
        P(),
        P("tok", "grp"),
        P("tok", "grp"),
        P("tok", "grp"),
        P(),
        P(),
        P(),
        P(),
        P(),
        P(),
    )
    out_specs = (
        P(),
        P(),
        P("tok", "grp"),
        P("tok", "grp"),
        P("tok", "grp"),
        P(),
        P(),
        P(),
        P(),
        P(),
        P(),
    )
    return jax.shard_map(body, mesh=mesh, in_specs=in_specs, out_specs=out_specs, check_vma=False)
```

```python
import functools

import jax
import jax.numpy as jnp
import numpy as np
from jax import lax
from jax.experimental import pallas as pl
from jax.experimental.pallas import tpu as pltpu
from jax.sharding import PartitionSpec as P

C = 320
HEADS = 5
HD = 64
FF = 1280
PIN = 1152
BLOCKS = 3
BIG_SIDE = 14
SMALL_SIDE = 6
STEP = 10
KVH = 49


EPS_NORM = 1e-06
BETA_ONE = 0.9
BETA_TWO = 0.999
ADAM_EPS = 1e-08
RATE_MATRIX = 0.05
RATE_VECTOR = 0.3
DECAY_RATE = 0.05
NEG_FILL = -1e30
PREC_HIGH = lax.Precision.HIGHEST


def layer_norm(values, gain_vec, shift_vec):
    center = values - jnp.mean(values, -1, keepdims=True)
    inverse = lax.rsqrt(jnp.mean(center * center, -1, keepdims=True) + EPS_NORM)
    return center * inverse * gain_vec + shift_vec


def adamw_step(weight, moment, second, gradient, rate_now, decay_now):
    moment = BETA_ONE * moment + (1.0 - BETA_ONE) * gradient
    second = BETA_TWO * second + (1.0 - BETA_TWO) * gradient * gradient
    m_hat = moment / (1.0 - BETA_ONE**STEP)
    v_hat = second / (1.0 - BETA_TWO**STEP)
    weight = weight - rate_now * (m_hat / (jnp.sqrt(v_hat) + ADAM_EPS) + decay_now * weight)
    return (moment, second, weight)


def product(left, right):
    return jnp.dot(left, right, preferred_element_type=jnp.float32)


def outer_sum(left, right):
    return lax.dot_general(
        left, right, (((0,), (0,)), ((), ())), preferred_element_type=jnp.float32
    )


def back_product(gradient, weight):
    return lax.dot_general(
        gradient, weight, (((1,), (1,)), ((), ())), preferred_element_type=jnp.float32
    )


def norm_back(values, gain_vec, shift_vec, gradient):
    _, pull_back = jax.vjp(layer_norm, values, gain_vec, shift_vec)
    return pull_back(gradient)


OVER = 4 * KVH - 4


def image_layout(positions, counts):
    big_tok = BIG_SIDE * BIG_SIDE
    small_tok = SMALL_SIDE * SMALL_SIDE
    big_end = counts[0] * big_tok
    small_end = big_end + counts[1] * small_tok
    is_big = positions < big_end
    is_small = jnp.logical_and(positions >= big_end, positions < small_end)
    half_side = jnp.where(is_big, BIG_SIDE // 2, SMALL_SIDE // 2)
    begin_at = jnp.where(
        is_big,
        positions // big_tok * big_tok,
        jnp.where(is_small, big_end + (positions - big_end) // small_tok * small_tok, small_end),
    )
    tile_idx = (positions - begin_at) // 4
    return (begin_at, half_side, tile_idx // half_side, tile_idx % half_side, positions < small_end)


def shift_stacks(half_side, tile_y, tile_x, is_real):
    tiles = half_side.shape[0]
    step_y = np.array([[0, 1 - 2 * (sub // 2), 1 - 2 * (sub // 2)] for sub in range(4)], np.int32)[:, :, None]
    step_x = np.array([[1 - 2 * (sub % 2), 0, 1 - 2 * (sub % 2)] for sub in range(4)], np.int32)[:, :, None]
    at_y = tile_y + step_y
    at_x = tile_x + step_x
    inside = is_real & (at_y >= 0) & (at_y < half_side) & (at_x >= 0) & (at_x < half_side)
    source = jnp.arange(tiles, dtype=jnp.int32) + step_y * half_side + step_x
    source = jnp.where(inside, source, -1)
    cut = row_cut(tiles)
    columns = jnp.arange(SPAN, dtype=jnp.int32)
    upper = (source[:, :, :cut, None] == columns).astype(jnp.bfloat16)
    lower = (source[:, :, cut:, None] == columns + (tiles - SPAN)).astype(jnp.bfloat16)
    return (upper.reshape(4, 3 * cut, SPAN), lower.reshape(4, 3 * (tiles - cut), SPAN))


def tap_source(sub, tap):
    y_at = sub // 2 + tap // 3 - 1
    x_at = sub % 2 + tap % 3 - 1
    return (y_at % 2 * 2 + x_at % 2, y_at // 2, x_at // 2)


SQRT_HALF = 0.7071067811865476
INV_SQRT_TWO_PI = 0.3989422804014327
TAPS_OF = [[tap_source(sub, tap) for tap in range(9)] for sub in range(4)]
VMEM_LIMIT = 56 * 1024 * 1024
SPAN = 256
ROWS = 16
LANES = 128


def row_cut(tiles):
    return (tiles // 2 + 15) // 16 * 16


def move_planes(planes_ref, upper_ref, lower_ref, moved_ref):
    tiles = planes_ref.shape[0] // 4
    cut = row_cut(tiles)
    for sub in range(4):
        base = sub * tiles
        part = product(upper_ref[sub], planes_ref[base : base + SPAN, :])
        for key in range(3):
            moved_ref[sub, key, :cut, :] = part[key * cut : (key + 1) * cut]
        part = product(lower_ref[sub], planes_ref[base + tiles - SPAN : base + tiles, :])
        for key in range(3):
            moved_ref[sub, key, cut:, :] = part[key * (tiles - cut) : (key + 1) * (tiles - cut)]


def chunk_sources(planes_ref, moved_ref, row, lanes):
    tiles = planes_ref.shape[0] // 4
    found = {}
    for sub in range(4):
        found[sub, 0, 0] = planes_ref[pl.ds(pl.multiple_of(sub * tiles + row, ROWS), ROWS), lanes].astype(jnp.float32)
        step_y = 1 - 2 * (sub // 2)
        step_x = 1 - 2 * (sub % 2)
        for key, step in enumerate(((0, step_x), (step_y, 0), (step_y, step_x))):
            found[(sub,) + step] = moved_ref[sub, key, pl.ds(row, ROWS), lanes]
    return found


def norm_rows(values, gain, shift):
    center = values - jnp.mean(values, -1, keepdims=True)
    inverse = lax.rsqrt(jnp.mean(center * center, -1, keepdims=True) + EPS_NORM)
    unit = center * inverse
    return (unit, inverse, unit * gain + shift)


def norm_rows_back(unit, inverse, gain, grad):
    scaled = grad * gain
    return inverse * (
        scaled - jnp.mean(scaled, -1, keepdims=True) - unit * jnp.mean(scaled * unit, -1, keepdims=True)
    )


def mlp_forward_kernel(
    middle_ref, gains_ref, up_ref, down_ref, kern_ref, upper_ref, lower_ref, real_ref,
    out_ref, hidden_ref, active_ref, slope_ref, turned_ref,
    normed_ref, moved_ref, planes_ref,
):
    rows = middle_ref.shape[0]
    block = hidden_ref.shape[1]
    tiles = rows // 4

    @pl.when(pl.program_id(0) == 0)
    def _():
        normed = norm_rows(middle_ref[...], gains_ref[0:1, :], gains_ref[1:2, :])[2]
        normed_ref[...] = normed.astype(jnp.bfloat16)
        out_ref[...] = middle_ref[...]
        spread_rows(up_ref[0], planes_ref)
        for quarter in range(FF // C):
            for at, lane, width in lane_parts(C):
                part = planes_ref[at, pl.ds(quarter, C, stride=FF // C), :][:, :width]
                begin = quarter * C + lane
                turned_ref[:, begin : begin + width] = part.astype(jnp.bfloat16)

    for sub in range(4):
        columns = pl.ds(pl.multiple_of(pl.program_id(0) * block, block), block)
        part = product(normed_ref[sub * tiles : (sub + 1) * tiles, :], turned_ref[:, columns])
        hidden_ref[sub * tiles : (sub + 1) * tiles, :] = part.astype(jnp.bfloat16)
    move_planes(hidden_ref, upper_ref, lower_ref, moved_ref)

    for lane in range(0, hidden_ref.shape[1], LANES):
        lanes = slice(lane, lane + LANES)
        kern = [kern_ref[0, tap : tap + 1, lanes] for tap in range(9)]

        @pl.loop(0, tiles // ROWS, unroll=tiles // ROWS)
        def _(at):
            row = pl.multiple_of(at * ROWS, ROWS)
            found = chunk_sources(hidden_ref, moved_ref, row, lanes)
            real = real_ref[pl.ds(row, ROWS), :] > 0.0
            for sub in range(4):
                center = found[sub, 0, 0] * kern[4]
                total = center
                for tap in range(9):
                    if tap != 4:
                        total = total + found[TAPS_OF[sub][tap]] * kern[tap]
                mixed = jnp.where(real, total, center)
                half = 0.5 + 0.5 * lax.erf(mixed * SQRT_HALF)
                bell = jnp.exp(-0.5 * mixed * mixed) * INV_SQRT_TWO_PI
                span = pl.ds(pl.multiple_of(sub * tiles + row, ROWS), ROWS)
                active_ref[span, lanes] = (mixed * half).astype(jnp.bfloat16)
                slope_ref[span, lanes] = (half + mixed * bell).astype(jnp.bfloat16)

    for sub in range(4):
        span = slice(sub * tiles, (sub + 1) * tiles)
        out_ref[span, :] += product(active_ref[span, :], down_ref[0])


def lane_parts(width):
    return [(at, lane, min(LANES, width - lane)) for at, lane in enumerate(range(0, width, LANES))]


def spread_rows(source, planes_ref):
    for at, lane, width in lane_parts(source.shape[1]):
        planes_ref[at, :, :width] = source[:, lane : lane + width].astype(jnp.float32)


class Plan:
    def __init__(self, value, out, scratch, make, space=None):
        self.value, self.out, self.scratch, self.make = value, out, scratch, make
        self.in_spec = pl.BlockSpec(memory_space=space) if space is not None else whole(value.shape)
        self.out_spec = whole(out.shape)


def plan_sum(value, begin, end):
    make = functools.partial(SumRide, begin=begin, end=end)
    return Plan(value, jax.ShapeDtypeStruct(value.shape, value.dtype), sum_scratch(value.shape, jnp.bfloat16), make)


def plan_units(value, begin, end):
    if begin == 0:
        value = unit_blocks(value)
    total, (chunk, width) = value.shape[0], value.shape[-2:]
    inside = unit_layout(unit_order(0))[end] if end < len(bit_order()) else ()
    out = jax.ShapeDtypeStruct((total,) + inside + (chunk, width), value.dtype)

    def make(ride_in, ride_out, scratch):
        sources = [(ride_in, at) for at in range(total)]
        return UnitRide(sources, ride_out, scratch, begin, end)

    space = pl.ANY if begin == 0 else None
    return Plan(value, out, unit_scratch(total, chunk, width, begin, end), make, space)


class Rides:
    def __init__(self, rides):
        self.rides = rides
        self.phases = max(ride.phases for ride in rides)
        names = [name for name in bit_order() if any(name in ride.names for ride in rides)]
        self.peers = [UnitRide.partner(rides[0], name) for name in names]

    def signal(self):
        signal_all(self.peers)

    def advance(self, phase):
        if phase == 0:
            pl.semaphore_wait(pltpu.get_barrier_semaphore(), len(self.peers))
        for ride in self.rides:
            if phase <= ride.phases:
                ride.advance(phase)


def rides_of(plans, ins, outs, scratch):
    rides = []
    for plan, ride_in, ride_out in zip(plans, ins, outs):
        count = len(plan.scratch)
        rides.append(plan.make(ride_in, ride_out, scratch[:count]))
        scratch = scratch[count:]
    return Rides(rides)


def ridden(kernel, inputs, outputs, scratch, steps, plans):
    def run(*refs):
        own_in, refs = refs[:inputs], refs[inputs:]
        ride_in, refs = refs[: len(plans)], refs[len(plans) :]
        own_out, refs = refs[:outputs], refs[outputs:]
        ride_out, rest = refs[: len(plans)], refs[len(plans) :]
        rides = rides_of(plans, ride_in, ride_out, rest[scratch:])
        places = [0] + list(range(1, steps - 1, 2))
        for phase, step in enumerate(places):
            if phase == 0:

                @pl.when(pl.program_id(0) == step)
                def _():
                    rides.signal()
                    rides.advance(0)
            elif phase <= rides.phases:
                pl.when(pl.program_id(0) == step)(functools.partial(rides.advance, phase))
        kernel(*own_in, *own_out, *rest[:scratch])

        @pl.when(pl.program_id(0) == steps - 1)
        def _():
            for phase in range(len(places), rides.phases + 1):
                rides.advance(phase)

    return run


def whole(shape):
    return pl.BlockSpec(shape, lambda j: (0,) * len(shape))


def unit_spec(at):
    return pl.BlockSpec((1, FF, C), lambda j: (at, 0, 0))


def mlp_forward(middle, gains, units, at, kernel, layer_at, stacks, real_rows):
    rows = middle.shape[0]
    block = 256
    by_lane = pl.BlockSpec((rows, block), lambda j: (0, j))
    low = jax.ShapeDtypeStruct((rows, FF), jnp.bfloat16)
    return pl.pallas_call(
        mlp_forward_kernel,
        grid=(FF // block,),
        out_shape=(
            jax.ShapeDtypeStruct((rows, C), jnp.float32),
            low,
            low,
            low,
            jax.ShapeDtypeStruct((C, FF), jnp.bfloat16),
        ),
        in_specs=[
            whole((rows, C)),
            whole((2, C)),
            unit_spec(at),
            pl.BlockSpec((1, block, C), lambda j: (at + 1, j, 0)),
            pl.BlockSpec((1, 9, block), lambda j: (layer_at, 0, j)),
            whole(stacks[0].shape),
            whole(stacks[1].shape),
            whole(real_rows.shape),
        ],
        out_specs=(whole((rows, C)), by_lane, by_lane, by_lane, whole((C, FF))),
        scratch_shapes=[
            pltpu.VMEM((rows, C), jnp.bfloat16),
            pltpu.VMEM((4, 3, rows // 4, block), jnp.float32),
            pltpu.VMEM((3, FF, LANES), jnp.float32),
        ],
        compiler_params=pltpu.CompilerParams(vmem_limit_bytes=VMEM_LIMIT),
        cost_estimate=pl.CostEstimate(flops=14 * 10**9, bytes_accessed=18 * 10**6, transcendentals=4 * 10**6),
        name="mlp_forward",
    )(middle, gains, units, units, kernel, stacks[0], stacks[1], real_rows)


def mlp_backward_kernel(
    grad_ref, middle_ref, gains_ref, up_ref, down_ref, kern_ref, upper_ref, lower_ref, real_ref,
    hidden_ref, active_ref, slope_ref,
    out_ref, dunits_ref, dkern_ref, dgain_ref,
    low_ref, low_t_ref, normed_t_ref, mixed_ref, dhid_ref, moved_ref, back_ref, wide_ref, planes_ref,
):
    rows = grad_ref.shape[0]
    tiles = rows // 4
    block = hidden_ref.shape[1]

    @pl.when(pl.program_id(0) == 0)
    def _():
        for sub in range(4):
            span = slice(sub * tiles, (sub + 1) * tiles)
            low_ref[span, :] = grad_ref[span, :].astype(jnp.bfloat16)
        normed = norm_rows(middle_ref[...], gains_ref[0:1, :], gains_ref[1:2, :])[2]
        normed_t_ref[...] = normed.astype(jnp.bfloat16).T
        low_t_ref[...] = low_ref[...].T
        back_ref[...] = jnp.zeros_like(back_ref)

    for sub in range(4):
        span = slice(sub * tiles, (sub + 1) * tiles)
        part = back_product(low_ref[span, :], down_ref[0]).astype(jnp.bfloat16).astype(jnp.float32)
        mixed_ref[span, :] = (part * slope_ref[span, :].astype(jnp.float32)).astype(jnp.bfloat16)
    down_rows = pl.ds(pl.multiple_of(pl.program_id(0) * block, block), block)
    dunits_ref[1, down_rows, :] = product(low_t_ref[...], active_ref[...]).T.astype(jnp.bfloat16)
    move_planes(mixed_ref, upper_ref, lower_ref, moved_ref)

    for lane in range(0, block, LANES):
        lanes = slice(lane, lane + LANES)
        kern = [kern_ref[0, tap : tap + 1, lanes] for tap in range(9)]

        def step(at, sums):
            row = pl.multiple_of(at * ROWS, ROWS)
            found = chunk_sources(mixed_ref, moved_ref, row, lanes)
            real = real_ref[pl.ds(row, ROWS), :] > 0.0
            sums = list(sums)
            for sub in range(4):
                span = pl.ds(pl.multiple_of(sub * tiles + row, ROWS), ROWS)
                hidden = hidden_ref[span, lanes].astype(jnp.float32)
                center = found[sub, 0, 0] * kern[4]
                total = center
                for tap in range(9):
                    term = found[TAPS_OF[sub][tap]]
                    if tap != 4:
                        total = total + term * kern[8 - tap]
                    piece = hidden * term
                    sums[tap] = sums[tap] + piece[:8] + piece[8:]
                dhid_ref[span, lanes] = jnp.where(real, total, center).astype(jnp.bfloat16)
            return tuple(sums)

        sums = lax.fori_loop(0, tiles // ROWS, step, (jnp.zeros((8, LANES), jnp.float32),) * 9, unroll=True)
        for tap in range(9):
            dkern_ref[8 - tap : 9 - tap, lanes] = jnp.sum(sums[tap], 0, keepdims=True)

    columns = pl.ds(pl.multiple_of(pl.program_id(0) * block, block), block)
    wide_ref[:, columns] = product(normed_t_ref[...], dhid_ref[...])
    for sub in range(4):
        span = slice(sub * tiles, (sub + 1) * tiles)
        back_ref[span, :] += back_product(dhid_ref[span, :], up_ref[...])

    @pl.when(pl.program_id(0) == pl.num_programs(0) - 1)
    def _():
        grad = back_ref[...]
        unit, inverse, _ = norm_rows(middle_ref[...], gains_ref[0:1, :], gains_ref[1:2, :])
        out_ref[...] = grad_ref[...] + norm_rows_back(unit, inverse, gains_ref[0:1, :], grad)
        dgain_ref[0:1, :] = jnp.sum(grad * unit, 0, keepdims=True)
        dgain_ref[1:2, :] = jnp.sum(grad, 0, keepdims=True)
        for quarter in range(FF // C):
            for at, lane, width in lane_parts(C):
                begin = quarter * C + lane
                part = wide_ref[:, begin : begin + width]
                if width < LANES:
                    part = jnp.concatenate([part, jnp.zeros((C, LANES - width), jnp.float32)], 1)
                planes_ref[at, pl.ds(quarter, C, stride=FF // C), :] = part
        for at, lane, width in lane_parts(C):
            dunits_ref[0, :, lane : lane + width] = planes_ref[at, :, :width].astype(jnp.bfloat16)


def mlp_backward(grad, middle, gains, w_up, units, at, kernel, layer_at, stacks, real_rows, kept, plans, meeting):
    rows = middle.shape[0]
    block = 256
    by_lane = pl.BlockSpec((rows, block), lambda j: (0, j))
    up_spec = pl.BlockSpec((C, block), lambda j: (0, j))
    tap_spec = pl.BlockSpec((9, block), lambda j: (0, j))
    return pl.pallas_call(
        ridden(mlp_backward_kernel, 12, 4, 9, FF // block, plans),
        grid=(FF // block,),
        out_shape=(
            jax.ShapeDtypeStruct((rows, C), jnp.float32),
            jax.ShapeDtypeStruct((2, FF, C), jnp.bfloat16),
            jax.ShapeDtypeStruct((9, FF), jnp.float32),
            jax.ShapeDtypeStruct((2, C), jnp.float32),
            *[plan.out for plan in plans],
        ),
        in_specs=[
            whole((rows, C)),
            whole((rows, C)),
            whole((2, C)),
            up_spec,
            pl.BlockSpec((1, block, C), lambda j: (at + 1, j, 0)),
            pl.BlockSpec((1, 9, block), lambda j: (layer_at, 0, j)),
            whole(stacks[0].shape),
            whole(stacks[1].shape),
            whole(real_rows.shape),
            by_lane,
            by_lane,
            by_lane,
        ]
        + [plan.in_spec for plan in plans],
        out_specs=(whole((rows, C)), whole((2, FF, C)), tap_spec, whole((2, C)))
        + tuple(plan.out_spec for plan in plans),
        scratch_shapes=[
            pltpu.VMEM((rows, C), jnp.bfloat16),
            pltpu.VMEM((C, rows), jnp.bfloat16),
            pltpu.VMEM((C, rows), jnp.bfloat16),
            pltpu.VMEM((rows, block), jnp.bfloat16),
            pltpu.VMEM((rows, block), jnp.bfloat16),
            pltpu.VMEM((4, 3, rows // 4, block), jnp.float32),
            pltpu.VMEM((rows, C), jnp.float32),
            pltpu.VMEM((C, FF), jnp.float32),
            pltpu.VMEM((3, FF, LANES), jnp.float32),
        ]
        + sum([plan.scratch for plan in plans], []),
        compiler_params=pltpu.CompilerParams(
            collective_id=meeting, has_side_effects=True, vmem_limit_bytes=VMEM_LIMIT
        ),
        cost_estimate=pl.CostEstimate(flops=18 * 10**9, bytes_accessed=18 * 10**6, transcendentals=0),
        name="mlp_backward",
    )(grad, middle, gains, w_up, units, kernel, stacks[0], stacks[1], real_rows, *kept, *[plan.value for plan in plans])


WIDE = 384
BLOCK_TILES = 32
KEY_SPAN = 128


def block_places(tiles):
    places = []
    for index in range(-(-tiles // BLOCK_TILES)):
        start = min(index * BLOCK_TILES, tiles - BLOCK_TILES)
        places.append((start, min(max(start - 48, 0), tiles - KEY_SPAN)))
    return places


def block_bias(tiles, image_at):
    starts, lows = np.array(block_places(tiles), np.int32).T[:, :, None]
    columns = starts + np.tile(np.arange(BLOCK_TILES, dtype=np.int32), 4)
    rows = lows + np.arange(KEY_SPAN, dtype=np.int32)
    same = image_at(jnp.asarray(rows))[:, :, None] == image_at(jnp.asarray(columns))[:, None, :]
    return jnp.where(same, 0.0, NEG_FILL)


def place_of(index, tiles):
    start = jnp.minimum(index * BLOCK_TILES, tiles - BLOCK_TILES)
    low = jnp.clip(start - 48, 0, tiles - KEY_SPAN)
    return (pl.multiple_of(start, ROWS), pl.multiple_of(low, ROWS))


def four_planes(ref, start, lanes):
    tiles = ref.shape[0] // 4
    return jnp.concatenate(
        [ref[pl.ds(pl.multiple_of(sub * tiles + start, ROWS), BLOCK_TILES), lanes] for sub in range(4)], 0
    )


def put_planes(ref, start, lanes, values):
    tiles = ref.shape[0] // 4
    for sub in range(4):
        ref[pl.ds(pl.multiple_of(sub * tiles + start, ROWS), BLOCK_TILES), lanes] = values[
            sub * BLOCK_TILES : (sub + 1) * BLOCK_TILES
        ]


def head_pair(values, group):
    if group == 2:
        return values
    first = lax.broadcasted_iota(jnp.int32, values.shape, 1) < HD
    zero = jnp.zeros_like(values)
    return jnp.concatenate([jnp.where(first, values, zero), jnp.where(first, zero, values)], 0)


def softmax_columns(raw, bias):
    parts = []
    for half in range(raw.shape[0] // KEY_SPAN):
        scores = raw[half * KEY_SPAN : (half + 1) * KEY_SPAN] * HD ** (-0.5) + bias
        weights = jnp.exp(scores - jnp.max(scores, 0, keepdims=True))
        parts.append(weights * (1.0 / jnp.sum(weights, 0, keepdims=True)))
    return parts


def norm_store(source_ref, gains_ref, at, target_ref):
    normed = norm_rows(source_ref[...], gains_ref[at : at + 1, :], gains_ref[at + 1 : at + 2, :])[2]
    target_ref[...] = normed.astype(jnp.bfloat16)


def part_keyval(unit_ref, planes_ref, kv_ref):
    spread_rows(unit_ref[0, 2 * C :, :], planes_ref)
    for which in range(2):
        for at, lane, width in lane_parts(C):
            part = planes_ref[at, pl.ds(which, C, stride=2), :][:, :width]
            kv_ref[which, :, lane : lane + width] = part.astype(jnp.bfloat16)


def attention_forward_kernel(
    resid_ref, gains_ref, unit_ref, reduce_ref, bias_ref,
    middle_ref, normed_ref, query_ref, reduced_ref, key_ref, value_ref, attended_ref, kv_ref,
    planes_ref,
):
    part_keyval(unit_ref, planes_ref, kv_ref)
    rows = resid_ref.shape[0]
    tiles = rows // 4
    norm_store(resid_ref, gains_ref, 0, normed_ref)
    query_ref[:, C:] = jnp.zeros((rows, WIDE - C), jnp.bfloat16)
    reduced = jnp.zeros((tiles, C), jnp.float32)
    for sub in range(4):
        span = slice(sub * tiles, (sub + 1) * tiles)
        query_ref[span, :C] = product(normed_ref[span, :], unit_ref[0, :C, :]).astype(jnp.bfloat16)
        reduced = reduced + product(normed_ref[span, :], reduce_ref[0, sub * C : (sub + 1) * C, :])
    reduced_ref[...] = reduced
    normed_kv = norm_rows(reduced, gains_ref[2:3, :], gains_ref[3:4, :])[2].astype(jnp.bfloat16)
    for which, ref in enumerate((key_ref, value_ref)):
        ref[:, C:] = jnp.zeros((tiles, WIDE - C), jnp.bfloat16)
        ref[:, :C] = product(normed_kv, kv_ref[which]).astype(jnp.bfloat16)

    @pl.loop(0, bias_ref.shape[0], unroll=bias_ref.shape[0])
    def _(index):
        start, low = place_of(index, tiles)
        bias = bias_ref[index]
        for group in range(3):
            lanes = slice(group * LANES, (group + 1) * LANES)
            query = four_planes(query_ref, start, lanes)
            keys = head_pair(key_ref[pl.ds(low, KEY_SPAN), lanes], group)
            values = head_pair(value_ref[pl.ds(low, KEY_SPAN), lanes], group)
            probs = softmax_columns(back_product(keys, query), bias)
            probs = jnp.concatenate(probs, 0).astype(jnp.bfloat16).T
            put_planes(attended_ref, start, lanes, product(probs, values).astype(jnp.bfloat16))

    for sub in range(4):
        span = slice(sub * tiles, (sub + 1) * tiles)
        middle_ref[span, :] = resid_ref[span, :] + product(attended_ref[span, :C], unit_ref[0, C : 2 * C, :])


def attention_forward(resid, gains, units, at, reduces, reduce_at, bias):
    rows = resid.shape[0]
    tiles = rows // 4
    low = jnp.bfloat16
    shapes = (
        jax.ShapeDtypeStruct((rows, C), jnp.float32),
        jax.ShapeDtypeStruct((rows, C), low),
        jax.ShapeDtypeStruct((rows, WIDE), low),
        jax.ShapeDtypeStruct((tiles, C), jnp.float32),
        jax.ShapeDtypeStruct((tiles, WIDE), low),
        jax.ShapeDtypeStruct((tiles, WIDE), low),
        jax.ShapeDtypeStruct((rows, WIDE), low),
        jax.ShapeDtypeStruct((2, C, C), low),
    )
    return pl.pallas_call(
        attention_forward_kernel,
        grid=(1,),
        out_shape=shapes,
        in_specs=[whole((rows, C)), whole((4, C)), unit_spec(at), unit_spec(reduce_at), whole(bias.shape)],
        out_specs=tuple(whole(shape.shape) for shape in shapes),
        scratch_shapes=[pltpu.VMEM((3, 2 * C, LANES), jnp.float32)],
        compiler_params=pltpu.CompilerParams(vmem_limit_bytes=VMEM_LIMIT),
        cost_estimate=pl.CostEstimate(flops=6 * 10**9, bytes_accessed=14 * 10**6, transcendentals=10**6),
        name="attention_forward",
    )(resid, gains, units, reduces, bias)


def embed_forward_kernel(
    patches_ref, halo_ref, unit_ref, gains_ref, pre_ref, resid_ref, kern_ref, planes_ref, taps_ref
):
    rows = pre_ref.shape[0]
    tiles = rows // 4
    used = FF * 9 * BLOCKS // C
    for ref, base in ((patches_ref, 0), (halo_ref, patches_ref.shape[0])):
        step = 64

        @pl.loop(0, ref.shape[0] // step, unroll=4)
        def _(at):
            span = pl.ds(pl.multiple_of(at * step, step), step)
            into = pl.ds(pl.multiple_of(base + at * step, step), step)
            part = product(ref[span, :], unit_ref[0, :PIN, :])
            for place, lane, width in lane_parts(C):
                planes_ref[place, into, :width] = part[:, lane : lane + width]

    for sub in range(4):
        for place, lane, width in lane_parts(C):
            pre_ref[sub * tiles : (sub + 1) * tiles, lane : lane + width] = planes_ref[
                place, pl.ds(sub, tiles, stride=4), :
            ][:, :width]
    taps = unit_ref[0, PIN : PIN + taps_ref.shape[1], :]
    spread_rows(taps, taps_ref)
    for layer_at in range(BLOCKS):
        for quarter in range(FF // C):
            for place, lane, width in lane_parts(C):
                begin = quarter * C + lane
                kern_ref[layer_at, :, begin : begin + width] = taps_ref[
                    place, pl.ds(layer_at * (used // BLOCKS) + quarter, 9, stride=FF // C), :
                ][:, :width]

    resid_ref[...] = norm_rows(pre_ref[...], gains_ref[0:1, :], gains_ref[1:2, :])[2]


def embed_forward(patches, halo, units, gains):
    rows = patches.shape[0] + halo.shape[0]
    wide = jax.ShapeDtypeStruct((rows, C), jnp.float32)
    taps = jax.ShapeDtypeStruct((BLOCKS, 9, FF), jnp.float32)
    return pl.pallas_call(
        embed_forward_kernel,
        grid=(1,),
        out_shape=(wide, wide, taps),
        in_specs=[whole(patches.shape), whole(halo.shape), unit_spec(0), whole((2, C))],
        out_specs=(whole(wide.shape), whole(wide.shape), whole(taps.shape)),
        scratch_shapes=[
            pltpu.VMEM((3, rows, LANES), jnp.float32),
            pltpu.VMEM((3, FF - PIN, LANES), jnp.float32),
        ],
        compiler_params=pltpu.CompilerParams(vmem_limit_bytes=VMEM_LIMIT),
        cost_estimate=pl.CostEstimate(flops=10**9, bytes_accessed=8 * 10**6, transcendentals=0),
        name="embed_forward",
    )(patches, halo, units, gains)


def embed_backward_kernel(
    grad_ref, pre_ref, gains_ref, patches_ref, halo_ref, *refs
):
    taps_refs = refs[:BLOCKS]
    unit_ref, dgain_ref, planes_ref, turned_ref, taps_ref = refs[BLOCKS:]
    rows = pre_ref.shape[0]
    tiles = rows // 4
    half = tiles // 2
    used = FF * 9 * BLOCKS // C
    sums = [jnp.zeros((1, C), jnp.float32)] * 2
    for sub in range(4):
        for part_at in range(2):
            span = slice(sub * tiles + part_at * half, sub * tiles + (part_at + 1) * half)
            unit, inverse, _ = norm_rows(pre_ref[span, :], gains_ref[0:1, :], gains_ref[1:2, :])
            grad = grad_ref[span, :]
            back = norm_rows_back(unit, inverse, gains_ref[0:1, :], grad)
            sums[0] = sums[0] + jnp.sum(grad * unit, 0, keepdims=True)
            sums[1] = sums[1] + jnp.sum(grad, 0, keepdims=True)
            for place, lane, width in lane_parts(C):
                value = back[:, lane : lane + width]
                if width < LANES:
                    value = jnp.concatenate([value, jnp.zeros((half, LANES - width), jnp.float32)], 1)
                planes_ref[place, pl.ds(4 * part_at * half + sub, half, stride=4), :] = value
    dgain_ref[0:1, :] = sums[0]
    dgain_ref[1:2, :] = sums[1]
    for place, lane, width in lane_parts(C):
        turned_ref[lane : lane + width, :] = planes_ref[place].T[:width, :].astype(jnp.bfloat16)
    split = patches_ref.shape[0]
    grads = product(turned_ref[:, :split], patches_ref[...]) + product(turned_ref[:, split:], halo_ref[...])
    unit_ref[0, :PIN, :] = grads.T.astype(jnp.bfloat16)
    taps_ref[...] = jnp.zeros_like(taps_ref)
    for layer_at, ref in enumerate(taps_refs):
        for quarter in range(FF // C):
            for place, lane, width in lane_parts(C):
                begin = quarter * C + lane
                value = ref[:, begin : begin + width]
                if width < LANES:
                    value = jnp.concatenate([value, jnp.zeros((9, LANES - width), jnp.float32)], 1)
                taps_ref[place, pl.ds(layer_at * (used // BLOCKS) + quarter, 9, stride=FF // C), :] = value
    for place, lane, width in lane_parts(C):
        unit_ref[0, PIN:, lane : lane + width] = taps_ref[place, :, :width].astype(jnp.bfloat16)


def embed_backward(grad, pre, gains, patches, halo, taps):
    rows = pre.shape[0]
    shapes = (jax.ShapeDtypeStruct((1, FF, C), jnp.bfloat16), jax.ShapeDtypeStruct((2, C), jnp.float32))
    operands = (grad, pre, gains, patches, halo, *taps)
    return pl.pallas_call(
        embed_backward_kernel,
        grid=(1,),
        out_shape=shapes,
        in_specs=[whole(part.shape) for part in operands],
        out_specs=tuple(whole(shape.shape) for shape in shapes),
        scratch_shapes=[
            pltpu.VMEM((3, rows, LANES), jnp.float32),
            pltpu.VMEM((C, rows), jnp.bfloat16),
            pltpu.VMEM((3, FF - PIN, LANES), jnp.float32),
        ],
        compiler_params=pltpu.CompilerParams(vmem_limit_bytes=VMEM_LIMIT),
        cost_estimate=pl.CostEstimate(flops=10**9, bytes_accessed=8 * 10**6, transcendentals=0),
        name="embed_backward",
    )(*operands)


def head_kernel(
    resid_ref, gains_ref, weight_ref, label_ref, keep_ref, total_ref,
    grad_ref, dhead_ref, dgain_ref, loss_ref,
    final_ref, turned_ref,
):
    rows = resid_ref.shape[0]
    tiles = rows // 4
    classes = weight_ref.shape[1]
    low = weight_ref[...].astype(jnp.bfloat16)
    share = 1.0 / total_ref[0:1, 0:1]
    sums = [jnp.zeros((1, C), jnp.float32)] * 2
    loss = jnp.zeros((1, 1), jnp.float32)
    for sub in range(4):
        span = slice(sub * tiles, (sub + 1) * tiles)
        unit, inverse, final = norm_rows(resid_ref[span, :], gains_ref[0:1, :], gains_ref[1:2, :])
        final = final.astype(jnp.bfloat16)
        final_ref[span, :] = final
        logits = product(final, low)
        peak = jnp.max(logits, -1, keepdims=True)
        log_norm = peak + jnp.log(jnp.sum(jnp.exp(logits - peak), -1, keepdims=True))
        keep = keep_ref[span, :]
        hit = lax.broadcasted_iota(jnp.int32, (tiles, classes), 1) == label_ref[span, :]
        picked = jnp.sum(jnp.where(hit, logits, 0.0), -1, keepdims=True)
        loss = loss + jnp.sum((log_norm - picked) * keep, 0, keepdims=True)
        dlogits = (jnp.exp(logits - log_norm) - jnp.where(hit, 1.0, 0.0)) * (keep * share)
        turned_ref[:, span] = dlogits.T.astype(jnp.bfloat16)
        grad = back_product(dlogits.astype(jnp.bfloat16), low)
        grad_ref[span, :] = norm_rows_back(unit, inverse, gains_ref[0:1, :], grad)
        sums[0] = sums[0] + jnp.sum(grad * unit, 0, keepdims=True)
        sums[1] = sums[1] + jnp.sum(grad, 0, keepdims=True)
    dhead_ref[:classes, :] = product(turned_ref[...], final_ref[...])
    dhead_ref[classes:, :] = jnp.zeros((dhead_ref.shape[0] - classes, C), jnp.float32)
    dgain_ref[0:1, :] = sums[0]
    dgain_ref[1:2, :] = sums[1]
    loss_ref[...] = jnp.broadcast_to(loss, (1, C))


def head_step(resid, gains, weight, labels, keep, total):
    rows = resid.shape[0]
    classes = weight.shape[1]
    wide = jnp.float32
    shapes = (
        jax.ShapeDtypeStruct((rows, C), wide),
        jax.ShapeDtypeStruct((-(-classes // 8) * 8, C), wide),
        jax.ShapeDtypeStruct((2, C), wide),
        jax.ShapeDtypeStruct((1, C), wide),
    )
    operands = (resid, gains, weight, labels, keep, total)
    return pl.pallas_call(
        head_kernel,
        grid=(1,),
        out_shape=shapes,
        in_specs=[whole(part.shape) for part in operands],
        out_specs=tuple(whole(shape.shape) for shape in shapes),
        scratch_shapes=[
            pltpu.VMEM((rows, C), jnp.bfloat16),
            pltpu.VMEM((classes, rows), jnp.bfloat16),
        ],
        compiler_params=pltpu.CompilerParams(vmem_limit_bytes=VMEM_LIMIT),
        cost_estimate=pl.CostEstimate(flops=10**9, bytes_accessed=5 * 10**6, transcendentals=10**6),
        name="head_step",
    )(*operands)


def attention_backward_kernel(
    advance,
    grad_ref, resid_ref, gains_ref, unit_ref, reduce_ref, bias_ref,
    normed_ref, query_ref, reduced_ref, key_ref, value_ref, attended_ref, kv_ref,
    out_ref, dunits_ref, dgain_ref,
    turned_ref, datt_ref, dquery_ref, dkey_ref, dvalue_ref, first_ref, planes_ref,
):
    rows = resid_ref.shape[0]
    tiles = rows // 4
    low_type = jnp.bfloat16
    advance(0)
    datt_ref[:, C:] = jnp.zeros((rows, WIDE - C), low_type)
    turned_ref[...] = grad_ref[...].astype(low_type).T
    dunits_ref[0, C : 2 * C, :] = product(turned_ref[...], attended_ref[:, :C]).T.astype(low_type)
    for sub in range(4):
        span = slice(sub * tiles, (sub + 1) * tiles)
        datt_ref[span, :C] = back_product(grad_ref[span, :].astype(low_type), unit_ref[0, C : 2 * C, :]).astype(low_type)
    dkey_ref[...] = jnp.zeros_like(dkey_ref)
    dvalue_ref[...] = jnp.zeros_like(dvalue_ref)
    blocks = bias_ref.shape[0]

    def one_block(step):
        index = blocks - 1 - step
        start, low = place_of(index, tiles)
        bias = bias_ref[index]
        tile_at = lax.rem(lax.broadcasted_iota(jnp.int32, (4 * BLOCK_TILES, LANES), 0), BLOCK_TILES)
        fresh = tile_at >= index * BLOCK_TILES - start
        span = pl.ds(low, KEY_SPAN)
        for group in range(3):
            lanes = slice(group * LANES, (group + 1) * LANES)
            query = four_planes(query_ref, start, lanes)
            datt = four_planes(datt_ref, start, lanes)
            datt = jnp.where(fresh, datt, jnp.zeros_like(datt))
            keys = head_pair(key_ref[span, lanes], group)
            values = head_pair(value_ref[span, lanes], group)
            probs = softmax_columns(back_product(keys, query), bias)
            dprobs = back_product(values, datt)
            dscores = []
            for half, prob in enumerate(probs):
                dprob = dprobs[half * KEY_SPAN : (half + 1) * KEY_SPAN]
                inner = jnp.sum(prob * dprob, 0, keepdims=True)
                dscores.append(prob * (dprob - inner) * HD ** (-0.5))
            dscores = jnp.concatenate(dscores, 0)
            probs = jnp.concatenate(probs, 0).astype(low_type)
            dscores = dscores.astype(low_type)
            dquery = product(dscores.T, keys)
            put_planes(dquery_ref, start, lanes, dquery.astype(low_type))
            dkeys = product(dscores, query)
            dvalues = product(probs, datt)
            if group < 2:
                first = lax.broadcasted_iota(jnp.int32, (KEY_SPAN, LANES), 1) < HD
                dkeys = jnp.where(first, dkeys[:KEY_SPAN], dkeys[KEY_SPAN:])
                dvalues = jnp.where(first, dvalues[:KEY_SPAN], dvalues[KEY_SPAN:])
            dkey_ref[span, lanes] += dkeys
            dvalue_ref[span, lanes] += dvalues

    pl.loop(0, blocks // 2, unroll=blocks // 2)(one_block)
    advance(1)
    pl.loop(blocks // 2, blocks, unroll=blocks - blocks // 2)(one_block)
    unit, inverse, normed = norm_rows(reduced_ref[...], gains_ref[2:3, :], gains_ref[3:4, :])
    normed_t = normed.T.astype(low_type)
    dkeys = dkey_ref[:, :C].astype(low_type)
    dvalues = dvalue_ref[:, :C].astype(low_type)
    for which, grads in enumerate((dkeys, dvalues)):
        dweight = product(normed_t, grads)
        for at, lane, width in lane_parts(C):
            part = dweight[:, lane : lane + width]
            if width < LANES:
                part = jnp.concatenate([part, jnp.zeros((C, LANES - width), jnp.float32)], 1)
            planes_ref[at, pl.ds(which, C, stride=2), :] = part
    for at, lane, width in lane_parts(C):
        dunits_ref[0, 2 * C :, lane : lane + width] = planes_ref[at, :, :width].astype(low_type)
    dnormed = back_product(dkeys, kv_ref[0]) + back_product(dvalues, kv_ref[1])
    dgain_ref[2:3, :] = jnp.sum(dnormed * unit, 0, keepdims=True)
    dgain_ref[3:4, :] = jnp.sum(dnormed, 0, keepdims=True)
    dreduced = norm_rows_back(unit, inverse, gains_ref[2:3, :], dnormed).astype(low_type)
    advance(2)
    turned_ref[...] = normed_ref[...].T
    dunits_ref[0, :C, :] = product(turned_ref[...], dquery_ref[:, :C]).astype(low_type)
    for sub in range(4):
        span = slice(sub * tiles, (sub + 1) * tiles)
        part = slice(sub * C, (sub + 1) * C)
        dunits_ref[1, part, :] = outer_sum(normed_ref[span, :], dreduced).astype(low_type)
        first_ref[span, :] = back_product(
            dquery_ref[span, :C], unit_ref[0, :C, :]
        ) + back_product(dreduced, reduce_ref[0, part, :])

    grad = first_ref[...]
    unit, inverse, _ = norm_rows(resid_ref[...], gains_ref[0:1, :], gains_ref[1:2, :])
    out_ref[...] = grad_ref[...] + norm_rows_back(unit, inverse, gains_ref[0:1, :], grad)
    dgain_ref[0:1, :] = jnp.sum(grad * unit, 0, keepdims=True)
    dgain_ref[1:2, :] = jnp.sum(grad, 0, keepdims=True)


def attention_backward(grad, resid, gains, units, at, reduces, reduce_at, bias, kept, plans, meeting):
    rows = resid.shape[0]
    tiles = rows // 4
    low = jnp.bfloat16
    shapes = (
        jax.ShapeDtypeStruct((rows, C), jnp.float32),
        jax.ShapeDtypeStruct((2, FF, C), low),
        jax.ShapeDtypeStruct((4, C), jnp.float32),
    )
    count = len(plans)

    def run(*refs):
        own_in, ride_in = refs[:13], refs[13 : 13 + count]
        own_out, ride_out = refs[13 + count : 16 + count], refs[16 + count : 16 + 2 * count]
        rest = refs[16 + 2 * count :]
        rides = rides_of(plans, ride_in, ride_out, rest[7:])
        rides.signal()
        attention_backward_kernel(rides.advance, *own_in, *own_out, *rest[:7])
        for phase in range(3, rides.phases + 1):
            rides.advance(phase)

    return pl.pallas_call(
        run,
        grid=(1,),
        out_shape=shapes + tuple(plan.out for plan in plans),
        in_specs=[
            whole((rows, C)),
            whole((rows, C)),
            whole((4, C)),
            unit_spec(at),
            unit_spec(reduce_at),
            whole(bias.shape),
        ]
        + [whole(part.shape) for part in kept]
        + [plan.in_spec for plan in plans],
        out_specs=tuple(whole(shape.shape) for shape in shapes) + tuple(plan.out_spec for plan in plans),
        scratch_shapes=[
            pltpu.VMEM((C, rows), low),
            pltpu.VMEM((rows, WIDE), low),
            pltpu.VMEM((rows, WIDE), low),
            pltpu.VMEM((tiles, WIDE), jnp.float32),
            pltpu.VMEM((tiles, WIDE), jnp.float32),
            pltpu.VMEM((rows, C), jnp.float32),
            pltpu.VMEM((3, 2 * C, LANES), jnp.float32),
        ]
        + sum([plan.scratch for plan in plans], []),
        compiler_params=pltpu.CompilerParams(collective_id=meeting, has_side_effects=True, vmem_limit_bytes=VMEM_LIMIT),
        cost_estimate=pl.CostEstimate(flops=12 * 10**9, bytes_accessed=18 * 10**6, transcendentals=10**6),
        name="attention_backward",
    )(grad, resid, gains, units, reduces, bias, *kept, *[plan.value for plan in plans])


BOTH = ("grp", "tok")


def axis_bits(axis):
    count = lax.axis_size(axis)
    return [1 << place for place in reversed(range(count.bit_length() - 1))]


def bit_order():
    tok_bits = axis_bits("tok")
    return [("grp", bit) for bit in axis_bits("grp")] + [("tok", bit) for bit in tok_bits]


MESH = pl.DeviceIdType.MESH


def exchange_setup():
    grp, tok = lax.axis_index("grp"), lax.axis_index("tok")
    n_tok = lax.axis_size("tok")
    peers = [(lax.bitwise_xor(grp, bit), tok) for bit in axis_bits("grp")]
    peers += [(grp, lax.bitwise_xor(tok, step)) for step in range(1, n_tok)]
    return (grp, tok, n_tok, peers)


def signal_all(peers):
    barrier = pltpu.get_barrier_semaphore()
    for peer in peers:
        pl.semaphore_signal(barrier, inc=1, device_id=peer, device_id_type=MESH)


def greet(peers):
    signal_all(peers)
    pl.semaphore_wait(pltpu.get_barrier_semaphore(), len(peers))


def send(source, target, sems, at, peer):
    copy = pltpu.make_async_remote_copy(
        src_ref=source,
        dst_ref=target,
        send_sem=sems[0].at[at],
        recv_sem=sems[1].at[at],
        device_id=peer,
        device_id_type=MESH,
    )
    copy.start()
    return copy


def gather_view(ref, unit, place, done):
    index = [slice(None) if name in done else place(name) for name in bit_order()]
    return ref.at[tuple([unit] + index)]


class GatherRide:
    def __init__(self, full_ref, scratch):
        self.grp, self.tok = lax.axis_index("grp"), lax.axis_index("tok")
        self.phases = len(bit_order())
        self.names = bit_order()
        self.full_ref = full_ref
        self.sems = scratch[:2]

    def order(self, unit):
        grp_bits = [("grp", bit) for bit in axis_bits("grp")]
        flip = grp_bits[::-1] if unit % 2 else grp_bits
        return [("tok", bit) for bit in axis_bits("tok")[:-1]] + flip + [("tok", 1)]

    def place(self, name):
        return (self.grp if name[0] == "grp" else self.tok) // name[1] % 2

    def partner(self, name):
        axis, bit = name
        if axis == "grp":
            return (lax.bitwise_xor(self.grp, bit), self.tok)
        return (self.grp, lax.bitwise_xor(self.tok, bit))

    def copy(self, unit, phase):
        order = self.order(unit)
        held = gather_view(self.full_ref, unit, self.place, order[:phase])
        at = phase * self.full_ref.shape[0] + unit
        return pltpu.make_async_remote_copy(
            src_ref=held,
            dst_ref=held,
            send_sem=self.sems[0].at[at],
            recv_sem=self.sems[1].at[at],
            device_id=self.partner(order[phase]),
            device_id_type=MESH,
        )

    def put(self, unit, value):
        self.full_ref[(unit,) + tuple(self.place(name) for name in bit_order())] = value

    def advance(self, phase):
        for unit in range(self.full_ref.shape[0]):
            if phase:
                self.copy(unit, phase - 1).wait()
            if phase < self.phases:
                self.copy(unit, phase).start()


def gather_scratch(total):
    phases = len(bit_order())
    return [pltpu.SemaphoreType.DMA((phases * total,))] * 2


def slot_numbers(owner_ref, slot_rows):
    owners = [owner_ref[unit] for unit in range(owner_ref.shape[0])]
    slots = []
    for unit, owner in enumerate(owners):
        rank = jnp.int32(0)
        for earlier in owners[:unit]:
            rank = rank + (earlier == owner).astype(jnp.int32)
        slots.append(owner * slot_rows + rank)
    return slots


def start_kernel(
    owner_ref, piece_ref, count_ref, patch_ref, mark_ref,
    full_ref, later_ref, total_ref, patch_halo_ref, mark_halo_ref, scalar_ref,
    recv_ref, near_s, near_r, halo_s, halo_r, *scratch,
):
    grp, tok, n_tok, peers = exchange_setup()
    slot_rows = piece_ref.shape[1]
    units, first = owner_ref.shape[0], full_ref.shape[0]
    slots = slot_numbers(owner_ref, slot_rows)
    gather = GatherRide(full_ref, scratch[:2])
    count = SumRide(count_ref, total_ref, scratch[2:])
    greet(peers)
    copies = []
    for step in range(1, n_tok):
        peer = lax.bitwise_xor(tok, step)
        landing = recv_ref.at[pl.ds(tok * slot_rows, slot_rows)]
        copies.append(send(piece_ref.at[peer], landing, (near_s, near_r), step, (grp, peer)))
    recv_ref[pl.ds(tok * slot_rows, slot_rows)] = piece_ref[tok]
    count.advance(0)
    for copy in copies:
        copy.wait()
    for unit in range(first):
        gather.put(unit, recv_ref[slots[unit]])
    gather.advance(0)
    before = (grp, lax.rem(tok + n_tok - 1, n_tok))
    mark_copy = send(mark_ref, mark_halo_ref, (halo_s, halo_r), 0, before)
    patch_copy = send(patch_ref.at[pl.ds(0, patch_halo_ref.shape[0])], patch_halo_ref, (halo_s, halo_r), 1, before)
    for unit in range(first, units):
        later_ref[unit - first] = recv_ref[slots[unit]]
    for phase in range(1, gather.phases + 1):
        count.advance(phase)
        gather.advance(phase)
    total_ref[...] = jnp.broadcast_to(
        jnp.sum(jnp.sum(total_ref[...], 0, keepdims=True), 1, keepdims=True), total_ref.shape
    )
    scalar_ref[...] = total_ref[0:1, 0:1]
    mark_copy.wait()
    patch_copy.wait()


def start_exchange(owners, pieces, count, patches, marks, first):
    n_tok, slot_rows, chunk, width = pieces.shape
    phases = len(bit_order())
    units = owners.shape[0]
    vmem = pl.BlockSpec(memory_space=pltpu.VMEM)
    full_shape = (first,) + (2,) * phases + (chunk, width)
    return pl.pallas_call(
        start_kernel,
        out_shape=(
            jax.ShapeDtypeStruct(full_shape, pieces.dtype),
            jax.ShapeDtypeStruct((units - first, chunk, width), pieces.dtype),
            jax.ShapeDtypeStruct(count.shape, count.dtype),
            jax.ShapeDtypeStruct((OVER, patches.shape[1]), patches.dtype),
            jax.ShapeDtypeStruct(marks.shape, marks.dtype),
            jax.ShapeDtypeStruct((1, 1), jnp.float32),
        ),
        in_specs=[pl.BlockSpec(memory_space=pltpu.SMEM), vmem, vmem, pl.BlockSpec(memory_space=pl.ANY), vmem],
        out_specs=(vmem, vmem, vmem, pl.BlockSpec(memory_space=pl.ANY), vmem, vmem),
        scratch_shapes=[
            pltpu.VMEM((n_tok * slot_rows, chunk, width), pieces.dtype),
            pltpu.SemaphoreType.DMA((n_tok,)),
            pltpu.SemaphoreType.DMA((n_tok,)),
            pltpu.SemaphoreType.DMA((2,)),
            pltpu.SemaphoreType.DMA((2,)),
        ]
        + gather_scratch(first)
        + sum_scratch(count.shape),
        compiler_params=pltpu.CompilerParams(collective_id=0, has_side_effects=True, vmem_limit_bytes=VMEM_LIMIT),
        name="start_exchange",
    )(owners, pieces, count, patches, marks)


def unit_order(unit):
    grp_bits = [("grp", bit) for bit in axis_bits("grp")]
    if unit % 2:
        grp_bits = grp_bits[::-1]
    return [("tok", 1)] + grp_bits + [("tok", bit) for bit in axis_bits("tok")[:-1][::-1]]


def unit_layout(order):
    left = bit_order()
    shapes = []
    for name in order:
        at = left.index(name)
        shapes.append((1 << at, 2, 1 << (len(left) - 1 - at)))
        left.remove(name)
    return shapes


SPLIT = 3


class UnitRide:
    def __init__(self, sources, out_ref, scratch, begin=0, end=None, base=0):
        self.grp, self.tok = lax.axis_index("grp"), lax.axis_index("tok")
        self.begin = begin
        self.end = len(bit_order()) if end is None else end
        self.phases = self.end - begin
        self.names = unit_order(0)[self.begin : self.end]
        self.sources = sources
        self.out_ref, self.base = out_ref, base
        self.sems = scratch[:2]
        self.stays = []
        if begin == 0:
            self.stay_sem, self.stays = scratch[2], scratch[3 : 3 + len(sources)]
            scratch = scratch[1 + len(sources) :]
        self.buffers = scratch[2:]

    def partner(self, name):
        axis, bit = name
        if axis == "grp":
            return (lax.bitwise_xor(self.grp, bit), self.tok)
        return (self.grp, lax.bitwise_xor(self.tok, bit))

    def half_of(self, name):
        return (self.grp if name[0] == "grp" else self.tok) // name[1] % 2

    def before(self, unit, phase):
        if phase == 0:
            ref, at = self.sources[unit]
            return ref.at[at]
        return self.buffers[unit * 2 * self.phases + 2 * (phase - 1) + 1]

    def landing(self, unit, phase):
        return self.buffers[unit * 2 * self.phases + 2 * phase]

    def copy(self, unit, phase):
        name = unit_order(unit)[self.begin + phase]
        at = phase * len(self.sources) + unit
        return pltpu.make_async_remote_copy(
            src_ref=self.before(unit, phase).at[:, 1 - self.half_of(name)],
            dst_ref=self.landing(unit, phase),
            send_sem=self.sems[0].at[at],
            recv_sem=self.sems[1].at[at],
            device_id=self.partner(name),
            device_id_type=MESH,
        )

    def stay(self, unit):
        mine = self.half_of(unit_order(unit)[0])
        source = self.before(unit, 0).at[:, mine]
        return pltpu.make_async_copy(source, self.stays[unit], self.stay_sem.at[unit])

    def finish(self, unit, phase):
        order = unit_order(unit)
        shapes = unit_layout(order)
        self.copy(unit, phase).wait()
        outer, _, inner = shapes[self.begin + phase]
        landed = self.landing(unit, phase)
        kept = self.stays and phase == 0
        if kept:
            self.stay(unit).wait()
        source = self.stays[unit] if kept else self.before(unit, phase)
        mine = self.half_of(order[self.begin + phase])
        target = self.out_ref.at[self.base + unit]
        if phase + 1 < self.phases:
            target = self.before(unit, phase + 1)
        whole_done = self.begin + phase + 1 == len(order)
        if not whole_done:
            low = shapes[self.begin + phase + 1][2]

        @pl.loop(0, outer * inner, unroll=min(4, outer * inner))
        def _(at):
            own = source[at // inner, at % inner] if kept else source[at // inner, mine, at % inner]
            value = own + landed[at // inner, at % inner]
            if whole_done:
                target[...] = value
            else:
                target[at // (2 * low), at // low % 2, at % low] = value

    def advance(self, phase):
        for unit in range(len(self.sources)):
            if phase:
                self.finish(unit, phase - 1)
            if phase < self.phases:
                self.copy(unit, phase).start()
            if self.stays and phase == 0:
                self.stay(unit).start()


def unit_scratch(total, chunk, width, begin=0, end=None):
    end = len(bit_order()) if end is None else end
    dma = pltpu.SemaphoreType.DMA
    buffers = [dma(((end - begin) * total,)), dma(((end - begin) * total,))]
    if begin == 0:
        outer, _, inner = unit_layout(unit_order(0))[0]
        buffers += [dma((total,))] + [pltpu.VMEM((outer, inner, chunk, width), jnp.bfloat16)] * total
    for unit in range(total):
        shapes = unit_layout(unit_order(unit))
        for phase in range(begin, end):
            outer, _, inner = shapes[phase]
            buffers.append(pltpu.VMEM((outer, inner, chunk, width), jnp.bfloat16))
            following = shapes[phase + 1] if phase + 1 < end else (1, 1, 1)
            buffers.append(pltpu.VMEM(following + (chunk, width), jnp.bfloat16))
    return buffers


def unit_blocks(units):
    chunk = units.shape[1] >> len(bit_order())
    return units.reshape((units.shape[0],) + unit_layout(unit_order(0))[0] + (chunk, units.shape[2]))


class SumRide:
    def __init__(self, source_ref, total_ref, scratch, begin=0, end=None):
        self.grp, self.tok = lax.axis_index("grp"), lax.axis_index("tok")
        self.order = unit_order(0)[begin:end]
        self.names = self.order
        self.phases = len(self.order)
        self.source_ref, self.total_ref = source_ref, total_ref
        self.sums = scratch[2]
        self.sems = scratch[:2]

    partner = UnitRide.partner

    def copy(self, phase):
        return pltpu.make_async_remote_copy(
            src_ref=self.sums.at[2 * phase],
            dst_ref=self.sums.at[2 * phase + 1],
            send_sem=self.sems[0].at[phase],
            recv_sem=self.sems[1].at[phase],
            device_id=self.partner(self.order[phase]),
            device_id_type=MESH,
        )

    def advance(self, phase):
        if phase == 0:
            self.sums[0] = self.source_ref[...].astype(self.sums.dtype)
        else:
            self.copy(phase - 1).wait()
            self.sums[2 * phase] = self.sums[2 * phase - 2] + self.sums[2 * phase - 1]
        if phase < self.phases:
            self.copy(phase).start()
        else:
            self.total_ref[...] = self.sums[2 * phase].astype(self.total_ref.dtype)


def sum_scratch(shape, dtype=jnp.float32):
    phases = len(bit_order())
    dma = pltpu.SemaphoreType.DMA
    return [dma((phases,)), dma((phases,)), pltpu.VMEM((2 * phases + 1,) + shape, dtype)]


def tail_kernel(counts, rows, pieces, cut, *refs):
    owner_ref, part_ref, refs = refs[0], refs[1], refs[2:]
    early_refs, refs = refs[: len(pieces)], refs[len(pieces) :]
    blocks, refs = refs[: len(counts)], refs[len(counts) :]
    small_refs, refs = refs[: len(rows)], refs[len(rows) :]
    owned_ref, small_out_ref, loss_ref, chunk_ref, place_ref, near_s, near_r, small_ref = refs[:8]
    scratch = refs[8:]
    sources = [(ref, at) for ref, count in zip(blocks, counts) for at in range(count)]
    total = len(sources)
    parts = part_ref.shape[0]
    grp, tok, n_tok, peers = exchange_setup()
    signal_all(peers)
    begin = 0
    for ref, count in zip(small_refs, rows):
        small_ref[begin : begin + count, :] = ref[...]
        begin += count
    small_ref[begin:, :] = jnp.zeros((small_ref.shape[0] - begin, C), jnp.float32)
    rides = Rides(
        [
            UnitRide(sources, chunk_ref, scratch[3:cut]),
            SumRide(small_ref, small_out_ref, scratch[:3]),
            UnitRide([(part_ref, at) for at in range(parts)], chunk_ref, scratch[cut:], SPLIT, None, total),
        ]
    )
    rides.peers = peers
    for phase in range(rides.phases + 1):
        rides.advance(phase)
    total += parts
    loss_ref[...] = small_out_ref[begin - 1 : begin, 0:1]
    last = total
    for ref, count in zip(early_refs, pieces):
        for at in range(count):
            chunk_ref[last + at] = ref[at]
        last += count
    chunk_ref[last] = jnp.zeros(chunk_ref.shape[1:], chunk_ref.dtype)
    slot_rows = owned_ref.shape[1]
    slots = slot_numbers(owner_ref, slot_rows)

    @pl.loop(0, n_tok * slot_rows)
    def _(at):
        unit_at = jnp.int32(last)
        for unit, slot in enumerate(slots):
            unit_at = jnp.where(slot == at, unit, unit_at)
        place_ref[at // slot_rows, at % slot_rows] = chunk_ref[unit_at]

    copies = []
    for step in range(1, n_tok):
        peer = lax.bitwise_xor(tok, step)
        copies.append(send(place_ref.at[peer], owned_ref.at[tok], (near_s, near_r), step, (grp, peer)))
    owned_ref[tok] = place_ref[tok]
    for copy in copies:
        copy.wait()


def tail_exchange(owners, slot_rows, early, part, sources, smalls, n_tok):
    chunk, width = early[0].shape[1:]
    pieces = tuple(value.shape[0] for value in early)
    counts = tuple(source.shape[0] for source in sources)
    rows = tuple(small.shape[0] for small in smalls)
    total = sum(counts)
    low = part.dtype
    vmem = pl.BlockSpec(memory_space=pltpu.VMEM)
    units = unit_scratch(total, chunk, width)
    dma = pltpu.SemaphoreType.DMA
    small = (-(-sum(rows) // 8) * 8, C)
    return pl.pallas_call(
        lambda *refs: tail_kernel(counts, rows, pieces, 3 + len(units), *refs),
        out_shape=(
            jax.ShapeDtypeStruct((n_tok, slot_rows, chunk, width), low),
            jax.ShapeDtypeStruct(small, jnp.float32),
            jax.ShapeDtypeStruct((1, 1), jnp.float32),
        ),
        in_specs=[pl.BlockSpec(memory_space=pltpu.SMEM)]
        + [vmem] * (1 + len(early))
        + [pl.BlockSpec(memory_space=pl.ANY)] * len(sources)
        + [vmem] * len(smalls),
        out_specs=(vmem, vmem, vmem),
        scratch_shapes=[
            pltpu.VMEM((total + part.shape[0] + sum(pieces) + 1, chunk, width), low),
            pltpu.VMEM((n_tok, slot_rows, chunk, width), low),
            dma((n_tok,)),
            dma((n_tok,)),
            pltpu.VMEM(small, jnp.float32),
        ]
        + sum_scratch(small)
        + units
        + unit_scratch(part.shape[0], chunk, width, SPLIT),
        compiler_params=pltpu.CompilerParams(collective_id=1, has_side_effects=True, vmem_limit_bytes=VMEM_LIMIT),
        name="tail_exchange",
    )(owners, part, *early, *[unit_blocks(source) for source in sources], *smalls)


def body(
    patches,
    labels,
    valid_mask,
    crop_counts,
    owners,
    slot_weight,
    slot_moment,
    slot_second,
    norm_params,
    norm_moment,
    norm_second,
    head_weight,
    head_moment,
    head_second,
):
    tok_dev = patches.shape[0]
    n_tok = lax.axis_size("tok")
    n_grp = lax.axis_size("grp")
    tok_index = lax.axis_index("tok")
    group_tok = tok_dev * n_tok
    counts = crop_counts[0]
    n_unit = owners.shape[0]
    slot_rows, columns = slot_weight.shape
    chunk = columns // n_tok // C
    first_tok = tok_index * tok_dev
    small_end = counts[0] * BIG_SIDE**2 + counts[1] * SMALL_SIDE**2
    counted = valid_mask * (first_tok + jnp.arange(tok_dev, dtype=jnp.int32) < small_end)
    counted = counted.astype(jnp.float32).reshape(-1, LANES)
    pieces = slot_weight.astype(jnp.bfloat16).reshape(slot_rows, n_tok, chunk, C).transpose(1, 0, 2, 3)
    first_units = 1 + 2 * (n_unit // BLOCKS)
    marks = jnp.stack([labels, valid_mask])
    own, later, counted, patch_halo, mark_halo, pixel_total = start_exchange(
        owners, pieces, counted, patches, marks[:, :OVER], first_units
    )
    pixel_total = pixel_total.reshape(())
    own = own.reshape(first_units, FF, C)
    units = lax.all_gather(later, BOTH, axis=1, tiled=True)
    layers = [
        ((own, 1, own, 2), (own, 3)),
        ((own, 5, own, 6), (own, 7)),
        ((units, 0, units, 1), (units, 2)),
    ]

    window = tok_dev + OVER
    tiles = window // 4
    marks = jnp.concatenate([marks, mark_halo], 1)
    marks = marks.reshape(2, tiles, 4).transpose(0, 2, 1).reshape(2, window)
    labels = marks[0]
    positions = first_tok + 4 * jnp.arange(tiles, dtype=jnp.int32)
    begin_at, half_side, tile_y, tile_x, is_real = image_layout(positions, counts)
    own_image = (begin_at >= first_tok) & (begin_at < first_tok + tok_dev) & (positions < group_tok)
    stacks = shift_stacks(half_side, tile_y, tile_x, is_real)

    def image_at(tile):
        at = first_tok + 4 * tile
        return jnp.where(at < group_tok, image_layout(at, counts)[0], -1)

    bias = block_bias(tiles, image_at)
    real_rows = jnp.broadcast_to(is_real.astype(jnp.float32)[:, None], (tiles, LANES))
    keep_mask = marks[1].astype(jnp.float32) * jnp.tile((own_image & is_real).astype(jnp.float32), 4)
    tail = 6 * BLOCKS
    embed_pre, resid, kernels = embed_forward(patches, patch_halo, own, norm_params[tail : tail + 2])
    kept_all = []
    for layer_at in range(BLOCKS):
        attn_units, mlp_units = layers[layer_at]
        at = 6 * layer_at
        middle, *attn_kept = attention_forward(resid, norm_params[at : at + 4], *attn_units, bias)
        output, *mlp_kept = mlp_forward(
            middle, norm_params[at + 4 : at + 6], *mlp_units, kernels, layer_at, stacks, real_rows,
        )
        w_up = mlp_kept.pop()
        kept_all.append((resid, attn_kept, middle, mlp_kept, w_up))
        resid = output
    grad_res, d_head, final_gains, loss_row = head_step(
        resid, norm_params[tail + 2 : tail + 4], head_weight, labels[:, None], keep_mask[:, None], counted
    )
    unit_plans = []
    head_cuts = [0, SPLIT, len(bit_order())]
    early = []
    kernel_grads = [None] * BLOCKS
    gain_grads = []
    phases = len(bit_order())

    def head_plans(value):
        if len(head_cuts) < 2:
            return []
        begin = head_cuts.pop(0)
        return [plan_sum(value, begin, head_cuts[0])]

    for layer_at in reversed(range(BLOCKS)):
        attn_units, mlp_units = layers[layer_at]
        at = 6 * layer_at
        entry, attn_kept, middle, mlp_kept, w_up = kept_all[layer_at]
        grad_res, mlp_grads, kernel_grads[layer_at], mlp_gains, *ridden_out = mlp_backward(
            grad_res, middle, norm_params[at + 4 : at + 6], w_up, *mlp_units, kernels, layer_at,
            stacks, real_rows, mlp_kept, unit_plans + head_plans(d_head), 2 + layer_at,
        )
        if layer_at + 1 == BLOCKS:
            d_head = ridden_out.pop()
        unit_plans = [plan_units(mlp_grads, 0, SPLIT)]
        if ridden_out:
            early.insert(0, ridden_out[1])
            unit_plans.append(plan_units(ridden_out[0], SPLIT, phases))
        plans = unit_plans + head_plans(d_head)
        grad_res, attn_grads, attn_gains, *ridden_out = attention_backward(
            grad_res, entry, norm_params[at : at + 4], *attn_units, bias, attn_kept, plans, 2 + BLOCKS + layer_at
        )
        if len(plans) > len(unit_plans):
            d_head = ridden_out.pop()
        if layer_at + 1 < BLOCKS:
            early.insert(0, ridden_out[1])
        unit_plans = [plan_units(attn_grads, 0, SPLIT), plan_units(ridden_out[0], SPLIT, phases)]
        gain_grads = [attn_gains, mlp_gains] + gain_grads
    head_total = d_head[: head_weight.shape[1]].T
    part = ridden_out[0]
    first_grad, embed_gains = embed_backward(
        grad_res, embed_pre, norm_params[tail : tail + 2], patches, patch_halo, kernel_grads
    )
    smalls = gain_grads + [embed_gains, final_gains, loss_row]
    owned, small, loss_sum = tail_exchange(owners, slot_rows, early, part, [first_grad, attn_grads], smalls, n_tok)
    owned = owned.transpose(1, 0, 2, 3).astype(jnp.float32).reshape(slot_rows, columns)
    norm_rows_all = norm_params.shape[0]
    norm_total = small[:norm_rows_all]
    loss_sum = loss_sum.reshape(())
    slot_m, slot_v, slot_w = adamw_step(
        slot_weight, slot_moment, slot_second, owned, RATE_MATRIX, DECAY_RATE
    )
    norm_m, norm_v, norm_w = adamw_step(
        norm_params, norm_moment, norm_second, norm_total, RATE_VECTOR, 0.0
    )
    head_m, head_v, head_w = adamw_step(
        head_weight, head_moment, head_second, head_total, RATE_MATRIX, DECAY_RATE
    )
    return (
        loss_sum,
        pixel_total,
        slot_m,
        slot_v,
        slot_w,
        norm_m,
        norm_v,
        norm_w,
        head_m,
        head_v,
        head_w,
    )


def solution(mesh):
    in_specs = (
        P(("grp", "tok"), None),
        P(("grp", "tok")),
        P(("grp", "tok")),
        P("grp", None),
        P(),
        P("tok", "grp"),
        P("tok", "grp"),
        P("tok", "grp"),
        P(),
        P(),
        P(),
        P(),
        P(),
        P(),
    )
    out_specs = (
        P(),
        P(),
        P("tok", "grp"),
        P("tok", "grp"),
        P("tok", "grp"),
        P(),
        P(),
        P(),
        P(),
        P(),
        P(),
    )
    return jax.shard_map(body, mesh=mesh, in_specs=in_specs, out_specs=out_specs, check_vma=False)
```

```python
import functools

import jax
import jax.numpy as jnp
import numpy as np
from jax import lax
from jax.experimental import pallas as pl
from jax.experimental.pallas import tpu as pltpu
from jax.sharding import PartitionSpec as P

C = 320
HEADS = 5
HD = 64
FF = 1280
PIN = 1152
BLOCKS = 3
BIG_SIDE = 14
SMALL_SIDE = 6
STEP = 10
KVH = 49


EPS_NORM = 1e-06
BETA_ONE = 0.9
BETA_TWO = 0.999
ADAM_EPS = 1e-08
RATE_MATRIX = 0.05
RATE_VECTOR = 0.3
DECAY_RATE = 0.05
NEG_FILL = -1e30
PREC_HIGH = lax.Precision.HIGHEST


def layer_norm(values, gain_vec, shift_vec):
    center = values - jnp.mean(values, -1, keepdims=True)
    inverse = lax.rsqrt(jnp.mean(center * center, -1, keepdims=True) + EPS_NORM)
    return center * inverse * gain_vec + shift_vec


def adamw_step(weight, moment, second, gradient, rate_now, decay_now):
    moment = BETA_ONE * moment + (1.0 - BETA_ONE) * gradient
    second = BETA_TWO * second + (1.0 - BETA_TWO) * gradient * gradient
    m_hat = moment / (1.0 - BETA_ONE**STEP)
    v_hat = second / (1.0 - BETA_TWO**STEP)
    weight = weight - rate_now * (m_hat / (jnp.sqrt(v_hat) + ADAM_EPS) + decay_now * weight)
    return (moment, second, weight)


def product(left, right):
    return jnp.dot(left, right, preferred_element_type=jnp.float32)


def outer_sum(left, right):
    return lax.dot_general(
        left, right, (((0,), (0,)), ((), ())), preferred_element_type=jnp.float32
    )


def back_product(gradient, weight):
    return lax.dot_general(
        gradient, weight, (((1,), (1,)), ((), ())), preferred_element_type=jnp.float32
    )


def norm_back(values, gain_vec, shift_vec, gradient):
    _, pull_back = jax.vjp(layer_norm, values, gain_vec, shift_vec)
    return pull_back(gradient)


OVER = 4 * KVH - 4


def image_layout(positions, counts):
    big_tok = BIG_SIDE * BIG_SIDE
    small_tok = SMALL_SIDE * SMALL_SIDE
    big_end = counts[0] * big_tok
    small_end = big_end + counts[1] * small_tok
    is_big = positions < big_end
    is_small = jnp.logical_and(positions >= big_end, positions < small_end)
    half_side = jnp.where(is_big, BIG_SIDE // 2, SMALL_SIDE // 2)
    begin_at = jnp.where(
        is_big,
        positions // big_tok * big_tok,
        jnp.where(is_small, big_end + (positions - big_end) // small_tok * small_tok, small_end),
    )
    tile_idx = (positions - begin_at) // 4
    return (begin_at, half_side, tile_idx // half_side, tile_idx % half_side, positions < small_end)


def shift_stacks(half_side, tile_y, tile_x, is_real):
    tiles = half_side.shape[0]
    step_y = np.array([[0, 1 - 2 * (sub // 2), 1 - 2 * (sub // 2)] for sub in range(4)], np.int32)[:, :, None]
    step_x = np.array([[1 - 2 * (sub % 2), 0, 1 - 2 * (sub % 2)] for sub in range(4)], np.int32)[:, :, None]
    at_y = tile_y + step_y
    at_x = tile_x + step_x
    inside = is_real & (at_y >= 0) & (at_y < half_side) & (at_x >= 0) & (at_x < half_side)
    source = jnp.arange(tiles, dtype=jnp.int32) + step_y * half_side + step_x
    source = jnp.where(inside, source, -1)
    cut = row_cut(tiles)
    columns = jnp.arange(SPAN, dtype=jnp.int32)
    upper = (source[:, :, :cut, None] == columns).astype(jnp.bfloat16)
    lower = (source[:, :, cut:, None] == columns + (tiles - SPAN)).astype(jnp.bfloat16)
    return (upper.reshape(4, 3 * cut, SPAN), lower.reshape(4, 3 * (tiles - cut), SPAN))


def tap_source(sub, tap):
    y_at = sub // 2 + tap // 3 - 1
    x_at = sub % 2 + tap % 3 - 1
    return (y_at % 2 * 2 + x_at % 2, y_at // 2, x_at // 2)


SQRT_HALF = 0.7071067811865476
INV_SQRT_TWO_PI = 0.3989422804014327
TAPS_OF = [[tap_source(sub, tap) for tap in range(9)] for sub in range(4)]
VMEM_LIMIT = 56 * 1024 * 1024
SPAN = 256
ROWS = 16
LANES = 128


def row_cut(tiles):
    return (tiles // 2 + 15) // 16 * 16


def move_planes(planes_ref, upper_ref, lower_ref, moved_ref):
    tiles = planes_ref.shape[0] // 4
    cut = row_cut(tiles)
    for sub in range(4):
        base = sub * tiles
        part = product(upper_ref[sub], planes_ref[base : base + SPAN, :])
        for key in range(3):
            moved_ref[sub, key, :cut, :] = part[key * cut : (key + 1) * cut]
        part = product(lower_ref[sub], planes_ref[base + tiles - SPAN : base + tiles, :])
        for key in range(3):
            moved_ref[sub, key, cut:, :] = part[key * (tiles - cut) : (key + 1) * (tiles - cut)]


def chunk_sources(planes_ref, moved_ref, row, lanes):
    tiles = planes_ref.shape[0] // 4
    found = {}
    for sub in range(4):
        found[sub, 0, 0] = planes_ref[pl.ds(pl.multiple_of(sub * tiles + row, ROWS), ROWS), lanes].astype(jnp.float32)
        step_y = 1 - 2 * (sub // 2)
        step_x = 1 - 2 * (sub % 2)
        for key, step in enumerate(((0, step_x), (step_y, 0), (step_y, step_x))):
            found[(sub,) + step] = moved_ref[sub, key, pl.ds(row, ROWS), lanes]
    return found


def norm_rows(values, gain, shift):
    center = values - jnp.mean(values, -1, keepdims=True)
    inverse = lax.rsqrt(jnp.mean(center * center, -1, keepdims=True) + EPS_NORM)
    unit = center * inverse
    return (unit, inverse, unit * gain + shift)


def norm_rows_back(unit, inverse, gain, grad):
    scaled = grad * gain
    return inverse * (
        scaled - jnp.mean(scaled, -1, keepdims=True) - unit * jnp.mean(scaled * unit, -1, keepdims=True)
    )


def mlp_forward_kernel(
    middle_ref, gains_ref, up_ref, down_ref, kern_ref, upper_ref, lower_ref, real_ref,
    out_ref, hidden_ref, active_ref, slope_ref, turned_ref,
    normed_ref, moved_ref, planes_ref,
):
    rows = middle_ref.shape[0]
    block = hidden_ref.shape[1]
    tiles = rows // 4

    @pl.when(pl.program_id(0) == 0)
    def _():
        normed = norm_rows(middle_ref[...], gains_ref[0:1, :], gains_ref[1:2, :])[2]
        normed_ref[...] = normed.astype(jnp.bfloat16)
        out_ref[...] = middle_ref[...]
        spread_rows(up_ref[0], planes_ref)
        for quarter in range(FF // C):
            for at, lane, width in lane_parts(C):
                part = planes_ref[at, pl.ds(quarter, C, stride=FF // C), :][:, :width]
                begin = quarter * C + lane
                turned_ref[:, begin : begin + width] = part.astype(jnp.bfloat16)

    for sub in range(4):
        columns = pl.ds(pl.multiple_of(pl.program_id(0) * block, block), block)
        part = product(normed_ref[sub * tiles : (sub + 1) * tiles, :], turned_ref[:, columns])
        hidden_ref[sub * tiles : (sub + 1) * tiles, :] = part.astype(jnp.bfloat16)
    move_planes(hidden_ref, upper_ref, lower_ref, moved_ref)

    for lane in range(0, hidden_ref.shape[1], LANES):
        lanes = slice(lane, lane + LANES)
        kern = [kern_ref[0, tap : tap + 1, lanes] for tap in range(9)]

        @pl.loop(0, tiles // ROWS, unroll=tiles // ROWS)
        def _(at):
            row = pl.multiple_of(at * ROWS, ROWS)
            found = chunk_sources(hidden_ref, moved_ref, row, lanes)
            real = real_ref[pl.ds(row, ROWS), :] > 0.0
            for sub in range(4):
                center = found[sub, 0, 0] * kern[4]
                total = center
                for tap in range(9):
                    if tap != 4:
                        total = total + found[TAPS_OF[sub][tap]] * kern[tap]
                mixed = jnp.where(real, total, center)
                half = 0.5 + 0.5 * lax.erf(mixed * SQRT_HALF)
                bell = jnp.exp(-0.5 * mixed * mixed) * INV_SQRT_TWO_PI
                span = pl.ds(pl.multiple_of(sub * tiles + row, ROWS), ROWS)
                active_ref[span, lanes] = (mixed * half).astype(jnp.bfloat16)
                slope_ref[span, lanes] = (half + mixed * bell).astype(jnp.bfloat16)

    for sub in range(4):
        span = slice(sub * tiles, (sub + 1) * tiles)
        out_ref[span, :] += product(active_ref[span, :], down_ref[0])


def lane_parts(width):
    return [(at, lane, min(LANES, width - lane)) for at, lane in enumerate(range(0, width, LANES))]


def spread_rows(source, planes_ref):
    for at, lane, width in lane_parts(source.shape[1]):
        planes_ref[at, :, :width] = source[:, lane : lane + width].astype(jnp.float32)


class Plan:
    def __init__(self, value, out, scratch, make, space=None):
        self.value, self.out, self.scratch, self.make = value, out, scratch, make
        self.in_spec = pl.BlockSpec(memory_space=space) if space is not None else whole(value.shape)
        self.out_spec = whole(out.shape)


def plan_sum(value, begin, end):
    make = functools.partial(SumRide, begin=begin, end=end)
    return Plan(value, jax.ShapeDtypeStruct(value.shape, value.dtype), sum_scratch(value.shape, jnp.bfloat16), make)


def plan_units(value, begin, end):
    if begin == 0:
        value = unit_blocks(value)
    total, (chunk, width) = value.shape[0], value.shape[-2:]
    inside = unit_layout(unit_order(0))[end] if end < len(bit_order()) else ()
    out = jax.ShapeDtypeStruct((total,) + inside + (chunk, width), value.dtype)

    def make(ride_in, ride_out, scratch):
        sources = [(ride_in, at) for at in range(total)]
        return UnitRide(sources, ride_out, scratch, begin, end)

    space = pl.ANY if begin == 0 else None
    return Plan(value, out, unit_scratch(total, chunk, width, begin, end), make, space)


class Rides:
    def __init__(self, rides):
        self.rides = rides
        self.phases = max(ride.phases for ride in rides)
        names = [name for name in bit_order() if any(name in ride.names for ride in rides)]
        self.peers = [UnitRide.partner(rides[0], name) for name in names]

    def signal(self):
        signal_all(self.peers)

    def advance(self, phase):
        if phase == 0:
            pl.semaphore_wait(pltpu.get_barrier_semaphore(), len(self.peers))
        for ride in self.rides:
            if phase <= ride.phases:
                ride.advance(phase)


def rides_of(plans, ins, outs, scratch):
    rides = []
    for plan, ride_in, ride_out in zip(plans, ins, outs):
        count = len(plan.scratch)
        rides.append(plan.make(ride_in, ride_out, scratch[:count]))
        scratch = scratch[count:]
    return Rides(rides)


def ridden(kernel, inputs, outputs, scratch, steps, plans):
    def run(*refs):
        own_in, refs = refs[:inputs], refs[inputs:]
        ride_in, refs = refs[: len(plans)], refs[len(plans) :]
        own_out, refs = refs[:outputs], refs[outputs:]
        ride_out, rest = refs[: len(plans)], refs[len(plans) :]
        rides = rides_of(plans, ride_in, ride_out, rest[scratch:])
        places = [0] + list(range(1, steps - 1, 2))
        for phase, step in enumerate(places):
            if phase == 0:

                @pl.when(pl.program_id(0) == step)
                def _():
                    rides.signal()
                    rides.advance(0)
            elif phase <= rides.phases:
                pl.when(pl.program_id(0) == step)(functools.partial(rides.advance, phase))
        kernel(*own_in, *own_out, *rest[:scratch])

        @pl.when(pl.program_id(0) == steps - 1)
        def _():
            for phase in range(len(places), rides.phases + 1):
                rides.advance(phase)

    return run


def whole(shape):
    return pl.BlockSpec(shape, lambda j: (0,) * len(shape))


def unit_spec(at):
    return pl.BlockSpec((1, FF, C), lambda j: (at, 0, 0))


def mlp_forward(middle, gains, units, at, kernel, layer_at, stacks, real_rows):
    rows = middle.shape[0]
    block = 256
    by_lane = pl.BlockSpec((rows, block), lambda j: (0, j))
    low = jax.ShapeDtypeStruct((rows, FF), jnp.bfloat16)
    return pl.pallas_call(
        mlp_forward_kernel,
        grid=(FF // block,),
        out_shape=(
            jax.ShapeDtypeStruct((rows, C), jnp.float32),
            low,
            low,
            low,
            jax.ShapeDtypeStruct((C, FF), jnp.bfloat16),
        ),
        in_specs=[
            whole((rows, C)),
            whole((2, C)),
            unit_spec(at),
            pl.BlockSpec((1, block, C), lambda j: (at + 1, j, 0)),
            pl.BlockSpec((1, 9, block), lambda j: (layer_at, 0, j)),
            whole(stacks[0].shape),
            whole(stacks[1].shape),
            whole(real_rows.shape),
        ],
        out_specs=(whole((rows, C)), by_lane, by_lane, by_lane, whole((C, FF))),
        scratch_shapes=[
            pltpu.VMEM((rows, C), jnp.bfloat16),
            pltpu.VMEM((4, 3, rows // 4, block), jnp.float32),
            pltpu.VMEM((3, FF, LANES), jnp.float32),
        ],
        compiler_params=pltpu.CompilerParams(vmem_limit_bytes=VMEM_LIMIT),
        cost_estimate=pl.CostEstimate(flops=14 * 10**9, bytes_accessed=18 * 10**6, transcendentals=4 * 10**6),
        name="mlp_forward",
    )(middle, gains, units, units, kernel, stacks[0], stacks[1], real_rows)


def mlp_backward_kernel(
    grad_ref, middle_ref, gains_ref, up_ref, down_ref, kern_ref, upper_ref, lower_ref, real_ref,
    hidden_ref, active_ref, slope_ref,
    out_ref, dunits_ref, dkern_ref, dgain_ref,
    low_ref, low_t_ref, normed_t_ref, mixed_ref, dhid_ref, moved_ref, back_ref, wide_ref, planes_ref,
):
    rows = grad_ref.shape[0]
    tiles = rows // 4
    block = hidden_ref.shape[1]

    @pl.when(pl.program_id(0) == 0)
    def _():
        for sub in range(4):
            span = slice(sub * tiles, (sub + 1) * tiles)
            low_ref[span, :] = grad_ref[span, :].astype(jnp.bfloat16)
        normed = norm_rows(middle_ref[...], gains_ref[0:1, :], gains_ref[1:2, :])[2]
        normed_t_ref[...] = normed.astype(jnp.bfloat16).T
        low_t_ref[...] = low_ref[...].T
        back_ref[...] = jnp.zeros_like(back_ref)

    for sub in range(4):
        span = slice(sub * tiles, (sub + 1) * tiles)
        part = back_product(low_ref[span, :], down_ref[0]).astype(jnp.bfloat16).astype(jnp.float32)
        mixed_ref[span, :] = (part * slope_ref[span, :].astype(jnp.float32)).astype(jnp.bfloat16)
    down_rows = pl.ds(pl.multiple_of(pl.program_id(0) * block, block), block)
    dunits_ref[1, down_rows, :] = product(low_t_ref[...], active_ref[...]).T.astype(jnp.bfloat16)
    move_planes(mixed_ref, upper_ref, lower_ref, moved_ref)

    for lane in range(0, block, LANES):
        lanes = slice(lane, lane + LANES)
        kern = [kern_ref[0, tap : tap + 1, lanes] for tap in range(9)]

        def step(at, sums):
            row = pl.multiple_of(at * ROWS, ROWS)
            found = chunk_sources(mixed_ref, moved_ref, row, lanes)
            real = real_ref[pl.ds(row, ROWS), :] > 0.0
            sums = list(sums)
            for sub in range(4):
                span = pl.ds(pl.multiple_of(sub * tiles + row, ROWS), ROWS)
                hidden = hidden_ref[span, lanes].astype(jnp.float32)
                center = found[sub, 0, 0] * kern[4]
                total = center
                for tap in range(9):
                    term = found[TAPS_OF[sub][tap]]
                    if tap != 4:
                        total = total + term * kern[8 - tap]
                    piece = hidden * term
                    sums[tap] = sums[tap] + piece[:8] + piece[8:]
                dhid_ref[span, lanes] = jnp.where(real, total, center).astype(jnp.bfloat16)
            return tuple(sums)

        sums = lax.fori_loop(0, tiles // ROWS, step, (jnp.zeros((8, LANES), jnp.float32),) * 9, unroll=True)
        for tap in range(9):
            dkern_ref[8 - tap : 9 - tap, lanes] = jnp.sum(sums[tap], 0, keepdims=True)

    columns = pl.ds(pl.multiple_of(pl.program_id(0) * block, block), block)
    wide_ref[:, columns] = product(normed_t_ref[...], dhid_ref[...])
    for sub in range(4):
        span = slice(sub * tiles, (sub + 1) * tiles)
        back_ref[span, :] += back_product(dhid_ref[span, :], up_ref[...])

    @pl.when(pl.program_id(0) == pl.num_programs(0) - 1)
    def _():
        grad = back_ref[...]
        unit, inverse, _ = norm_rows(middle_ref[...], gains_ref[0:1, :], gains_ref[1:2, :])
        out_ref[...] = grad_ref[...] + norm_rows_back(unit, inverse, gains_ref[0:1, :], grad)
        dgain_ref[0:1, :] = jnp.sum(grad * unit, 0, keepdims=True)
        dgain_ref[1:2, :] = jnp.sum(grad, 0, keepdims=True)
        for quarter in range(FF // C):
            for at, lane, width in lane_parts(C):
                begin = quarter * C + lane
                part = wide_ref[:, begin : begin + width]
                if width < LANES:
                    part = jnp.concatenate([part, jnp.zeros((C, LANES - width), jnp.float32)], 1)
                planes_ref[at, pl.ds(quarter, C, stride=FF // C), :] = part
        for at, lane, width in lane_parts(C):
            dunits_ref[0, :, lane : lane + width] = planes_ref[at, :, :width].astype(jnp.bfloat16)


def mlp_backward(grad, middle, gains, w_up, units, at, kernel, layer_at, stacks, real_rows, kept, plans, meeting):
    rows = middle.shape[0]
    block = 256
    by_lane = pl.BlockSpec((rows, block), lambda j: (0, j))
    up_spec = pl.BlockSpec((C, block), lambda j: (0, j))
    tap_spec = pl.BlockSpec((9, block), lambda j: (0, j))
    return pl.pallas_call(
        ridden(mlp_backward_kernel, 12, 4, 9, FF // block, plans),
        grid=(FF // block,),
        out_shape=(
            jax.ShapeDtypeStruct((rows, C), jnp.float32),
            jax.ShapeDtypeStruct((2, FF, C), jnp.bfloat16),
            jax.ShapeDtypeStruct((9, FF), jnp.float32),
            jax.ShapeDtypeStruct((2, C), jnp.float32),
            *[plan.out for plan in plans],
        ),
        in_specs=[
            whole((rows, C)),
            whole((rows, C)),
            whole((2, C)),
            up_spec,
            pl.BlockSpec((1, block, C), lambda j: (at + 1, j, 0)),
            pl.BlockSpec((1, 9, block), lambda j: (layer_at, 0, j)),
            whole(stacks[0].shape),
            whole(stacks[1].shape),
            whole(real_rows.shape),
            by_lane,
            by_lane,
            by_lane,
        ]
        + [plan.in_spec for plan in plans],
        out_specs=(whole((rows, C)), whole((2, FF, C)), tap_spec, whole((2, C)))
        + tuple(plan.out_spec for plan in plans),
        scratch_shapes=[
            pltpu.VMEM((rows, C), jnp.bfloat16),
            pltpu.VMEM((C, rows), jnp.bfloat16),
            pltpu.VMEM((C, rows), jnp.bfloat16),
            pltpu.VMEM((rows, block), jnp.bfloat16),
            pltpu.VMEM((rows, block), jnp.bfloat16),
            pltpu.VMEM((4, 3, rows // 4, block), jnp.float32),
            pltpu.VMEM((rows, C), jnp.float32),
            pltpu.VMEM((C, FF), jnp.float32),
            pltpu.VMEM((3, FF, LANES), jnp.float32),
        ]
        + sum([plan.scratch for plan in plans], []),
        compiler_params=pltpu.CompilerParams(
            collective_id=meeting, has_side_effects=True, vmem_limit_bytes=VMEM_LIMIT
        ),
        cost_estimate=pl.CostEstimate(flops=18 * 10**9, bytes_accessed=18 * 10**6, transcendentals=0),
        name="mlp_backward",
    )(grad, middle, gains, w_up, units, kernel, stacks[0], stacks[1], real_rows, *kept, *[plan.value for plan in plans])


WIDE = 384
BLOCK_TILES = 32
KEY_SPAN = 128


def block_places(tiles):
    places = []
    for index in range(-(-tiles // BLOCK_TILES)):
        start = min(index * BLOCK_TILES, tiles - BLOCK_TILES)
        places.append((start, min(max(start - 48, 0), tiles - KEY_SPAN)))
    return places


def block_bias(tiles, image_at):
    starts, lows = np.array(block_places(tiles), np.int32).T[:, :, None]
    columns = starts + np.tile(np.arange(BLOCK_TILES, dtype=np.int32), 4)
    rows = lows + np.arange(KEY_SPAN, dtype=np.int32)
    same = image_at(jnp.asarray(rows))[:, :, None] == image_at(jnp.asarray(columns))[:, None, :]
    return jnp.where(same, 0.0, NEG_FILL)


def place_of(index, tiles):
    start = jnp.minimum(index * BLOCK_TILES, tiles - BLOCK_TILES)
    low = jnp.clip(start - 48, 0, tiles - KEY_SPAN)
    return (pl.multiple_of(start, ROWS), pl.multiple_of(low, ROWS))


def four_planes(ref, start, lanes):
    tiles = ref.shape[0] // 4
    return jnp.concatenate(
        [ref[pl.ds(pl.multiple_of(sub * tiles + start, ROWS), BLOCK_TILES), lanes] for sub in range(4)], 0
    )


def put_planes(ref, start, lanes, values):
    tiles = ref.shape[0] // 4
    for sub in range(4):
        ref[pl.ds(pl.multiple_of(sub * tiles + start, ROWS), BLOCK_TILES), lanes] = values[
            sub * BLOCK_TILES : (sub + 1) * BLOCK_TILES
        ]


def head_pair(values, group):
    if group == 2:
        return values
    first = lax.broadcasted_iota(jnp.int32, values.shape, 1) < HD
    zero = jnp.zeros_like(values)
    return jnp.concatenate([jnp.where(first, values, zero), jnp.where(first, zero, values)], 0)


def softmax_columns(raw, bias):
    parts = []
    for half in range(raw.shape[0] // KEY_SPAN):
        scores = raw[half * KEY_SPAN : (half + 1) * KEY_SPAN] * HD ** (-0.5) + bias
        weights = jnp.exp(scores - jnp.max(scores, 0, keepdims=True))
        parts.append(weights * (1.0 / jnp.sum(weights, 0, keepdims=True)))
    return parts


def norm_store(source_ref, gains_ref, at, target_ref):
    normed = norm_rows(source_ref[...], gains_ref[at : at + 1, :], gains_ref[at + 1 : at + 2, :])[2]
    target_ref[...] = normed.astype(jnp.bfloat16)


def part_keyval(unit_ref, planes_ref, kv_ref):
    spread_rows(unit_ref[0, 2 * C :, :], planes_ref)
    for which in range(2):
        for at, lane, width in lane_parts(C):
            part = planes_ref[at, pl.ds(which, C, stride=2), :][:, :width]
            kv_ref[which, :, lane : lane + width] = part.astype(jnp.bfloat16)


def attention_forward_kernel(
    resid_ref, gains_ref, unit_ref, reduce_ref, bias_ref,
    middle_ref, normed_ref, query_ref, reduced_ref, key_ref, value_ref, attended_ref, kv_ref,
    planes_ref,
):
    part_keyval(unit_ref, planes_ref, kv_ref)
    rows = resid_ref.shape[0]
    tiles = rows // 4
    norm_store(resid_ref, gains_ref, 0, normed_ref)
    query_ref[:, C:] = jnp.zeros((rows, WIDE - C), jnp.bfloat16)
    reduced = jnp.zeros((tiles, C), jnp.float32)
    for sub in range(4):
        span = slice(sub * tiles, (sub + 1) * tiles)
        query_ref[span, :C] = product(normed_ref[span, :], unit_ref[0, :C, :]).astype(jnp.bfloat16)
        reduced = reduced + product(normed_ref[span, :], reduce_ref[0, sub * C : (sub + 1) * C, :])
    reduced_ref[...] = reduced
    normed_kv = norm_rows(reduced, gains_ref[2:3, :], gains_ref[3:4, :])[2].astype(jnp.bfloat16)
    for which, ref in enumerate((key_ref, value_ref)):
        ref[:, C:] = jnp.zeros((tiles, WIDE - C), jnp.bfloat16)
        ref[:, :C] = product(normed_kv, kv_ref[which]).astype(jnp.bfloat16)

    @pl.loop(0, bias_ref.shape[0], unroll=bias_ref.shape[0])
    def _(index):
        start, low = place_of(index, tiles)
        bias = bias_ref[index]
        for group in range(3):
            lanes = slice(group * LANES, (group + 1) * LANES)
            query = four_planes(query_ref, start, lanes)
            keys = head_pair(key_ref[pl.ds(low, KEY_SPAN), lanes], group)
            values = head_pair(value_ref[pl.ds(low, KEY_SPAN), lanes], group)
            probs = softmax_columns(back_product(keys, query), bias)
            probs = jnp.concatenate(probs, 0).astype(jnp.bfloat16).T
            put_planes(attended_ref, start, lanes, product(probs, values).astype(jnp.bfloat16))

    for sub in range(4):
        span = slice(sub * tiles, (sub + 1) * tiles)
        middle_ref[span, :] = resid_ref[span, :] + product(attended_ref[span, :C], unit_ref[0, C : 2 * C, :])


def attention_forward(resid, gains, units, at, reduces, reduce_at, bias):
    rows = resid.shape[0]
    tiles = rows // 4
    low = jnp.bfloat16
    shapes = (
        jax.ShapeDtypeStruct((rows, C), jnp.float32),
        jax.ShapeDtypeStruct((rows, C), low),
        jax.ShapeDtypeStruct((rows, WIDE), low),
        jax.ShapeDtypeStruct((tiles, C), jnp.float32),
        jax.ShapeDtypeStruct((tiles, WIDE), low),
        jax.ShapeDtypeStruct((tiles, WIDE), low),
        jax.ShapeDtypeStruct((rows, WIDE), low),
        jax.ShapeDtypeStruct((2, C, C), low),
    )
    return pl.pallas_call(
        attention_forward_kernel,
        grid=(1,),
        out_shape=shapes,
        in_specs=[whole((rows, C)), whole((4, C)), unit_spec(at), unit_spec(reduce_at), whole(bias.shape)],
        out_specs=tuple(whole(shape.shape) for shape in shapes),
        scratch_shapes=[pltpu.VMEM((3, 2 * C, LANES), jnp.float32)],
        compiler_params=pltpu.CompilerParams(vmem_limit_bytes=VMEM_LIMIT),
        cost_estimate=pl.CostEstimate(flops=6 * 10**9, bytes_accessed=14 * 10**6, transcendentals=10**6),
        name="attention_forward",
    )(resid, gains, units, reduces, bias)


def embed_forward_kernel(
    patches_ref, halo_ref, unit_ref, gains_ref, pre_ref, resid_ref, kern_ref, planes_ref, taps_ref
):
    rows = pre_ref.shape[0]
    tiles = rows // 4
    used = FF * 9 * BLOCKS // C
    for ref, base in ((patches_ref, 0), (halo_ref, patches_ref.shape[0])):
        step = 256 if ref.shape[0] % 256 == 0 else ref.shape[0]
        for at in range(ref.shape[0] // step):
            span = slice(at * step, (at + 1) * step)
            into = slice(base + at * step, base + (at + 1) * step)
            part = product(ref[span, :], unit_ref[0, :PIN, :])
            for place, lane, width in lane_parts(C):
                planes_ref[place, into, :width] = part[:, lane : lane + width]

    for sub in range(4):
        for place, lane, width in lane_parts(C):
            pre_ref[sub * tiles : (sub + 1) * tiles, lane : lane + width] = planes_ref[
                place, pl.ds(sub, tiles, stride=4), :
            ][:, :width]
    taps = unit_ref[0, PIN : PIN + taps_ref.shape[1], :]
    spread_rows(taps, taps_ref)
    for layer_at in range(BLOCKS):
        for quarter in range(FF // C):
            for place, lane, width in lane_parts(C):
                begin = quarter * C + lane
                kern_ref[layer_at, :, begin : begin + width] = taps_ref[
                    place, pl.ds(layer_at * (used // BLOCKS) + quarter, 9, stride=FF // C), :
                ][:, :width]

    resid_ref[...] = norm_rows(pre_ref[...], gains_ref[0:1, :], gains_ref[1:2, :])[2]


def embed_forward(patches, halo, units, gains):
    rows = patches.shape[0] + halo.shape[0]
    wide = jax.ShapeDtypeStruct((rows, C), jnp.float32)
    taps = jax.ShapeDtypeStruct((BLOCKS, 9, FF), jnp.float32)
    return pl.pallas_call(
        embed_forward_kernel,
        grid=(1,),
        out_shape=(wide, wide, taps),
        in_specs=[whole(patches.shape), whole(halo.shape), unit_spec(0), whole((2, C))],
        out_specs=(whole(wide.shape), whole(wide.shape), whole(taps.shape)),
        scratch_shapes=[
            pltpu.VMEM((3, rows, LANES), jnp.float32),
            pltpu.VMEM((3, FF - PIN, LANES), jnp.float32),
        ],
        compiler_params=pltpu.CompilerParams(vmem_limit_bytes=VMEM_LIMIT),
        cost_estimate=pl.CostEstimate(flops=10**9, bytes_accessed=8 * 10**6, transcendentals=0),
        name="embed_forward",
    )(patches, halo, units, gains)


def embed_backward_kernel(
    grad_ref, pre_ref, gains_ref, patches_ref, halo_ref, *refs
):
    taps_refs = refs[:BLOCKS]
    unit_ref, dgain_ref, planes_ref, turned_ref, taps_ref = refs[BLOCKS:]
    rows = pre_ref.shape[0]
    tiles = rows // 4
    half = tiles // 2
    used = FF * 9 * BLOCKS // C
    sums = [jnp.zeros((1, C), jnp.float32)] * 2
    for sub in range(4):
        for part_at in range(2):
            span = slice(sub * tiles + part_at * half, sub * tiles + (part_at + 1) * half)
            unit, inverse, _ = norm_rows(pre_ref[span, :], gains_ref[0:1, :], gains_ref[1:2, :])
            grad = grad_ref[span, :]
            back = norm_rows_back(unit, inverse, gains_ref[0:1, :], grad)
            sums[0] = sums[0] + jnp.sum(grad * unit, 0, keepdims=True)
            sums[1] = sums[1] + jnp.sum(grad, 0, keepdims=True)
            for place, lane, width in lane_parts(C):
                value = back[:, lane : lane + width]
                if width < LANES:
                    value = jnp.concatenate([value, jnp.zeros((half, LANES - width), jnp.float32)], 1)
                planes_ref[place, pl.ds(4 * part_at * half + sub, half, stride=4), :] = value
    dgain_ref[0:1, :] = sums[0]
    dgain_ref[1:2, :] = sums[1]
    for place, lane, width in lane_parts(C):
        turned_ref[lane : lane + width, :] = planes_ref[place].T[:width, :].astype(jnp.bfloat16)
    split = patches_ref.shape[0]
    grads = product(turned_ref[:, :split], patches_ref[...]) + product(turned_ref[:, split:], halo_ref[...])
    unit_ref[0, :PIN, :] = grads.T.astype(jnp.bfloat16)
    taps_ref[...] = jnp.zeros_like(taps_ref)
    for layer_at, ref in enumerate(taps_refs):
        for quarter in range(FF // C):
            for place, lane, width in lane_parts(C):
                begin = quarter * C + lane
                value = ref[:, begin : begin + width]
                if width < LANES:
                    value = jnp.concatenate([value, jnp.zeros((9, LANES - width), jnp.float32)], 1)
                taps_ref[place, pl.ds(layer_at * (used // BLOCKS) + quarter, 9, stride=FF // C), :] = value
    for place, lane, width in lane_parts(C):
        unit_ref[0, PIN:, lane : lane + width] = taps_ref[place, :, :width].astype(jnp.bfloat16)


def embed_backward(grad, pre, gains, patches, halo, taps):
    rows = pre.shape[0]
    shapes = (jax.ShapeDtypeStruct((1, FF, C), jnp.bfloat16), jax.ShapeDtypeStruct((2, C), jnp.float32))
    operands = (grad, pre, gains, patches, halo, *taps)
    return pl.pallas_call(
        embed_backward_kernel,
        grid=(1,),
        out_shape=shapes,
        in_specs=[whole(part.shape) for part in operands],
        out_specs=tuple(whole(shape.shape) for shape in shapes),
        scratch_shapes=[
            pltpu.VMEM((3, rows, LANES), jnp.float32),
            pltpu.VMEM((C, rows), jnp.bfloat16),
            pltpu.VMEM((3, FF - PIN, LANES), jnp.float32),
        ],
        compiler_params=pltpu.CompilerParams(vmem_limit_bytes=VMEM_LIMIT),
        cost_estimate=pl.CostEstimate(flops=10**9, bytes_accessed=8 * 10**6, transcendentals=0),
        name="embed_backward",
    )(*operands)


def head_kernel(
    resid_ref, gains_ref, weight_ref, mark_ref, total_ref,
    grad_ref, dhead_ref, dgain_ref, loss_ref,
    final_ref, turned_ref,
):
    rows = resid_ref.shape[0]
    tiles = rows // 4
    classes = weight_ref.shape[1]
    low = weight_ref[...].astype(jnp.bfloat16)
    share = 1.0 / total_ref[0:1, 0:1]
    sums = [jnp.zeros((1, C), jnp.float32)] * 2
    loss = jnp.zeros((1, 1), jnp.float32)
    for sub in range(4):
        span = slice(sub * tiles, (sub + 1) * tiles)
        unit, inverse, final = norm_rows(resid_ref[span, :], gains_ref[0:1, :], gains_ref[1:2, :])
        final = final.astype(jnp.bfloat16)
        final_ref[span, :] = final
        logits = product(final, low)
        peak = jnp.max(logits, -1, keepdims=True)
        log_norm = peak + jnp.log(jnp.sum(jnp.exp(logits - peak), -1, keepdims=True))
        keep = mark_ref[span, 1:2]
        hit = lax.broadcasted_iota(jnp.int32, (tiles, classes), 1).astype(jnp.float32) == mark_ref[span, 0:1]
        picked = jnp.sum(jnp.where(hit, logits, 0.0), -1, keepdims=True)
        loss = loss + jnp.sum((log_norm - picked) * keep, 0, keepdims=True)
        dlogits = (jnp.exp(logits - log_norm) - jnp.where(hit, 1.0, 0.0)) * (keep * share)
        turned_ref[:, span] = dlogits.T.astype(jnp.bfloat16)
        grad = back_product(dlogits.astype(jnp.bfloat16), low)
        grad_ref[span, :] = norm_rows_back(unit, inverse, gains_ref[0:1, :], grad)
        sums[0] = sums[0] + jnp.sum(grad * unit, 0, keepdims=True)
        sums[1] = sums[1] + jnp.sum(grad, 0, keepdims=True)
    dhead_ref[:classes, :] = product(turned_ref[...], final_ref[...])
    dhead_ref[classes:, :] = jnp.zeros((dhead_ref.shape[0] - classes, C), jnp.float32)
    dgain_ref[0:1, :] = sums[0]
    dgain_ref[1:2, :] = sums[1]
    loss_ref[...] = jnp.broadcast_to(loss, (1, C))


def head_step(resid, gains, weight, marks, total):
    rows = resid.shape[0]
    classes = weight.shape[1]
    wide = jnp.float32
    shapes = (
        jax.ShapeDtypeStruct((rows, C), wide),
        jax.ShapeDtypeStruct((-(-classes // 8) * 8, C), wide),
        jax.ShapeDtypeStruct((2, C), wide),
        jax.ShapeDtypeStruct((1, C), wide),
    )
    operands = (resid, gains, weight, marks, total)
    return pl.pallas_call(
        head_kernel,
        grid=(1,),
        out_shape=shapes,
        in_specs=[whole(part.shape) for part in operands],
        out_specs=tuple(whole(shape.shape) for shape in shapes),
        scratch_shapes=[
            pltpu.VMEM((rows, C), jnp.bfloat16),
            pltpu.VMEM((classes, rows), jnp.bfloat16),
        ],
        compiler_params=pltpu.CompilerParams(vmem_limit_bytes=VMEM_LIMIT),
        cost_estimate=pl.CostEstimate(flops=10**9, bytes_accessed=5 * 10**6, transcendentals=10**6),
        name="head_step",
    )(*operands)


def attention_backward_kernel(
    advance,
    grad_ref, resid_ref, gains_ref, unit_ref, reduce_ref, bias_ref,
    normed_ref, query_ref, reduced_ref, key_ref, value_ref, attended_ref, kv_ref,
    out_ref, dunits_ref, dgain_ref,
    turned_ref, datt_ref, dquery_ref, dkey_ref, dvalue_ref, first_ref, planes_ref,
):
    rows = resid_ref.shape[0]
    tiles = rows // 4
    low_type = jnp.bfloat16
    advance(0)
    datt_ref[:, C:] = jnp.zeros((rows, WIDE - C), low_type)
    turned_ref[...] = grad_ref[...].astype(low_type).T
    dunits_ref[0, C : 2 * C, :] = product(turned_ref[...], attended_ref[:, :C]).T.astype(low_type)
    for sub in range(4):
        span = slice(sub * tiles, (sub + 1) * tiles)
        datt_ref[span, :C] = back_product(grad_ref[span, :].astype(low_type), unit_ref[0, C : 2 * C, :]).astype(low_type)
    dkey_ref[...] = jnp.zeros_like(dkey_ref)
    dvalue_ref[...] = jnp.zeros_like(dvalue_ref)
    blocks = bias_ref.shape[0]

    def one_block(step):
        index = blocks - 1 - step
        start, low = place_of(index, tiles)
        bias = bias_ref[index]
        tile_at = lax.rem(lax.broadcasted_iota(jnp.int32, (4 * BLOCK_TILES, LANES), 0), BLOCK_TILES)
        fresh = tile_at >= index * BLOCK_TILES - start
        span = pl.ds(low, KEY_SPAN)
        for group in range(3):
            lanes = slice(group * LANES, (group + 1) * LANES)
            query = four_planes(query_ref, start, lanes)
            datt = four_planes(datt_ref, start, lanes)
            datt = jnp.where(fresh, datt, jnp.zeros_like(datt))
            keys = head_pair(key_ref[span, lanes], group)
            values = head_pair(value_ref[span, lanes], group)
            probs = softmax_columns(back_product(keys, query), bias)
            dprobs = back_product(values, datt)
            dscores = []
            for half, prob in enumerate(probs):
                dprob = dprobs[half * KEY_SPAN : (half + 1) * KEY_SPAN]
                inner = jnp.sum(prob * dprob, 0, keepdims=True)
                dscores.append(prob * (dprob - inner) * HD ** (-0.5))
            dscores = jnp.concatenate(dscores, 0)
            probs = jnp.concatenate(probs, 0).astype(low_type)
            dscores = dscores.astype(low_type)
            dquery = product(dscores.T, keys)
            put_planes(dquery_ref, start, lanes, dquery.astype(low_type))
            dkeys = product(dscores, query)
            dvalues = product(probs, datt)
            if group < 2:
                first = lax.broadcasted_iota(jnp.int32, (KEY_SPAN, LANES), 1) < HD
                dkeys = jnp.where(first, dkeys[:KEY_SPAN], dkeys[KEY_SPAN:])
                dvalues = jnp.where(first, dvalues[:KEY_SPAN], dvalues[KEY_SPAN:])
            dkey_ref[span, lanes] += dkeys
            dvalue_ref[span, lanes] += dvalues

    pl.loop(0, blocks // 2, unroll=blocks // 2)(one_block)
    advance(1)
    pl.loop(blocks // 2, blocks, unroll=blocks - blocks // 2)(one_block)
    unit, inverse, normed = norm_rows(reduced_ref[...], gains_ref[2:3, :], gains_ref[3:4, :])
    normed_t = normed.T.astype(low_type)
    dkeys = dkey_ref[:, :C].astype(low_type)
    dvalues = dvalue_ref[:, :C].astype(low_type)
    for which, grads in enumerate((dkeys, dvalues)):
        dweight = product(normed_t, grads)
        for at, lane, width in lane_parts(C):
            part = dweight[:, lane : lane + width]
            if width < LANES:
                part = jnp.concatenate([part, jnp.zeros((C, LANES - width), jnp.float32)], 1)
            planes_ref[at, pl.ds(which, C, stride=2), :] = part
    for at, lane, width in lane_parts(C):
        dunits_ref[0, 2 * C :, lane : lane + width] = planes_ref[at, :, :width].astype(low_type)
    dnormed = back_product(dkeys, kv_ref[0]) + back_product(dvalues, kv_ref[1])
    dgain_ref[2:3, :] = jnp.sum(dnormed * unit, 0, keepdims=True)
    dgain_ref[3:4, :] = jnp.sum(dnormed, 0, keepdims=True)
    dreduced = norm_rows_back(unit, inverse, gains_ref[2:3, :], dnormed).astype(low_type)
    advance(2)
    turned_ref[...] = normed_ref[...].T
    dunits_ref[0, :C, :] = product(turned_ref[...], dquery_ref[:, :C]).astype(low_type)
    for sub in range(4):
        span = slice(sub * tiles, (sub + 1) * tiles)
        part = slice(sub * C, (sub + 1) * C)
        dunits_ref[1, part, :] = outer_sum(normed_ref[span, :], dreduced).astype(low_type)
        first_ref[span, :] = back_product(
            dquery_ref[span, :C], unit_ref[0, :C, :]
        ) + back_product(dreduced, reduce_ref[0, part, :])

    grad = first_ref[...]
    unit, inverse, _ = norm_rows(resid_ref[...], gains_ref[0:1, :], gains_ref[1:2, :])
    out_ref[...] = grad_ref[...] + norm_rows_back(unit, inverse, gains_ref[0:1, :], grad)
    dgain_ref[0:1, :] = jnp.sum(grad * unit, 0, keepdims=True)
    dgain_ref[1:2, :] = jnp.sum(grad, 0, keepdims=True)


def attention_backward(grad, resid, gains, units, at, reduces, reduce_at, bias, kept, plans, meeting):
    rows = resid.shape[0]
    tiles = rows // 4
    low = jnp.bfloat16
    shapes = (
        jax.ShapeDtypeStruct((rows, C), jnp.float32),
        jax.ShapeDtypeStruct((2, FF, C), low),
        jax.ShapeDtypeStruct((4, C), jnp.float32),
    )
    count = len(plans)

    def run(*refs):
        own_in, ride_in = refs[:13], refs[13 : 13 + count]
        own_out, ride_out = refs[13 + count : 16 + count], refs[16 + count : 16 + 2 * count]
        rest = refs[16 + 2 * count :]
        rides = rides_of(plans, ride_in, ride_out, rest[7:])
        rides.signal()
        attention_backward_kernel(rides.advance, *own_in, *own_out, *rest[:7])
        for phase in range(3, rides.phases + 1):
            rides.advance(phase)

    return pl.pallas_call(
        run,
        grid=(1,),
        out_shape=shapes + tuple(plan.out for plan in plans),
        in_specs=[
            whole((rows, C)),
            whole((rows, C)),
            whole((4, C)),
            unit_spec(at),
            unit_spec(reduce_at),
            whole(bias.shape),
        ]
        + [whole(part.shape) for part in kept]
        + [plan.in_spec for plan in plans],
        out_specs=tuple(whole(shape.shape) for shape in shapes) + tuple(plan.out_spec for plan in plans),
        scratch_shapes=[
            pltpu.VMEM((C, rows), low),
            pltpu.VMEM((rows, WIDE), low),
            pltpu.VMEM((rows, WIDE), low),
            pltpu.VMEM((tiles, WIDE), jnp.float32),
            pltpu.VMEM((tiles, WIDE), jnp.float32),
            pltpu.VMEM((rows, C), jnp.float32),
            pltpu.VMEM((3, 2 * C, LANES), jnp.float32),
        ]
        + sum([plan.scratch for plan in plans], []),
        compiler_params=pltpu.CompilerParams(collective_id=meeting, has_side_effects=True, vmem_limit_bytes=VMEM_LIMIT),
        cost_estimate=pl.CostEstimate(flops=12 * 10**9, bytes_accessed=18 * 10**6, transcendentals=10**6),
        name="attention_backward",
    )(grad, resid, gains, units, reduces, bias, *kept, *[plan.value for plan in plans])


BOTH = ("grp", "tok")


def axis_bits(axis):
    count = lax.axis_size(axis)
    return [1 << place for place in reversed(range(count.bit_length() - 1))]


def bit_order():
    tok_bits = axis_bits("tok")
    return [("grp", bit) for bit in axis_bits("grp")] + [("tok", bit) for bit in tok_bits]


MESH = pl.DeviceIdType.MESH


def exchange_setup():
    grp, tok = lax.axis_index("grp"), lax.axis_index("tok")
    n_tok = lax.axis_size("tok")
    peers = [(lax.bitwise_xor(grp, bit), tok) for bit in axis_bits("grp")]
    peers += [(grp, lax.bitwise_xor(tok, step)) for step in range(1, n_tok)]
    return (grp, tok, n_tok, peers)


def signal_all(peers):
    barrier = pltpu.get_barrier_semaphore()
    for peer in peers:
        pl.semaphore_signal(barrier, inc=1, device_id=peer, device_id_type=MESH)


def greet(peers):
    signal_all(peers)
    pl.semaphore_wait(pltpu.get_barrier_semaphore(), len(peers))


def send(source, target, sems, at, peer):
    copy = pltpu.make_async_remote_copy(
        src_ref=source,
        dst_ref=target,
        send_sem=sems[0].at[at],
        recv_sem=sems[1].at[at],
        device_id=peer,
        device_id_type=MESH,
    )
    copy.start()
    return copy


def gather_view(ref, unit, place, done):
    index = [slice(None) if name in done else place(name) for name in bit_order()]
    return ref.at[tuple([unit] + index)]


class GatherRide:
    def __init__(self, full_ref, scratch):
        self.grp, self.tok = lax.axis_index("grp"), lax.axis_index("tok")
        self.phases = len(bit_order())
        self.names = bit_order()
        self.full_ref = full_ref
        self.sems = scratch[:2]

    def order(self, unit):
        grp_bits = [("grp", bit) for bit in axis_bits("grp")]
        flip = grp_bits[::-1] if unit % 2 else grp_bits
        return [("tok", bit) for bit in axis_bits("tok")[:-1]] + flip + [("tok", 1)]

    def place(self, name):
        return (self.grp if name[0] == "grp" else self.tok) // name[1] % 2

    def partner(self, name):
        axis, bit = name
        if axis == "grp":
            return (lax.bitwise_xor(self.grp, bit), self.tok)
        return (self.grp, lax.bitwise_xor(self.tok, bit))

    def copy(self, unit, phase):
        order = self.order(unit)
        held = gather_view(self.full_ref, unit, self.place, order[:phase])
        at = phase * self.full_ref.shape[0] + unit
        return pltpu.make_async_remote_copy(
            src_ref=held,
            dst_ref=held,
            send_sem=self.sems[0].at[at],
            recv_sem=self.sems[1].at[at],
            device_id=self.partner(order[phase]),
            device_id_type=MESH,
        )

    def put(self, unit, value):
        self.full_ref[(unit,) + tuple(self.place(name) for name in bit_order())] = value

    def advance(self, phase):
        for unit in range(self.full_ref.shape[0]):
            if phase:
                self.copy(unit, phase - 1).wait()
            if phase < self.phases:
                self.copy(unit, phase).start()


def gather_scratch(total):
    phases = len(bit_order())
    return [pltpu.SemaphoreType.DMA((phases * total,))] * 2


def slot_numbers(owner_ref, slot_rows):
    owners = [owner_ref[unit] for unit in range(owner_ref.shape[0])]
    slots = []
    for unit, owner in enumerate(owners):
        rank = jnp.int32(0)
        for earlier in owners[:unit]:
            rank = rank + (earlier == owner).astype(jnp.int32)
        slots.append(owner * slot_rows + rank)
    return slots


def start_kernel(
    owner_ref, piece_ref, count_ref, patch_ref, mark_ref,
    full_ref, later_ref, total_ref, patch_halo_ref, mark_halo_ref, scalar_ref,
    recv_ref, near_s, near_r, halo_s, halo_r, *scratch,
):
    grp, tok, n_tok, peers = exchange_setup()
    slot_rows = piece_ref.shape[1]
    units, first = owner_ref.shape[0], full_ref.shape[0]
    slots = slot_numbers(owner_ref, slot_rows)
    gather = GatherRide(full_ref, scratch[:2])
    count = SumRide(count_ref, total_ref, scratch[2:])
    greet(peers)
    copies = []
    for step in range(1, n_tok):
        peer = lax.bitwise_xor(tok, step)
        landing = recv_ref.at[pl.ds(tok * slot_rows, slot_rows)]
        copies.append(send(piece_ref.at[peer], landing, (near_s, near_r), step, (grp, peer)))
    recv_ref[pl.ds(tok * slot_rows, slot_rows)] = piece_ref[tok]
    count.advance(0)
    for copy in copies:
        copy.wait()
    for unit in range(first):
        gather.put(unit, recv_ref[slots[unit]])
    gather.advance(0)
    before = (grp, lax.rem(tok + n_tok - 1, n_tok))
    mark_copy = send(mark_ref, mark_halo_ref, (halo_s, halo_r), 0, before)
    patch_copy = send(patch_ref.at[pl.ds(0, patch_halo_ref.shape[0])], patch_halo_ref, (halo_s, halo_r), 1, before)
    for unit in range(first, units):
        later_ref[unit - first] = recv_ref[slots[unit]]
    for phase in range(1, gather.phases + 1):
        count.advance(phase)
        gather.advance(phase)
    total_ref[...] = jnp.broadcast_to(
        jnp.sum(jnp.sum(total_ref[...], 0, keepdims=True), 1, keepdims=True), total_ref.shape
    )
    scalar_ref[...] = total_ref[0:1, 0:1]
    mark_copy.wait()
    patch_copy.wait()


def start_exchange(owners, pieces, count, patches, marks, first):
    n_tok, slot_rows, chunk, width = pieces.shape
    phases = len(bit_order())
    units = owners.shape[0]
    vmem = pl.BlockSpec(memory_space=pltpu.VMEM)
    full_shape = (first,) + (2,) * phases + (chunk, width)
    return pl.pallas_call(
        start_kernel,
        out_shape=(
            jax.ShapeDtypeStruct(full_shape, pieces.dtype),
            jax.ShapeDtypeStruct((units - first, chunk, width), pieces.dtype),
            jax.ShapeDtypeStruct(count.shape, count.dtype),
            jax.ShapeDtypeStruct((OVER, patches.shape[1]), patches.dtype),
            jax.ShapeDtypeStruct(marks.shape, marks.dtype),
            jax.ShapeDtypeStruct((1, 1), jnp.float32),
        ),
        in_specs=[pl.BlockSpec(memory_space=pltpu.SMEM), vmem, vmem, pl.BlockSpec(memory_space=pl.ANY), vmem],
        out_specs=(vmem, vmem, vmem, pl.BlockSpec(memory_space=pl.ANY), vmem, vmem),
        scratch_shapes=[
            pltpu.VMEM((n_tok * slot_rows, chunk, width), pieces.dtype),
            pltpu.SemaphoreType.DMA((n_tok,)),
            pltpu.SemaphoreType.DMA((n_tok,)),
            pltpu.SemaphoreType.DMA((2,)),
            pltpu.SemaphoreType.DMA((2,)),
        ]
        + gather_scratch(first)
        + sum_scratch(count.shape),
        compiler_params=pltpu.CompilerParams(collective_id=0, has_side_effects=True, vmem_limit_bytes=VMEM_LIMIT),
        name="start_exchange",
    )(owners, pieces, count, patches, marks)


def unit_order(unit):
    grp_bits = [("grp", bit) for bit in axis_bits("grp")]
    if unit % 2:
        grp_bits = grp_bits[::-1]
    return [("tok", 1)] + grp_bits + [("tok", bit) for bit in axis_bits("tok")[:-1][::-1]]


def unit_layout(order):
    left = bit_order()
    shapes = []
    for name in order:
        at = left.index(name)
        shapes.append((1 << at, 2, 1 << (len(left) - 1 - at)))
        left.remove(name)
    return shapes


SPLIT = 3


class UnitRide:
    def __init__(self, sources, out_ref, scratch, begin=0, end=None, base=0):
        self.grp, self.tok = lax.axis_index("grp"), lax.axis_index("tok")
        self.begin = begin
        self.end = len(bit_order()) if end is None else end
        self.phases = self.end - begin
        self.names = unit_order(0)[self.begin : self.end]
        self.sources = sources
        self.out_ref, self.base = out_ref, base
        self.sems = scratch[:2]
        self.stays = []
        if begin == 0:
            self.stay_sem, self.stays = scratch[2], scratch[3 : 3 + len(sources)]
            scratch = scratch[1 + len(sources) :]
        self.buffers = scratch[2:]

    def partner(self, name):
        axis, bit = name
        if axis == "grp":
            return (lax.bitwise_xor(self.grp, bit), self.tok)
        return (self.grp, lax.bitwise_xor(self.tok, bit))

    def half_of(self, name):
        return (self.grp if name[0] == "grp" else self.tok) // name[1] % 2

    def before(self, unit, phase):
        if phase == 0:
            ref, at = self.sources[unit]
            return ref.at[at]
        return self.buffers[unit * 2 * self.phases + 2 * (phase - 1) + 1]

    def landing(self, unit, phase):
        return self.buffers[unit * 2 * self.phases + 2 * phase]

    def copy(self, unit, phase):
        name = unit_order(unit)[self.begin + phase]
        at = phase * len(self.sources) + unit
        return pltpu.make_async_remote_copy(
            src_ref=self.before(unit, phase).at[:, 1 - self.half_of(name)],
            dst_ref=self.landing(unit, phase),
            send_sem=self.sems[0].at[at],
            recv_sem=self.sems[1].at[at],
            device_id=self.partner(name),
            device_id_type=MESH,
        )

    def stay(self, unit):
        mine = self.half_of(unit_order(unit)[0])
        source = self.before(unit, 0).at[:, mine]
        return pltpu.make_async_copy(source, self.stays[unit], self.stay_sem.at[unit])

    def finish(self, unit, phase):
        order = unit_order(unit)
        shapes = unit_layout(order)
        self.copy(unit, phase).wait()
        outer, _, inner = shapes[self.begin + phase]
        landed = self.landing(unit, phase)
        kept = self.stays and phase == 0
        if kept:
            self.stay(unit).wait()
        source = self.stays[unit] if kept else self.before(unit, phase)
        mine = self.half_of(order[self.begin + phase])
        target = self.out_ref.at[self.base + unit]
        if phase + 1 < self.phases:
            target = self.before(unit, phase + 1)
        whole_done = self.begin + phase + 1 == len(order)
        if not whole_done:
            low = shapes[self.begin + phase + 1][2]

        @pl.loop(0, outer * inner, unroll=min(4, outer * inner))
        def _(at):
            own = source[at // inner, at % inner] if kept else source[at // inner, mine, at % inner]
            value = own + landed[at // inner, at % inner]
            if whole_done:
                target[...] = value
            else:
                target[at // (2 * low), at // low % 2, at % low] = value

    def advance(self, phase):
        for unit in range(len(self.sources)):
            if phase:
                self.finish(unit, phase - 1)
            if phase < self.phases:
                self.copy(unit, phase).start()
            if self.stays and phase == 0:
                self.stay(unit).start()


def unit_scratch(total, chunk, width, begin=0, end=None):
    end = len(bit_order()) if end is None else end
    dma = pltpu.SemaphoreType.DMA
    buffers = [dma(((end - begin) * total,)), dma(((end - begin) * total,))]
    if begin == 0:
        outer, _, inner = unit_layout(unit_order(0))[0]
        buffers += [dma((total,))] + [pltpu.VMEM((outer, inner, chunk, width), jnp.bfloat16)] * total
    for unit in range(total):
        shapes = unit_layout(unit_order(unit))
        for phase in range(begin, end):
            outer, _, inner = shapes[phase]
            buffers.append(pltpu.VMEM((outer, inner, chunk, width), jnp.bfloat16))
            following = shapes[phase + 1] if phase + 1 < end else (1, 1, 1)
            buffers.append(pltpu.VMEM(following + (chunk, width), jnp.bfloat16))
    return buffers


def unit_blocks(units):
    chunk = units.shape[1] >> len(bit_order())
    return units.reshape((units.shape[0],) + unit_layout(unit_order(0))[0] + (chunk, units.shape[2]))


class SumRide:
    def __init__(self, source_ref, total_ref, scratch, begin=0, end=None):
        self.grp, self.tok = lax.axis_index("grp"), lax.axis_index("tok")
        self.order = unit_order(0)[begin:end]
        self.names = self.order
        self.phases = len(self.order)
        self.source_ref, self.total_ref = source_ref, total_ref
        self.sums = scratch[2]
        self.sems = scratch[:2]

    partner = UnitRide.partner

    def copy(self, phase):
        return pltpu.make_async_remote_copy(
            src_ref=self.sums.at[2 * phase],
            dst_ref=self.sums.at[2 * phase + 1],
            send_sem=self.sems[0].at[phase],
            recv_sem=self.sems[1].at[phase],
            device_id=self.partner(self.order[phase]),
            device_id_type=MESH,
        )

    def advance(self, phase):
        if phase == 0:
            self.sums[0] = self.source_ref[...].astype(self.sums.dtype)
        else:
            self.copy(phase - 1).wait()
            self.sums[2 * phase] = self.sums[2 * phase - 2] + self.sums[2 * phase - 1]
        if phase < self.phases:
            self.copy(phase).start()
        else:
            self.total_ref[...] = self.sums[2 * phase].astype(self.total_ref.dtype)


def sum_scratch(shape, dtype=jnp.float32):
    phases = len(bit_order())
    dma = pltpu.SemaphoreType.DMA
    return [dma((phases,)), dma((phases,)), pltpu.VMEM((2 * phases + 1,) + shape, dtype)]


def tail_kernel(counts, rows, pieces, cut, *refs):
    owner_ref, part_ref, refs = refs[0], refs[1], refs[2:]
    early_refs, refs = refs[: len(pieces)], refs[len(pieces) :]
    blocks, refs = refs[: len(counts)], refs[len(counts) :]
    small_refs, refs = refs[: len(rows)], refs[len(rows) :]
    owned_ref, small_out_ref, loss_ref, chunk_ref, place_ref, near_s, near_r, small_ref = refs[:8]
    scratch = refs[8:]
    sources = [(ref, at) for ref, count in zip(blocks, counts) for at in range(count)]
    total = len(sources)
    parts = part_ref.shape[0]
    grp, tok, n_tok, peers = exchange_setup()
    signal_all(peers)
    begin = 0
    for ref, count in zip(small_refs, rows):
        small_ref[begin : begin + count, :] = ref[...]
        begin += count
    small_ref[begin:, :] = jnp.zeros((small_ref.shape[0] - begin, C), jnp.float32)
    rides = Rides(
        [
            UnitRide(sources, chunk_ref, scratch[3:cut]),
            SumRide(small_ref, small_out_ref, scratch[:3]),
            UnitRide([(part_ref, at) for at in range(parts)], chunk_ref, scratch[cut:], SPLIT, None, total),
        ]
    )
    rides.peers = peers
    for phase in range(rides.phases + 1):
        rides.advance(phase)
    total += parts
    loss_ref[...] = small_out_ref[begin - 1 : begin, 0:1]
    last = total
    for ref, count in zip(early_refs, pieces):
        for at in range(count):
            chunk_ref[last + at] = ref[at]
        last += count
    chunk_ref[last] = jnp.zeros(chunk_ref.shape[1:], chunk_ref.dtype)
    slot_rows = owned_ref.shape[1]
    slots = slot_numbers(owner_ref, slot_rows)

    @pl.loop(0, n_tok * slot_rows)
    def _(at):
        unit_at = jnp.int32(last)
        for unit, slot in enumerate(slots):
            unit_at = jnp.where(slot == at, unit, unit_at)
        place_ref[at // slot_rows, at % slot_rows] = chunk_ref[unit_at]

    copies = []
    for step in range(1, n_tok):
        peer = lax.bitwise_xor(tok, step)
        copies.append(send(place_ref.at[peer], owned_ref.at[tok], (near_s, near_r), step, (grp, peer)))
    owned_ref[tok] = place_ref[tok]
    for copy in copies:
        copy.wait()


def tail_exchange(owners, slot_rows, early, part, sources, smalls, n_tok):
    chunk, width = early[0].shape[1:]
    pieces = tuple(value.shape[0] for value in early)
    counts = tuple(source.shape[0] for source in sources)
    rows = tuple(small.shape[0] for small in smalls)
    total = sum(counts)
    low = part.dtype
    vmem = pl.BlockSpec(memory_space=pltpu.VMEM)
    units = unit_scratch(total, chunk, width)
    dma = pltpu.SemaphoreType.DMA
    small = (-(-sum(rows) // 8) * 8, C)
    return pl.pallas_call(
        lambda *refs: tail_kernel(counts, rows, pieces, 3 + len(units), *refs),
        out_shape=(
            jax.ShapeDtypeStruct((n_tok, slot_rows, chunk, width), low),
            jax.ShapeDtypeStruct(small, jnp.float32),
            jax.ShapeDtypeStruct((1, 1), jnp.float32),
        ),
        in_specs=[pl.BlockSpec(memory_space=pltpu.SMEM)]
        + [vmem] * (1 + len(early))
        + [pl.BlockSpec(memory_space=pl.ANY)] * len(sources)
        + [vmem] * len(smalls),
        out_specs=(vmem, vmem, vmem),
        scratch_shapes=[
            pltpu.VMEM((total + part.shape[0] + sum(pieces) + 1, chunk, width), low),
            pltpu.VMEM((n_tok, slot_rows, chunk, width), low),
            dma((n_tok,)),
            dma((n_tok,)),
            pltpu.VMEM(small, jnp.float32),
        ]
        + sum_scratch(small)
        + units
        + unit_scratch(part.shape[0], chunk, width, SPLIT),
        compiler_params=pltpu.CompilerParams(collective_id=1, has_side_effects=True, vmem_limit_bytes=VMEM_LIMIT),
        name="tail_exchange",
    )(owners, part, *early, *[unit_blocks(source) for source in sources], *smalls)


def body(
    patches,
    labels,
    valid_mask,
    crop_counts,
    owners,
    slot_weight,
    slot_moment,
    slot_second,
    norm_params,
    norm_moment,
    norm_second,
    head_weight,
    head_moment,
    head_second,
):
    tok_dev = patches.shape[0]
    n_tok = lax.axis_size("tok")
    n_grp = lax.axis_size("grp")
    tok_index = lax.axis_index("tok")
    group_tok = tok_dev * n_tok
    counts = crop_counts[0]
    n_unit = owners.shape[0]
    slot_rows, columns = slot_weight.shape
    chunk = columns // n_tok // C
    first_tok = tok_index * tok_dev
    small_end = counts[0] * BIG_SIDE**2 + counts[1] * SMALL_SIDE**2
    counted = valid_mask * (first_tok + jnp.arange(tok_dev, dtype=jnp.int32) < small_end)
    counted = counted.astype(jnp.float32).reshape(-1, LANES)
    pieces = slot_weight.astype(jnp.bfloat16).reshape(slot_rows, n_tok, chunk, C).transpose(1, 0, 2, 3)
    first_units = 1 + 2 * (n_unit // BLOCKS)
    marks = jnp.stack([labels, valid_mask])
    own, later, counted, patch_halo, mark_halo, pixel_total = start_exchange(
        owners, pieces, counted, patches, marks[:, :OVER], first_units
    )
    pixel_total = pixel_total.reshape(())
    own = own.reshape(first_units, FF, C)
    units = lax.all_gather(later, BOTH, axis=1, tiled=True)
    layers = [
        ((own, 1, own, 2), (own, 3)),
        ((own, 5, own, 6), (own, 7)),
        ((units, 0, units, 1), (units, 2)),
    ]

    window = tok_dev + OVER
    tiles = window // 4
    marks = jnp.concatenate([marks, mark_halo], 1)
    marks = marks.reshape(2, tiles, 4).transpose(0, 2, 1).reshape(2, window)
    labels = marks[0]
    positions = first_tok + 4 * jnp.arange(tiles, dtype=jnp.int32)
    begin_at, half_side, tile_y, tile_x, is_real = image_layout(positions, counts)
    own_image = (begin_at >= first_tok) & (begin_at < first_tok + tok_dev) & (positions < group_tok)
    stacks = shift_stacks(half_side, tile_y, tile_x, is_real)

    def image_at(tile):
        at = first_tok + 4 * tile
        return jnp.where(at < group_tok, image_layout(at, counts)[0], -1)

    bias = block_bias(tiles, image_at)
    real_rows = jnp.broadcast_to(is_real.astype(jnp.float32)[:, None], (tiles, LANES))
    keep_mask = marks[1].astype(jnp.float32) * jnp.tile((own_image & is_real).astype(jnp.float32), 4)
    tail = 6 * BLOCKS
    embed_pre, resid, kernels = embed_forward(patches, patch_halo, own, norm_params[tail : tail + 2])
    kept_all = []
    for layer_at in range(BLOCKS):
        attn_units, mlp_units = layers[layer_at]
        at = 6 * layer_at
        middle, *attn_kept = attention_forward(resid, norm_params[at : at + 4], *attn_units, bias)
        output, *mlp_kept = mlp_forward(
            middle, norm_params[at + 4 : at + 6], *mlp_units, kernels, layer_at, stacks, real_rows,
        )
        w_up = mlp_kept.pop()
        kept_all.append((resid, attn_kept, middle, mlp_kept, w_up))
        resid = output
    grad_res, d_head, final_gains, loss_row = head_step(
        resid, norm_params[tail + 2 : tail + 4], head_weight, jnp.stack([labels.astype(jnp.float32), keep_mask], 1), counted
    )
    unit_plans = []
    head_cuts = [0, SPLIT, len(bit_order())]
    early = []
    kernel_grads = [None] * BLOCKS
    gain_grads = []
    phases = len(bit_order())

    def head_plans(value):
        if len(head_cuts) < 2:
            return []
        begin = head_cuts.pop(0)
        return [plan_sum(value, begin, head_cuts[0])]

    for layer_at in reversed(range(BLOCKS)):
        attn_units, mlp_units = layers[layer_at]
        at = 6 * layer_at
        entry, attn_kept, middle, mlp_kept, w_up = kept_all[layer_at]
        grad_res, mlp_grads, kernel_grads[layer_at], mlp_gains, *ridden_out = mlp_backward(
            grad_res, middle, norm_params[at + 4 : at + 6], w_up, *mlp_units, kernels, layer_at,
            stacks, real_rows, mlp_kept, unit_plans + head_plans(d_head), 2 + layer_at,
        )
        if layer_at + 1 == BLOCKS:
            d_head = ridden_out.pop()
        unit_plans = [plan_units(mlp_grads, 0, SPLIT)]
        if ridden_out:
            early.insert(0, ridden_out[1])
            unit_plans.append(plan_units(ridden_out[0], SPLIT, phases))
        plans = unit_plans + head_plans(d_head)
        grad_res, attn_grads, attn_gains, *ridden_out = attention_backward(
            grad_res, entry, norm_params[at : at + 4], *attn_units, bias, attn_kept, plans, 2 + BLOCKS + layer_at
        )
        if len(plans) > len(unit_plans):
            d_head = ridden_out.pop()
        if layer_at + 1 < BLOCKS:
            early.insert(0, ridden_out[1])
        unit_plans = [plan_units(attn_grads, 0, SPLIT), plan_units(ridden_out[0], SPLIT, phases)]
        gain_grads = [attn_gains, mlp_gains] + gain_grads
    head_total = d_head[: head_weight.shape[1]].T
    part = ridden_out[0]
    first_grad, embed_gains = embed_backward(
        grad_res, embed_pre, norm_params[tail : tail + 2], patches, patch_halo, kernel_grads
    )
    smalls = gain_grads + [embed_gains, final_gains, loss_row]
    owned, small, loss_sum = tail_exchange(owners, slot_rows, early, part, [first_grad, attn_grads], smalls, n_tok)
    owned = owned.transpose(1, 0, 2, 3).astype(jnp.float32).reshape(slot_rows, columns)
    norm_rows_all = norm_params.shape[0]
    norm_total = small[:norm_rows_all]
    loss_sum = loss_sum.reshape(())
    slot_m, slot_v, slot_w = adamw_step(
        slot_weight, slot_moment, slot_second, owned, RATE_MATRIX, DECAY_RATE
    )
    norm_m, norm_v, norm_w = adamw_step(
        norm_params, norm_moment, norm_second, norm_total, RATE_VECTOR, 0.0
    )
    head_m, head_v, head_w = adamw_step(
        head_weight, head_moment, head_second, head_total, RATE_MATRIX, DECAY_RATE
    )
    return (
        loss_sum,
        pixel_total,
        slot_m,
        slot_v,
        slot_w,
        norm_m,
        norm_v,
        norm_w,
        head_m,
        head_v,
        head_w,
    )


def solution(mesh):
    in_specs = (
        P(("grp", "tok"), None),
        P(("grp", "tok")),
        P(("grp", "tok")),
        P("grp", None),
        P(),
        P("tok", "grp"),
        P("tok", "grp"),
        P("tok", "grp"),
        P(),
        P(),
        P(),
        P(),
        P(),
        P(),
    )
    out_specs = (
        P(),
        P(),
        P("tok", "grp"),
        P("tok", "grp"),
        P("tok", "grp"),
        P(),
        P(),
        P(),
        P(),
        P(),
        P(),
    )
    return jax.shard_map(body, mesh=mesh, in_specs=in_specs, out_specs=out_specs, check_vma=False)
```
